32 devices in a mesh: dp: 8 (over y, x, core), tensor: 4 (over z).
Axes of the slice: x: 2, y: 2, z: 4, core: 2. Of those that a mesh axis runs over, the one named last changes fastest.
Arguments:
- frames: bfloat16 [16384, 1024], P('dp'), may hold values from -6 to 6
- text_states: bfloat16 [24, 128, 768], P('dp'), may hold values from -6 to 6
- clip_lengths: int32 [8, 3], P('dp'), may hold values from 1 to 1024, 2048 in all within a row
- text_lengths: int32 [8, 3], P('dp'), may hold values from 5 to 120
- norm_gains: float32 [3, 1024], replicated, may hold values from 0.25 to 1.75
- norm_biases: float32 [3, 1024], replicated, may hold values from -2 to 2
- self_qkv: bfloat16 [1024, 3072], P(None, 'tensor'), may hold values from -0.1875 to 0.1875
- self_out: bfloat16 [1024, 1024], P('tensor'), may hold values from -0.75 to 0.75
- cross_query: bfloat16 [1024, 1024], P(None, 'tensor'), may hold values from -0.1875 to 0.1875
- cross_kv: bfloat16 [768, 2048], P(None, 'tensor'), may hold values from -0.21875 to 0.21875
- cross_out: bfloat16 [1024, 1024], P('tensor'), may hold values from -0.75 to 0.75
- ffn_in: bfloat16 [1024, 4096], P(None, 'tensor'), may hold values from -0.1875 to 0.1875
- ffn_out: bfloat16 [4096, 1024], P('tensor'), may hold values from -0.09375 to 0.09375
- out_grad: bfloat16 [16384, 1024], P('dp'), may hold values from -6 to 6
Outputs:
- mixed: bfloat16 [16384, 1024], P(('dp', 'tensor'))
- frames_grad: bfloat16 [16384, 1024], P(('dp', 'tensor'))
- text_grad: float32 [24, 128, 768], P('dp', None, 'tensor')
- norm_grads: float32 [2, 3, 1024], P(None, None, 'tensor')
- self_qkv_grad: float32 [1024, 3072], P(None, 'tensor')
- self_out_grad: float32 [1024, 1024], P('tensor')
- cross_query_grad: float32 [1024, 1024], P(None, 'tensor')
- cross_kv_grad: float32 [768, 2048], P(None, 'tensor')
- cross_out_grad: float32 [1024, 1024], P('tensor')
- ffn_in_grad: float32 [1024, 4096], P(None, 'tensor')
- ffn_out_grad: float32 [4096, 1024], P('tensor')
The draws below stay inside these ranges and needn't reach their ends.
Inputs may be any that keep to these rules, and one draw needn't show every extreme that they name: `clip_lengths`: each row holds 3 clip lengths summing to 2048; its longest clip has exactly 1024 frames.
All inputs are finite; a program needn't handle non-finite values.
Results may differ from the reference program's by a relative error of at most 0.03.
Values may be sent and summed in bfloat16 or wider, within the bound.
No kernel may reach another device: no remote copies, remote signals or barrier semaphores. Data moves between devices by JAX's collectives and lax.ppermute only.
A program may use at most 192 MiB of HBM per device.

```python
import math
import jax
import jax.numpy as jnp
import numpy as np
from jax import lax

D = 1024
HEADS = 16
HEAD = 64
FF = 4096
ENC = 768
TXT = 128
TOK_DEV = 2048
CLIPS = 3
MOST = 1024
TOKENS = 16384
ALL_CLIPS = 24
N_DP = 8
N_TENSOR = 4


def place_ends(drawn, own_key, smallest, high):
    spot = [jax.random.randint(jax.random.fold_in(own_key, axis), (), 0, length) for axis, length in enumerate(drawn.shape)]
    longest = drawn.shape.index(max(drawn.shape))
    neighbour = spot[:longest] + [(spot[longest] + 1) % drawn.shape[longest]] + spot[longest + 1:]
    return drawn.at[tuple(spot)].set(smallest).at[tuple(neighbour)].set(high)


def levels(key, extent, shards, least, top_value):
    def one(position, blocks):
        steps = jax.random.uniform(jax.random.fold_in(jax.random.fold_in(key, 6), position), (blocks,), jnp.float32, least / len(shards), top_value / len(shards))
        return jnp.repeat(jnp.exp(steps), extent[position] // blocks).reshape((-1,) + (1,) * (len(extent) - position - 1))

    factor_of = one(*shards[0])
    for cut in shards[1:]:
        factor_of = factor_of * one(*cut)
    return factor_of


def split_up(number_of, total, reach, lean):
    loads = [(1 << 20) // math.isqrt(standing ** lean) + 1 for standing in range(2, number_of + 1)]
    rest, holding = total - reach - (number_of - 1), [1] * (number_of - 1)
    while rest > 0:
        free = [i for i in range(number_of - 1) if holding[i] < reach]
        mass, budget = sum([loads[i] for i in free]), rest
        for i in free:
            addition = min(reach - holding[i], max(1, budget * loads[i] // mass), rest)
            holding[i] = holding[i] + addition
            rest = rest - addition
    return np.array([reach] + holding)


def ragged(own_key, count, total, most, slope):
    if count == 2:
        one = jax.random.randint(own_key, (), max(1, total - most), min(most, total - 1) + 1)
        return jnp.stack([one, total - one])
    sizes = jnp.asarray(split_up(count, total, most, slope), jnp.int32)
    pairs = (count - 1) // 2
    giver, receiver = sizes[1:1 + 2 * pairs:2], sizes[2:2 + 2 * pairs:2]
    slack = jnp.minimum(giver - 1, most - receiver)
    passed = jax.random.randint(jax.random.fold_in(own_key, 1), (pairs,), 0, 1 << 20) % (slack + 1)
    sizes = sizes.at[1:1 + 2 * pairs:2].set(giver - passed).at[2:2 + 2 * pairs:2].set(receiver + passed)
    return sizes[jax.random.permutation(jax.random.fold_in(own_key, 2), count)]


def bell_draw(own_key, extent, deviation, reach, pieces=(), kind=jnp.bfloat16):
    level = levels(own_key, extent, pieces, -0.22, 0.18) if pieces else 1.0
    values = jax.random.normal(own_key, extent, jnp.float32) * deviation * level
    return jnp.minimum(jnp.maximum(values, -reach), reach).astype(kind)


def setup_inputs(seed: int = 0) -> dict:
    key_list = jax.random.split(jax.random.key(seed), 15)
    return {
        "frames": bell_draw(key_list[0], (TOKENS, D), 1.0, 6.0, ((0, 8),)),
        "text_states": bell_draw(key_list[1], (ALL_CLIPS, TXT, ENC), 1.0, 6.0, ((0, 8),)),
        "clip_lengths": jax.vmap(lambda own: ragged(own, CLIPS, TOK_DEV, MOST, 2))(jax.random.split(key_list[2], N_DP)).reshape((N_DP, CLIPS)).astype(jnp.int32),
        "text_lengths": place_ends(jax.random.randint(key_list[3], (N_DP, CLIPS), 5, min(TXT, 120) + 1), jax.random.fold_in(key_list[3], 1), 5, min(TXT, 120)).astype(jnp.int32),
        "norm_gains": jnp.clip(1.0 + 0.15 * jax.random.normal(key_list[4], (3, D), jnp.float32), 0.25, 1.75),
        "norm_biases": bell_draw(key_list[5], (3, D), 0.3, 2.0, (), jnp.float32),
        "self_qkv": bell_draw(key_list[6], (D, 3 * HEADS * HEAD), D ** -0.5, 0.1875, ((1, 4),)),
        "self_out": bell_draw(key_list[7], (HEADS * HEAD, D), HEAD ** -0.5, 0.75, ((0, 4),)),
        "cross_query": bell_draw(key_list[8], (D, HEADS * HEAD), D ** -0.5, 0.1875, ((1, 4),)),
        "cross_kv": bell_draw(key_list[9], (ENC, 2 * HEADS * HEAD), ENC ** -0.5, 0.21875, ((1, 4),)),
        "cross_out": bell_draw(key_list[10], (HEADS * HEAD, D), HEAD ** -0.5, 0.75, ((0, 4),)),
        "ffn_in": bell_draw(key_list[11], (D, FF), D ** -0.5, 0.1875, ((1, 4),)),
        "ffn_out": bell_draw(key_list[12], (FF, D), FF ** -0.5, 0.09375, ((0, 4),)),
        "out_grad": bell_draw(key_list[13], (TOKENS, D), 1.0, 6.0, ((0, 8),)),
    }


@jax.custom_vjp
def low(v):
    return lax.optimization_barrier(v.astype(jnp.bfloat16)).astype(jnp.float32)

@jax.custom_vjp
def low_back(v):
    return v

def low_keep(v):
    return (low(v), None)

def low_pass(kept, grad):
    return (grad,)

def back_keep(v):
    return (v, None)

def back_low(kept, grad):
    return (low(grad),)
low.defvjp(low_keep, low_pass)
low_back.defvjp(back_keep, back_low)
HIGHEST_PRECISION = lax.Precision.HIGHEST
EPSILON = 1e-05
NEGATIVE = -1e+30

def normalize(row_values, gain_row, shift_row):
    center = row_values - lax.optimization_barrier(jnp.mean(row_values, axis=1, keepdims=True))
    inverse = lax.rsqrt(lax.optimization_barrier(jnp.mean(center * center, axis=1, keepdims=True)) + EPSILON)
    return center * inverse * gain_row + shift_row

def attention(queries, key_rows, value_rows, allowed):
    frame_count = queries.shape[0]
    block_rows = min(512, frame_count)
    blocks = queries.reshape(frame_count // block_rows, block_rows, queries.shape[1], queries.shape[2])
    starts = jnp.arange(frame_count // block_rows, dtype=jnp.int32) * block_rows

    def single(item):
        q_block, first_row = item
        row_ids = first_row + jnp.arange(block_rows, dtype=jnp.int32)
        scores = low_back(jnp.einsum('bhe,khe->hbk', q_block, key_rows, precision=HIGHEST_PRECISION) * 0.125)
        scores = jnp.where(allowed(row_ids)[None], scores, NEGATIVE)
        weights = low(jax.nn.softmax(scores, axis=2))
        return jnp.einsum('hbk,khe->bhe', weights, value_rows, precision=HIGHEST_PRECISION)
    return lax.map(jax.checkpoint(single), (blocks, starts)).reshape(queries.shape)

def branch_sum(branch_in, weight):
    parts = branch_in.reshape(branch_in.shape[0], N_TENSOR, -1)
    slabs = weight.reshape(N_TENSOR, -1, weight.shape[1])
    running = jnp.zeros((branch_in.shape[0], weight.shape[1]), jnp.float32)
    for group in range(N_TENSOR):
        running = running + low(jnp.dot(parts[:, group], slabs[group], precision=HIGHEST_PRECISION))
    return low_back(running)

def layer(params, frame_rows, text_rows, segment, key_clip, key_live):
    gains, shifts, w_qkv, w_self, w_query, w_pair, w_cross, w_first, w_second = params
    frame_count = frame_rows.shape[0]
    head_count = w_self.shape[0] // HEAD
    positions = jnp.arange(frame_count, dtype=jnp.int32)

    def self_allowed(row_ids):
        return (segment[row_ids][:, None] == segment[None, :]) & (positions[None, :] <= row_ids[:, None])

    def cross_allowed(row_ids):
        return (segment[row_ids][:, None] == key_clip[None, :]) & key_live[None, :]
    first = low(normalize(frame_rows, gains[0], shifts[0]))
    packed = low(low_back(jnp.dot(first, w_qkv, precision=HIGHEST_PRECISION))).reshape(frame_count, head_count, 3, HEAD)
    self_mix = low(low_back(attention(packed[:, :, 0], packed[:, :, 1], packed[:, :, 2], self_allowed)))
    after_self = frame_rows + branch_sum(self_mix.reshape(frame_count, head_count * HEAD), w_self)
    second = low(normalize(after_self, gains[1], shifts[1]))
    cross_q = low(low_back(jnp.dot(second, w_query, precision=HIGHEST_PRECISION))).reshape(frame_count, head_count, HEAD)
    pair = low(low_back(jnp.dot(text_rows, w_pair, precision=HIGHEST_PRECISION))).reshape(text_rows.shape[0], head_count, 2, HEAD)
    cross_mix = low(low_back(attention(cross_q, pair[:, :, 0], pair[:, :, 1], cross_allowed)))
    after_cross = after_self + branch_sum(cross_mix.reshape(frame_count, head_count * HEAD), w_cross)
    third = low(normalize(after_cross, gains[2], shifts[2]))
    hidden = low(jax.nn.gelu(low_back(jnp.dot(third, w_first, precision=HIGHEST_PRECISION)), approximate=False))
    return after_cross + branch_sum(hidden, w_second)

def reference(frames, text_states, clip_lengths, text_lengths, norm_gains, norm_biases, self_qkv, self_out, cross_query, cross_kv, cross_out, ffn_in, ffn_out, out_grad):
    params = (norm_gains.astype(jnp.float32), norm_biases.astype(jnp.float32), self_qkv.astype(jnp.float32), self_out.astype(jnp.float32), cross_query.astype(jnp.float32), cross_kv.astype(jnp.float32), cross_out.astype(jnp.float32), ffn_in.astype(jnp.float32), ffn_out.astype(jnp.float32))
    group_frames = frames.astype(jnp.float32).reshape(N_DP, TOK_DEV, D)
    group_text = text_states.astype(jnp.float32).reshape(N_DP, CLIPS * TXT, ENC)
    group_grad = out_grad.astype(jnp.float32).reshape(N_DP, TOK_DEV, D)
    positions = jnp.arange(TOK_DEV, dtype=jnp.int32)
    key_index = jnp.arange(CLIPS * TXT, dtype=jnp.int32)
    key_clip = (key_index // TXT).astype(jnp.int32)
    key_slot = (key_index % TXT).astype(jnp.int32)
    clip_ids = jnp.arange(CLIPS, dtype=jnp.int32)

    def one_group(totals, item):
        frame_rows, text_rows, grad_rows, lengths, spans = item
        ends = jnp.cumsum(lengths).astype(jnp.int32)
        segment = lax.optimization_barrier(jnp.sum((positions[:, None] >= ends[None, :]).astype(jnp.int32), axis=1)).astype(jnp.int32)
        key_live = jnp.any((key_clip[:, None] == clip_ids[None, :]) & (key_slot[:, None] < spans[None, :]), axis=1)

        def forward(param_set, input_rows, input_text):
            return layer(param_set, input_rows, input_text, segment, key_clip, key_live)
        result, pullback = jax.vjp(forward, params, frame_rows, text_rows)
        grads, frame_grad, text_grad = pullback(grad_rows)
        totals = jax.tree.map(jnp.add, totals, grads)
        return (totals, (result, frame_grad, text_grad))
    zeros = jax.tree.map(jnp.zeros_like, params)
    totals, (result, frame_grad, text_grad) = lax.scan(one_group, zeros, (group_frames, group_text, group_grad, clip_lengths, text_lengths))
    mixed = result.reshape(TOKENS, D).astype(jnp.bfloat16)
    frames_grad = frame_grad.reshape(TOKENS, D).astype(jnp.bfloat16)
    text_out = text_grad.reshape(ALL_CLIPS, TXT, ENC)
    norm_grads = jnp.stack([totals[0], totals[1]])
    return (mixed, frames_grad, text_out, norm_grads, totals[2], totals[3], totals[4], totals[5], totals[6], totals[7], totals[8])
```

```python
import jax
import jax.numpy as jnp
from jax import lax
from jax.sharding import Mesh
from jax.sharding import PartitionSpec as P

HEAD = 64


EPSILON = 1e-05
NEGATIVE = -1e30


def norm_forward(row_values, gain_row, shift_row):
    center = row_values - jnp.mean(row_values, axis=1, keepdims=True)
    inverse = lax.rsqrt(jnp.mean(center * center, axis=1, keepdims=True) + EPSILON)
    unit_part = center * inverse
    return (unit_part * gain_row + shift_row, unit_part, inverse)


def norm_backward(gradient, unit_part, inverse, gain_row):
    scaled = gradient * gain_row
    inner_part = (
        scaled
        - jnp.mean(scaled, axis=1, keepdims=True)
        - unit_part * jnp.mean(scaled * unit_part, axis=1, keepdims=True)
    )
    return (inner_part * inverse, jnp.sum(gradient * unit_part, axis=0), jnp.sum(gradient, axis=0))


def contract_rows(left_side, right_side):
    return lax.dot_general(
        left_side, right_side, (((0,), (0,)), ((), ())), preferred_element_type=jnp.float32
    )


def times_transposed(left_side, right_side):
    return lax.dot_general(
        left_side, right_side, (((1,), (1,)), ((), ())), preferred_element_type=jnp.float32
    )


def masked_scores(q_block, key_rows, allowed, first_row, block_rows):
    scores = (
        jnp.einsum("bhe,khe->hbk", q_block, key_rows, preferred_element_type=jnp.float32) * 0.125
    )
    return jnp.where(allowed(first_row, block_rows)[None], scores, NEGATIVE)


def attend(queries, key_rows, value_rows, allowed):
    frame_count = queries.shape[0]
    block_rows = min(512, frame_count)

    def step(state, block_index):
        first_row = block_index * block_rows
        q_block = lax.dynamic_slice_in_dim(queries, first_row, block_rows, 0)
        scores = masked_scores(q_block, key_rows, allowed, first_row, block_rows)
        row_max = jnp.max(scores, axis=2, keepdims=True)
        exponent = jnp.exp(scores - row_max)
        row_total = jnp.sum(exponent, axis=2, keepdims=True)
        weights = (exponent / row_total).astype(jnp.bfloat16)
        block_out = jnp.einsum(
            "hbk,khe->bhe", weights, value_rows, preferred_element_type=jnp.float32
        )
        return (state, (block_out.astype(jnp.bfloat16), (row_max + jnp.log(row_total))[:, :, 0]))

    _, (block_outs, log_totals) = lax.scan(
        step, 0, jnp.arange(frame_count // block_rows, dtype=jnp.int32)
    )
    return (block_outs.reshape(queries.shape), log_totals)


def attend_back(queries, key_rows, value_rows, log_totals, out_grads, allowed):
    frame_count = queries.shape[0]
    block_rows = min(512, frame_count)
    empty = jnp.zeros(key_rows.shape, jnp.float32)

    def step(state_pair, block_index):
        key_acc, value_acc = state_pair
        first_row = block_index * block_rows
        q_block = lax.dynamic_slice_in_dim(queries, first_row, block_rows, 0)
        grad_block = lax.dynamic_slice_in_dim(out_grads, first_row, block_rows, 0)
        scores = masked_scores(q_block, key_rows, allowed, first_row, block_rows)
        probs = jnp.exp(scores - log_totals[block_index][:, :, None])
        weights = probs.astype(jnp.bfloat16)
        prob_grad = jnp.einsum(
            "bhe,khe->hbk", grad_block, value_rows, preferred_element_type=jnp.float32
        )
        score_grad = (
            probs * (prob_grad - jnp.sum(probs * prob_grad, axis=2, keepdims=True))
        ).astype(jnp.bfloat16)
        query_grad = (
            jnp.einsum("hbk,khe->bhe", score_grad, key_rows, preferred_element_type=jnp.float32)
            * 0.125
        )
        key_acc = (
            key_acc
            + jnp.einsum("hbk,bhe->khe", score_grad, q_block, preferred_element_type=jnp.float32)
            * 0.125
        )
        value_acc = value_acc + jnp.einsum(
            "hbk,bhe->khe", weights, grad_block, preferred_element_type=jnp.float32
        )
        return ((key_acc, value_acc), query_grad.astype(jnp.bfloat16))

    (key_acc, value_acc), query_grads = lax.scan(
        step, (empty, empty), jnp.arange(frame_count // block_rows, dtype=jnp.int32)
    )
    return (
        query_grads.reshape(queries.shape),
        key_acc.astype(jnp.bfloat16),
        value_acc.astype(jnp.bfloat16),
    )


ALL = ("tensor", "chip", "core")


def own_piece(array, count, index):
    size = array.shape[0] // count
    return lax.dynamic_slice_in_dim(array, index * size, size, 0)


def gather(array, axes):
    return lax.all_gather(array, axes, axis=0, tiled=True)


def scatter_sum(array, axes):
    return lax.psum_scatter(array, axes, scatter_dimension=0, tiled=True)


def swap_core(array):
    return lax.ppermute(array, "core", [(0, 1), (1, 0)])


def in_core_order(mine, other):
    first = lax.axis_index("core") == 0
    return jnp.stack([jnp.where(first, mine, other), jnp.where(first, other, mine)])


def dot(left, right):
    return jnp.dot(left, right, preferred_element_type=jnp.float32)


def per_device(
    frames,
    text_states,
    clip_lengths,
    text_lengths,
    norm_gains,
    norm_biases,
    self_qkv,
    self_out,
    cross_query,
    cross_kv,
    cross_out,
    ffn_in,
    ffn_out,
    out_grad,
):
    groups = lax.axis_size("tensor")
    chips = lax.axis_size("chip")
    group = lax.axis_index("tensor")
    chip = lax.axis_index("chip")
    core = lax.axis_index("core")
    bf16 = jnp.bfloat16
    frame_count, width = frames.shape
    own_rows = frame_count // groups
    offset = group * own_rows
    clip_count, text_slots, text_width = text_states.shape
    head_count = self_out.shape[0] // HEAD
    all_heads = head_count * groups
    positions = jnp.arange(frame_count, dtype=jnp.int32)
    ends = jnp.cumsum(clip_lengths[0])
    segment = jnp.sum((positions[:, None] >= ends[None, :]).astype(jnp.int32), axis=1)
    key_index = jnp.arange(clip_count * text_slots, dtype=jnp.int32)
    key_clip = key_index // text_slots
    key_slot = key_index % text_slots
    clip_ids = jnp.arange(clip_count, dtype=jnp.int32)
    key_live = jnp.any(
        (key_clip[:, None] == clip_ids[None, :]) & (key_slot[:, None] < text_lengths[0][None, :]),
        axis=1,
    )

    share = 2 * chips
    place = chip * 2 + core

    def packed_piece(weight):
        return own_piece(weight, share, place).reshape(-1, width)

    small = [packed_piece(w) for w in (self_out, cross_query, cross_kv, cross_out)]
    small_rows = [w.shape[0] for w in small]
    small_all = gather(jnp.concatenate(small, 0), ALL).reshape(groups, share, -1, width)
    cuts = [sum(small_rows[:i]) for i in range(5)]
    w_so, w_cq, w_ckv, w_co = [small_all[:, :, cuts[i] : cuts[i + 1]] for i in range(4)]
    w_so = w_so.reshape(width, width)
    w_co = w_co.reshape(width, width)
    w_cq = w_cq.reshape(groups, width, -1).transpose(1, 0, 2).reshape(width, width)
    w_ckv = w_ckv.reshape(groups, text_width, -1).transpose(1, 0, 2).reshape(text_width, 2 * width)

    half = ffn_out.shape[0] // 2
    piece = half // chips
    unit_first = core * half + chip * piece
    ffn_piece = jnp.concatenate(
        [
            lax.dynamic_slice_in_dim(ffn_in, unit_first, piece, 1).T,
            lax.dynamic_slice_in_dim(ffn_out, unit_first, piece, 0),
        ],
        0,
    )
    ffn_all = gather(ffn_piece, ("tensor", "chip")).reshape(groups, chips, 2, piece, width)
    w_in = ffn_all[:, :, 0].reshape(groups * half, width)
    w_out = ffn_all[:, :, 1].reshape(groups * half, width)
    grad_own_bf = lax.dynamic_slice_in_dim(out_grad, offset, own_rows, 0)
    grad_pair = jnp.concatenate([grad_own_bf, swap_core(grad_own_bf)], 0)

    def self_allowed(first_row, block_rows):
        block_segment = lax.dynamic_slice_in_dim(segment, first_row, block_rows, 0)
        block_ids = first_row + jnp.arange(block_rows, dtype=jnp.int32)
        return (block_segment[:, None] == segment[None, :]) & (
            positions[None, :] <= block_ids[:, None]
        )

    own_segment = lax.dynamic_slice_in_dim(segment, offset, own_rows, 0)

    def cross_allowed(first_row, block_rows):
        block_segment = lax.dynamic_slice_in_dim(own_segment, first_row, block_rows, 0)
        return (block_segment[:, None] == key_clip[None, :]) & key_live[None, :]

    inputs = frames.astype(jnp.float32)
    own_inputs = lax.dynamic_slice_in_dim(inputs, offset, own_rows, 0)
    first_all, _, _ = norm_forward(inputs, norm_gains[0], norm_biases[0])
    _, unit_one, inverse_one = norm_forward(own_inputs, norm_gains[0], norm_biases[0])
    rows_one = first_all.astype(bf16)
    packed = dot(rows_one, self_qkv).astype(bf16).reshape(frame_count, head_count, 3, HEAD)
    queries, key_rows, value_rows = (packed[:, :, 0], packed[:, :, 1], packed[:, :, 2])
    self_mix, self_logs = attend(queries, key_rows, value_rows, self_allowed)
    self_flat = lax.all_to_all(
        self_mix.reshape(frame_count, head_count * HEAD), "tensor", 0, 1, tiled=True
    )

    after_self = own_inputs + dot(self_flat, w_so)
    second_own, unit_two, inverse_two = norm_forward(after_self, norm_gains[1], norm_biases[1])
    rows_two = second_own.astype(bf16)
    cross_q = dot(rows_two, w_cq).astype(bf16).reshape(own_rows, all_heads, HEAD)
    text_flat = text_states.reshape(clip_count * text_slots, text_width)
    pair = (
        dot(text_flat, w_ckv).astype(bf16).reshape(clip_count * text_slots, all_heads, 2, HEAD)
    )
    cross_mix, cross_logs = attend(cross_q, pair[:, :, 0], pair[:, :, 1], cross_allowed)
    cross_flat = cross_mix.reshape(own_rows, width)
    after_cross = after_self + dot(cross_flat, w_co)
    third_own, unit_three, inverse_three = norm_forward(after_cross, norm_gains[2], norm_biases[2])

    rows_three = third_own.astype(bf16)
    rows_pair = jnp.concatenate([rows_three, swap_core(rows_three)], 0)
    hidden_pre = times_transposed(rows_pair, w_in)
    gelu = lambda v: jax.nn.gelu(v, approximate=False)
    hidden_exact, gelu_back = jax.vjp(gelu, hidden_pre)
    hidden = hidden_exact.astype(bf16)
    out_pair = dot(hidden, w_out)
    hidden_grad = times_transposed(grad_pair, w_out)
    pre_grad = gelu_back(hidden_grad)[0].astype(bf16)
    third_pair = dot(pre_grad, w_in)
    result = (
        after_cross
        + out_pair[:own_rows]
        + swap_core(out_pair[own_rows:].astype(bf16)).astype(jnp.float32)
    )
    mixed = result.astype(bf16)
    third_grad = third_pair[:own_rows] + swap_core(third_pair[own_rows:].astype(bf16)).astype(
        jnp.float32
    )

    def spread(grad, parts):
        return grad.reshape(groups, parts, -1, grad.shape[1]).transpose(1, 0, 2, 3)

    ffn_part = jnp.concatenate(
        [
            spread(contract_rows(pre_grad, rows_pair).astype(bf16), chips),
            spread(contract_rows(hidden, grad_pair).astype(bf16), chips),
        ],
        2,
    )
    ffn_sum = gather(
        scatter_sum(scatter_sum(ffn_part, "chip")[0], "tensor"), "chip"
    ).reshape(chips, 2, piece, width)
    ffn_sum = in_core_order(ffn_sum, swap_core(ffn_sum)).astype(jnp.float32)
    ffn_in_grad = ffn_sum[:, :, 0].reshape(2 * half, width).T
    ffn_out_grad = ffn_sum[:, :, 1].reshape(2 * half, width)

    back_three, gain_three, shift_three = norm_backward(
        third_grad, unit_three, inverse_three, norm_gains[2]
    )
    cross_side = grad_own_bf.astype(jnp.float32) + back_three
    cross_grad = cross_side.astype(bf16)
    cross_out_grad = contract_rows(cross_flat, cross_grad)
    cross_mix_grad = (
        times_transposed(cross_grad, w_co).astype(bf16).reshape(own_rows, all_heads, HEAD)
    )
    cq_grad, ck_grad, cv_grad = attend_back(
        cross_q, pair[:, :, 0], pair[:, :, 1], cross_logs, cross_mix_grad, cross_allowed
    )
    cq_flat = cq_grad.reshape(own_rows, width)
    cross_query_grad = contract_rows(cq_flat, rows_two)
    pair_grad = jnp.stack([ck_grad, cv_grad], axis=2).reshape(clip_count * text_slots, 2 * width)
    cross_kv_grad = contract_rows(pair_grad, text_flat)
    text_part = times_transposed(pair_grad, w_ckv)
    back_two, gain_two, shift_two = norm_backward(
        times_transposed(cq_flat, w_cq), unit_two, inverse_two, norm_gains[1]
    )
    self_side = cross_side + back_two
    self_grad = self_side.astype(bf16)
    self_out_grad = contract_rows(self_flat, self_grad)
    self_mix_grad = lax.all_to_all(
        times_transposed(self_grad, w_so).astype(bf16), "tensor", 1, 0, tiled=True
    ).reshape(frame_count, head_count, HEAD)

    small_grads = [self_out_grad, cross_query_grad, cross_kv_grad, cross_out_grad]
    small_part = jnp.concatenate(
        [
            spread(grad.astype(bf16), share).reshape(2, chips, groups, -1, width)
            for grad in small_grads
        ],
        3,
    )
    kept = lax.dynamic_index_in_dim(small_part, core, 0, keepdims=False)
    sent = lax.dynamic_index_in_dim(small_part, 1 - core, 0, keepdims=False)
    small_part = kept + swap_core(sent)
    small_sum = gather(scatter_sum(scatter_sum(small_part, "chip")[0], "tensor"), "chip")
    small_sum = in_core_order(small_sum, swap_core(small_sum)).reshape(share, -1, width)

    def unpacked(index, columns):
        return (
            small_sum[:, cuts[index] : cuts[index + 1]].reshape(-1, columns).astype(jnp.float32)
        )

    query_grad, key_grad, value_grad = attend_back(
        queries, key_rows, value_rows, self_logs, self_mix_grad, self_allowed
    )
    packed_grad = jnp.stack([query_grad, key_grad, value_grad], axis=2).reshape(
        frame_count, head_count * 3 * HEAD
    )
    self_qkv_grad = lax.psum(
        contract_rows(rows_one, packed_grad).astype(bf16), ("chip", "core")
    ).astype(jnp.float32)
    first_grad = scatter_sum(times_transposed(packed_grad, self_qkv).astype(bf16), "tensor").astype(
        jnp.float32
    )
    back_one, gain_one, shift_one = norm_backward(first_grad, unit_one, inverse_one, norm_gains[0])
    frames_grad = (self_side + back_one).astype(bf16)
    norm_part = jnp.stack(
        [
            jnp.stack([gain_one, gain_two, gain_three]),
            jnp.stack([shift_one, shift_two, shift_three]),
        ]
    )
    text_grad = lax.psum_scatter(
        text_part.reshape(clip_count, text_slots, text_width).astype(bf16),
        "tensor",
        scatter_dimension=2,
        tiled=True,
    ).astype(jnp.float32)
    norm_part = lax.psum_scatter(
        lax.psum(norm_part, ("chip", "core")), "tensor", scatter_dimension=2, tiled=True
    )
    return (
        mixed,
        frames_grad,
        text_grad,
        norm_part,
        self_qkv_grad,
        unpacked(0, width),
        unpacked(1, width).T,
        unpacked(2, text_width).T,
        unpacked(3, width),
        ffn_in_grad,
        ffn_out_grad,
    )


def solution(mesh):
    rows, groups = mesh.devices.shape
    inner = Mesh(mesh.devices.reshape(rows // 2, 2, groups), ("chip", "core", "tensor"))
    data = ("chip", "core")
    in_specs = (
        P(data, None),
        P(data, None, None),
        P(data, None),
        P(data, None),
        P(),
        P(),
        P(None, "tensor"),
        P("tensor", None),
        P(None, "tensor"),
        P(None, "tensor"),
        P("tensor", None),
        P(None, "tensor"),
        P("tensor", None),
        P(data, None),
    )
    out_specs = (
        P((*data, "tensor"), None),
        P((*data, "tensor"), None),
        P(data, None, "tensor"),
        P(None, None, "tensor"),
        P(None, "tensor"),
        P("tensor", None),
        P(None, "tensor"),
        P(None, "tensor"),
        P("tensor", None),
        P(None, "tensor"),
        P("tensor", None),
    )
    return jax.shard_map(
        per_device, mesh=inner, in_specs=in_specs, out_specs=out_specs, check_vma=False
    )
```

```python
from functools import partial

import jax
import jax.numpy as jnp
from jax import lax
from jax.experimental import pallas as pl
from jax.experimental.pallas import tpu as pltpu
from jax.sharding import Mesh
from jax.sharding import PartitionSpec as P

HEAD = 64


EPSILON = 1e-05
NEGATIVE = -1e30
VMEM_BYTES = 56 * 1024 * 1024


def norm_forward(row_values, gain_row, shift_row):
    center = row_values - jnp.mean(row_values, axis=1, keepdims=True)
    inverse = lax.rsqrt(jnp.mean(center * center, axis=1, keepdims=True) + EPSILON)
    unit_part = center * inverse
    return (unit_part * gain_row + shift_row, unit_part, inverse)


def norm_backward(gradient, unit_part, inverse, gain_row):
    scaled = gradient * gain_row
    inner_part = (
        scaled
        - jnp.mean(scaled, axis=1, keepdims=True)
        - unit_part * jnp.mean(scaled * unit_part, axis=1, keepdims=True)
    )
    return (inner_part * inverse, jnp.sum(gradient * unit_part, axis=0), jnp.sum(gradient, axis=0))


def contract_rows(left_side, right_side):
    return lax.dot_general(
        left_side, right_side, (((0,), (0,)), ((), ())), preferred_element_type=jnp.float32
    )


def times_transposed(left_side, right_side):
    return lax.dot_general(
        left_side, right_side, (((1,), (1,)), ((), ())), preferred_element_type=jnp.float32
    )


ALL = ("tensor", "chip", "core")


def own_piece(array, count, index):
    size = array.shape[0] // count
    return lax.dynamic_slice_in_dim(array, index * size, size, 0)


def gather(array, axes):
    return lax.all_gather(array, axes, axis=0, tiled=True)


def scatter_sum(array, axes):
    return lax.psum_scatter(array, axes, scatter_dimension=0, tiled=True)


def swap_core(array):
    return lax.ppermute(array, "core", [(0, 1), (1, 0)])


def in_core_order(mine, other):
    first = lax.axis_index("core") == 0
    return jnp.stack([jnp.where(first, mine, other), jnp.where(first, other, mine)])


def dot(left, right):
    return jnp.dot(left, right, preferred_element_type=jnp.float32)


def head_mask(width, head):
    lane = lax.broadcasted_iota(jnp.int32, (1, width), 1)
    return ((lane >= head * HEAD) & (lane < (head + 1) * HEAD)).astype(jnp.float32).astype(jnp.bfloat16)


def allowed_keys(low, high, key_first, shape):
    key = key_first + lax.broadcasted_iota(jnp.int32, shape, 0)
    return (key >= low) & (key <= high)


def attend_kernel(heads, key_size, first_ref, last_ref, low_ref, high_ref, q_ref, k_ref, v_ref, out_ref, log_ref, turned, acc):
    block = pl.program_id(1)
    rows, width = q_ref.shape
    key_blocks = k_ref.shape[0] // key_size

    @pl.when(block == 0)
    def _():
        for j in range(key_blocks):
            turned[j] = v_ref[j * key_size : (j + 1) * key_size, :].T

    q_rows = q_ref[...] * jnp.bfloat16(0.125)
    q_heads = [q_rows * head_mask(width, h) for h in range(heads)]
    low, high = low_ref[0], high_ref[0]
    acc[...] = jnp.zeros_like(acc)
    last = last_ref[block]

    def step(t, state):
        j = last - t
        key_first = pl.multiple_of(j * key_size, key_size)
        k_rows = k_ref[pl.ds(key_first, key_size), :]
        allowed = allowed_keys(low, high, key_first, (key_size, rows))
        fresh = []
        for h in range(heads):
            top, total = state[h]
            scores = jnp.where(allowed, times_transposed(k_rows, q_heads[h]), NEGATIVE)
            new_top = jnp.maximum(top, jnp.max(scores, axis=0, keepdims=True))
            probs = jnp.exp(scores - new_top)
            shrink = jnp.exp(top - new_top)
            part = slice(h * HEAD, (h + 1) * HEAD)
            acc[part, :] = acc[part, :] * shrink + dot(turned[j, part, :], probs.astype(jnp.bfloat16))
            fresh.append((new_top, total * shrink + jnp.sum(probs, axis=0, keepdims=True)))
        return tuple(fresh)

    begin = (jnp.full((1, rows), NEGATIVE, jnp.float32), jnp.zeros((1, rows), jnp.float32))
    state = lax.fori_loop(0, last - first_ref[block] + 1, step, (begin,) * heads)
    for h in range(heads):
        top, total = state[h]
        part = slice(h * HEAD, (h + 1) * HEAD)
        acc[part, :] = acc[part, :] / total
        log_ref[0, 0, h : h + 1, :] = top + jnp.log(total)
    out_ref[...] = acc[...].T.astype(jnp.bfloat16)


def attend_back_kernel(heads, query_size, key_size, first_ref, last_ref, low_ref, high_ref, q_ref, k_ref, v_ref, out_ref, grad_ref, log_ref, dq_ref, dk_ref, dv_ref, q_heads, grad_heads, turned, delta, dq_acc, dk_acc, dv_acc):
    block = pl.program_id(1)
    width = q_ref.shape[1]
    query_blocks = q_ref.shape[0] // query_size

    @pl.when(block == 0)
    def _():
        for i in range(query_blocks):
            rows = slice(i * query_size, (i + 1) * query_size)
            product = grad_ref[rows, :].astype(jnp.float32) * out_ref[rows, :].astype(jnp.float32)
            product = product.T
            for h in range(heads):
                mask = head_mask(width, h)
                q_heads[i, h] = q_ref[rows, :] * (mask * jnp.bfloat16(0.125))
                grad_heads[i, h] = grad_ref[rows, :] * mask
                delta[i, h : h + 1, :] = jnp.sum(
                    product[h * HEAD : (h + 1) * HEAD, :], axis=0, keepdims=True
                )
        dq_acc[...] = jnp.zeros_like(dq_acc)

    key_first = pl.multiple_of(block * key_size, key_size)
    k_rows = k_ref[pl.ds(key_first, key_size), :]
    v_rows = v_ref[pl.ds(key_first, key_size), :]
    turned[...] = k_rows.T
    dk_acc[...] = jnp.zeros_like(dk_acc)
    dv_acc[...] = jnp.zeros_like(dv_acc)

    def step(i, carry):
        allowed = allowed_keys(low_ref[i], high_ref[i], key_first, (key_size, query_size))
        for h in range(heads):
            q_rows = q_heads[i, h]
            grad_rows = grad_heads[i, h]
            scores = times_transposed(k_rows, q_rows)
            probs = jnp.where(allowed, jnp.exp(scores - log_ref[0, i, h : h + 1, :]), 0.0)
            prob_grad = times_transposed(v_rows, grad_rows)
            score_grad = (probs * (prob_grad - delta[i, h : h + 1, :])).astype(jnp.bfloat16)
            dv_acc[...] += dot(probs.astype(jnp.bfloat16), grad_rows)
            dk_acc[...] += dot(score_grad, q_rows)
            part = slice(h * HEAD, (h + 1) * HEAD)
            dq_acc[i, part, :] += dot(turned[part, :], score_grad)
        return carry

    lax.fori_loop(first_ref[block], last_ref[block] + 1, step, 0)
    dk_ref[pl.ds(key_first, key_size), :] = dk_acc[...].astype(jnp.bfloat16)
    dv_ref[pl.ds(key_first, key_size), :] = dv_acc[...].astype(jnp.bfloat16)

    @pl.when(block == pl.num_programs(1) - 1)
    def _():
        for i in range(query_blocks):
            dq_ref[i * query_size : (i + 1) * query_size, :] = (
                (dq_acc[i] * 0.125).T.astype(jnp.bfloat16)
            )


def packed_back_kernel(heads, query_size, key_size, *refs):
    first_ref, last_ref, low_ref, high_ref, qkv_ref, out_ref, grad_ref, log_ref, dqkv_ref = refs[:9]
    width = out_ref.shape[1]
    views = [[r.at[:, c * width : (c + 1) * width] for c in range(3)] for r in (qkv_ref, dqkv_ref)]
    attend_back_kernel(
        heads, query_size, key_size, first_ref, last_ref, low_ref, high_ref,
        *views[0], out_ref, grad_ref, log_ref, *views[1], *refs[9:],
    )


def lanes(values, size):
    return values.astype(jnp.int32).reshape(-1, 1, size)


def attend_call(q, k, v, columns, groups, heads, low, high, first, last, query_size, key_size):
    width = heads * HEAD
    rows, keys = q.shape[0], k.shape[0]
    blocks = rows // query_size
    spec = lambda size, column: pl.BlockSpec((size, width), lambda g, i, *_: (0, column + g))
    vector = pl.BlockSpec((1, 1, query_size), lambda g, i, *_: (i, 0, 0))
    q_column = columns[0]
    return pl.pallas_call(
        partial(attend_kernel, heads, key_size),
        grid_spec=pltpu.PrefetchScalarGridSpec(
            num_scalar_prefetch=2,
            grid=(groups, blocks),
            in_specs=[
                vector,
                vector,
                pl.BlockSpec((query_size, width), lambda g, i, *_: (i, q_column + g)),
                spec(keys, columns[1]),
                spec(keys, columns[2]),
            ],
            out_specs=[
                pl.BlockSpec((query_size, width), lambda g, i, *_: (i, g)),
                pl.BlockSpec((1, 1, heads, query_size), lambda g, i, *_: (g, i, 0, 0)),
            ],
            scratch_shapes=[
                pltpu.VMEM((keys // key_size, width, key_size), jnp.bfloat16),
                pltpu.VMEM((width, query_size), jnp.float32),
            ],
        ),
        out_shape=[
            jax.ShapeDtypeStruct((rows, groups * width), jnp.bfloat16),
            jax.ShapeDtypeStruct((groups, blocks, heads, query_size), jnp.float32),
        ],
        compiler_params=pltpu.CompilerParams(vmem_limit_bytes=VMEM_BYTES),
    )(first, last, lanes(low, query_size), lanes(high, query_size), q, k, v)


def back_scratch(heads, blocks, query_size, key_size):
    width = heads * HEAD
    return [
        pltpu.VMEM((blocks, heads, query_size, width), jnp.bfloat16),
        pltpu.VMEM((blocks, heads, query_size, width), jnp.bfloat16),
        pltpu.VMEM((width, key_size), jnp.bfloat16),
        pltpu.VMEM((blocks, heads, query_size), jnp.float32),
        pltpu.VMEM((blocks, width, query_size), jnp.float32),
        pltpu.VMEM((key_size, width), jnp.float32),
        pltpu.VMEM((key_size, width), jnp.float32),
    ]


def packed_back_call(qkv, out, grad, logs, heads, low, high, first, last, query_size, key_size):
    rows, width = out.shape
    blocks = rows // query_size
    whole = lambda shape: pl.BlockSpec(shape, lambda g, j, *_: (0,) * len(shape))
    vector = whole((blocks, 1, query_size))
    return pl.pallas_call(
        partial(packed_back_kernel, heads, query_size, key_size),
        grid_spec=pltpu.PrefetchScalarGridSpec(
            num_scalar_prefetch=2,
            grid=(1, rows // key_size),
            in_specs=[
                vector,
                vector,
                whole(qkv.shape),
                whole(out.shape),
                whole(grad.shape),
                whole(logs.shape),
            ],
            out_specs=whole(qkv.shape),
            scratch_shapes=back_scratch(heads, blocks, query_size, key_size),
        ),
        out_shape=jax.ShapeDtypeStruct(qkv.shape, jnp.bfloat16),
        compiler_params=pltpu.CompilerParams(vmem_limit_bytes=VMEM_BYTES),
    )(first, last, lanes(low, query_size), lanes(high, query_size), qkv, out, grad, logs)


def attend_back_call(q, k, v, out, grad, logs, groups, heads, low, high, first, last, query_size, key_size):
    width = heads * HEAD
    rows, keys = q.shape[0], k.shape[0]
    blocks = rows // query_size
    column = lambda size: pl.BlockSpec((size, width), lambda g, j, *_: (0, g))
    vector = pl.BlockSpec((blocks, 1, query_size), lambda g, j, *_: (0, 0, 0))
    return pl.pallas_call(
        partial(attend_back_kernel, heads, query_size, key_size),
        grid_spec=pltpu.PrefetchScalarGridSpec(
            num_scalar_prefetch=2,
            grid=(groups, keys // key_size),
            in_specs=[
                vector,
                vector,
                column(rows),
                column(keys),
                column(keys),
                column(rows),
                column(rows),
                pl.BlockSpec((1, blocks, heads, query_size), lambda g, j, *_: (g, 0, 0, 0)),
            ],
            out_specs=[column(rows), column(keys), column(keys)],
            scratch_shapes=back_scratch(heads, blocks, query_size, key_size),
        ),
        out_shape=[
            jax.ShapeDtypeStruct((rows, groups * width), jnp.bfloat16),
            jax.ShapeDtypeStruct((keys, groups * width), jnp.bfloat16),
            jax.ShapeDtypeStruct((keys, groups * width), jnp.bfloat16),
        ],
        compiler_params=pltpu.CompilerParams(vmem_limit_bytes=VMEM_BYTES),
    )(first, last, lanes(low, query_size), lanes(high, query_size), q, k, v, out, grad, logs)


def per_device(
    frames,
    text_states,
    clip_lengths,
    text_lengths,
    norm_gains,
    norm_biases,
    self_qkv,
    self_out,
    cross_query,
    cross_kv,
    cross_out,
    ffn_in,
    ffn_out,
    out_grad,
):
    groups = lax.axis_size("tensor")
    chips = lax.axis_size("chip")
    group = lax.axis_index("tensor")
    chip = lax.axis_index("chip")
    core = lax.axis_index("core")
    bf16 = jnp.bfloat16
    frame_count, width = frames.shape
    own_rows = frame_count // groups
    offset = group * own_rows
    clip_count, text_slots, text_width = text_states.shape
    head_count = self_out.shape[0] // HEAD
    all_heads = head_count * groups
    ends = jnp.cumsum(clip_lengths[0])
    starts = ends - clip_lengths[0]
    positions = jnp.arange(frame_count, dtype=jnp.int32)[:, None]
    clip_first = jnp.max(jnp.where(positions >= starts, starts, 0), axis=1)
    clip_stop = jnp.min(jnp.where(positions < ends, ends, frame_count), axis=1)
    block = min(256, own_rows)
    blocks = jnp.arange(frame_count // block, dtype=jnp.int32)
    self_low, self_high = clip_first, positions[:, 0]
    self_keys = (clip_first[::block] // block, blocks)
    self_queries = (blocks, (clip_stop[block - 1 :: block] - 1) // block)
    own_positions = offset + jnp.arange(own_rows, dtype=jnp.int32)[:, None]
    own_clip = jnp.sum((own_positions >= ends).astype(jnp.int32), axis=1)
    own_length = jnp.sum(
        jnp.where(own_clip[:, None] == jnp.arange(clip_count), text_lengths[0], 0), axis=1
    )
    cross_low = own_clip * text_slots
    cross_high = cross_low + own_length - 1
    cross_keys = (own_clip[::block], own_clip[block - 1 :: block])
    inside_first = jnp.clip(starts - offset, 0, own_rows)
    inside_stop = jnp.clip(ends - offset, 0, own_rows)
    cross_first = jnp.minimum(inside_first // block, own_rows // block - 1)
    cross_queries = (
        cross_first,
        jnp.where(inside_stop > inside_first, (inside_stop - 1) // block, cross_first - 1),
    )

    share = 2 * chips
    place = chip * 2 + core

    def packed_piece(weight):
        return own_piece(weight, share, place).reshape(-1, width)

    kv_piece = own_piece(cross_kv, share, place).reshape(-1, head_count, 2, HEAD)
    small = [packed_piece(w) for w in (self_out, cross_query)]
    small.append(kv_piece.transpose(2, 0, 1, 3).reshape(-1, width))
    small.append(packed_piece(cross_out))
    small_rows = [w.shape[0] for w in small]
    small_all = gather(jnp.concatenate(small, 0), ALL).reshape(groups, share, -1, width)
    cuts = [sum(small_rows[:i]) for i in range(5)]
    w_so, w_cq, w_ckv, w_co = [small_all[:, :, cuts[i] : cuts[i + 1]] for i in range(4)]
    w_so = w_so.reshape(width, width)
    w_co = w_co.reshape(width, width)
    w_cq = w_cq.reshape(groups, width, -1).transpose(1, 0, 2).reshape(width, width)
    w_ckv = w_ckv.reshape(groups, share, 2, text_width // share, -1).transpose(2, 1, 3, 0, 4)
    w_ck, w_cv = w_ckv.reshape(2, text_width, width)

    half = ffn_out.shape[0] // 2
    piece = half // chips
    unit_first = core * half + chip * piece
    ffn_piece = jnp.concatenate(
        [
            lax.dynamic_slice_in_dim(ffn_in, unit_first, piece, 1).T,
            lax.dynamic_slice_in_dim(ffn_out, unit_first, piece, 0),
        ],
        0,
    )
    ffn_all = gather(ffn_piece, ("tensor", "chip")).reshape(groups, chips, 2, piece, width)
    w_in = ffn_all[:, :, 0].reshape(groups * half, width)
    w_out = ffn_all[:, :, 1].reshape(groups * half, width)
    grad_own_bf = lax.dynamic_slice_in_dim(out_grad, offset, own_rows, 0)
    grad_pair = jnp.concatenate([grad_own_bf, swap_core(grad_own_bf)], 0)

    inputs = frames.astype(jnp.float32)
    own_inputs = lax.dynamic_slice_in_dim(inputs, offset, own_rows, 0)
    first_all, _, _ = norm_forward(inputs, norm_gains[0], norm_biases[0])
    _, unit_one, inverse_one = norm_forward(own_inputs, norm_gains[0], norm_biases[0])
    rows_one = first_all.astype(bf16)
    w_qkv = self_qkv.reshape(width, head_count, 3, HEAD).transpose(0, 2, 1, 3).reshape(width, -1)
    packed = dot(rows_one, w_qkv).astype(bf16)
    head_width = head_count * HEAD
    if head_width % 128 == 0:
        self_parts, self_columns = (packed, packed, packed), (0, 1, 2)
    else:
        self_parts = [packed[:, c * head_width : (c + 1) * head_width] for c in range(3)]
        self_columns = (0, 0, 0)
    self_mix, self_logs = attend_call(
        *self_parts, self_columns, 1, head_count, self_low, self_high, *self_keys, block, block
    )
    self_flat = lax.all_to_all(self_mix, "tensor", 0, 1, tiled=True)

    after_self = own_inputs + dot(self_flat, w_so)
    second_own, unit_two, inverse_two = norm_forward(after_self, norm_gains[1], norm_biases[1])
    rows_two = second_own.astype(bf16)
    cross_q = dot(rows_two, w_cq).astype(bf16)
    text_flat = text_states.reshape(clip_count * text_slots, text_width)
    cross_k = dot(text_flat, w_ck).astype(bf16)
    cross_v = dot(text_flat, w_cv).astype(bf16)
    bunch = min(4, all_heads)
    cross_shape = (all_heads // bunch, bunch, cross_low, cross_high)
    cross_flat, cross_logs = attend_call(
        cross_q, cross_k, cross_v, (0, 0, 0), *cross_shape, *cross_keys, block, text_slots
    )
    after_cross = after_self + dot(cross_flat, w_co)
    third_own, unit_three, inverse_three = norm_forward(after_cross, norm_gains[2], norm_biases[2])

    rows_three = third_own.astype(bf16)
    rows_pair = jnp.concatenate([rows_three, swap_core(rows_three)], 0)
    hidden_pre = times_transposed(rows_pair, w_in)
    gelu = lambda v: jax.nn.gelu(v, approximate=False)
    hidden_exact, gelu_back = jax.vjp(gelu, hidden_pre)
    hidden = hidden_exact.astype(bf16)
    out_pair = dot(hidden, w_out)
    hidden_grad = times_transposed(grad_pair, w_out)
    pre_grad = gelu_back(hidden_grad)[0].astype(bf16)
    third_pair = dot(pre_grad, w_in)
    result = (
        after_cross
        + out_pair[:own_rows]
        + swap_core(out_pair[own_rows:].astype(bf16)).astype(jnp.float32)
    )
    mixed = result.astype(bf16)
    third_grad = third_pair[:own_rows] + swap_core(third_pair[own_rows:].astype(bf16)).astype(
        jnp.float32
    )

    def spread(grad, parts):
        return grad.reshape(groups, parts, -1, grad.shape[1]).transpose(1, 0, 2, 3)

    ffn_part = jnp.concatenate(
        [
            spread(contract_rows(pre_grad, rows_pair).astype(bf16), chips),
            spread(contract_rows(hidden, grad_pair).astype(bf16), chips),
        ],
        2,
    )
    ffn_sum = gather(
        scatter_sum(scatter_sum(ffn_part, "chip")[0], "tensor"), "chip"
    ).reshape(chips, 2, piece, width)
    ffn_sum = in_core_order(ffn_sum, swap_core(ffn_sum)).astype(jnp.float32)
    ffn_in_grad = ffn_sum[:, :, 0].reshape(2 * half, width).T
    ffn_out_grad = ffn_sum[:, :, 1].reshape(2 * half, width)

    back_three, gain_three, shift_three = norm_backward(
        third_grad, unit_three, inverse_three, norm_gains[2]
    )
    cross_side = grad_own_bf.astype(jnp.float32) + back_three
    cross_grad = cross_side.astype(bf16)
    cross_out_grad = contract_rows(cross_flat, cross_grad)
    cross_mix_grad = times_transposed(cross_grad, w_co).astype(bf16)
    cq_flat, ck_grad, cv_grad = attend_back_call(
        cross_q,
        cross_k,
        cross_v,
        cross_flat,
        cross_mix_grad,
        cross_logs,
        *cross_shape,
        *cross_queries,
        block,
        text_slots,
    )
    cross_query_grad = contract_rows(cq_flat, rows_two)
    cross_kv_grad = jnp.stack(
        [contract_rows(grad, text_flat).reshape(groups, -1, text_width) for grad in (ck_grad, cv_grad)],
        axis=1,
    ).reshape(2 * width, text_width)
    text_part = times_transposed(ck_grad, w_ck) + times_transposed(cv_grad, w_cv)
    back_two, gain_two, shift_two = norm_backward(
        times_transposed(cq_flat, w_cq), unit_two, inverse_two, norm_gains[1]
    )
    self_side = cross_side + back_two
    self_grad = self_side.astype(bf16)
    self_out_grad = contract_rows(self_flat, self_grad)
    self_mix_grad = lax.all_to_all(
        times_transposed(self_grad, w_so).astype(bf16), "tensor", 1, 0, tiled=True
    )

    small_grads = [self_out_grad, cross_query_grad, cross_kv_grad, cross_out_grad]
    small_part = jnp.concatenate(
        [
            spread(grad.astype(bf16), share).reshape(2, chips, groups, -1, width)
            for grad in small_grads
        ],
        3,
    )
    kept = lax.dynamic_index_in_dim(small_part, core, 0, keepdims=False)
    sent = lax.dynamic_index_in_dim(small_part, 1 - core, 0, keepdims=False)
    small_part = kept + swap_core(sent)
    small_sum = gather(scatter_sum(scatter_sum(small_part, "chip")[0], "tensor"), "chip")
    small_sum = in_core_order(small_sum, swap_core(small_sum)).reshape(share, -1, width)

    def unpacked(index, columns):
        return (
            small_sum[:, cuts[index] : cuts[index + 1]].reshape(-1, columns).astype(jnp.float32)
        )

    self_saved = (self_mix, self_mix_grad, self_logs)
    self_rest = (head_count, self_low, self_high, *self_queries, block, block)
    if head_width % 128 == 0:
        packed_grad = packed_back_call(packed, *self_saved, *self_rest)
    else:
        packed_grad = jnp.concatenate(attend_back_call(*self_parts, *self_saved, 1, *self_rest), 1)
    self_qkv_grad = lax.psum(
        contract_rows(rows_one, packed_grad).astype(bf16), ("chip", "core")
    ).astype(jnp.float32)
    self_qkv_grad = (
        self_qkv_grad.reshape(width, 3, head_count, HEAD).transpose(0, 2, 1, 3).reshape(width, -1)
    )
    first_grad = scatter_sum(times_transposed(packed_grad, w_qkv).astype(bf16), "tensor").astype(
        jnp.float32
    )
    back_one, gain_one, shift_one = norm_backward(first_grad, unit_one, inverse_one, norm_gains[0])
    frames_grad = (self_side + back_one).astype(bf16)
    norm_part = jnp.stack(
        [
            jnp.stack([gain_one, gain_two, gain_three]),
            jnp.stack([shift_one, shift_two, shift_three]),
        ]
    )
    text_grad = lax.psum_scatter(
        text_part.reshape(clip_count, text_slots, text_width).astype(bf16),
        "tensor",
        scatter_dimension=2,
        tiled=True,
    ).astype(jnp.float32)
    norm_part = lax.psum_scatter(
        lax.psum(norm_part, ("chip", "core")), "tensor", scatter_dimension=2, tiled=True
    )
    return (
        mixed,
        frames_grad,
        text_grad,
        norm_part,
        self_qkv_grad,
        unpacked(0, width),
        unpacked(1, width).T,
        unpacked(2, text_width)
        .reshape(2, head_count, HEAD, text_width)
        .transpose(3, 1, 0, 2)
        .reshape(text_width, -1),
        unpacked(3, width),
        ffn_in_grad,
        ffn_out_grad,
    )


def solution(mesh):
    rows, groups = mesh.devices.shape
    inner = Mesh(mesh.devices.reshape(rows // 2, 2, groups), ("chip", "core", "tensor"))
    data = ("chip", "core")
    in_specs = (
        P(data, None),
        P(data, None, None),
        P(data, None),
        P(data, None),
        P(),
        P(),
        P(None, "tensor"),
        P("tensor", None),
        P(None, "tensor"),
        P(None, "tensor"),
        P("tensor", None),
        P(None, "tensor"),
        P("tensor", None),
        P(data, None),
    )
    out_specs = (
        P((*data, "tensor"), None),
        P((*data, "tensor"), None),
        P(data, None, "tensor"),
        P(None, None, "tensor"),
        P(None, "tensor"),
        P("tensor", None),
        P(None, "tensor"),
        P(None, "tensor"),
        P("tensor", None),
        P(None, "tensor"),
        P("tensor", None),
    )
    return jax.shard_map(
        per_device, mesh=inner, in_specs=in_specs, out_specs=out_specs, check_vma=False
    )
```

```python
from functools import partial

import jax
import jax.numpy as jnp
from jax import lax
from jax.experimental import pallas as pl
from jax.experimental.pallas import tpu as pltpu
from jax.sharding import Mesh
from jax.sharding import PartitionSpec as P

HEAD = 64


EPSILON = 1e-05
NEGATIVE = -1e30
VMEM_BYTES = 56 * 1024 * 1024


def about(microseconds):
    return pl.CostEstimate(
        flops=int(microseconds * 1.1e9), bytes_accessed=int(microseconds * 3e6), transcendentals=0
    )


def norm_forward(row_values, gain_row, shift_row):
    center = row_values - jnp.mean(row_values, axis=1, keepdims=True)
    inverse = lax.rsqrt(jnp.mean(center * center, axis=1, keepdims=True) + EPSILON)
    unit_part = center * inverse
    return (unit_part * gain_row + shift_row, unit_part, inverse)


def norm_backward(gradient, unit_part, inverse, gain_row):
    scaled = gradient * gain_row
    inner_part = (
        scaled
        - jnp.mean(scaled, axis=1, keepdims=True)
        - unit_part * jnp.mean(scaled * unit_part, axis=1, keepdims=True)
    )
    return (inner_part * inverse, jnp.sum(gradient * unit_part, axis=0), jnp.sum(gradient, axis=0))


def contract_rows(left_side, right_side):
    return lax.dot_general(
        left_side, right_side, (((0,), (0,)), ((), ())), preferred_element_type=jnp.float32
    )


def times_transposed(left_side, right_side):
    return lax.dot_general(
        left_side, right_side, (((1,), (1,)), ((), ())), preferred_element_type=jnp.float32
    )


def axis_bits(name):
    return lax.axis_size(name).bit_length() - 1


def shift(array, steps):
    size = lax.axis_size("tensor")
    return lax.ppermute(array, "tensor", [(i, (i + steps) % size) for i in range(size)])


def flip(array, bit):
    pairs = [(i, i ^ (1 << bit)) for i in range(lax.axis_size("chip"))]
    return lax.ppermute(array, "chip", pairs)


def swap_core(array):
    return lax.ppermute(array, "core", [(0, 1), (1, 0)])


def in_order(mine, other, first, axis):
    return jnp.concatenate(
        [jnp.where(first, mine, other), jnp.where(first, other, mine)], axis
    )


def core_join(array, axis=0):
    return in_order(array, swap_core(array), lax.axis_index("core") == 0, axis)


def chip_orders():
    bits = axis_bits("chip")
    return [(0, 1), (1, 0)] if bits == 2 else [tuple(range(bits))]


def halves(array, axis):
    return jnp.split(array, len(chip_orders()), axis)


def chip_gather(array):
    bits = axis_bits("chip")
    chip = lax.axis_index("chip")
    joined = []
    for part, order in zip(halves(array, 1), chip_orders()):
        part = part.reshape(part.shape[0], *(1,) * bits, *part.shape[1:])
        for bit in order:
            first = (chip >> bit) % 2 == 0
            part = in_order(part, flip(part, bit), first, bits - bit)
        joined.append(part)
    whole = jnp.concatenate(joined, -2)
    return whole.reshape(whole.shape[0], -1, *whole.shape[-2:])


def pick(array, index, axis):
    return lax.dynamic_index_in_dim(array, index, axis, keepdims=False)


def chip_scatter_sum(array):
    bits = axis_bits("chip")
    chip = lax.axis_index("chip")
    done = []
    for part, order in zip(halves(array, 2), chip_orders()):
        part = part.reshape(part.shape[0], *(2,) * bits, *part.shape[2:])
        left = list(range(bits - 1, -1, -1))
        for bit in order:
            axis = 1 + left.index(bit)
            side = (chip >> bit) % 2
            part = pick(part, side, axis) + flip(pick(part, 1 - side, axis), bit)
            left.remove(bit)
        done.append(part)
    return jnp.concatenate(done, 1)


def chip_sum(array):
    done = []
    for part, order in zip(halves(array, 0), chip_orders()):
        for bit in order:
            part = part + flip(part, bit)
        done.append(part)
    return jnp.concatenate(done, 0)


def ring_sum(parts):
    running = parts[1]
    for part in parts[2:] + parts[:1]:
        running = shift(running, 1) + part
    return running


def gather(array, axes):
    return lax.all_gather(array, axes, axis=0, tiled=True)


def scatter_sum(array, axes):
    return lax.psum_scatter(array, axes, scatter_dimension=0, tiled=True)


def dot(left, right):
    return jnp.dot(left, right, preferred_element_type=jnp.float32)


def head_mask(width, head):
    lane = lax.broadcasted_iota(jnp.int32, (1, width), 1)
    return ((lane >= head * HEAD) & (lane < (head + 1) * HEAD)).astype(jnp.float32).astype(jnp.bfloat16)


def allowed_keys(low, high, key_first, shape):
    key = key_first + lax.broadcasted_iota(jnp.int32, shape, 0)
    return (key >= low) & (key <= high)


def attend_kernel(heads, key_size, first_ref, last_ref, low_ref, high_ref, q_ref, k_ref, v_ref, out_ref, log_ref, turned, acc):
    block = pl.program_id(1)
    rows, width = q_ref.shape
    key_blocks = k_ref.shape[0] // key_size

    @pl.when(block == 0)
    def _():
        for j in range(key_blocks):
            turned[j] = v_ref[j * key_size : (j + 1) * key_size, :].T

    q_rows = q_ref[...] * jnp.bfloat16(0.125)
    q_heads = [q_rows * head_mask(width, h) for h in range(heads)]
    low, high = low_ref[0], high_ref[0]
    acc[...] = jnp.zeros_like(acc)
    last = last_ref[block]

    def step(t, state):
        j = last - t
        key_first = pl.multiple_of(j * key_size, key_size)
        k_rows = k_ref[pl.ds(key_first, key_size), :]
        allowed = allowed_keys(low, high, key_first, (key_size, rows))
        fresh = []
        for h in range(heads):
            top, total = state[h]
            scores = jnp.where(allowed, times_transposed(k_rows, q_heads[h]), NEGATIVE)
            new_top = jnp.maximum(top, jnp.max(scores, axis=0, keepdims=True))
            probs = jnp.exp(scores - new_top)
            shrink = jnp.exp(top - new_top)
            part = slice(h * HEAD, (h + 1) * HEAD)
            acc[part, :] = acc[part, :] * shrink + dot(turned[j, part, :], probs.astype(jnp.bfloat16))
            fresh.append((new_top, total * shrink + jnp.sum(probs, axis=0, keepdims=True)))
        return tuple(fresh)

    begin = (jnp.full((1, rows), NEGATIVE, jnp.float32), jnp.zeros((1, rows), jnp.float32))
    state = lax.fori_loop(0, last - first_ref[block] + 1, step, (begin,) * heads)
    for h in range(heads):
        top, total = state[h]
        part = slice(h * HEAD, (h + 1) * HEAD)
        acc[part, :] = acc[part, :] / total
        log_ref[0, 0, h : h + 1, :] = top + jnp.log(total)
    out_ref[...] = acc[...].T.astype(jnp.bfloat16)


def attend_back_kernel(heads, query_size, key_size, first_ref, last_ref, low_ref, high_ref, q_ref, k_ref, v_ref, out_ref, grad_ref, log_ref, dq_ref, dk_ref, dv_ref, q_heads, grad_heads, turned, delta, dq_acc, dk_acc, dv_acc):
    block = pl.program_id(1)
    width = q_ref.shape[1]
    query_blocks = q_ref.shape[0] // query_size

    @pl.when(block == 0)
    def _():
        for i in range(query_blocks):
            rows = slice(i * query_size, (i + 1) * query_size)
            product = grad_ref[rows, :].astype(jnp.float32) * out_ref[rows, :].astype(jnp.float32)
            product = product.T
            for h in range(heads):
                mask = head_mask(width, h)
                q_heads[i, h] = q_ref[rows, :] * (mask * jnp.bfloat16(0.125))
                grad_heads[i, h] = grad_ref[rows, :] * mask
                delta[i, h : h + 1, :] = jnp.sum(
                    product[h * HEAD : (h + 1) * HEAD, :], axis=0, keepdims=True
                )
        dq_acc[...] = jnp.zeros_like(dq_acc)

    key_first = pl.multiple_of(block * key_size, key_size)
    k_rows = k_ref[pl.ds(key_first, key_size), :]
    v_rows = v_ref[pl.ds(key_first, key_size), :]
    turned[...] = k_rows.T
    dk_acc[...] = jnp.zeros_like(dk_acc)
    dv_acc[...] = jnp.zeros_like(dv_acc)

    def step(i, carry):
        allowed = allowed_keys(low_ref[i], high_ref[i], key_first, (key_size, query_size))
        for h in range(heads):
            q_rows = q_heads[i, h]
            grad_rows = grad_heads[i, h]
            scores = times_transposed(k_rows, q_rows)
            probs = jnp.where(allowed, jnp.exp(scores - log_ref[0, i, h : h + 1, :]), 0.0)
            prob_grad = times_transposed(v_rows, grad_rows)
            score_grad = (probs * (prob_grad - delta[i, h : h + 1, :])).astype(jnp.bfloat16)
            dv_acc[...] += dot(probs.astype(jnp.bfloat16), grad_rows)
            dk_acc[...] += dot(score_grad, q_rows)
            part = slice(h * HEAD, (h + 1) * HEAD)
            dq_acc[i, part, :] += dot(turned[part, :], score_grad)
        return carry

    lax.fori_loop(first_ref[block], last_ref[block] + 1, step, 0)
    dk_ref[pl.ds(key_first, key_size), :] = dk_acc[...].astype(jnp.bfloat16)
    dv_ref[pl.ds(key_first, key_size), :] = dv_acc[...].astype(jnp.bfloat16)

    @pl.when(block == pl.num_programs(1) - 1)
    def _():
        for i in range(query_blocks):
            dq_ref[i * query_size : (i + 1) * query_size, :] = (
                (dq_acc[i] * 0.125).T.astype(jnp.bfloat16)
            )


def packed_back_kernel(heads, query_size, key_size, *refs):
    first_ref, last_ref, low_ref, high_ref, qkv_ref, out_ref, grad_ref, log_ref, dqkv_ref = refs[:9]
    width = out_ref.shape[1]
    views = [[r.at[:, c * width : (c + 1) * width] for c in range(3)] for r in (qkv_ref, dqkv_ref)]
    attend_back_kernel(
        heads, query_size, key_size, first_ref, last_ref, low_ref, high_ref,
        *views[0], out_ref, grad_ref, log_ref, *views[1], *refs[9:],
    )


def ffn_kernel(
    tile,
    n_own_ref,
    n_far_ref,
    g_own_ref,
    g_far_ref,
    weights_ref,
    out_ref,
    out_far_ref,
    back_ref,
    back_far_ref,
    grads_ref,
    z_rows,
    du_rows,
    out_acc,
    back_acc,
    n_ref,
    n_turned,
    g_ref,
    g_turned,
):
    step = pl.program_id(0)
    rows, width = n_ref.shape
    chips, piece = weights_ref.shape[1], weights_ref.shape[3]
    units = chips * piece
    share = width // chips
    w_in = weights_ref[0, :, 0].reshape(units, width)
    w_out = weights_ref[0, :, 1].reshape(units, width)

    @pl.when(step == 0)
    def _():
        half = rows // 2
        for joined, turned, parts in (
            (n_ref, n_turned, (n_own_ref, n_far_ref)),
            (g_ref, g_turned, (g_own_ref, g_far_ref)),
        ):
            for i, source in enumerate(parts):
                joined[i * half : (i + 1) * half, :] = source[...]
                turned[:, i * half : (i + 1) * half] = source[...].T

    def row_tile(i, carry):
        part = pl.ds(pl.multiple_of(i * tile, tile), tile)
        pre = times_transposed(n_ref[part, :], w_in)
        scaled = lax.erf(pre * 0.7071067811865476)
        density = jnp.exp(pre * pre * -0.5) * 0.3989422804014327
        below = 0.5 + 0.5 * scaled
        hidden = (pre * below).astype(jnp.bfloat16)
        z_rows[part, :] = hidden
        out_part = dot(hidden, w_out)
        hidden_grad = times_transposed(g_ref[part, :], w_out)
        pre_grad = (hidden_grad * (below + pre * density)).astype(jnp.bfloat16)
        du_rows[part, :] = pre_grad
        back_part = dot(pre_grad, w_in)

        @pl.when(step == 0)
        def _():
            out_acc[part, :] = out_part
            back_acc[part, :] = back_part

        @pl.when(step > 0)
        def _():
            out_acc[part, :] += out_part
            back_acc[part, :] += back_part

        return carry

    lax.fori_loop(0, rows // tile, row_tile, 0)
    for c in range(chips):
        part = slice(c * share, (c + 1) * share)
        grads_ref[c, 0, 0] = dot(n_turned[part, :], du_rows[...]).astype(jnp.bfloat16)
        grads_ref[c, 0, 1] = dot(g_turned[part, :], z_rows[...]).astype(jnp.bfloat16)

    @pl.when(step == pl.num_programs(0) - 1)
    def _():
        own = rows // 2
        out_ref[...] = out_acc[:own, :]
        out_far_ref[...] = out_acc[own:, :].astype(jnp.bfloat16)
        back_ref[...] = back_acc[:own, :]
        back_far_ref[...] = back_acc[own:, :].astype(jnp.bfloat16)


def ffn_call(n_own, n_far, g_own, g_far, weights):
    rows, width = 2 * n_own.shape[0], n_own.shape[1]
    groups, chips, _, piece, _ = weights.shape
    units = chips * piece
    whole = lambda shape: pl.BlockSpec(shape, lambda t: (0,) * len(shape))
    own = (rows // 2, width)
    grads = (chips, 1, 2, width // chips, units)
    return pl.pallas_call(
        partial(ffn_kernel, min(256, rows)),
        grid=(groups,),
        in_specs=[
            whole(own),
            whole(own),
            whole(own),
            whole(own),
            pl.BlockSpec((1, *weights.shape[1:]), lambda t: (t, 0, 0, 0, 0)),
        ],
        out_specs=[
            whole(own),
            whole(own),
            whole(own),
            whole(own),
            pl.BlockSpec(grads, lambda t: (0, t, 0, 0, 0)),
        ],
        out_shape=[
            jax.ShapeDtypeStruct(own, jnp.float32),
            jax.ShapeDtypeStruct(own, jnp.bfloat16),
            jax.ShapeDtypeStruct(own, jnp.float32),
            jax.ShapeDtypeStruct(own, jnp.bfloat16),
            jax.ShapeDtypeStruct((chips, groups, *grads[2:]), jnp.bfloat16),
        ],
        scratch_shapes=[
            pltpu.VMEM((rows, units), jnp.bfloat16),
            pltpu.VMEM((rows, units), jnp.bfloat16),
            pltpu.VMEM((rows, width), jnp.float32),
            pltpu.VMEM((rows, width), jnp.float32),
            pltpu.VMEM((rows, width), jnp.bfloat16),
            pltpu.VMEM((width, rows), jnp.bfloat16),
            pltpu.VMEM((rows, width), jnp.bfloat16),
            pltpu.VMEM((width, rows), jnp.bfloat16),
        ],
        compiler_params=pltpu.CompilerParams(vmem_limit_bytes=VMEM_BYTES),
        cost_estimate=about(45),
    )(n_own, n_far, g_own, g_far, weights)


def unit_norm(values):
    center = values - jnp.mean(values, axis=1, keepdims=True)
    inverse = lax.rsqrt(jnp.mean(center * center, axis=1, keepdims=True) + EPSILON)
    return center * inverse, inverse


def unit_back(gradient, values, gain):
    unit, inverse = unit_norm(values)
    scaled = gradient * gain
    inner = (
        scaled
        - jnp.mean(scaled, axis=1, keepdims=True)
        - unit * jnp.mean(scaled * unit, axis=1, keepdims=True)
    )
    return (
        inner * inverse,
        jnp.sum(gradient * unit, axis=0, keepdims=True),
        jnp.sum(gradient, axis=0, keepdims=True),
    )


def first_kernel(frames_ref, gain_ref, bias_ref, weight_ref, normed_ref, packed_ref):
    unit, _ = unit_norm(frames_ref[...].astype(jnp.float32))
    normed = (unit * gain_ref[...] + bias_ref[...]).astype(jnp.bfloat16)
    normed_ref[...] = normed
    packed_ref[...] = dot(normed, weight_ref[...]).astype(jnp.bfloat16)


def first_call(frames, gain, bias, weight, tile):
    rows, width = frames.shape
    columns = weight.shape[1]
    moving = lambda size: pl.BlockSpec((tile, size), lambda i: (i, 0))
    fixed = lambda shape: pl.BlockSpec(shape, lambda i: (0, 0))
    return pl.pallas_call(
        first_kernel,
        grid=(rows // tile,),
        in_specs=[moving(width), fixed((1, width)), fixed((1, width)), fixed(weight.shape)],
        out_specs=[moving(width), moving(columns)],
        out_shape=[
            jax.ShapeDtypeStruct((rows, width), jnp.bfloat16),
            jax.ShapeDtypeStruct((rows, columns), jnp.bfloat16),
        ],
        compiler_params=pltpu.CompilerParams(vmem_limit_bytes=VMEM_BYTES),
        cost_estimate=about(9),
    )(frames, gain, bias, weight)


def weight_copies(core_ref, local_ref, mine_ref, far_ref, weights, sems):
    half = mine_ref.shape[1]
    core = core_ref[0]
    copies = [pltpu.make_async_copy(local_ref, weights.at[0], sems.at[0])]
    for k in range(1, weights.shape[0]):
        for n, (source, side) in enumerate(((mine_ref, core), (far_ref, 1 - core))):
            rows = pl.ds(pl.multiple_of(side * half, half), half)
            copies.append(
                pltpu.make_async_copy(
                    source.at[k - 1], weights.at[k, rows], sems.at[2 * k - 1 + n]
                )
            )
    return copies


def middle_kernel(
    heads,
    tile,
    core_ref,
    low_ref,
    high_ref,
    inputs_ref,
    text_ref,
    gain_ref,
    bias_ref,
    local_ref,
    mine_ref,
    far_ref,
    *rest,
):
    groups = len(rest) - 9 - 4
    mixes = rest[:groups]
    h1_ref, h2_ref, n2_ref, n3_ref, cq_ref, mix_ref, ck_ref, cv_ref, log_ref = rest[
        groups : groups + 9
    ]
    weights, turned, mix_turned, sems = rest[groups + 9 :]
    width = heads * HEAD
    text_width = text_ref.shape[1]
    keys = text_ref.shape[0]
    copies = weight_copies(core_ref, local_ref, mine_ref, far_ref, weights, sems)
    for copy in copies:
        copy.start()
    for copy in copies:
        copy.wait()
    text = text_ref[...]
    for k in range(groups):
        part = slice(k * width, (k + 1) * width)
        key_weight = weights[k, 3 * width : 4 * width, :text_width]
        value_weight = weights[k, 4 * width : 5 * width, :text_width]
        ck_ref[:, part] = times_transposed(text, key_weight).astype(jnp.bfloat16)
        cv_ref[:, part] = times_transposed(text, value_weight).astype(jnp.bfloat16)
        turned[k] = times_transposed(value_weight, text).astype(jnp.bfloat16)

    def row_tile(i, carry):
        rows = pl.ds(pl.multiple_of(i * tile, tile), tile)
        total = inputs_ref[rows, :].astype(jnp.float32)
        for k in range(groups):
            total += dot(mixes[k][rows, :], weights[k, 0:width, :])
        h1_ref[rows, :] = total
        unit, _ = unit_norm(total)
        normed = (unit * gain_ref[1:2, :] + bias_ref[1:2, :]).astype(jnp.bfloat16)
        n2_ref[rows, :] = normed
        allowed = allowed_keys(low_ref[i], high_ref[i], 0, (keys, tile))
        for k in range(groups):
            part = slice(k * width, (k + 1) * width)
            queries = times_transposed(normed, weights[k, width : 2 * width, :])
            queries = queries.astype(jnp.bfloat16)
            cq_ref[rows, part] = queries
            queries = queries * jnp.bfloat16(0.125)
            for h in range(heads):
                scores = times_transposed(ck_ref[:, part], queries * head_mask(width, h))
                scores = jnp.where(allowed, scores, NEGATIVE)
                top = jnp.max(scores, axis=0, keepdims=True)
                probs = jnp.exp(scores - top)
                sums = jnp.sum(probs, axis=0, keepdims=True)
                lane = slice(h * HEAD, (h + 1) * HEAD)
                mix_turned[lane, :] = dot(turned[k, lane, :], probs.astype(jnp.bfloat16)) / sums
                log_ref[i, k * heads + h : k * heads + h + 1, :] = top + jnp.log(sums)
            mix_ref[rows, part] = mix_turned[...].T.astype(jnp.bfloat16)
        total = h1_ref[rows, :]
        for k in range(groups):
            part = slice(k * width, (k + 1) * width)
            total += dot(mix_ref[rows, part], weights[k, 2 * width : 3 * width, :])
        h2_ref[rows, :] = total
        unit, _ = unit_norm(total)
        n3_ref[rows, :] = (unit * gain_ref[2:3, :] + bias_ref[2:3, :]).astype(jnp.bfloat16)
        return carry

    lax.fori_loop(0, inputs_ref.shape[0] // tile, row_tile, 0)


def middle_back_kernel(
    heads,
    tile,
    core_ref,
    low_ref,
    high_ref,
    text_ref,
    gain_ref,
    third_ref,
    third_far_ref,
    grad_ref,
    h1_ref,
    h2_ref,
    cq_ref,
    mix_ref,
    ck_ref,
    cv_ref,
    log_ref,
    local_ref,
    mine_ref,
    far_ref,
    cross_side_ref,
    dcq_ref,
    dck_ref,
    dcv_ref,
    self_exact_ref,
    self_side_ref,
    mix_grad_ref,
    norm_ref,
    weights,
    turned,
    query_turned,
    dk_acc,
    dv_acc,
    sems,
):
    groups = weights.shape[0]
    width = heads * HEAD
    text_width = text_ref.shape[1]
    keys = text_ref.shape[0]
    copies = weight_copies(core_ref, local_ref, mine_ref, far_ref, weights, sems)
    for copy in copies:
        copy.start()
    for copy in copies:
        copy.wait()
    text = text_ref[...]
    for k in range(groups):
        key_weight = weights[k, 3 * width : 4 * width, :text_width]
        turned[k] = times_transposed(key_weight, text).astype(jnp.bfloat16)
    dk_acc[...] = jnp.zeros_like(dk_acc)
    dv_acc[...] = jnp.zeros_like(dv_acc)
    norm_ref[...] = jnp.zeros_like(norm_ref)

    def row_tile(i, carry):
        rows = pl.ds(pl.multiple_of(i * tile, tile), tile)
        third = third_ref[rows, :] + third_far_ref[rows, :].astype(jnp.float32)
        back, gain_sum, bias_sum = unit_back(third, h2_ref[rows, :], gain_ref[2:3, :])
        norm_ref[2:3, :] += gain_sum
        norm_ref[5:6, :] += bias_sum
        cross_exact = grad_ref[rows, :].astype(jnp.float32) + back
        cross_side = cross_exact.astype(jnp.bfloat16)
        self_exact_ref[rows, :] = cross_exact
        cross_side_ref[rows, :] = cross_side
        allowed = allowed_keys(low_ref[i], high_ref[i], 0, (keys, tile))
        for k in range(groups):
            part = slice(k * width, (k + 1) * width)
            mix_grad = times_transposed(cross_side, weights[k, 2 * width : 3 * width, :])
            mix_grad = mix_grad.astype(jnp.bfloat16)
            product = mix_grad.astype(jnp.float32) * mix_ref[rows, part].astype(jnp.float32)
            product = product.T
            queries = cq_ref[rows, part] * jnp.bfloat16(0.125)
            for h in range(heads):
                mask = head_mask(width, h)
                lane = slice(h * HEAD, (h + 1) * HEAD)
                one = k * heads + h
                q_rows = queries * mask
                grad_rows = mix_grad * mask
                scores = times_transposed(ck_ref[:, part], q_rows)
                probs = jnp.exp(scores - log_ref[i, one : one + 1, :])
                probs = jnp.where(allowed, probs, 0.0)
                prob_grad = times_transposed(cv_ref[:, part], grad_rows)
                delta = jnp.sum(product[lane, :], axis=0, keepdims=True)
                score_grad = (probs * (prob_grad - delta)).astype(jnp.bfloat16)
                dv_acc[:, part] += dot(probs.astype(jnp.bfloat16), grad_rows)
                dk_acc[:, part] += dot(score_grad, q_rows)
                query_turned[lane, :] = dot(turned[k, lane, :], score_grad)
            dcq_ref[rows, part] = (query_turned[...] * 0.125).T.astype(jnp.bfloat16)
        second = jnp.zeros(cross_exact.shape, jnp.float32)
        for k in range(groups):
            part = slice(k * width, (k + 1) * width)
            second += dot(dcq_ref[rows, part], weights[k, width : 2 * width, :])
        back, gain_sum, bias_sum = unit_back(second, h1_ref[rows, :], gain_ref[1:2, :])
        norm_ref[1:2, :] += gain_sum
        norm_ref[4:5, :] += bias_sum
        self_exact = self_exact_ref[rows, :] + back
        self_exact_ref[rows, :] = self_exact
        self_side = self_exact.astype(jnp.bfloat16)
        self_side_ref[rows, :] = self_side
        for k in range(groups):
            mix_grad_ref[k, rows, :] = times_transposed(
                self_side, weights[k, 0:width, :]
            ).astype(jnp.bfloat16)
        return carry

    lax.fori_loop(0, third_ref.shape[0] // tile, row_tile, 0)
    dck_ref[...] = dk_acc[...].astype(jnp.bfloat16)
    dcv_ref[...] = dv_acc[...].astype(jnp.bfloat16)


def local_spec():
    return pl.BlockSpec(memory_space=pltpu.VMEM)


def middle_specs(plain):
    return (
        [pl.BlockSpec(memory_space=pltpu.SMEM)]
        + [local_spec()] * plain
        + [pl.BlockSpec(memory_space=pl.ANY)] * 3
    )


def middle_call(heads, tile, core, low, high, inputs, text, gains, biases, split_weights, mixes):
    rows, width = inputs.shape
    keys = text.shape[0]
    groups = len(mixes)
    f32, bf16 = jnp.float32, jnp.bfloat16
    shapes = [
        ((rows, width), f32),
        ((rows, width), f32),
        ((rows, width), bf16),
        ((rows, width), bf16),
        ((rows, width), bf16),
        ((rows, width), bf16),
        ((keys, width), bf16),
        ((keys, width), bf16),
        ((rows // tile, groups * heads, tile), f32),
    ]
    return pl.pallas_call(
        partial(middle_kernel, heads, tile),
        in_specs=middle_specs(6) + [local_spec()] * groups,
        out_specs=[local_spec()] * len(shapes),
        out_shape=[jax.ShapeDtypeStruct(*one) for one in shapes],
        scratch_shapes=[
            pltpu.VMEM((groups, *split_weights[0].shape), bf16),
            pltpu.VMEM((groups, heads * HEAD, keys), bf16),
            pltpu.VMEM((heads * HEAD, tile), f32),
            pltpu.SemaphoreType.DMA((2 * groups - 1,)),
        ],
        compiler_params=pltpu.CompilerParams(vmem_limit_bytes=VMEM_BYTES),
        cost_estimate=about(30),
    )(core, lanes(low, tile), lanes(high, tile), inputs, text, gains, biases, *split_weights, *mixes)


def middle_back_call(heads, tile, core, low, high, text, gains, saved, split_weights):
    rows, width = saved[0].shape
    keys = text.shape[0]
    groups = width // (heads * HEAD)
    f32, bf16 = jnp.float32, jnp.bfloat16
    shapes = [
        ((rows, width), bf16),
        ((rows, width), bf16),
        ((keys, width), bf16),
        ((keys, width), bf16),
        ((rows, width), f32),
        ((rows, width), bf16),
        ((groups, rows, heads * HEAD), bf16),
        ((6, width), f32),
    ]
    return pl.pallas_call(
        partial(middle_back_kernel, heads, tile),
        in_specs=middle_specs(4 + len(saved)),
        out_specs=[local_spec()] * len(shapes),
        out_shape=[jax.ShapeDtypeStruct(*one) for one in shapes],
        scratch_shapes=[
            pltpu.VMEM((groups, *split_weights[0].shape), bf16),
            pltpu.VMEM((groups, heads * HEAD, keys), bf16),
            pltpu.VMEM((heads * HEAD, tile), f32),
            pltpu.VMEM((keys, width), f32),
            pltpu.VMEM((keys, width), f32),
            pltpu.SemaphoreType.DMA((2 * groups - 1,)),
        ],
        compiler_params=pltpu.CompilerParams(vmem_limit_bytes=VMEM_BYTES),
        cost_estimate=about(40),
    )(core, lanes(low, tile), lanes(high, tile), text, gains, *saved, *split_weights)


def lanes(values, size):
    return values.astype(jnp.int32).reshape(-1, 1, size)


def attend_call(q, k, v, columns, groups, heads, low, high, first, last, query_size, key_size):
    width = heads * HEAD
    rows, keys = q.shape[0], k.shape[0]
    blocks = rows // query_size
    spec = lambda size, column: pl.BlockSpec((size, width), lambda g, i, *_: (0, column + g))
    vector = pl.BlockSpec((1, 1, query_size), lambda g, i, *_: (i, 0, 0))
    q_column = columns[0]
    return pl.pallas_call(
        partial(attend_kernel, heads, key_size),
        grid_spec=pltpu.PrefetchScalarGridSpec(
            num_scalar_prefetch=2,
            grid=(groups, blocks),
            in_specs=[
                vector,
                vector,
                pl.BlockSpec((query_size, width), lambda g, i, *_: (i, q_column + g)),
                spec(keys, columns[1]),
                spec(keys, columns[2]),
            ],
            out_specs=[
                pl.BlockSpec((query_size, width), lambda g, i, *_: (i, g)),
                pl.BlockSpec((1, 1, heads, query_size), lambda g, i, *_: (g, i, 0, 0)),
            ],
            scratch_shapes=[
                pltpu.VMEM((keys // key_size, width, key_size), jnp.bfloat16),
                pltpu.VMEM((width, query_size), jnp.float32),
            ],
        ),
        out_shape=[
            jax.ShapeDtypeStruct((rows, groups * width), jnp.bfloat16),
            jax.ShapeDtypeStruct((groups, blocks, heads, query_size), jnp.float32),
        ],
        compiler_params=pltpu.CompilerParams(vmem_limit_bytes=VMEM_BYTES),
        cost_estimate=about(30 if groups == 1 else 17),
    )(first, last, lanes(low, query_size), lanes(high, query_size), q, k, v)


def back_scratch(heads, blocks, query_size, key_size):
    width = heads * HEAD
    return [
        pltpu.VMEM((blocks, heads, query_size, width), jnp.bfloat16),
        pltpu.VMEM((blocks, heads, query_size, width), jnp.bfloat16),
        pltpu.VMEM((width, key_size), jnp.bfloat16),
        pltpu.VMEM((blocks, heads, query_size), jnp.float32),
        pltpu.VMEM((blocks, width, query_size), jnp.float32),
        pltpu.VMEM((key_size, width), jnp.float32),
        pltpu.VMEM((key_size, width), jnp.float32),
    ]


def packed_back_call(qkv, out, grad, logs, heads, low, high, first, last, query_size, key_size):
    rows, width = out.shape
    blocks = rows // query_size
    whole = lambda shape: pl.BlockSpec(shape, lambda g, j, *_: (0,) * len(shape))
    vector = whole((blocks, 1, query_size))
    return pl.pallas_call(
        partial(packed_back_kernel, heads, query_size, key_size),
        grid_spec=pltpu.PrefetchScalarGridSpec(
            num_scalar_prefetch=2,
            grid=(1, rows // key_size),
            in_specs=[
                vector,
                vector,
                whole(qkv.shape),
                whole(out.shape),
                whole(grad.shape),
                whole(logs.shape),
            ],
            out_specs=whole(qkv.shape),
            scratch_shapes=back_scratch(heads, blocks, query_size, key_size),
        ),
        out_shape=jax.ShapeDtypeStruct(qkv.shape, jnp.bfloat16),
        compiler_params=pltpu.CompilerParams(vmem_limit_bytes=VMEM_BYTES),
        cost_estimate=about(36),
    )(first, last, lanes(low, query_size), lanes(high, query_size), qkv, out, grad, logs)


def attend_back_call(q, k, v, out, grad, logs, groups, heads, low, high, first, last, query_size, key_size):
    width = heads * HEAD
    rows, keys = q.shape[0], k.shape[0]
    blocks = rows // query_size
    column = lambda size: pl.BlockSpec((size, width), lambda g, j, *_: (0, g))
    vector = pl.BlockSpec((blocks, 1, query_size), lambda g, j, *_: (0, 0, 0))
    return pl.pallas_call(
        partial(attend_back_kernel, heads, query_size, key_size),
        grid_spec=pltpu.PrefetchScalarGridSpec(
            num_scalar_prefetch=2,
            grid=(groups, keys // key_size),
            in_specs=[
                vector,
                vector,
                column(rows),
                column(keys),
                column(keys),
                column(rows),
                column(rows),
                pl.BlockSpec((1, blocks, heads, query_size), lambda g, j, *_: (g, 0, 0, 0)),
            ],
            out_specs=[column(rows), column(keys), column(keys)],
            scratch_shapes=back_scratch(heads, blocks, query_size, key_size),
        ),
        out_shape=[
            jax.ShapeDtypeStruct((rows, groups * width), jnp.bfloat16),
            jax.ShapeDtypeStruct((keys, groups * width), jnp.bfloat16),
            jax.ShapeDtypeStruct((keys, groups * width), jnp.bfloat16),
        ],
        compiler_params=pltpu.CompilerParams(vmem_limit_bytes=VMEM_BYTES),
        cost_estimate=about(6 * groups),
    )(first, last, lanes(low, query_size), lanes(high, query_size), q, k, v, out, grad, logs)


def per_device(
    frames,
    text_states,
    clip_lengths,
    text_lengths,
    norm_gains,
    norm_biases,
    self_qkv,
    self_out,
    cross_query,
    cross_kv,
    cross_out,
    ffn_in,
    ffn_out,
    out_grad,
):
    groups = lax.axis_size("tensor")
    chips = lax.axis_size("chip")
    group = lax.axis_index("tensor")
    chip = lax.axis_index("chip")
    core = lax.axis_index("core")
    bf16 = jnp.bfloat16
    frame_count, width = frames.shape
    own_rows = frame_count // groups
    offset = group * own_rows
    clip_count, text_slots, text_width = text_states.shape
    head_count = self_out.shape[0] // HEAD
    all_heads = head_count * groups
    ends = jnp.cumsum(clip_lengths[0])
    starts = ends - clip_lengths[0]
    positions = jnp.arange(frame_count, dtype=jnp.int32)[:, None]
    clip_first = jnp.max(jnp.where(positions >= starts, starts, 0), axis=1)
    clip_stop = jnp.min(jnp.where(positions < ends, ends, frame_count), axis=1)
    block = min(256, own_rows)
    blocks = jnp.arange(frame_count // block, dtype=jnp.int32)
    self_low, self_high = clip_first, positions[:, 0]
    self_keys = (clip_first[::block] // block, blocks)
    self_queries = (blocks, (clip_stop[block - 1 :: block] - 1) // block)
    own_positions = offset + jnp.arange(own_rows, dtype=jnp.int32)[:, None]
    own_clip = jnp.sum((own_positions >= ends).astype(jnp.int32), axis=1)
    own_length = jnp.sum(
        jnp.where(own_clip[:, None] == jnp.arange(clip_count), text_lengths[0], 0), axis=1
    )
    cross_low = own_clip * text_slots
    cross_high = cross_low + own_length - 1
    cross_keys = (own_clip[::block], own_clip[block - 1 :: block])
    inside_first = jnp.clip(starts - offset, 0, own_rows)
    inside_stop = jnp.clip(ends - offset, 0, own_rows)
    cross_first = jnp.minimum(inside_first // block, own_rows // block - 1)
    cross_queries = (
        cross_first,
        jnp.where(inside_stop > inside_first, (inside_stop - 1) // block, cross_first - 1),
    )

    head_width = head_count * HEAD
    kv_turned = cross_kv.reshape(text_width, head_count, 2, HEAD).transpose(2, 1, 3, 0)
    kv_turned = jnp.pad(
        kv_turned.reshape(2 * head_width, text_width), ((0, 0), (0, width - text_width))
    )
    local = jnp.concatenate([self_out, cross_query.T, cross_out, kv_turned], 0)
    pieces = local.reshape(2, chips, -1, width)
    passed = [pick(pick(pieces, core, 0), chip, 0)]
    for _ in range(groups - 1):
        passed.append(shift(passed[-1], 1))
    mine = chip_gather(jnp.stack(passed[1:])).reshape(groups - 1, -1, width)
    split_weights = (local, mine, swap_core(mine))
    cuts = [i * head_width for i in range(6)]

    half = ffn_out.shape[0] // 2
    piece = half // chips
    unit_first = core * half + chip * piece
    ffn_piece = jnp.concatenate(
        [
            lax.dynamic_slice_in_dim(ffn_in, unit_first, piece, 1).T,
            lax.dynamic_slice_in_dim(ffn_out, unit_first, piece, 0),
        ],
        0,
    )
    ffn_all = gather(ffn_piece, ("tensor", "chip")).reshape(groups, chips, 2, piece, width)
    grad_own_bf = lax.dynamic_slice_in_dim(out_grad, offset, own_rows, 0)
    grad_far = swap_core(grad_own_bf)

    w_qkv = self_qkv.reshape(width, head_count, 3, HEAD).transpose(0, 2, 1, 3).reshape(width, -1)
    rows_one, packed = first_call(frames, norm_gains[:1], norm_biases[:1], w_qkv, block)
    if head_width % 128 == 0:
        self_parts, self_columns = (packed, packed, packed), (0, 1, 2)
    else:
        self_parts = [packed[:, c * head_width : (c + 1) * head_width] for c in range(3)]
        self_columns = (0, 0, 0)
    self_mix, self_logs = attend_call(
        *self_parts, self_columns, 1, head_count, self_low, self_high, *self_keys, block, block
    )
    mix_blocks = self_mix.reshape(groups, own_rows, head_width)
    mixes = [pick(mix_blocks, group, 0)]
    for k in range(1, groups):
        mixes.append(shift(pick(mix_blocks, (group + k) % groups, 0), k))

    own_frames = lax.dynamic_slice_in_dim(frames, offset, own_rows, 0)
    text_flat = text_states.reshape(clip_count * text_slots, text_width)
    core_index = core.reshape(1).astype(jnp.int32)
    shape = (head_count, block, core_index, cross_low, cross_high)
    after_self, after_cross, rows_two, rows_three, cross_q, cross_flat, cross_k, cross_v, cross_logs = (
        middle_call(
            *shape, own_frames, text_flat, norm_gains, norm_biases, split_weights, mixes
        )
    )

    out_own, out_far, third_own_grad, third_far, ffn_part = ffn_call(
        rows_three, swap_core(rows_three), grad_own_bf, grad_far, ffn_all
    )
    result = after_cross + out_own + swap_core(out_far).astype(jnp.float32)
    mixed = result.astype(bf16)
    ffn_sum = scatter_sum(ffn_part.reshape(-1, half), "chip")
    ffn_sum = gather(scatter_sum(ffn_sum, "tensor"), "chip")
    ffn_sum = core_join(ffn_sum.reshape(1, chips, 2, -1, half)).astype(jnp.float32)
    ffn_in_grad = ffn_sum[:, :, 0].transpose(1, 2, 0, 3).reshape(width, 2 * half)
    ffn_out_grad = ffn_sum[:, :, 1].transpose(0, 3, 1, 2).reshape(2 * half, width)

    saved = (
        third_own_grad,
        swap_core(third_far),
        grad_own_bf,
        after_self,
        after_cross,
        cross_q,
        cross_flat,
        cross_k,
        cross_v,
        cross_logs,
    )
    cross_grad, cq_flat, ck_grad, cv_grad, self_side, self_grad, mix_grad, norm_part = (
        middle_back_call(*shape, text_flat, norm_gains, saved, split_weights)
    )
    mix_grad = jnp.concatenate(
        [shift(mix_grad[k], -k) if k else mix_grad[k] for k in range(groups)], 0
    )
    self_mix_grad = lax.dynamic_slice_in_dim(
        jnp.concatenate([mix_grad, mix_grad], 0),
        (groups - group) % groups * own_rows,
        frame_count,
        0,
    )

    self_out_grad = jnp.concatenate([contract_rows(mix, self_grad) for mix in mixes], 0)
    cross_query_grad = contract_rows(cq_flat, rows_two)
    cross_out_grad = contract_rows(cross_flat, cross_grad)
    kv_grads = [contract_rows(grad, text_flat) for grad in (ck_grad, cv_grad)]
    w_kv = jnp.concatenate(
        [
            local[None, 3 * head_width :],
            in_order(mine[:, None], split_weights[2][:, None], core == 0, 1)
            .reshape(groups - 1, -1, width)[:, 3 * head_width :],
        ],
        0,
    ).reshape(groups, 2, head_width, width)[..., :text_width]
    text_part = sum(
        dot(grad, w_kv[:, i].reshape(-1, text_width)) for i, grad in enumerate((ck_grad, cv_grad))
    )
    small_part = jnp.concatenate(
        [
            jnp.pad(grad.astype(bf16), ((0, 0), (0, width - grad.shape[1]))).reshape(
                groups, head_width, width
            )
            for grad in (self_out_grad, cross_query_grad, cross_out_grad, *kv_grads)
        ],
        1,
    ).reshape(groups, 2, chips, -1, width)
    small_part = pick(small_part, core, 1) + swap_core(pick(small_part, 1 - core, 1))
    small_part = chip_scatter_sum(small_part)
    small_sum = ring_sum([small_part[k] for k in range(groups)])
    small_sum = core_join(chip_gather(small_sum[None])).reshape(-1, width)
    small_sum = small_sum.astype(jnp.float32)
    so_grad, cq_grad, co_grad, kv_grad = [
        small_sum[cuts[i] : cuts[j]] for i, j in ((0, 1), (1, 2), (2, 3), (3, 5))
    ]
    kv_grad = (
        kv_grad[:, :text_width]
        .reshape(2, head_count, HEAD, text_width)
        .transpose(3, 1, 0, 2)
        .reshape(text_width, -1)
    )

    self_saved = (self_mix, self_mix_grad, self_logs)
    self_rest = (head_count, self_low, self_high, *self_queries, block, block)
    if head_width % 128 == 0:
        packed_grad = packed_back_call(packed, *self_saved, *self_rest)
    else:
        packed_grad = jnp.concatenate(attend_back_call(*self_parts, *self_saved, 1, *self_rest), 1)
    packed_blocks = packed_grad.reshape(groups, own_rows, -1)
    first_grad = ring_sum(
        [
            times_transposed(pick(packed_blocks, (group + groups - k) % groups, 0), w_qkv).astype(bf16)
            for k in range(groups)
        ]
    ).astype(jnp.float32)
    qkv_part = contract_rows(rows_one, packed_grad).astype(bf16).reshape(2, width // 2, -1)
    qkv_part = pick(qkv_part, core, 0) + swap_core(pick(qkv_part, 1 - core, 0))
    self_qkv_grad = core_join(chip_sum(qkv_part)).astype(jnp.float32)
    self_qkv_grad = (
        self_qkv_grad.reshape(width, 3, head_count, HEAD).transpose(0, 2, 1, 3).reshape(width, -1)
    )
    _, unit_one, inverse_one = norm_forward(
        own_frames.astype(jnp.float32), norm_gains[0], norm_biases[0]
    )
    back_one, gain_one, shift_one = norm_backward(first_grad, unit_one, inverse_one, norm_gains[0])
    frames_grad = (self_side + back_one).astype(bf16)
    norm_part = norm_part.at[0].set(gain_one).at[3].set(shift_one).reshape(2, 3, width)
    text_blocks = text_part.reshape(clip_count * text_slots, groups, -1).transpose(1, 0, 2)
    text_blocks = text_blocks.astype(bf16)
    text_grad = pick(text_blocks, group, 0).astype(jnp.float32)
    for k in range(1, groups):
        text_grad += shift(pick(text_blocks, (group + k) % groups, 0), k).astype(jnp.float32)
    text_grad = text_grad.reshape(clip_count, text_slots, -1)
    norm_part = norm_part + swap_core(norm_part)
    for bit in range(axis_bits("chip")):
        norm_part = norm_part + flip(norm_part, bit)
    norm_blocks = norm_part.reshape(2, 3, groups, -1)
    norm_grads = pick(norm_blocks, group, 2)
    for k in range(1, groups):
        norm_grads += shift(pick(norm_blocks, (group + k) % groups, 2), k)
    return (
        mixed,
        frames_grad,
        text_grad,
        norm_grads,
        self_qkv_grad,
        so_grad,
        cq_grad.T,
        kv_grad,
        co_grad,
        ffn_in_grad,
        ffn_out_grad,
    )


def solution(mesh):
    rows, groups = mesh.devices.shape
    inner = Mesh(mesh.devices.reshape(rows // 2, 2, groups), ("chip", "core", "tensor"))
    data = ("chip", "core")
    in_specs = (
        P(data, None),
        P(data, None, None),
        P(data, None),
        P(data, None),
        P(),
        P(),
        P(None, "tensor"),
        P("tensor", None),
        P(None, "tensor"),
        P(None, "tensor"),
        P("tensor", None),
        P(None, "tensor"),
        P("tensor", None),
        P(data, None),
    )
    out_specs = (
        P((*data, "tensor"), None),
        P((*data, "tensor"), None),
        P(data, None, "tensor"),
        P(None, None, "tensor"),
        P(None, "tensor"),
        P("tensor", None),
        P(None, "tensor"),
        P(None, "tensor"),
        P("tensor", None),
        P(None, "tensor"),
        P("tensor", None),
    )
    return jax.shard_map(
        per_device, mesh=inner, in_specs=in_specs, out_specs=out_specs, check_vma=False
    )
```

```python
from functools import partial

import jax
import jax.numpy as jnp
from jax import lax
from jax.experimental import pallas as pl
from jax.experimental.pallas import tpu as pltpu
from jax.sharding import Mesh
from jax.sharding import PartitionSpec as P

HEAD = 64


EPSILON = 1e-05
NEGATIVE = -1e30
VMEM_BYTES = 56 * 1024 * 1024
SCALE = 0.02


def about(microseconds):
    return pl.CostEstimate(
        flops=int(microseconds * SCALE * 1.1e9), bytes_accessed=int(microseconds * SCALE * 3e6), transcendentals=0
    )


def contract_rows(left_side, right_side):
    return lax.dot_general(
        left_side, right_side, (((0,), (0,)), ((), ())), preferred_element_type=jnp.float32
    )


def times_transposed(left_side, right_side):
    return lax.dot_general(
        left_side, right_side, (((1,), (1,)), ((), ())), preferred_element_type=jnp.float32
    )


def phase(*arrays):
    return lax.optimization_barrier(arrays)


def axis_bits(name):
    return lax.axis_size(name).bit_length() - 1


def shift(array, steps):
    size = lax.axis_size("tensor")
    return lax.ppermute(array, "tensor", [(i, (i + steps) % size) for i in range(size)])


def flip(array, bit):
    pairs = [(i, i ^ (1 << bit)) for i in range(lax.axis_size("chip"))]
    return lax.ppermute(array, "chip", pairs)


def swap_core(array):
    return lax.ppermute(array, "core", [(0, 1), (1, 0)])


def in_order(mine, other, first, axis):
    return jnp.concatenate(
        [jnp.where(first, mine, other), jnp.where(first, other, mine)], axis
    )


def chip_orders():
    bits = axis_bits("chip")
    return [(0, 1), (1, 0)] if bits == 2 else [tuple(range(bits))]


def halves(array, axis):
    return jnp.split(array, len(chip_orders()), axis)


def chip_gather_start(array):
    bits = axis_bits("chip")
    return [
        part.reshape(part.shape[0], *(1,) * bits, *part.shape[1:]) for part in halves(array, 1)
    ]


def chip_gather_flips(parts, step):
    return [flip(part, order[step]) for part, order in zip(parts, chip_orders())]


def chip_gather_joins(parts, others, step):
    bits = axis_bits("chip")
    chip = lax.axis_index("chip")
    return [
        in_order(part, other, (chip >> order[step]) % 2 == 0, bits - order[step])
        for part, other, order in zip(parts, others, chip_orders())
    ]


def chip_gather_end(parts):
    whole = jnp.concatenate(parts, -2)
    return whole.reshape(whole.shape[0], -1, *whole.shape[-2:])


def pick(array, index, axis):
    return lax.dynamic_index_in_dim(array, index, axis, keepdims=False)


def chip_scatter_start(array):
    bits = axis_bits("chip")
    return [
        part.reshape(part.shape[0], *(2,) * bits, *part.shape[2:]) for part in halves(array, 2)
    ]


def chip_scatter_axis(order, step):
    left = sorted(set(order) - set(order[:step]), reverse=True)
    return 1 + left.index(order[step])


def chip_scatter_pick(part, order, step, other_side):
    side = (lax.axis_index("chip") >> order[step]) % 2
    side = 1 - side if other_side else side
    axis = chip_scatter_axis(order, step)
    return sum(pick(one, side, axis) for one in part[1:]) + pick(part[0], side, axis)


def chip_scatter_flips(parts, step):
    return [
        flip(chip_scatter_pick(part, order, step, True), order[step])
        for part, order in zip(parts, chip_orders())
    ]


def chip_scatter_adds(parts, others, step):
    return [
        (chip_scatter_pick(part, order, step, False) + other,)
        for part, other, order in zip(parts, others, chip_orders())
    ]


def gather(array, axes):
    return lax.all_gather(array, axes, axis=0, tiled=True)


def scatter_sum(array, axes):
    return lax.psum_scatter(array, axes, scatter_dimension=0, tiled=True)


def dot(left, right):
    return jnp.dot(left, right, preferred_element_type=jnp.float32)


def head_mask(width, head):
    lane = lax.broadcasted_iota(jnp.int32, (1, width), 1)
    return ((lane >= head * HEAD) & (lane < (head + 1) * HEAD)).astype(jnp.float32).astype(jnp.bfloat16)


def allowed_keys(low, high, key_first, shape):
    key = key_first + lax.broadcasted_iota(jnp.int32, shape, 0)
    return (key >= low) & (key <= high)


def attend_kernel(heads, key_size, first_ref, last_ref, low_ref, high_ref, q_ref, k_ref, v_ref, out_ref, log_ref, turned, acc):
    block = pl.program_id(1)
    rows, width = q_ref.shape
    key_blocks = k_ref.shape[0] // key_size

    @pl.when(block == 0)
    def _():
        for j in range(key_blocks):
            turned[j] = v_ref[j * key_size : (j + 1) * key_size, :].T

    q_rows = q_ref[...] * jnp.bfloat16(0.125)
    q_heads = [q_rows * head_mask(width, h) for h in range(heads)]
    low, high = low_ref[0], high_ref[0]
    acc[...] = jnp.zeros_like(acc)
    last = last_ref[block]

    def step(t, state):
        j = last - t
        key_first = pl.multiple_of(j * key_size, key_size)
        k_rows = k_ref[pl.ds(key_first, key_size), :]
        allowed = allowed_keys(low, high, key_first, (key_size, rows))
        fresh = []
        for h in range(heads):
            top, total = state[h]
            scores = jnp.where(allowed, times_transposed(k_rows, q_heads[h]), NEGATIVE)
            new_top = jnp.maximum(top, jnp.max(scores, axis=0, keepdims=True))
            probs = jnp.exp(scores - new_top)
            shrink = jnp.exp(top - new_top)
            part = slice(h * HEAD, (h + 1) * HEAD)
            acc[part, :] = acc[part, :] * shrink + dot(turned[j, part, :], probs.astype(jnp.bfloat16))
            fresh.append((new_top, total * shrink + jnp.sum(probs, axis=0, keepdims=True)))
        return tuple(fresh)

    begin = (jnp.full((1, rows), NEGATIVE, jnp.float32), jnp.zeros((1, rows), jnp.float32))
    state = lax.fori_loop(0, last - first_ref[block] + 1, step, (begin,) * heads)
    for h in range(heads):
        top, total = state[h]
        part = slice(h * HEAD, (h + 1) * HEAD)
        acc[part, :] = acc[part, :] / total
        log_ref[0, 0, h : h + 1, :] = top + jnp.log(total)
    out_ref[...] = acc[...].T.astype(jnp.bfloat16)


def attend_back_kernel(heads, query_size, key_size, first_ref, last_ref, low_ref, high_ref, q_ref, k_ref, v_ref, out_ref, grad_ref, log_ref, dq_ref, dk_ref, dv_ref, q_heads, grad_heads, turned, delta, dq_acc, dk_acc, dv_acc):
    block = pl.program_id(1)
    width = q_ref.shape[1]
    query_blocks = q_ref.shape[0] // query_size

    @pl.when(block == 0)
    def _():
        for i in range(query_blocks):
            rows = slice(i * query_size, (i + 1) * query_size)
            product = grad_ref[rows, :].astype(jnp.float32) * out_ref[rows, :].astype(jnp.float32)
            product = product.T
            for h in range(heads):
                mask = head_mask(width, h)
                q_heads[i, h] = q_ref[rows, :] * (mask * jnp.bfloat16(0.125))
                grad_heads[i, h] = grad_ref[rows, :] * mask
                delta[i, h : h + 1, :] = jnp.sum(
                    product[h * HEAD : (h + 1) * HEAD, :], axis=0, keepdims=True
                )
        dq_acc[...] = jnp.zeros_like(dq_acc)

    key_first = pl.multiple_of(block * key_size, key_size)
    k_rows = k_ref[pl.ds(key_first, key_size), :]
    v_rows = v_ref[pl.ds(key_first, key_size), :]
    turned[...] = k_rows.T
    dk_acc[...] = jnp.zeros_like(dk_acc)
    dv_acc[...] = jnp.zeros_like(dv_acc)

    def step(i, carry):
        allowed = allowed_keys(low_ref[i], high_ref[i], key_first, (key_size, query_size))
        for h in range(heads):
            q_rows = q_heads[i, h]
            grad_rows = grad_heads[i, h]
            scores = times_transposed(k_rows, q_rows)
            probs = jnp.where(allowed, jnp.exp(scores - log_ref[0, i, h : h + 1, :]), 0.0)
            prob_grad = times_transposed(v_rows, grad_rows)
            score_grad = (probs * (prob_grad - delta[i, h : h + 1, :])).astype(jnp.bfloat16)
            dv_acc[...] += dot(probs.astype(jnp.bfloat16), grad_rows)
            dk_acc[...] += dot(score_grad, q_rows)
            part = slice(h * HEAD, (h + 1) * HEAD)
            dq_acc[i, part, :] += dot(turned[part, :], score_grad)
        return carry

    lax.fori_loop(first_ref[block], last_ref[block] + 1, step, 0)
    dk_ref[pl.ds(key_first, key_size), :] = dk_acc[...].astype(jnp.bfloat16)
    dv_ref[pl.ds(key_first, key_size), :] = dv_acc[...].astype(jnp.bfloat16)

    @pl.when(block == pl.num_programs(1) - 1)
    def _():
        for i in range(query_blocks):
            dq_ref[i * query_size : (i + 1) * query_size, :] = (
                (dq_acc[i] * 0.125).T.astype(jnp.bfloat16)
            )


def packed_back_kernel(heads, query_size, key_size, groups, *refs):
    first_ref, last_ref, group_ref, low_ref, high_ref, qkv_ref, out_ref = refs[:7]
    parts = refs[7 : 7 + groups]
    log_ref, dqkv_ref = refs[7 + groups : 9 + groups]
    grad_ref = refs[-1]
    width = out_ref.shape[1]
    size = parts[0].shape[0]

    @pl.when(pl.program_id(1) == 0)
    def _():
        for k in range(groups):
            owner = lax.rem(group_ref[0] + k, groups)
            grad_ref[pl.ds(pl.multiple_of(owner * size, size), size), :] = parts[k][...]

    views = [[r.at[:, c * width : (c + 1) * width] for c in range(3)] for r in (qkv_ref, dqkv_ref)]
    attend_back_kernel(
        heads,
        query_size,
        key_size,
        first_ref,
        last_ref,
        low_ref,
        high_ref,
        *views[0],
        out_ref,
        grad_ref,
        log_ref,
        *views[1],
        *refs[9 + groups : -1],
    )


def ffn_kernel(tile, carried, *refs):
    n_own_ref, n_far_ref, g_own_ref, g_far_ref, weights_ref = refs[:5]
    out_in_ref, back_in_ref = refs[5:7] if carried else (None, None)
    results = refs[7:-8] if carried else refs[5:-8]
    z_rows, du_rows, out_acc, back_acc, n_ref, n_turned, g_ref, g_turned = refs[-8:]
    grads_ref = results[0]
    step = pl.program_id(0)
    rows, width = n_ref.shape
    chips, piece = weights_ref.shape[0], weights_ref.shape[3]
    units = chips * piece
    share = width // chips
    w_in = weights_ref[:, 0, 0].reshape(units, width)
    w_out = weights_ref[:, 0, 1].reshape(units, width)

    @pl.when(step == 0)
    def _():
        half = rows // 2
        for joined, turned, parts in (
            (n_ref, n_turned, (n_own_ref, n_far_ref)),
            (g_ref, g_turned, (g_own_ref, g_far_ref)),
        ):
            for i, source in enumerate(parts):
                joined[i * half : (i + 1) * half, :] = source[...]
                turned[:, i * half : (i + 1) * half] = source[...].T
        if carried:
            out_acc[...] = out_in_ref[...]
            back_acc[...] = back_in_ref[...]
        else:
            out_acc[...] = jnp.zeros_like(out_acc)
            back_acc[...] = jnp.zeros_like(back_acc)

    def row_tile(i, carry):
        part = pl.ds(pl.multiple_of(i * tile, tile), tile)
        pre = times_transposed(n_ref[part, :], w_in)
        scaled = lax.erf(pre * 0.7071067811865476)
        density = jnp.exp(pre * pre * -0.5) * 0.3989422804014327
        below = 0.5 + 0.5 * scaled
        hidden = (pre * below).astype(jnp.bfloat16)
        z_rows[part, :] = hidden
        out_acc[part, :] += dot(hidden, w_out)
        hidden_grad = times_transposed(g_ref[part, :], w_out)
        pre_grad = (hidden_grad * (below + pre * density)).astype(jnp.bfloat16)
        du_rows[part, :] = pre_grad
        back_acc[part, :] += dot(pre_grad, w_in)
        return carry

    lax.fori_loop(0, rows // tile, row_tile, 0)
    for c in range(chips):
        part = slice(c * share, (c + 1) * share)
        grads_ref[c, 0, 0] = dot(n_turned[part, :], du_rows[...]).astype(jnp.bfloat16)
        grads_ref[c, 0, 1] = dot(g_turned[part, :], z_rows[...]).astype(jnp.bfloat16)

    @pl.when(step == pl.num_programs(0) - 1)
    def _():
        own = rows // 2
        if carried:
            out_ref, out_far_ref, back_ref, back_far_ref = results[1:]
            out_ref[...] = out_acc[:own, :]
            out_far_ref[...] = out_acc[own:, :].astype(jnp.bfloat16)
            back_ref[...] = back_acc[:own, :]
            back_far_ref[...] = back_acc[own:, :].astype(jnp.bfloat16)
        else:
            results[1][...] = out_acc[...]
            results[2][...] = back_acc[...]


def ffn_call(n_own, n_far, g_own, g_far, weights, sums):
    rows, width = 2 * n_own.shape[0], n_own.shape[1]
    chips, groups, _, piece, _ = weights.shape
    units = chips * piece
    whole = lambda shape: pl.BlockSpec(shape, lambda t: (0,) * len(shape))
    own = (rows // 2, width)
    grads = (chips, 1, 2, width // chips, units)
    f32, bf16 = jnp.float32, jnp.bfloat16
    if sums:
        results = [(own, f32), (own, bf16), (own, f32), (own, bf16)]
    else:
        results = [((rows, width), f32)] * 2
    return pl.pallas_call(
        partial(ffn_kernel, min(256, rows), bool(sums)),
        grid=(groups,),
        in_specs=[whole(own)] * 4
        + [pl.BlockSpec((chips, 1, 2, piece, width), lambda t: (0, t, 0, 0, 0))]
        + [whole((rows, width))] * len(sums),
        out_specs=[pl.BlockSpec(grads, lambda t: (0, t, 0, 0, 0))]
        + [whole(shape) for shape, _ in results],
        out_shape=[jax.ShapeDtypeStruct((chips, groups, *grads[2:]), bf16)]
        + [jax.ShapeDtypeStruct(*one) for one in results],
        scratch_shapes=[
            pltpu.VMEM((rows, units), bf16),
            pltpu.VMEM((rows, units), bf16),
            pltpu.VMEM((rows, width), f32),
            pltpu.VMEM((rows, width), f32),
            pltpu.VMEM((rows, width), bf16),
            pltpu.VMEM((width, rows), bf16),
            pltpu.VMEM((rows, width), bf16),
            pltpu.VMEM((width, rows), bf16),
        ],
        compiler_params=pltpu.CompilerParams(vmem_limit_bytes=VMEM_BYTES),
        cost_estimate=about(23),
    )(n_own, n_far, g_own, g_far, weights, *sums)


def unit_norm(values):
    center = values - jnp.mean(values, axis=1, keepdims=True)
    inverse = lax.rsqrt(jnp.mean(center * center, axis=1, keepdims=True) + EPSILON)
    return center * inverse, inverse


def unit_back(gradient, values, gain):
    unit, inverse = unit_norm(values)
    scaled = gradient * gain
    inner = (
        scaled
        - jnp.mean(scaled, axis=1, keepdims=True)
        - unit * jnp.mean(scaled * unit, axis=1, keepdims=True)
    )
    return (
        inner * inverse,
        jnp.sum(gradient * unit, axis=0, keepdims=True),
        jnp.sum(gradient, axis=0, keepdims=True),
    )


def first_kernel(frames_ref, gain_ref, bias_ref, weight_ref, normed_ref, packed_ref):
    unit, _ = unit_norm(frames_ref[...].astype(jnp.float32))
    normed = (unit * gain_ref[0:1, :] + bias_ref[0:1, :]).astype(jnp.bfloat16)
    normed_ref[...] = normed
    packed_ref[...] = dot(normed, weight_ref[...]).astype(jnp.bfloat16)


def first_call(frames, gain, bias, weight, tile):
    rows, width = frames.shape
    columns = weight.shape[1]
    moving = lambda size: pl.BlockSpec((tile, size), lambda i: (i, 0))
    fixed = lambda shape: pl.BlockSpec(shape, lambda i: (0, 0))
    return pl.pallas_call(
        first_kernel,
        grid=(rows // tile,),
        in_specs=[moving(width), fixed(gain.shape), fixed(bias.shape), fixed(weight.shape)],
        out_specs=[moving(width), moving(columns)],
        out_shape=[
            jax.ShapeDtypeStruct((rows, width), jnp.bfloat16),
            jax.ShapeDtypeStruct((rows, columns), jnp.bfloat16),
        ],
        compiler_params=pltpu.CompilerParams(vmem_limit_bytes=VMEM_BYTES),
        cost_estimate=about(9),
    )(frames, gain, bias, weight)


def weight_copies(core_ref, local_ref, mine_ref, far_ref, weights, sems):
    half = mine_ref.shape[1]
    core = core_ref[0]
    copies = [pltpu.make_async_copy(local_ref, weights.at[0], sems.at[0])]
    for k in range(1, weights.shape[0]):
        for n, (source, side) in enumerate(((mine_ref, core), (far_ref, 1 - core))):
            rows = pl.ds(pl.multiple_of(side * half, half), half)
            copies.append(
                pltpu.make_async_copy(
                    source.at[k - 1], weights.at[k, rows], sems.at[2 * k - 1 + n]
                )
            )
    return copies


def middle_kernel(
    heads,
    tile,
    core_ref,
    low_ref,
    high_ref,
    inputs_ref,
    text_ref,
    gain_ref,
    bias_ref,
    local_ref,
    mine_ref,
    far_ref,
    *rest,
):
    groups = len(rest) - 9 - 4
    mixes = rest[:groups]
    h1_ref, h2_ref, n2_ref, n3_ref, cq_ref, mix_ref, ck_ref, cv_ref, log_ref = rest[
        groups : groups + 9
    ]
    weights, turned, mix_turned, sems = rest[groups + 9 :]
    width = heads * HEAD
    text_width = text_ref.shape[1]
    keys = text_ref.shape[0]
    copies = weight_copies(core_ref, local_ref, mine_ref, far_ref, weights, sems)
    for copy in copies:
        copy.start()
    for copy in copies:
        copy.wait()
    text = text_ref[...]
    for k in range(groups):
        part = slice(k * width, (k + 1) * width)
        key_weight = weights[k, 3 * width : 4 * width, :text_width]
        value_weight = weights[k, 4 * width : 5 * width, :text_width]
        ck_ref[:, part] = times_transposed(text, key_weight).astype(jnp.bfloat16)
        cv_ref[:, part] = times_transposed(text, value_weight).astype(jnp.bfloat16)
        turned[k] = times_transposed(value_weight, text).astype(jnp.bfloat16)

    def row_tile(i, carry):
        rows = pl.ds(pl.multiple_of(i * tile, tile), tile)
        total = inputs_ref[rows, :].astype(jnp.float32)
        for k in range(groups):
            total += dot(mixes[k][rows, :], weights[k, 0:width, :])
        h1_ref[rows, :] = total
        unit, _ = unit_norm(total)
        normed = (unit * gain_ref[1:2, :] + bias_ref[1:2, :]).astype(jnp.bfloat16)
        n2_ref[rows, :] = normed
        allowed = allowed_keys(low_ref[i], high_ref[i], 0, (keys, tile))
        for k in range(groups):
            part = slice(k * width, (k + 1) * width)
            queries = times_transposed(normed, weights[k, width : 2 * width, :])
            queries = queries.astype(jnp.bfloat16)
            cq_ref[rows, part] = queries
            queries = queries * jnp.bfloat16(0.125)
            for h in range(heads):
                scores = times_transposed(ck_ref[:, part], queries * head_mask(width, h))
                scores = jnp.where(allowed, scores, NEGATIVE)
                top = jnp.max(scores, axis=0, keepdims=True)
                probs = jnp.exp(scores - top)
                sums = jnp.sum(probs, axis=0, keepdims=True)
                lane = slice(h * HEAD, (h + 1) * HEAD)
                mix_turned[lane, :] = dot(turned[k, lane, :], probs.astype(jnp.bfloat16)) / sums
                log_ref[i, k * heads + h : k * heads + h + 1, :] = top + jnp.log(sums)
            mix_ref[rows, part] = mix_turned[...].T.astype(jnp.bfloat16)
        total = h1_ref[rows, :]
        for k in range(groups):
            part = slice(k * width, (k + 1) * width)
            total += dot(mix_ref[rows, part], weights[k, 2 * width : 3 * width, :])
        h2_ref[rows, :] = total
        unit, _ = unit_norm(total)
        n3_ref[rows, :] = (unit * gain_ref[2:3, :] + bias_ref[2:3, :]).astype(jnp.bfloat16)
        return carry

    lax.fori_loop(0, inputs_ref.shape[0] // tile, row_tile, 0)


def middle_back_kernel(
    heads,
    tile,
    core_ref,
    low_ref,
    high_ref,
    text_ref,
    gain_ref,
    third_ref,
    third_far_ref,
    grad_ref,
    h1_ref,
    h2_ref,
    cq_ref,
    mix_ref,
    ck_ref,
    cv_ref,
    log_ref,
    local_ref,
    mine_ref,
    far_ref,
    cross_side_ref,
    dcq_ref,
    dck_ref,
    dcv_ref,
    self_exact_ref,
    self_side_ref,
    mix_grad_ref,
    norm_ref,
    text_part_ref,
    weights,
    turned,
    query_turned,
    dk_acc,
    dv_acc,
    sems,
):
    groups = weights.shape[0]
    width = heads * HEAD
    text_width = text_ref.shape[1]
    keys = text_ref.shape[0]
    copies = weight_copies(core_ref, local_ref, mine_ref, far_ref, weights, sems)
    for copy in copies:
        copy.start()
    for copy in copies:
        copy.wait()
    text = text_ref[...]
    for k in range(groups):
        key_weight = weights[k, 3 * width : 4 * width, :text_width]
        turned[k] = times_transposed(key_weight, text).astype(jnp.bfloat16)
    dk_acc[...] = jnp.zeros_like(dk_acc)
    dv_acc[...] = jnp.zeros_like(dv_acc)
    norm_ref[...] = jnp.zeros_like(norm_ref)

    def row_tile(i, carry):
        rows = pl.ds(pl.multiple_of(i * tile, tile), tile)
        third = third_ref[rows, :] + third_far_ref[rows, :].astype(jnp.float32)
        back, gain_sum, bias_sum = unit_back(third, h2_ref[rows, :], gain_ref[2:3, :])
        norm_ref[2:3, :] += gain_sum
        norm_ref[5:6, :] += bias_sum
        cross_exact = grad_ref[rows, :].astype(jnp.float32) + back
        cross_side = cross_exact.astype(jnp.bfloat16)
        self_exact_ref[rows, :] = cross_exact
        cross_side_ref[rows, :] = cross_side
        allowed = allowed_keys(low_ref[i], high_ref[i], 0, (keys, tile))
        for k in range(groups):
            part = slice(k * width, (k + 1) * width)
            mix_grad = times_transposed(cross_side, weights[k, 2 * width : 3 * width, :])
            mix_grad = mix_grad.astype(jnp.bfloat16)
            product = mix_grad.astype(jnp.float32) * mix_ref[rows, part].astype(jnp.float32)
            product = product.T
            queries = cq_ref[rows, part] * jnp.bfloat16(0.125)
            for h in range(heads):
                mask = head_mask(width, h)
                lane = slice(h * HEAD, (h + 1) * HEAD)
                one = k * heads + h
                q_rows = queries * mask
                grad_rows = mix_grad * mask
                scores = times_transposed(ck_ref[:, part], q_rows)
                probs = jnp.exp(scores - log_ref[i, one : one + 1, :])
                probs = jnp.where(allowed, probs, 0.0)
                prob_grad = times_transposed(cv_ref[:, part], grad_rows)
                delta = jnp.sum(product[lane, :], axis=0, keepdims=True)
                score_grad = (probs * (prob_grad - delta)).astype(jnp.bfloat16)
                dv_acc[:, part] += dot(probs.astype(jnp.bfloat16), grad_rows)
                dk_acc[:, part] += dot(score_grad, q_rows)
                query_turned[lane, :] = dot(turned[k, lane, :], score_grad)
            dcq_ref[rows, part] = (query_turned[...] * 0.125).T.astype(jnp.bfloat16)
        second = jnp.zeros(cross_exact.shape, jnp.float32)
        for k in range(groups):
            part = slice(k * width, (k + 1) * width)
            second += dot(dcq_ref[rows, part], weights[k, width : 2 * width, :])
        back, gain_sum, bias_sum = unit_back(second, h1_ref[rows, :], gain_ref[1:2, :])
        norm_ref[1:2, :] += gain_sum
        norm_ref[4:5, :] += bias_sum
        self_exact = self_exact_ref[rows, :] + back
        self_exact_ref[rows, :] = self_exact
        self_side = self_exact.astype(jnp.bfloat16)
        self_side_ref[rows, :] = self_side
        for k in range(groups):
            mix_grad_ref[k, rows, :] = times_transposed(
                self_side, weights[k, 0:width, :]
            ).astype(jnp.bfloat16)
        return carry

    lax.fori_loop(0, third_ref.shape[0] // tile, row_tile, 0)
    dck_ref[...] = dk_acc[...].astype(jnp.bfloat16)
    dcv_ref[...] = dv_acc[...].astype(jnp.bfloat16)
    text_part = jnp.zeros(text_part_ref.shape, jnp.float32)
    for k in range(groups):
        part = slice(k * width, (k + 1) * width)
        text_part += dot(dck_ref[:, part], weights[k, 3 * width : 4 * width, :text_width])
        text_part += dot(dcv_ref[:, part], weights[k, 4 * width : 5 * width, :text_width])
    text_part_ref[...] = text_part.astype(jnp.bfloat16)


def weight_grads_kernel(heads, core_ref, *refs):
    kept_ref, sent_ref = refs[-2:]
    self_ref, n2_ref, cq_ref, mix_ref, cross_ref, dck_ref, dcv_ref, text_ref = refs[:8]
    mixes = refs[8:-2]
    width = heads * HEAD
    half = kept_ref.shape[1]
    text_width = text_ref.shape[1]
    for k in range(kept_ref.shape[0]):
        part = slice(k * width, (k + 1) * width)
        pairs = [
            (mixes[k][...], self_ref),
            (cq_ref[:, part], n2_ref),
            (mix_ref[:, part], cross_ref),
            (dck_ref[:, part], text_ref),
            (dcv_ref[:, part], text_ref),
        ]
        for n, (left, right) in enumerate(pairs):
            product = contract_rows(left, right[...]).astype(jnp.bfloat16)
            for side in range(2):
                low, high = max(n * width, side * half), min((n + 1) * width, (side + 1) * half)
                if low >= high:
                    continue
                rows = slice(low - side * half, high - side * half)
                block = product[low - n * width : high - n * width, :]
                for target, wanted in ((kept_ref, side), (sent_ref, 1 - side)):

                    @pl.when(core_ref[0] == wanted)
                    def _(target=target, rows=rows, block=block, n=n):
                        if n < 3:
                            target[k, rows, :] = block
                        else:
                            target[k, rows, :text_width] = block
                            target[k, rows, text_width:] = jnp.zeros(
                                (block.shape[0], target.shape[2] - text_width), jnp.bfloat16
                            )


def weight_grads_call(heads, core, arrays, mixes):
    groups, width = len(mixes), arrays[0].shape[1]
    half = 5 * heads * HEAD // 2
    return pl.pallas_call(
        partial(weight_grads_kernel, heads),
        in_specs=[pl.BlockSpec(memory_space=pltpu.SMEM)]
        + [local_spec()] * (len(arrays) + groups),
        out_specs=[local_spec()] * 2,
        out_shape=[jax.ShapeDtypeStruct((groups, half, width), jnp.bfloat16)] * 2,
        compiler_params=pltpu.CompilerParams(vmem_limit_bytes=VMEM_BYTES),
        cost_estimate=about(15),
    )(core, *arrays, *mixes)


def last_kernel(frames_ref, gain_ref, exact_ref, sum_ref, term_ref, out_ref, norm_ref):
    gradient = sum_ref[...].astype(jnp.float32) + term_ref[...]
    back, gain_sum, bias_sum = unit_back(
        gradient, frames_ref[...].astype(jnp.float32), gain_ref[0:1, :]
    )
    out_ref[...] = (exact_ref[...] + back).astype(jnp.bfloat16)
    norm_ref[0:1, :] = gain_sum
    norm_ref[1:2, :] = bias_sum


def last_call(frames, gains, exact, sums, term):
    rows, width = frames.shape
    return pl.pallas_call(
        last_kernel,
        in_specs=[local_spec()] * 5,
        out_specs=[local_spec()] * 2,
        out_shape=[
            jax.ShapeDtypeStruct((rows, width), jnp.bfloat16),
            jax.ShapeDtypeStruct((2, width), jnp.float32),
        ],
        compiler_params=pltpu.CompilerParams(vmem_limit_bytes=VMEM_BYTES),
        cost_estimate=about(4),
    )(frames, gains, exact, sums, term)


def ffn_end_kernel(core_ref, mine_ref, far_ref, in_ref, out_ref):
    units = mine_ref.shape[3]
    for source, side in ((mine_ref, core_ref[0]), (far_ref, 1 - core_ref[0])):
        part = pl.ds(pl.multiple_of(side * units, units), units)
        in_ref[:, part] = source[0, 0].astype(jnp.float32)
        out_ref[part, :] = source[0, 1].astype(jnp.float32).T


def ffn_end_call(core, mine, far):
    chips, _, features, units = mine.shape
    source = pl.BlockSpec((1, 2, features, units), lambda c: (c, 0, 0, 0))
    return pl.pallas_call(
        ffn_end_kernel,
        grid=(chips,),
        in_specs=[pl.BlockSpec(memory_space=pltpu.SMEM), source, source],
        out_specs=[
            pl.BlockSpec((features, 2 * units), lambda c: (c, 0)),
            pl.BlockSpec((2 * units, features), lambda c: (0, c)),
        ],
        out_shape=[
            jax.ShapeDtypeStruct((chips * features, 2 * units), jnp.float32),
            jax.ShapeDtypeStruct((2 * units, chips * features), jnp.float32),
        ],
        compiler_params=pltpu.CompilerParams(vmem_limit_bytes=VMEM_BYTES),
        cost_estimate=about(5),
    )(core, mine, far)


def small_end_kernel(
    heads, text_width, core_ref, mine_ref, far_ref, qkv_mine_ref, qkv_far_ref, *refs
):
    self_ref, query_ref, cross_ref, pair_ref, qkv_ref, joined = refs
    width = heads * HEAD
    half = mine_ref.shape[0]
    for source, side in ((mine_ref, core_ref[0]), (far_ref, 1 - core_ref[0])):
        joined[pl.ds(pl.multiple_of(side * half, half), half), :] = source[...]
    self_ref[...] = joined[0:width, :].astype(jnp.float32)
    query_ref[...] = joined[width : 2 * width, :].astype(jnp.float32).T
    cross_ref[...] = joined[2 * width : 3 * width, :].astype(jnp.float32)
    for h in range(heads):
        rows = [slice((3 + c) * width + h * HEAD, (3 + c) * width + (h + 1) * HEAD) for c in (0, 1)]
        both = jnp.concatenate([joined[part, :text_width] for part in rows], 0)
        pair_ref[:, 2 * h * HEAD : 2 * (h + 1) * HEAD] = both.astype(jnp.float32).T
    size = qkv_mine_ref.shape[0]
    for source, side in ((qkv_mine_ref, core_ref[0]), (qkv_far_ref, 1 - core_ref[0])):
        values = source[...].astype(jnp.float32)
        columns = [
            values[:, c * width + h * HEAD : c * width + (h + 1) * HEAD]
            for h in range(heads)
            for c in range(3)
        ]
        qkv_ref[pl.ds(pl.multiple_of(side * size, size), size), :] = jnp.concatenate(columns, 1)


def small_end_call(heads, text_width, core, mine, far, qkv_mine, qkv_far):
    width = mine.shape[1]
    head_width = heads * HEAD
    shapes = [
        (head_width, width),
        (width, head_width),
        (head_width, width),
        (text_width, 2 * head_width),
        (2 * qkv_mine.shape[0], qkv_mine.shape[1]),
    ]
    return pl.pallas_call(
        partial(small_end_kernel, heads, text_width),
        in_specs=[pl.BlockSpec(memory_space=pltpu.SMEM)] + [local_spec()] * 4,
        out_specs=[local_spec()] * 5,
        out_shape=[jax.ShapeDtypeStruct(shape, jnp.float32) for shape in shapes],
        scratch_shapes=[pltpu.VMEM((2 * mine.shape[0], width), jnp.bfloat16)],
        compiler_params=pltpu.CompilerParams(vmem_limit_bytes=VMEM_BYTES),
        cost_estimate=about(5),
    )(core, mine, far, qkv_mine, qkv_far)


def local_spec():
    return pl.BlockSpec(memory_space=pltpu.VMEM)


def middle_specs(plain):
    return (
        [pl.BlockSpec(memory_space=pltpu.SMEM)]
        + [local_spec()] * plain
        + [pl.BlockSpec(memory_space=pl.ANY)] * 3
    )


def middle_call(heads, tile, core, low, high, inputs, text, gains, biases, split_weights, mixes):
    rows, width = inputs.shape
    keys = text.shape[0]
    groups = len(mixes)
    f32, bf16 = jnp.float32, jnp.bfloat16
    shapes = [
        ((rows, width), f32),
        ((rows, width), f32),
        ((rows, width), bf16),
        ((rows, width), bf16),
        ((rows, width), bf16),
        ((rows, width), bf16),
        ((keys, width), bf16),
        ((keys, width), bf16),
        ((rows // tile, groups * heads, tile), f32),
    ]
    return pl.pallas_call(
        partial(middle_kernel, heads, tile),
        in_specs=middle_specs(6) + [local_spec()] * groups,
        out_specs=[local_spec()] * len(shapes),
        out_shape=[jax.ShapeDtypeStruct(*one) for one in shapes],
        scratch_shapes=[
            pltpu.VMEM((groups, *split_weights[0].shape), bf16),
            pltpu.VMEM((groups, heads * HEAD, keys), bf16),
            pltpu.VMEM((heads * HEAD, tile), f32),
            pltpu.SemaphoreType.DMA((2 * groups - 1,)),
        ],
        compiler_params=pltpu.CompilerParams(vmem_limit_bytes=VMEM_BYTES),
        cost_estimate=about(30),
    )(core, lanes(low, tile), lanes(high, tile), inputs, text, gains, biases, *split_weights, *mixes)


def middle_back_call(heads, tile, core, low, high, text, gains, saved, split_weights):
    rows, width = saved[0].shape
    keys = text.shape[0]
    groups = width // (heads * HEAD)
    f32, bf16 = jnp.float32, jnp.bfloat16
    shapes = [
        ((rows, width), bf16),
        ((rows, width), bf16),
        ((keys, width), bf16),
        ((keys, width), bf16),
        ((rows, width), f32),
        ((rows, width), bf16),
        ((groups, rows, heads * HEAD), bf16),
        ((6, width), f32),
        (text.shape, bf16),
    ]
    return pl.pallas_call(
        partial(middle_back_kernel, heads, tile),
        in_specs=middle_specs(4 + len(saved)),
        out_specs=[local_spec()] * len(shapes),
        out_shape=[jax.ShapeDtypeStruct(*one) for one in shapes],
        scratch_shapes=[
            pltpu.VMEM((groups, *split_weights[0].shape), bf16),
            pltpu.VMEM((groups, heads * HEAD, keys), bf16),
            pltpu.VMEM((heads * HEAD, tile), f32),
            pltpu.VMEM((keys, width), f32),
            pltpu.VMEM((keys, width), f32),
            pltpu.SemaphoreType.DMA((2 * groups - 1,)),
        ],
        compiler_params=pltpu.CompilerParams(vmem_limit_bytes=VMEM_BYTES),
        cost_estimate=about(40),
    )(core, lanes(low, tile), lanes(high, tile), text, gains, *saved, *split_weights)


def lanes(values, size):
    return values.astype(jnp.int32).reshape(-1, 1, size)


def attend_call(q, k, v, columns, groups, heads, low, high, first, last, query_size, key_size):
    width = heads * HEAD
    rows, keys = q.shape[0], k.shape[0]
    blocks = rows // query_size
    spec = lambda size, column: pl.BlockSpec((size, width), lambda g, i, *_: (0, column + g))
    vector = pl.BlockSpec((1, 1, query_size), lambda g, i, *_: (i, 0, 0))
    q_column = columns[0]
    return pl.pallas_call(
        partial(attend_kernel, heads, key_size),
        grid_spec=pltpu.PrefetchScalarGridSpec(
            num_scalar_prefetch=2,
            grid=(groups, blocks),
            in_specs=[
                vector,
                vector,
                pl.BlockSpec((query_size, width), lambda g, i, *_: (i, q_column + g)),
                spec(keys, columns[1]),
                spec(keys, columns[2]),
            ],
            out_specs=[
                pl.BlockSpec((query_size, width), lambda g, i, *_: (i, g)),
                pl.BlockSpec((1, 1, heads, query_size), lambda g, i, *_: (g, i, 0, 0)),
            ],
            scratch_shapes=[
                pltpu.VMEM((keys // key_size, width, key_size), jnp.bfloat16),
                pltpu.VMEM((width, query_size), jnp.float32),
            ],
        ),
        out_shape=[
            jax.ShapeDtypeStruct((rows, groups * width), jnp.bfloat16),
            jax.ShapeDtypeStruct((groups, blocks, heads, query_size), jnp.float32),
        ],
        compiler_params=pltpu.CompilerParams(vmem_limit_bytes=VMEM_BYTES),
        cost_estimate=about(30 if groups == 1 else 17),
    )(first, last, lanes(low, query_size), lanes(high, query_size), q, k, v)


def back_scratch(heads, blocks, query_size, key_size):
    width = heads * HEAD
    return [
        pltpu.VMEM((blocks, heads, query_size, width), jnp.bfloat16),
        pltpu.VMEM((blocks, heads, query_size, width), jnp.bfloat16),
        pltpu.VMEM((width, key_size), jnp.bfloat16),
        pltpu.VMEM((blocks, heads, query_size), jnp.float32),
        pltpu.VMEM((blocks, width, query_size), jnp.float32),
        pltpu.VMEM((key_size, width), jnp.float32),
        pltpu.VMEM((key_size, width), jnp.float32),
    ]


def packed_back_call(
    qkv, out, parts, logs, heads, group, low, high, first, last, query_size, key_size
):
    rows, width = out.shape
    blocks = rows // query_size
    whole = lambda shape: pl.BlockSpec(shape, lambda g, j, *_: (0,) * len(shape))
    vector = whole((blocks, 1, query_size))
    return pl.pallas_call(
        partial(packed_back_kernel, heads, query_size, key_size, len(parts)),
        grid_spec=pltpu.PrefetchScalarGridSpec(
            num_scalar_prefetch=3,
            grid=(1, rows // key_size),
            in_specs=[vector, vector, whole(qkv.shape), whole(out.shape)]
            + [whole(part.shape) for part in parts]
            + [whole(logs.shape)],
            out_specs=whole(qkv.shape),
            scratch_shapes=back_scratch(heads, blocks, query_size, key_size)
            + [pltpu.VMEM(out.shape, jnp.bfloat16)],
        ),
        out_shape=jax.ShapeDtypeStruct(qkv.shape, jnp.bfloat16),
        compiler_params=pltpu.CompilerParams(vmem_limit_bytes=VMEM_BYTES),
        cost_estimate=about(30),
    )(
        first,
        last,
        group,
        lanes(low, query_size),
        lanes(high, query_size),
        qkv,
        out,
        *parts,
        logs,
    )


def attend_back_call(q, k, v, out, grad, logs, groups, heads, low, high, first, last, query_size, key_size):
    width = heads * HEAD
    rows, keys = q.shape[0], k.shape[0]
    blocks = rows // query_size
    column = lambda size: pl.BlockSpec((size, width), lambda g, j, *_: (0, g))
    vector = pl.BlockSpec((blocks, 1, query_size), lambda g, j, *_: (0, 0, 0))
    return pl.pallas_call(
        partial(attend_back_kernel, heads, query_size, key_size),
        grid_spec=pltpu.PrefetchScalarGridSpec(
            num_scalar_prefetch=2,
            grid=(groups, keys // key_size),
            in_specs=[
                vector,
                vector,
                column(rows),
                column(keys),
                column(keys),
                column(rows),
                column(rows),
                pl.BlockSpec((1, blocks, heads, query_size), lambda g, j, *_: (g, 0, 0, 0)),
            ],
            out_specs=[column(rows), column(keys), column(keys)],
            scratch_shapes=back_scratch(heads, blocks, query_size, key_size),
        ),
        out_shape=[
            jax.ShapeDtypeStruct((rows, groups * width), jnp.bfloat16),
            jax.ShapeDtypeStruct((keys, groups * width), jnp.bfloat16),
            jax.ShapeDtypeStruct((keys, groups * width), jnp.bfloat16),
        ],
        compiler_params=pltpu.CompilerParams(vmem_limit_bytes=VMEM_BYTES),
        cost_estimate=about(6 * groups),
    )(first, last, lanes(low, query_size), lanes(high, query_size), q, k, v, out, grad, logs)


def per_device(
    frames,
    text_states,
    clip_lengths,
    text_lengths,
    norm_gains,
    norm_biases,
    self_qkv,
    self_out,
    cross_query,
    cross_kv,
    cross_out,
    ffn_in,
    ffn_out,
    out_grad,
):
    groups = lax.axis_size("tensor")
    chips = lax.axis_size("chip")
    group = lax.axis_index("tensor")
    chip = lax.axis_index("chip")
    core = lax.axis_index("core")
    bf16 = jnp.bfloat16
    frame_count, width = frames.shape
    own_rows = frame_count // groups
    offset = group * own_rows
    clip_count, text_slots, text_width = text_states.shape
    head_count = self_out.shape[0] // HEAD
    all_heads = head_count * groups
    ends = jnp.cumsum(clip_lengths[0])
    starts = ends - clip_lengths[0]
    positions = jnp.arange(frame_count, dtype=jnp.int32)[:, None]
    clip_first = jnp.max(jnp.where(positions >= starts, starts, 0), axis=1)
    clip_stop = jnp.min(jnp.where(positions < ends, ends, frame_count), axis=1)
    block = min(256, own_rows)
    blocks = jnp.arange(frame_count // block, dtype=jnp.int32)
    self_low, self_high = clip_first, positions[:, 0]
    wide = min(2 * block, frame_count)
    wides = jnp.arange(frame_count // wide, dtype=jnp.int32)
    self_keys = (clip_first[::wide] // block, (wides * wide + wide - 1) // block)
    self_queries = (blocks * block // wide, (clip_stop[block - 1 :: block] - 1) // wide)
    own_positions = offset + jnp.arange(own_rows, dtype=jnp.int32)[:, None]
    own_clip = jnp.sum((own_positions >= ends).astype(jnp.int32), axis=1)
    own_length = jnp.sum(
        jnp.where(own_clip[:, None] == jnp.arange(clip_count), text_lengths[0], 0), axis=1
    )
    cross_low = own_clip * text_slots
    cross_high = cross_low + own_length - 1
    cross_keys = (own_clip[::block], own_clip[block - 1 :: block])
    inside_first = jnp.clip(starts - offset, 0, own_rows)
    inside_stop = jnp.clip(ends - offset, 0, own_rows)
    cross_first = jnp.minimum(inside_first // block, own_rows // block - 1)
    cross_queries = (
        cross_first,
        jnp.where(inside_stop > inside_first, (inside_stop - 1) // block, cross_first - 1),
    )

    head_width = head_count * HEAD
    kv_turned = cross_kv.reshape(text_width, head_count, 2, HEAD).transpose(2, 1, 3, 0)
    kv_turned = jnp.pad(
        kv_turned.reshape(2 * head_width, text_width), ((0, 0), (0, width - text_width))
    )
    local = jnp.concatenate([self_out, cross_query.T, cross_out, kv_turned], 0)
    pieces = local.reshape(2, chips, -1, width)
    cuts = [i * head_width for i in range(6)]

    half = ffn_out.shape[0] // 2
    piece = half // chips
    unit_first = core * half + chip * piece
    sent_piece = pick(pick(pieces, core, 0), chip, 0)
    sent_piece, frames, self_qkv, ffn_in, ffn_out = phase(
        sent_piece, frames, self_qkv, ffn_in, ffn_out
    )
    passed = [shift(sent_piece, k) for k in range(1, groups)]
    ffn_piece = jnp.concatenate(
        [
            lax.dynamic_slice_in_dim(ffn_in, unit_first, piece, 1).T,
            lax.dynamic_slice_in_dim(ffn_out, unit_first, piece, 0),
        ],
        0,
    )
    ffn_passed = [shift(ffn_piece, 1)]
    w_qkv = self_qkv.reshape(width, head_count, 3, HEAD).transpose(0, 2, 1, 3).reshape(width, -1)
    rows_one, packed = first_call(frames, norm_gains, norm_biases, w_qkv, block)
    if head_width % 128 == 0:
        self_parts, self_columns = (packed,) * 3, (0, 1, 2)
    else:
        self_parts, self_columns = jnp.split(packed, 3, 1), (0, 0, 0)
    self_mix, self_logs = attend_call(
        *self_parts, self_columns, 1, head_count, self_low, self_high, *self_keys, wide, block
    )
    ffn_passed[0], self_mix, *passed = phase(ffn_passed[0], self_mix, *passed)

    steps = axis_bits("chip")
    joined = chip_gather_start(jnp.stack(passed))
    ffn_joined = chip_gather_start(ffn_passed[0][None])
    flipped = chip_gather_flips(joined, 0)
    ffn_own = jnp.stack(
        [
            lax.dynamic_slice_in_dim(ffn_in, core * half, half, 1).T.reshape(chips, piece, width),
            lax.dynamic_slice_in_dim(ffn_out, core * half, half, 0).reshape(chips, piece, width),
        ],
        1,
    )
    own_frames = lax.dynamic_slice_in_dim(frames, offset, own_rows, 0)
    grad_own_bf = lax.dynamic_slice_in_dim(out_grad, offset, own_rows, 0)
    arrived, ffn_own, own_frames, grad_own_bf, *flipped = phase(
        shift(ffn_passed[0], 1), ffn_own, own_frames, grad_own_bf, *flipped
    )
    ffn_passed.append(arrived)
    joined = chip_gather_joins(joined, flipped, 0)

    mix_blocks = self_mix.reshape(groups, own_rows, head_width)
    mixes = [pick(mix_blocks, group, 0)] + [
        shift(pick(mix_blocks, (group + k) % groups, 0), k) for k in range(1, groups)
    ]
    flipped = chip_gather_flips(joined, 1)
    count = len(flipped)
    found = phase(*flipped, *mixes)
    flipped, mixes = found[:count], list(found[count:])
    joined = chip_gather_joins(joined, flipped, 1)
    for step in range(2, steps):
        joined = chip_gather_joins(joined, phase(*chip_gather_flips(joined, step)), step)
    for _ in range(groups - 3):
        ffn_passed.append(shift(ffn_passed[-1], 1))
    mine = chip_gather_end(joined).reshape(groups - 1, -1, width)
    flipped = chip_gather_flips(ffn_joined, 0)
    far, ffn_passed[-1], *flipped = phase(swap_core(mine), ffn_passed[-1], *flipped)
    ffn_joined = chip_gather_joins(ffn_joined, flipped, 0)
    split_weights = (local, mine, far)
    ffn_late = gather(jnp.stack(ffn_passed[1:])[None], "chip")
    ffn_late = ffn_late.reshape(chips, groups - 2, 2, piece, width)
    ffn_flipped = chip_gather_flips(ffn_joined, 1)

    text_flat = text_states.reshape(clip_count * text_slots, text_width)
    core_index = core.reshape(1).astype(jnp.int32)
    shape = (head_count, block, core_index, cross_low, cross_high)
    after_self, after_cross, rows_two, rows_three, cross_q, cross_flat, cross_k, cross_v, cross_logs = (
        middle_call(
            *shape, own_frames, text_flat, norm_gains, norm_biases, split_weights, mixes
        )
    )

    grad_far = swap_core(grad_own_bf)
    rows_three, grad_far, *ffn_flipped = phase(rows_three, grad_far, *ffn_flipped)
    rows_far = swap_core(rows_three)
    ffn_joined = chip_gather_joins(ffn_joined, ffn_flipped, 1)
    for step in range(2, steps):
        ffn_joined = chip_gather_joins(ffn_joined, chip_gather_flips(ffn_joined, step), step)
    ffn_first = chip_gather_end(ffn_joined).reshape(chips, 2, piece, width)
    ffn_first = jnp.stack([ffn_own, ffn_first], 1)
    row_sets = (rows_three, rows_far, grad_own_bf, grad_far)
    ffn_part, *sums = ffn_call(*row_sets, ffn_first, ())
    ffn_sum = scatter_sum(ffn_part.reshape(-1, half), "chip")
    ffn_late_part, out_own, out_far, third_own_grad, third_far = ffn_call(
        *row_sets, ffn_late, tuple(sums)
    )
    ffn_late_sum = scatter_sum(ffn_late_part.reshape(-1, half), "chip")
    saved = (
        third_own_grad,
        swap_core(third_far),
        grad_own_bf,
        after_self,
        after_cross,
        cross_q,
        cross_flat,
        cross_k,
        cross_v,
        cross_logs,
    )
    (
        cross_grad,
        cq_flat,
        ck_grad,
        cv_grad,
        self_side,
        self_grad,
        mix_grad,
        norm_part,
        text_part,
    ) = middle_back_call(*shape, text_flat, norm_gains, saved, split_weights)

    mix_parts = [mix_grad[0]] + [shift(mix_grad[k], -k) for k in range(1, groups)]
    out_far = swap_core(out_far)
    small_part, small_sent = weight_grads_call(
        head_count,
        core_index,
        (self_grad, rows_two, cq_flat, cross_flat, cross_grad, ck_grad, cv_grad, text_flat),
        mixes,
    )
    text_blocks = text_part.reshape(clip_count * text_slots, groups, -1).transpose(1, 0, 2)
    small_sent, small_part, out_far, text_blocks, ffn_sum, *mix_parts = phase(
        small_sent, small_part, out_far, text_blocks, ffn_sum, *mix_parts
    )
    ffn_sum = ffn_sum.reshape(2, -1, half)
    mixed = (after_cross + out_own + out_far.astype(jnp.float32)).astype(bf16)

    small_far = swap_core(small_sent)
    text_parts = [pick(text_blocks, group, 0)] + [
        shift(pick(text_blocks, (group + k) % groups, 0), k) for k in range(1, groups)
    ]
    self_rest = (self_low, self_high, *self_queries, wide, block)
    if head_width % 128 == 0:
        packed_grad = packed_back_call(
            packed, self_mix, mix_parts, self_logs, head_count, group.reshape(1), *self_rest
        )
    else:
        mix_grad = jnp.concatenate([*mix_parts, *mix_parts], 0)
        mix_grad = lax.dynamic_slice_in_dim(
            mix_grad, (groups - group) % groups * own_rows, frame_count, 0
        )
        packed_grad = jnp.concatenate(
            attend_back_call(
                *self_parts, self_mix, mix_grad, self_logs, 1, head_count, *self_rest
            ),
            1,
        )
    ffn_running = shift(ffn_sum[1], 1)
    small_far, packed_grad, ffn_running, ffn_late_sum, *text_parts = phase(
        small_far, packed_grad, ffn_running, ffn_late_sum, *text_parts
    )
    ffn_terms = [*ffn_late_sum.reshape(groups - 2, -1, half), ffn_sum[0]]
    text_grad = sum(part.astype(jnp.float32) for part in text_parts)
    text_grad = text_grad.reshape(clip_count, text_slots, -1)

    packed_blocks = packed_grad.reshape(groups, own_rows, -1)

    def first_term(k):
        rows = pick(packed_blocks, (group + groups - k) % groups, 0)
        return times_transposed(rows, w_qkv)

    running, packed_grad, small_part, small_far, ffn_running = phase(
        first_term(1).astype(bf16), packed_grad, small_part, small_far, ffn_running
    )
    packed_blocks = packed_grad.reshape(groups, own_rows, -1)
    spread = [
        chip_scatter_start(one.reshape(groups, chips, -1, width)) for one in (small_part, small_far)
    ]
    small_parts = list(zip(*spread))
    small_ring = None
    for hop in range(1, groups):
        running = shift(running, 1)
        if hop < groups - 1:
            ffn_running = shift(ffn_running + ffn_terms[hop - 1], 1)
        moved = []
        if hop <= steps:
            moved = chip_scatter_flips(small_parts, hop - 1)
        elif small_ring is not None:
            moved = [shift(small_ring, 1)]
        extra = []
        if hop == 1:
            qkv_part = contract_rows(rows_one, packed_grad).astype(bf16)
            qkv_part = qkv_part.reshape(2, width // 2, -1)
            extra = [pick(qkv_part, 1 - core, 0), pick(qkv_part, core, 0)]
        elif hop == 2:
            extra = [swap_core(qkv_sent)]
        elif hop == 3:
            extra = [
                flip(part, order[0]) for part, order in zip(halves(qkv_part, 0), chip_orders())
            ]
        term = first_term((hop + 1) % groups)
        running, term, ffn_running, *found = phase(running, term, ffn_running, *moved, *extra)
        if hop < groups - 1:
            running, *found = phase((running.astype(jnp.float32) + term).astype(bf16), *found)
        moved, extra = found[: len(moved)], found[len(moved) :]
        if hop <= steps:
            small_parts = chip_scatter_adds(small_parts, moved, hop - 1)
            if hop == steps:
                small_part = jnp.concatenate([part[0] for part in small_parts], 1)
                small_ring = small_part[1]
                ring_next = 2
        elif moved:
            small_ring = moved[0] + small_part[ring_next % groups]
            ring_next += 1
        if hop == 1:
            qkv_sent, qkv_part = extra
        elif hop == 2:
            qkv_part = qkv_part + extra[0]
        elif hop == 3:
            qkv_halves = [part + other for part, other in zip(halves(qkv_part, 0), extra)]
    ffn_running += ffn_terms[groups - 2]
    frames_grad, norm_first = last_call(own_frames, norm_gains, self_side, running, term)
    norm_part = norm_part.at[0].set(norm_first[0]).at[3].set(norm_first[1]).reshape(2, 3, width)

    ffn_joined = chip_gather_start(ffn_running.reshape(1, -1, half))
    qkv_step, ffn_step, small_step = 1, 0, 0
    small_joined = None
    ffn_mine = ffn_far = small_mine = small_far = qkv_far = None
    norm_step = 0
    norm_parts = None
    while ffn_far is None or small_far is None or qkv_far is None or norm_parts is None:
        moves = []
        if ring_next <= groups:
            moves.append(("ring", [shift(small_ring, 1)]))
        elif small_step < steps:
            if small_joined is None:
                small_joined = chip_gather_start(small_ring[None])
            moves.append(("small", chip_gather_flips(small_joined, small_step)))
        elif small_far is None:
            small_mine = chip_gather_end(small_joined)
            moves.append(("small_far", [swap_core(small_mine)]))
        if norm_step == 0:
            moves.append(("norm", [swap_core(norm_part)]))
        elif norm_step <= steps:
            moves.append(("norm", [flip(norm_part, norm_step - 1)]))
        elif norm_parts is None:
            blocks_of = norm_part.reshape(2, 3, groups, -1)
            norm_parts = [pick(blocks_of, group, 2)]
            moves.append(
                (
                    "norm_parts",
                    [
                        shift(pick(blocks_of, (group + k) % groups, 2), k)
                        for k in range(1, groups)
                    ],
                )
            )
        if qkv_step < steps:
            moves.append(
                (
                    "qkv",
                    [flip(part, order[qkv_step]) for part, order in zip(qkv_halves, chip_orders())],
                )
            )
        elif qkv_far is None:
            qkv_part = jnp.concatenate(qkv_halves, 0)
            moves.append(("qkv_far", [swap_core(qkv_part)]))
        if ffn_step < steps:
            moves.append(("ffn", chip_gather_flips(ffn_joined, ffn_step)))
        elif ffn_far is None:
            ffn_mine = chip_gather_end(ffn_joined).reshape(chips, 2, -1, half)
            moves.append(("ffn_far", [swap_core(ffn_mine)]))
        found = list(phase(*[array for _, arrays in moves for array in arrays]))
        for name, arrays in moves:
            got, found = found[: len(arrays)], found[len(arrays) :]
            if name == "ring":
                small_ring = got[0] + small_part[ring_next % groups]
                ring_next += 1
            elif name == "small":
                small_joined = chip_gather_joins(small_joined, got, small_step)
                small_step += 1
            elif name == "small_far":
                small_far = got[0]
            elif name == "norm":
                norm_part = norm_part + got[0]
                norm_step += 1
            elif name == "norm_parts":
                norm_parts = norm_parts + got
            elif name == "qkv":
                qkv_halves = [part + other for part, other in zip(qkv_halves, got)]
                qkv_step += 1
            elif name == "qkv_far":
                qkv_far = got[0]
            elif name == "ffn":
                ffn_joined = chip_gather_joins(ffn_joined, got, ffn_step)
                ffn_step += 1
            elif name == "ffn_far":
                ffn_far = got[0]
    ffn_in_grad, ffn_out_grad = ffn_end_call(core_index, ffn_mine, ffn_far)
    norm_grads = sum(norm_parts)
    so_grad, cq_grad, co_grad, kv_grad, qkv_grad = small_end_call(
        head_count,
        text_width,
        core_index,
        small_mine.reshape(-1, width),
        small_far.reshape(-1, width),
        qkv_part,
        qkv_far,
    )
    return (
        mixed,
        frames_grad,
        text_grad,
        norm_grads,
        qkv_grad,
        so_grad,
        cq_grad,
        kv_grad,
        co_grad,
        ffn_in_grad,
        ffn_out_grad,
    )


def solution(mesh):
    rows, groups = mesh.devices.shape
    inner = Mesh(mesh.devices.reshape(rows // 2, 2, groups), ("chip", "core", "tensor"))
    data = ("chip", "core")
    in_specs = (
        P(data, None),
        P(data, None, None),
        P(data, None),
        P(data, None),
        P(),
        P(),
        P(None, "tensor"),
        P("tensor", None),
        P(None, "tensor"),
        P(None, "tensor"),
        P("tensor", None),
        P(None, "tensor"),
        P("tensor", None),
        P(data, None),
    )
    out_specs = (
        P((*data, "tensor"), None),
        P((*data, "tensor"), None),
        P(data, None, "tensor"),
        P(None, None, "tensor"),
        P(None, "tensor"),
        P("tensor", None),
        P(None, "tensor"),
        P(None, "tensor"),
        P("tensor", None),
        P(None, "tensor"),
        P("tensor", None),
    )
    return jax.shard_map(
        per_device, mesh=inner, in_specs=in_specs, out_specs=out_specs, check_vma=False
    )
```

```python
from functools import partial

import jax
import jax.numpy as jnp
from jax import lax
from jax.experimental import pallas as pl
from jax.experimental.pallas import tpu as pltpu
from jax.sharding import Mesh
from jax.sharding import PartitionSpec as P

HEAD = 64


EPSILON = 1e-05
NEGATIVE = -1e30
VMEM_BYTES = 56 * 1024 * 1024
SCALE = 0.02


def about(microseconds):
    return pl.CostEstimate(
        flops=int(microseconds * SCALE * 1.1e9), bytes_accessed=int(microseconds * SCALE * 3e6), transcendentals=0
    )


def contract_rows(left_side, right_side):
    return lax.dot_general(
        left_side, right_side, (((0,), (0,)), ((), ())), preferred_element_type=jnp.float32
    )


def times_transposed(left_side, right_side):
    return lax.dot_general(
        left_side, right_side, (((1,), (1,)), ((), ())), preferred_element_type=jnp.float32
    )


def phase(*arrays):
    return lax.optimization_barrier(arrays)


def axis_bits(name):
    return lax.axis_size(name).bit_length() - 1


def shift(array, steps):
    size = lax.axis_size("tensor")
    return lax.ppermute(array, "tensor", [(i, (i + steps) % size) for i in range(size)])


def flip(array, bit):
    pairs = [(i, i ^ (1 << bit)) for i in range(lax.axis_size("chip"))]
    return lax.ppermute(array, "chip", pairs)


def swap_core(array):
    return lax.ppermute(array, "core", [(0, 1), (1, 0)])


def in_order(mine, other, first, axis):
    return jnp.concatenate(
        [jnp.where(first, mine, other), jnp.where(first, other, mine)], axis
    )


def chip_orders():
    bits = axis_bits("chip")
    return [(0, 1), (1, 0)] if bits == 2 else [tuple(range(bits))]


def halves(array, axis):
    return jnp.split(array, len(chip_orders()), axis)


def chip_gather_start(array):
    bits = axis_bits("chip")
    return [
        part.reshape(part.shape[0], *(1,) * bits, *part.shape[1:]) for part in halves(array, 1)
    ]


def chip_gather_flips(parts, step):
    return [flip(part, order[step]) for part, order in zip(parts, chip_orders())]


def chip_gather_joins(parts, others, step):
    bits = axis_bits("chip")
    chip = lax.axis_index("chip")
    return [
        in_order(part, other, (chip >> order[step]) % 2 == 0, bits - order[step])
        for part, other, order in zip(parts, others, chip_orders())
    ]


def chip_gather_end(parts):
    whole = jnp.concatenate(parts, -2)
    return whole.reshape(whole.shape[0], -1, *whole.shape[-2:])


def pick(array, index, axis):
    return lax.dynamic_index_in_dim(array, index, axis, keepdims=False)


def chip_scatter_start(array):
    bits = axis_bits("chip")
    return [array.reshape(array.shape[0], *(2,) * bits, *array.shape[2:])] * len(chip_orders())


def chip_scatter_pick(part, number, order, step, other_side):
    side = (lax.axis_index("chip") >> order[step]) % 2
    left = sorted(set(order) - set(order[:step]), reverse=True)
    picked = pick(part, 1 - side if other_side else side, 1 + left.index(order[step]))
    return halves(picked, picked.ndim - 2)[number] if step == 0 else picked


def chip_scatter_flips(parts, step):
    return [
        flip(chip_scatter_pick(part, n, order, step, True), order[step])
        for n, (part, order) in enumerate(zip(parts, chip_orders()))
    ]


def chip_scatter_adds(parts, others, step):
    return [
        chip_scatter_pick(part, n, order, step, False) + other
        for n, (part, other, order) in enumerate(zip(parts, others, chip_orders()))
    ]


def gather(array, axes):
    return lax.all_gather(array, axes, axis=0, tiled=True)


def scatter_sum(array, axes):
    return lax.psum_scatter(array, axes, scatter_dimension=0, tiled=True)


def dot(left, right):
    return jnp.dot(left, right, preferred_element_type=jnp.float32)


def head_mask(width, head):
    lane = lax.broadcasted_iota(jnp.int32, (1, width), 1)
    return ((lane >= head * HEAD) & (lane < (head + 1) * HEAD)).astype(jnp.float32).astype(jnp.bfloat16)


def allowed_keys(low, high, key_first, shape):
    key = key_first + lax.broadcasted_iota(jnp.int32, shape, 0)
    return (key >= low) & (key <= high)


def attend_kernel(heads, key_size, first_ref, last_ref, low_ref, high_ref, q_ref, k_ref, v_ref, out_ref, log_ref, turned, acc):
    block = pl.program_id(1)
    rows, width = q_ref.shape
    key_blocks = k_ref.shape[0] // key_size

    @pl.when(block == 0)
    def _():
        for j in range(key_blocks):
            turned[j] = v_ref[j * key_size : (j + 1) * key_size, :].T

    q_rows = q_ref[...] * jnp.bfloat16(0.125)
    q_heads = [q_rows * head_mask(width, h) for h in range(heads)]
    low, high = low_ref[0], high_ref[0]
    acc[...] = jnp.zeros_like(acc)
    last = last_ref[block]

    def step(t, state):
        j = last - t
        key_first = pl.multiple_of(j * key_size, key_size)
        k_rows = k_ref[pl.ds(key_first, key_size), :]
        allowed = allowed_keys(low, high, key_first, (key_size, rows))
        fresh = []
        for h in range(heads):
            top, total = state[h]
            scores = jnp.where(allowed, times_transposed(k_rows, q_heads[h]), NEGATIVE)
            new_top = jnp.maximum(top, jnp.max(scores, axis=0, keepdims=True))
            probs = jnp.exp(scores - new_top)
            shrink = jnp.exp(top - new_top)
            part = slice(h * HEAD, (h + 1) * HEAD)
            acc[part, :] = acc[part, :] * shrink + dot(turned[j, part, :], probs.astype(jnp.bfloat16))
            fresh.append((new_top, total * shrink + jnp.sum(probs, axis=0, keepdims=True)))
        return tuple(fresh)

    begin = (jnp.full((1, rows), NEGATIVE, jnp.float32), jnp.zeros((1, rows), jnp.float32))
    state = lax.fori_loop(0, last - first_ref[block] + 1, step, (begin,) * heads)
    for h in range(heads):
        top, total = state[h]
        part = slice(h * HEAD, (h + 1) * HEAD)
        acc[part, :] = acc[part, :] / total
        log_ref[0, 0, h : h + 1, :] = top + jnp.log(total)
    out_ref[...] = acc[...].T.astype(jnp.bfloat16)


def attend_back_kernel(heads, query_size, key_size, first_ref, last_ref, low_ref, high_ref, q_ref, k_ref, v_ref, out_ref, grad_ref, log_ref, dq_ref, dk_ref, dv_ref, q_heads, grad_heads, turned, delta, dq_acc, dk_acc, dv_acc):
    block = pl.program_id(1)
    width = q_ref.shape[1]
    query_blocks = q_ref.shape[0] // query_size

    @pl.when(block == 0)
    def _():
        for i in range(query_blocks):
            rows = slice(i * query_size, (i + 1) * query_size)
            product = grad_ref[rows, :].astype(jnp.float32) * out_ref[rows, :].astype(jnp.float32)
            product = product.T
            for h in range(heads):
                mask = head_mask(width, h)
                q_heads[i, h] = q_ref[rows, :] * (mask * jnp.bfloat16(0.125))
                grad_heads[i, h] = grad_ref[rows, :] * mask
                delta[i, h : h + 1, :] = jnp.sum(
                    product[h * HEAD : (h + 1) * HEAD, :], axis=0, keepdims=True
                )
        dq_acc[...] = jnp.zeros_like(dq_acc)

    key_first = pl.multiple_of(block * key_size, key_size)
    k_rows = k_ref[pl.ds(key_first, key_size), :]
    v_rows = v_ref[pl.ds(key_first, key_size), :]
    turned[...] = k_rows.T
    dk_acc[...] = jnp.zeros_like(dk_acc)
    dv_acc[...] = jnp.zeros_like(dv_acc)

    def step(i, carry):
        allowed = allowed_keys(low_ref[i], high_ref[i], key_first, (key_size, query_size))
        for h in range(heads):
            q_rows = q_heads[i, h]
            grad_rows = grad_heads[i, h]
            scores = times_transposed(k_rows, q_rows)
            probs = jnp.where(allowed, jnp.exp(scores - log_ref[0, i, h : h + 1, :]), 0.0)
            prob_grad = times_transposed(v_rows, grad_rows)
            score_grad = (probs * (prob_grad - delta[i, h : h + 1, :])).astype(jnp.bfloat16)
            dv_acc[...] += dot(probs.astype(jnp.bfloat16), grad_rows)
            dk_acc[...] += dot(score_grad, q_rows)
            part = slice(h * HEAD, (h + 1) * HEAD)
            dq_acc[i, part, :] += dot(turned[part, :], score_grad)
        return carry

    lax.fori_loop(first_ref[block], last_ref[block] + 1, step, 0)
    dk_ref[pl.ds(key_first, key_size), :] = dk_acc[...].astype(jnp.bfloat16)
    dv_ref[pl.ds(key_first, key_size), :] = dv_acc[...].astype(jnp.bfloat16)

    @pl.when(block == pl.num_programs(1) - 1)
    def _():
        for i in range(query_blocks):
            dq_ref[i * query_size : (i + 1) * query_size, :] = (
                (dq_acc[i] * 0.125).T.astype(jnp.bfloat16)
            )


def packed_back_kernel(heads, query_size, key_size, groups, *refs):
    first_ref, last_ref, group_ref, low_ref, high_ref, qkv_ref, out_ref = refs[:7]
    parts = refs[7 : 7 + groups]
    log_ref, dqkv_ref = refs[7 + groups : 9 + groups]
    grad_ref = refs[-1]
    width = out_ref.shape[1]
    size = parts[0].shape[0]

    @pl.when(pl.program_id(1) == 0)
    def _():
        for k in range(groups):
            owner = lax.rem(group_ref[0] + k, groups)
            grad_ref[pl.ds(pl.multiple_of(owner * size, size), size), :] = parts[k][...]

    views = [[r.at[:, c * width : (c + 1) * width] for c in range(3)] for r in (qkv_ref, dqkv_ref)]
    attend_back_kernel(
        heads,
        query_size,
        key_size,
        first_ref,
        last_ref,
        low_ref,
        high_ref,
        *views[0],
        out_ref,
        grad_ref,
        log_ref,
        *views[1],
        *refs[9 + groups : -1],
    )


def ffn_kernel(tile, carried, *refs):
    n_own_ref, n_far_ref, g_own_ref, g_far_ref = refs[:4]
    step = pl.program_id(0)
    if carried:
        weights_ref, out_in_ref, back_in_ref = refs[4:7]
    else:
        weights_ref = refs[-1]
        for i, source in enumerate(refs[4:6]):

            @pl.when(step == i)
            def _(source=source):
                weights_ref[:, 0] = source[...]

    results = refs[7:12] if carried else refs[6:9]
    z_rows, du_rows, out_acc, back_acc, n_ref, n_turned, g_ref, g_turned = (
        refs[12:20] if carried else refs[9:17]
    )
    grads_ref = results[0]
    rows, width = n_ref.shape
    chips, piece = weights_ref.shape[0], weights_ref.shape[3]
    units = chips * piece
    share = width // chips
    w_in = weights_ref[:, 0, 0].reshape(units, width)
    w_out = weights_ref[:, 0, 1].reshape(units, width)

    @pl.when(step == 0)
    def _():
        half = rows // 2
        for joined, turned, parts in (
            (n_ref, n_turned, (n_own_ref, n_far_ref)),
            (g_ref, g_turned, (g_own_ref, g_far_ref)),
        ):
            for i, source in enumerate(parts):
                joined[i * half : (i + 1) * half, :] = source[...]
                turned[:, i * half : (i + 1) * half] = source[...].T
        if carried:
            out_acc[...] = out_in_ref[...]
            back_acc[...] = back_in_ref[...]
        else:
            out_acc[...] = jnp.zeros_like(out_acc)
            back_acc[...] = jnp.zeros_like(back_acc)

    def row_tile(i, carry):
        part = pl.ds(pl.multiple_of(i * tile, tile), tile)
        pre = times_transposed(n_ref[part, :], w_in)
        scaled = lax.erf(pre * 0.7071067811865476)
        density = jnp.exp(pre * pre * -0.5) * 0.3989422804014327
        below = 0.5 + 0.5 * scaled
        hidden = (pre * below).astype(jnp.bfloat16)
        z_rows[part, :] = hidden
        out_acc[part, :] += dot(hidden, w_out)
        hidden_grad = times_transposed(g_ref[part, :], w_out)
        pre_grad = (hidden_grad * (below + pre * density)).astype(jnp.bfloat16)
        du_rows[part, :] = pre_grad
        back_acc[part, :] += dot(pre_grad, w_in)
        return carry

    lax.fori_loop(0, rows // tile, row_tile, 0)
    for c in range(chips):
        part = slice(c * share, (c + 1) * share)
        grads_ref[c, 0, :, :units] = dot(n_turned[part, :], du_rows[...]).astype(jnp.bfloat16)
        grads_ref[c, 0, :, units:] = dot(g_turned[part, :], z_rows[...]).astype(jnp.bfloat16)

    @pl.when(step == pl.num_programs(0) - 1)
    def _():
        own = rows // 2
        if carried:
            out_ref, out_far_ref, back_ref, back_far_ref = results[1:]
            out_ref[...] = out_acc[:own, :]
            out_far_ref[...] = out_acc[own:, :].astype(jnp.bfloat16)
            back_ref[...] = back_acc[:own, :]
            back_far_ref[...] = back_acc[own:, :].astype(jnp.bfloat16)
        else:
            results[1][...] = out_acc[...]
            results[2][...] = back_acc[...]


def ffn_call(n_own, n_far, g_own, g_far, weights, sums):
    rows, width = 2 * n_own.shape[0], n_own.shape[1]
    groups = len(weights) if not sums else weights[0].shape[1]
    chips, piece = weights[0].shape[0], weights[0].shape[-2]
    units = chips * piece
    whole = lambda shape: pl.BlockSpec(shape, lambda t: (0,) * len(shape))
    own = (rows // 2, width)
    grads = (chips, 1, width // chips, 2 * units)
    block = (chips, 1, 2, piece, width)
    f32, bf16 = jnp.float32, jnp.bfloat16
    scratch = [
        pltpu.VMEM((rows, units), bf16),
        pltpu.VMEM((rows, units), bf16),
        pltpu.VMEM((rows, width), f32),
        pltpu.VMEM((rows, width), f32),
        pltpu.VMEM((rows, width), bf16),
        pltpu.VMEM((width, rows), bf16),
        pltpu.VMEM((rows, width), bf16),
        pltpu.VMEM((width, rows), bf16),
    ]
    if sums:
        results = [(own, f32), (own, bf16), (own, f32), (own, bf16)]
        weight_specs = [pl.BlockSpec(block, lambda t: (0, t, 0, 0, 0))]
    else:
        results = [((rows, width), f32)] * 2
        weight_specs = [whole(one.shape) for one in weights]
        scratch.append(pltpu.VMEM(block, bf16))
    return pl.pallas_call(
        partial(ffn_kernel, min(256, rows), bool(sums)),
        grid=(groups,),
        in_specs=[whole(own)] * 4 + weight_specs + [whole((rows, width))] * len(sums),
        out_specs=[pl.BlockSpec(grads, lambda t: (0, t, 0, 0))]
        + [whole(shape) for shape, _ in results],
        out_shape=[jax.ShapeDtypeStruct((chips, groups, *grads[2:]), bf16)]
        + [jax.ShapeDtypeStruct(*one) for one in results],
        scratch_shapes=scratch,
        compiler_params=pltpu.CompilerParams(vmem_limit_bytes=VMEM_BYTES),
        cost_estimate=about(23),
    )(n_own, n_far, g_own, g_far, *weights, *sums)


def ffn_pack_kernel(core_ref, in_ref, out_ref, packed_ref):
    chips, _, piece, _ = packed_ref.shape
    half = chips * piece
    first = pl.multiple_of(core_ref[0] * half, half)
    turned = in_ref[:, pl.ds(first, half)].T
    for c in range(chips):
        packed_ref[c, 0] = turned[c * piece : (c + 1) * piece, :]
        packed_ref[c, 1] = out_ref[pl.ds(first + c * piece, piece), :]


def ffn_pack_call(core, ffn_in, ffn_out, chips):
    units, width = ffn_out.shape
    return pl.pallas_call(
        ffn_pack_kernel,
        in_specs=[pl.BlockSpec(memory_space=pltpu.SMEM)] + [local_spec()] * 2,
        out_specs=local_spec(),
        out_shape=jax.ShapeDtypeStruct((chips, 2, units // 2 // chips, width), jnp.bfloat16),
        compiler_params=pltpu.CompilerParams(vmem_limit_bytes=VMEM_BYTES),
        cost_estimate=about(5),
    )(core, ffn_in, ffn_out)


def unit_norm(values):
    center = values - jnp.mean(values, axis=1, keepdims=True)
    inverse = lax.rsqrt(jnp.mean(center * center, axis=1, keepdims=True) + EPSILON)
    return center * inverse, inverse


def unit_back(gradient, values, gain):
    unit, inverse = unit_norm(values)
    scaled = gradient * gain
    inner = (
        scaled
        - jnp.mean(scaled, axis=1, keepdims=True)
        - unit * jnp.mean(scaled * unit, axis=1, keepdims=True)
    )
    return (
        inner * inverse,
        jnp.sum(gradient * unit, axis=0, keepdims=True),
        jnp.sum(gradient, axis=0, keepdims=True),
    )


def first_kernel(
    heads, frames_ref, gain_ref, bias_ref, weight_ref, normed_ref, packed_ref, ordered_ref
):
    @pl.when(pl.program_id(0) == 0)
    def _():
        columns = [
            weight_ref[:, (3 * h + c) * HEAD : (3 * h + c + 1) * HEAD]
            for c in range(3)
            for h in range(heads)
        ]
        ordered_ref[...] = jnp.concatenate(columns, 1)

    unit, _ = unit_norm(frames_ref[...].astype(jnp.float32))
    normed = (unit * gain_ref[0:1, :] + bias_ref[0:1, :]).astype(jnp.bfloat16)
    normed_ref[...] = normed
    packed_ref[...] = dot(normed, ordered_ref[...]).astype(jnp.bfloat16)


def first_call(heads, frames, gain, bias, weight, tile):
    rows, width = frames.shape
    columns = weight.shape[1]
    moving = lambda size: pl.BlockSpec((tile, size), lambda i: (i, 0))
    fixed = lambda shape: pl.BlockSpec(shape, lambda i: (0, 0))
    return pl.pallas_call(
        partial(first_kernel, heads),
        grid=(rows // tile,),
        in_specs=[moving(width), fixed(gain.shape), fixed(bias.shape), fixed(weight.shape)],
        out_specs=[moving(width), moving(columns), fixed(weight.shape)],
        out_shape=[
            jax.ShapeDtypeStruct((rows, width), jnp.bfloat16),
            jax.ShapeDtypeStruct((rows, columns), jnp.bfloat16),
            jax.ShapeDtypeStruct(weight.shape, jnp.bfloat16),
        ],
        compiler_params=pltpu.CompilerParams(vmem_limit_bytes=VMEM_BYTES),
        cost_estimate=about(9),
    )(frames, gain, bias, weight)


def pack_kernel(heads, self_ref, query_ref, cross_ref, pair_ref, out_ref):
    width = heads * HEAD
    text_width = pair_ref.shape[0]
    out_ref[0:width, :] = self_ref[...]
    out_ref[width : 2 * width, :] = query_ref[...].T
    out_ref[2 * width : 3 * width, :] = cross_ref[...]
    turned = pair_ref[...].T
    for h in range(heads):
        for c in range(2):
            rows = slice((3 + c) * width + h * HEAD, (3 + c) * width + (h + 1) * HEAD)
            out_ref[rows, :text_width] = turned[(2 * h + c) * HEAD : (2 * h + c + 1) * HEAD, :]
    out_ref[3 * width :, text_width:] = jnp.zeros(
        (2 * width, out_ref.shape[1] - text_width), jnp.bfloat16
    )


def pack_call(heads, self_out, cross_query, cross_out, cross_kv):
    return pl.pallas_call(
        partial(pack_kernel, heads),
        in_specs=[local_spec()] * 4,
        out_specs=local_spec(),
        out_shape=jax.ShapeDtypeStruct((5 * heads * HEAD, self_out.shape[1]), jnp.bfloat16),
        compiler_params=pltpu.CompilerParams(vmem_limit_bytes=VMEM_BYTES),
        cost_estimate=about(3),
    )(self_out, cross_query, cross_out, cross_kv)


def weight_copies(core_ref, local_ref, mine_ref, far_ref, weights, sems):
    half = mine_ref.shape[1]
    core = core_ref[0]
    copies = [pltpu.make_async_copy(local_ref, weights.at[0], sems.at[0])]
    for k in range(1, weights.shape[0]):
        for n, (source, side) in enumerate(((mine_ref, core), (far_ref, 1 - core))):
            rows = pl.ds(pl.multiple_of(side * half, half), half)
            copies.append(
                pltpu.make_async_copy(
                    source.at[k - 1], weights.at[k, rows], sems.at[2 * k - 1 + n]
                )
            )
    return copies


def middle_kernel(
    heads,
    tile,
    core_ref,
    low_ref,
    high_ref,
    inputs_ref,
    text_ref,
    gain_ref,
    bias_ref,
    local_ref,
    mine_ref,
    far_ref,
    *rest,
):
    groups = len(rest) - 9 - 4
    mixes = rest[:groups]
    h1_ref, h2_ref, n2_ref, n3_ref, cq_ref, mix_ref, ck_ref, cv_ref, log_ref = rest[
        groups : groups + 9
    ]
    weights, turned, mix_turned, sems = rest[groups + 9 :]
    width = heads * HEAD
    text_width = text_ref.shape[1]
    keys = text_ref.shape[0]
    copies = weight_copies(core_ref, local_ref, mine_ref, far_ref, weights, sems)
    for copy in copies:
        copy.start()
    for copy in copies:
        copy.wait()
    text = text_ref[...]
    for k in range(groups):
        part = slice(k * width, (k + 1) * width)
        key_weight = weights[k, 3 * width : 4 * width, :text_width]
        value_weight = weights[k, 4 * width : 5 * width, :text_width]
        ck_ref[:, part] = times_transposed(text, key_weight).astype(jnp.bfloat16)
        cv_ref[:, part] = times_transposed(text, value_weight).astype(jnp.bfloat16)
        turned[k] = times_transposed(value_weight, text).astype(jnp.bfloat16)

    def row_tile(i, carry):
        rows = pl.ds(pl.multiple_of(i * tile, tile), tile)
        total = inputs_ref[rows, :].astype(jnp.float32)
        for k in range(groups):
            total += dot(mixes[k][rows, :], weights[k, 0:width, :])
        h1_ref[rows, :] = total
        unit, _ = unit_norm(total)
        normed = (unit * gain_ref[1:2, :] + bias_ref[1:2, :]).astype(jnp.bfloat16)
        n2_ref[rows, :] = normed
        allowed = allowed_keys(low_ref[i], high_ref[i], 0, (keys, tile))
        for k in range(groups):
            part = slice(k * width, (k + 1) * width)
            queries = times_transposed(normed, weights[k, width : 2 * width, :])
            queries = queries.astype(jnp.bfloat16)
            cq_ref[rows, part] = queries
            queries = queries * jnp.bfloat16(0.125)
            for h in range(heads):
                scores = times_transposed(ck_ref[:, part], queries * head_mask(width, h))
                scores = jnp.where(allowed, scores, NEGATIVE)
                top = jnp.max(scores, axis=0, keepdims=True)
                probs = jnp.exp(scores - top)
                sums = jnp.sum(probs, axis=0, keepdims=True)
                lane = slice(h * HEAD, (h + 1) * HEAD)
                mix_turned[lane, :] = dot(turned[k, lane, :], probs.astype(jnp.bfloat16)) / sums
                log_ref[i, k * heads + h : k * heads + h + 1, :] = top + jnp.log(sums)
            mix_ref[rows, part] = mix_turned[...].T.astype(jnp.bfloat16)
        total = h1_ref[rows, :]
        for k in range(groups):
            part = slice(k * width, (k + 1) * width)
            total += dot(mix_ref[rows, part], weights[k, 2 * width : 3 * width, :])
        h2_ref[rows, :] = total
        unit, _ = unit_norm(total)
        n3_ref[rows, :] = (unit * gain_ref[2:3, :] + bias_ref[2:3, :]).astype(jnp.bfloat16)
        return carry

    lax.fori_loop(0, inputs_ref.shape[0] // tile, row_tile, 0)


def middle_back_kernel(
    heads,
    tile,
    core_ref,
    low_ref,
    high_ref,
    text_ref,
    gain_ref,
    third_ref,
    third_far_ref,
    grad_ref,
    h1_ref,
    h2_ref,
    cq_ref,
    mix_ref,
    ck_ref,
    cv_ref,
    log_ref,
    local_ref,
    mine_ref,
    far_ref,
    cross_side_ref,
    dcq_ref,
    dck_ref,
    dcv_ref,
    self_exact_ref,
    self_side_ref,
    norm_ref,
    text_part_ref,
    *rest,
):
    mix_grads = rest[:-6]
    weights, turned, query_turned, dk_acc, dv_acc, sems = rest[-6:]
    groups = weights.shape[0]
    width = heads * HEAD
    text_width = text_ref.shape[1]
    keys = text_ref.shape[0]
    copies = weight_copies(core_ref, local_ref, mine_ref, far_ref, weights, sems)
    for copy in copies:
        copy.start()
    for copy in copies:
        copy.wait()
    text = text_ref[...]
    for k in range(groups):
        key_weight = weights[k, 3 * width : 4 * width, :text_width]
        turned[k] = times_transposed(key_weight, text).astype(jnp.bfloat16)
    dk_acc[...] = jnp.zeros_like(dk_acc)
    dv_acc[...] = jnp.zeros_like(dv_acc)
    norm_ref[...] = jnp.zeros_like(norm_ref)

    def row_tile(i, carry):
        rows = pl.ds(pl.multiple_of(i * tile, tile), tile)
        third = third_ref[rows, :] + third_far_ref[rows, :].astype(jnp.float32)
        back, gain_sum, bias_sum = unit_back(third, h2_ref[rows, :], gain_ref[2:3, :])
        norm_ref[2:3, :] += gain_sum
        norm_ref[5:6, :] += bias_sum
        cross_exact = grad_ref[rows, :].astype(jnp.float32) + back
        cross_side = cross_exact.astype(jnp.bfloat16)
        self_exact_ref[rows, :] = cross_exact
        cross_side_ref[rows, :] = cross_side
        allowed = allowed_keys(low_ref[i], high_ref[i], 0, (keys, tile))
        for k in range(groups):
            part = slice(k * width, (k + 1) * width)
            mix_grad = times_transposed(cross_side, weights[k, 2 * width : 3 * width, :])
            mix_grad = mix_grad.astype(jnp.bfloat16)
            product = mix_grad.astype(jnp.float32) * mix_ref[rows, part].astype(jnp.float32)
            product = product.T
            queries = cq_ref[rows, part] * jnp.bfloat16(0.125)
            for h in range(heads):
                mask = head_mask(width, h)
                lane = slice(h * HEAD, (h + 1) * HEAD)
                one = k * heads + h
                q_rows = queries * mask
                grad_rows = mix_grad * mask
                scores = times_transposed(ck_ref[:, part], q_rows)
                probs = jnp.exp(scores - log_ref[i, one : one + 1, :])
                probs = jnp.where(allowed, probs, 0.0)
                prob_grad = times_transposed(cv_ref[:, part], grad_rows)
                delta = jnp.sum(product[lane, :], axis=0, keepdims=True)
                score_grad = (probs * (prob_grad - delta)).astype(jnp.bfloat16)
                dv_acc[:, part] += dot(probs.astype(jnp.bfloat16), grad_rows)
                dk_acc[:, part] += dot(score_grad, q_rows)
                query_turned[lane, :] = dot(turned[k, lane, :], score_grad)
            dcq_ref[rows, part] = (query_turned[...] * 0.125).T.astype(jnp.bfloat16)
        second = jnp.zeros(cross_exact.shape, jnp.float32)
        for k in range(groups):
            part = slice(k * width, (k + 1) * width)
            second += dot(dcq_ref[rows, part], weights[k, width : 2 * width, :])
        back, gain_sum, bias_sum = unit_back(second, h1_ref[rows, :], gain_ref[1:2, :])
        norm_ref[1:2, :] += gain_sum
        norm_ref[4:5, :] += bias_sum
        self_exact = self_exact_ref[rows, :] + back
        self_exact_ref[rows, :] = self_exact
        self_side = self_exact.astype(jnp.bfloat16)
        self_side_ref[rows, :] = self_side
        for k in range(groups):
            mix_grads[k][rows, :] = times_transposed(self_side, weights[k, 0:width, :]).astype(
                jnp.bfloat16
            )
        return carry

    lax.fori_loop(0, third_ref.shape[0] // tile, row_tile, 0)
    dck_ref[...] = dk_acc[...].astype(jnp.bfloat16)
    dcv_ref[...] = dv_acc[...].astype(jnp.bfloat16)
    text_part = jnp.zeros(text_ref.shape, jnp.float32)
    for k in range(groups):
        part = slice(k * width, (k + 1) * width)
        text_part += dot(dck_ref[:, part], weights[k, 3 * width : 4 * width, :text_width])
        text_part += dot(dcv_ref[:, part], weights[k, 4 * width : 5 * width, :text_width])
    size = text_width // groups
    for k in range(groups):
        text_part_ref[k] = text_part[:, k * size : (k + 1) * size].astype(jnp.bfloat16)


def weight_grads_kernel(heads, added, side_ref, *refs):
    target = refs[-1]
    if added:
        far_ref, refs = refs[0], refs[1:]
    self_ref, n2_ref, cq_ref, mix_ref, cross_ref, dck_ref, dcv_ref, text_ref = refs[:8]
    mixes = refs[8:-1]
    width = heads * HEAD
    half = target.shape[1]
    text_width = text_ref.shape[1]
    for side in range(2):

        @pl.when(side_ref[0] == side)
        def _(side=side):
            for k in range(target.shape[0]):
                first = k * width
                pairs = [
                    (mixes[k], 0, self_ref),
                    (cq_ref, first, n2_ref),
                    (mix_ref, first, cross_ref),
                    (dck_ref, first, text_ref),
                    (dcv_ref, first, text_ref),
                ]
                for n, (left, lane, right) in enumerate(pairs):
                    low = max(n * width, side * half)
                    high = min((n + 1) * width, (side + 1) * half)
                    if low >= high:
                        continue
                    columns = left[:, lane + low - n * width : lane + high - n * width]
                    product = contract_rows(columns, right[...])
                    rows = slice(low - side * half, high - side * half)
                    if added:
                        product += far_ref[k, rows, : product.shape[1]].astype(jnp.float32)
                    product = product.astype(jnp.bfloat16)
                    target[k, rows, : product.shape[1]] = product
                    if product.shape[1] < target.shape[2]:
                        target[k, rows, text_width:] = jnp.zeros(
                            (high - low, target.shape[2] - text_width), jnp.bfloat16
                        )


def weight_grads_call(heads, side, arrays, mixes, far=()):
    groups, width = len(mixes), arrays[0].shape[1]
    half = 5 * heads * HEAD // 2
    return pl.pallas_call(
        partial(weight_grads_kernel, heads, bool(far)),
        in_specs=[pl.BlockSpec(memory_space=pltpu.SMEM)]
        + [local_spec()] * (len(far) + len(arrays) + groups),
        out_specs=local_spec(),
        out_shape=jax.ShapeDtypeStruct((groups, half, width), jnp.bfloat16),
        compiler_params=pltpu.CompilerParams(vmem_limit_bytes=VMEM_BYTES),
        cost_estimate=about(10),
    )(side, *far, *arrays, *mixes)


def last_kernel(frames_ref, gain_ref, exact_ref, sum_ref, term_ref, out_ref, norm_ref):
    gradient = sum_ref[...].astype(jnp.float32) + term_ref[...]
    back, gain_sum, bias_sum = unit_back(
        gradient, frames_ref[...].astype(jnp.float32), gain_ref[0:1, :]
    )
    out_ref[...] = (exact_ref[...] + back).astype(jnp.bfloat16)
    norm_ref[0:1, :] = gain_sum
    norm_ref[1:2, :] = bias_sum


def last_call(frames, gains, exact, sums, term):
    rows, width = frames.shape
    return pl.pallas_call(
        last_kernel,
        in_specs=[local_spec()] * 5,
        out_specs=[local_spec()] * 2,
        out_shape=[
            jax.ShapeDtypeStruct((rows, width), jnp.bfloat16),
            jax.ShapeDtypeStruct((2, width), jnp.float32),
        ],
        compiler_params=pltpu.CompilerParams(vmem_limit_bytes=VMEM_BYTES),
        cost_estimate=about(4),
    )(frames, gains, exact, sums, term)


def ffn_end_kernel(core_ref, mine_ref, far_ref, in_ref, out_ref):
    units = in_ref.shape[1] // 2
    for source, side in ((mine_ref, core_ref[0]), (far_ref, 1 - core_ref[0])):
        part = pl.ds(pl.multiple_of(side * units, units), units)
        in_ref[:, part] = source[0, :, :units].astype(jnp.float32)
        out_ref[part, :] = source[0, :, units:].astype(jnp.float32).T


def ffn_end_call(core, mine, far):
    chips, features, columns = mine.shape
    source = pl.BlockSpec((1, features, columns), lambda c: (c, 0, 0))
    return pl.pallas_call(
        ffn_end_kernel,
        grid=(chips,),
        in_specs=[pl.BlockSpec(memory_space=pltpu.SMEM), source, source],
        out_specs=[
            pl.BlockSpec((features, columns), lambda c: (c, 0)),
            pl.BlockSpec((columns, features), lambda c: (0, c)),
        ],
        out_shape=[
            jax.ShapeDtypeStruct((chips * features, columns), jnp.float32),
            jax.ShapeDtypeStruct((columns, chips * features), jnp.float32),
        ],
        compiler_params=pltpu.CompilerParams(vmem_limit_bytes=VMEM_BYTES),
        cost_estimate=about(5),
    )(core, mine, far)


def qkv_grad_kernel(left_ref, right_ref, out_ref):
    out_ref[...] = contract_rows(left_ref[...], right_ref[...]).astype(jnp.bfloat16)


def qkv_grad_call(normed, packed_grad):
    rows, width = normed.shape
    columns = packed_grad.shape[1]
    tile = min(256, width)
    return pl.pallas_call(
        qkv_grad_kernel,
        grid=(width // tile,),
        in_specs=[
            pl.BlockSpec((rows, tile), lambda i: (0, i)),
            pl.BlockSpec((rows, columns), lambda i: (0, 0)),
        ],
        out_specs=pl.BlockSpec((tile, columns), lambda i: (i, 0)),
        out_shape=jax.ShapeDtypeStruct((width, columns), jnp.bfloat16),
        compiler_params=pltpu.CompilerParams(vmem_limit_bytes=VMEM_BYTES),
        cost_estimate=about(5),
    )(normed, packed_grad)


def qkv_end_kernel(heads, core_ref, mine_ref, far_ref, out_ref):
    width = heads * HEAD
    size = mine_ref.shape[0]
    for source, side in ((mine_ref, core_ref[0]), (far_ref, 1 - core_ref[0])):
        columns = [
            source[:, c * width + h * HEAD : c * width + (h + 1) * HEAD]
            for h in range(heads)
            for c in range(3)
        ]
        rows = pl.ds(pl.multiple_of(side * size, size), size)
        out_ref[rows, :] = jnp.concatenate(columns, 1).astype(jnp.float32)


def qkv_end_call(heads, core, mine, far):
    rows, columns = mine.shape
    return pl.pallas_call(
        partial(qkv_end_kernel, heads),
        in_specs=[pl.BlockSpec(memory_space=pltpu.SMEM)] + [local_spec()] * 2,
        out_specs=local_spec(),
        out_shape=jax.ShapeDtypeStruct((2 * rows, columns), jnp.float32),
        compiler_params=pltpu.CompilerParams(vmem_limit_bytes=VMEM_BYTES),
        cost_estimate=about(3),
    )(core, mine, far)


def small_end_kernel(heads, core_ref, mine_ref, far_ref, *refs):
    self_ref, query_ref, cross_ref, pair_ref, joined = refs
    width = heads * HEAD
    text_width = pair_ref.shape[0]
    half = joined.shape[0] // 2
    for source, side in ((mine_ref, core_ref[0]), (far_ref, 1 - core_ref[0])):
        joined[pl.ds(pl.multiple_of(side * half, half), half), :] = source[...]
    self_ref[...] = joined[0:width, :].astype(jnp.float32)
    query_ref[...] = joined[width : 2 * width, :].astype(jnp.float32).T
    cross_ref[...] = joined[2 * width : 3 * width, :].astype(jnp.float32)
    for h in range(heads):
        rows = [slice((3 + c) * width + h * HEAD, (3 + c) * width + (h + 1) * HEAD) for c in (0, 1)]
        both = jnp.concatenate([joined[part, :text_width] for part in rows], 0)
        pair_ref[:, 2 * h * HEAD : 2 * (h + 1) * HEAD] = both.astype(jnp.float32).T


def small_end_call(heads, text_width, core, mine, far):
    width = mine.shape[1]
    head_width = heads * HEAD
    shapes = [
        (head_width, width),
        (width, head_width),
        (head_width, width),
        (text_width, 2 * head_width),
    ]
    return pl.pallas_call(
        partial(small_end_kernel, heads),
        in_specs=[pl.BlockSpec(memory_space=pltpu.SMEM)] + [local_spec()] * 2,
        out_specs=[local_spec()] * 4,
        out_shape=[jax.ShapeDtypeStruct(shape, jnp.float32) for shape in shapes],
        scratch_shapes=[pltpu.VMEM((5 * head_width, width), jnp.bfloat16)],
        compiler_params=pltpu.CompilerParams(vmem_limit_bytes=VMEM_BYTES),
        cost_estimate=about(4),
    )(core, mine, far)


def local_spec():
    return pl.BlockSpec(memory_space=pltpu.VMEM)


def middle_specs(plain):
    return (
        [pl.BlockSpec(memory_space=pltpu.SMEM)]
        + [local_spec()] * plain
        + [pl.BlockSpec(memory_space=pl.ANY)] * 3
    )


def middle_call(heads, tile, core, low, high, inputs, text, gains, biases, split_weights, mixes):
    rows, width = inputs.shape
    keys = text.shape[0]
    groups = len(mixes)
    f32, bf16 = jnp.float32, jnp.bfloat16
    shapes = [
        ((rows, width), f32),
        ((rows, width), f32),
        ((rows, width), bf16),
        ((rows, width), bf16),
        ((rows, width), bf16),
        ((rows, width), bf16),
        ((keys, width), bf16),
        ((keys, width), bf16),
        ((rows // tile, groups * heads, tile), f32),
    ]
    return pl.pallas_call(
        partial(middle_kernel, heads, tile),
        in_specs=middle_specs(6) + [local_spec()] * groups,
        out_specs=[local_spec()] * len(shapes),
        out_shape=[jax.ShapeDtypeStruct(*one) for one in shapes],
        scratch_shapes=[
            pltpu.VMEM((groups, *split_weights[0].shape), bf16),
            pltpu.VMEM((groups, heads * HEAD, keys), bf16),
            pltpu.VMEM((heads * HEAD, tile), f32),
            pltpu.SemaphoreType.DMA((2 * groups - 1,)),
        ],
        compiler_params=pltpu.CompilerParams(vmem_limit_bytes=VMEM_BYTES),
        cost_estimate=about(30),
    )(core, lanes(low, tile), lanes(high, tile), inputs, text, gains, biases, *split_weights, *mixes)


def middle_back_call(heads, tile, core, low, high, text, gains, saved, split_weights):
    rows, width = saved[0].shape
    keys = text.shape[0]
    groups = width // (heads * HEAD)
    f32, bf16 = jnp.float32, jnp.bfloat16
    shapes = [
        ((rows, width), bf16),
        ((rows, width), bf16),
        ((keys, width), bf16),
        ((keys, width), bf16),
        ((rows, width), f32),
        ((rows, width), bf16),
        ((6, width), f32),
        ((groups, keys, text.shape[1] // groups), bf16),
    ] + [((rows, heads * HEAD), bf16)] * groups
    return pl.pallas_call(
        partial(middle_back_kernel, heads, tile),
        in_specs=middle_specs(4 + len(saved)),
        out_specs=[local_spec()] * len(shapes),
        out_shape=[jax.ShapeDtypeStruct(*one) for one in shapes],
        scratch_shapes=[
            pltpu.VMEM((groups, *split_weights[0].shape), bf16),
            pltpu.VMEM((groups, heads * HEAD, keys), bf16),
            pltpu.VMEM((heads * HEAD, tile), f32),
            pltpu.VMEM((keys, width), f32),
            pltpu.VMEM((keys, width), f32),
            pltpu.SemaphoreType.DMA((2 * groups - 1,)),
        ],
        compiler_params=pltpu.CompilerParams(vmem_limit_bytes=VMEM_BYTES),
        cost_estimate=about(40),
    )(core, lanes(low, tile), lanes(high, tile), text, gains, *saved, *split_weights)


def lanes(values, size):
    return values.astype(jnp.int32).reshape(-1, 1, size)


def attend_call(q, k, v, columns, groups, heads, low, high, first, last, query_size, key_size):
    width = heads * HEAD
    rows, keys = q.shape[0], k.shape[0]
    blocks = rows // query_size
    spec = lambda size, column: pl.BlockSpec((size, width), lambda g, i, *_: (0, column + g))
    vector = pl.BlockSpec((1, 1, query_size), lambda g, i, *_: (i, 0, 0))
    q_column = columns[0]
    return pl.pallas_call(
        partial(attend_kernel, heads, key_size),
        grid_spec=pltpu.PrefetchScalarGridSpec(
            num_scalar_prefetch=2,
            grid=(groups, blocks),
            in_specs=[
                vector,
                vector,
                pl.BlockSpec((query_size, width), lambda g, i, *_: (i, q_column + g)),
                spec(keys, columns[1]),
                spec(keys, columns[2]),
            ],
            out_specs=[
                pl.BlockSpec((query_size, width), lambda g, i, *_: (i, g)),
                pl.BlockSpec((1, 1, heads, query_size), lambda g, i, *_: (g, i, 0, 0)),
            ],
            scratch_shapes=[
                pltpu.VMEM((keys // key_size, width, key_size), jnp.bfloat16),
                pltpu.VMEM((width, query_size), jnp.float32),
            ],
        ),
        out_shape=[
            jax.ShapeDtypeStruct((rows, groups * width), jnp.bfloat16),
            jax.ShapeDtypeStruct((groups, blocks, heads, query_size), jnp.float32),
        ],
        compiler_params=pltpu.CompilerParams(vmem_limit_bytes=VMEM_BYTES),
        cost_estimate=about(30 if groups == 1 else 17),
    )(first, last, lanes(low, query_size), lanes(high, query_size), q, k, v)


def back_scratch(heads, blocks, query_size, key_size):
    width = heads * HEAD
    return [
        pltpu.VMEM((blocks, heads, query_size, width), jnp.bfloat16),
        pltpu.VMEM((blocks, heads, query_size, width), jnp.bfloat16),
        pltpu.VMEM((width, key_size), jnp.bfloat16),
        pltpu.VMEM((blocks, heads, query_size), jnp.float32),
        pltpu.VMEM((blocks, width, query_size), jnp.float32),
        pltpu.VMEM((key_size, width), jnp.float32),
        pltpu.VMEM((key_size, width), jnp.float32),
    ]


def packed_back_call(
    qkv, out, parts, logs, heads, group, low, high, first, last, query_size, key_size
):
    rows, width = out.shape
    blocks = rows // query_size
    whole = lambda shape: pl.BlockSpec(shape, lambda g, j, *_: (0,) * len(shape))
    vector = whole((blocks, 1, query_size))
    return pl.pallas_call(
        partial(packed_back_kernel, heads, query_size, key_size, len(parts)),
        grid_spec=pltpu.PrefetchScalarGridSpec(
            num_scalar_prefetch=3,
            grid=(1, rows // key_size),
            in_specs=[vector, vector, whole(qkv.shape), whole(out.shape)]
            + [whole(part.shape) for part in parts]
            + [whole(logs.shape)],
            out_specs=whole(qkv.shape),
            scratch_shapes=back_scratch(heads, blocks, query_size, key_size)
            + [pltpu.VMEM(out.shape, jnp.bfloat16)],
        ),
        out_shape=jax.ShapeDtypeStruct(qkv.shape, jnp.bfloat16),
        compiler_params=pltpu.CompilerParams(vmem_limit_bytes=VMEM_BYTES),
        cost_estimate=about(30),
    )(
        first,
        last,
        group,
        lanes(low, query_size),
        lanes(high, query_size),
        qkv,
        out,
        *parts,
        logs,
    )


def attend_back_call(q, k, v, out, grad, logs, groups, heads, low, high, first, last, query_size, key_size):
    width = heads * HEAD
    rows, keys = q.shape[0], k.shape[0]
    blocks = rows // query_size
    column = lambda size: pl.BlockSpec((size, width), lambda g, j, *_: (0, g))
    vector = pl.BlockSpec((blocks, 1, query_size), lambda g, j, *_: (0, 0, 0))
    return pl.pallas_call(
        partial(attend_back_kernel, heads, query_size, key_size),
        grid_spec=pltpu.PrefetchScalarGridSpec(
            num_scalar_prefetch=2,
            grid=(groups, keys // key_size),
            in_specs=[
                vector,
                vector,
                column(rows),
                column(keys),
                column(keys),
                column(rows),
                column(rows),
                pl.BlockSpec((1, blocks, heads, query_size), lambda g, j, *_: (g, 0, 0, 0)),
            ],
            out_specs=[column(rows), column(keys), column(keys)],
            scratch_shapes=back_scratch(heads, blocks, query_size, key_size),
        ),
        out_shape=[
            jax.ShapeDtypeStruct((rows, groups * width), jnp.bfloat16),
            jax.ShapeDtypeStruct((keys, groups * width), jnp.bfloat16),
            jax.ShapeDtypeStruct((keys, groups * width), jnp.bfloat16),
        ],
        compiler_params=pltpu.CompilerParams(vmem_limit_bytes=VMEM_BYTES),
        cost_estimate=about(6 * groups),
    )(first, last, lanes(low, query_size), lanes(high, query_size), q, k, v, out, grad, logs)


def per_device(
    frames,
    text_states,
    clip_lengths,
    text_lengths,
    norm_gains,
    norm_biases,
    self_qkv,
    self_out,
    cross_query,
    cross_kv,
    cross_out,
    ffn_in,
    ffn_out,
    out_grad,
):
    groups = lax.axis_size("tensor")
    chips = lax.axis_size("chip")
    group = lax.axis_index("tensor")
    chip = lax.axis_index("chip")
    core = lax.axis_index("core")
    bf16 = jnp.bfloat16
    frame_count, width = frames.shape
    own_rows = frame_count // groups
    offset = group * own_rows
    clip_count, text_slots, text_width = text_states.shape
    head_count = self_out.shape[0] // HEAD
    all_heads = head_count * groups
    ends = jnp.cumsum(clip_lengths[0])
    starts = ends - clip_lengths[0]
    positions = jnp.arange(frame_count, dtype=jnp.int32)[:, None]
    clip_first = jnp.max(jnp.where(positions >= starts, starts, 0), axis=1)
    clip_stop = jnp.min(jnp.where(positions < ends, ends, frame_count), axis=1)
    block = min(256, own_rows)
    blocks = jnp.arange(frame_count // block, dtype=jnp.int32)
    self_low, self_high = clip_first, positions[:, 0]
    wide = min(2 * block, frame_count)
    wides = jnp.arange(frame_count // wide, dtype=jnp.int32)
    self_keys = (clip_first[::wide] // block, (wides * wide + wide - 1) // block)
    self_queries = (blocks * block // wide, (clip_stop[block - 1 :: block] - 1) // wide)
    own_positions = offset + jnp.arange(own_rows, dtype=jnp.int32)[:, None]
    own_clip = jnp.sum((own_positions >= ends).astype(jnp.int32), axis=1)
    own_length = jnp.sum(
        jnp.where(own_clip[:, None] == jnp.arange(clip_count), text_lengths[0], 0), axis=1
    )
    cross_low = own_clip * text_slots
    cross_high = cross_low + own_length - 1
    cross_keys = (own_clip[::block], own_clip[block - 1 :: block])
    inside_first = jnp.clip(starts - offset, 0, own_rows)
    inside_stop = jnp.clip(ends - offset, 0, own_rows)
    cross_first = jnp.minimum(inside_first // block, own_rows // block - 1)
    cross_queries = (
        cross_first,
        jnp.where(inside_stop > inside_first, (inside_stop - 1) // block, cross_first - 1),
    )

    head_width = head_count * HEAD
    local = pack_call(head_count, self_out, cross_query, cross_out, cross_kv)
    pieces = local.reshape(2, chips, -1, width)
    half = ffn_out.shape[0] // 2
    piece = half // chips
    core_index = core.reshape(1).astype(jnp.int32)
    sent_piece = pick(pick(pieces, core, 0), chip, 0)
    sent_piece, frames, self_qkv, ffn_in, ffn_out, out_grad = phase(
        sent_piece, frames, self_qkv, ffn_in, ffn_out, out_grad
    )
    passed = [shift(sent_piece, k) for k in range(1, groups)]
    ffn_own = ffn_pack_call(core_index, ffn_in, ffn_out, chips)
    ffn_piece = pick(ffn_own, chip, 0).reshape(2 * piece, width)
    own_frames = lax.dynamic_slice_in_dim(frames, offset, own_rows, 0)
    grad_own_bf = lax.dynamic_slice_in_dim(out_grad, offset, own_rows, 0)
    rows_one, packed, w_qkv = first_call(
        head_count, frames, norm_gains, norm_biases, self_qkv, block
    )
    packed, ffn_piece, own_frames, grad_own_bf, *passed = phase(
        packed, ffn_piece, own_frames, grad_own_bf, *passed
    )
    if head_width % 128 == 0:
        self_parts, self_columns = (packed,) * 3, (0, 1, 2)
    else:
        self_parts, self_columns = jnp.split(packed, 3, 1), (0, 0, 0)
    steps = axis_bits("chip")
    joined = chip_gather_start(jnp.stack(passed))
    flipped = chip_gather_flips(joined, 0)
    ffn_all = gather(ffn_piece[None], "tensor")
    self_mix, self_logs = attend_call(
        *self_parts, self_columns, 1, head_count, self_low, self_high, *self_keys, wide, block
    )
    self_mix, *flipped = phase(self_mix, *flipped)
    joined = chip_gather_joins(joined, flipped, 0)

    mix_blocks = self_mix.reshape(groups, own_rows, head_width)
    mixes = [pick(mix_blocks, group, 0)] + [
        shift(pick(mix_blocks, (group + k) % groups, 0), k) for k in range(1, groups)
    ]
    flipped = chip_gather_flips(joined, 1)
    count = len(flipped)
    ffn_all, *found = phase(ffn_all, *flipped, *mixes)
    flipped, mixes = found[:count], list(found[count:])
    joined = chip_gather_joins(joined, flipped, 1)
    for step in range(2, steps):
        joined = chip_gather_joins(joined, phase(*chip_gather_flips(joined, step)), step)
    ffn_passed = [pick(ffn_all, (group + groups - k) % groups, 0) for k in range(1, groups)]
    ffn_joined = chip_gather_start(ffn_passed[0][None])
    ffn_late = gather(jnp.stack(ffn_passed[1:])[None], "chip")
    ffn_late = ffn_late.reshape(chips, groups - 2, 2, piece, width)
    mine = chip_gather_end(joined).reshape(groups - 1, -1, width)
    flipped = chip_gather_flips(ffn_joined, 0)
    far, *flipped = phase(swap_core(mine), *flipped)
    ffn_joined = chip_gather_joins(ffn_joined, flipped, 0)
    split_weights = (local, mine, far)
    ffn_flipped = chip_gather_flips(ffn_joined, 1)

    text_flat = text_states.reshape(clip_count * text_slots, text_width)
    shape = (head_count, block, core_index, cross_low, cross_high)
    after_self, after_cross, rows_two, rows_three, cross_q, cross_flat, cross_k, cross_v, cross_logs = (
        middle_call(
            *shape, own_frames, text_flat, norm_gains, norm_biases, split_weights, mixes
        )
    )

    grad_far = swap_core(grad_own_bf)
    rows_three, grad_far, *ffn_flipped = phase(rows_three, grad_far, *ffn_flipped)
    rows_far = swap_core(rows_three)
    ffn_joined = chip_gather_joins(ffn_joined, ffn_flipped, 1)
    for step in range(2, steps):
        ffn_joined = chip_gather_joins(ffn_joined, chip_gather_flips(ffn_joined, step), step)
    ffn_first = chip_gather_end(ffn_joined).reshape(chips, 2, piece, width)
    row_sets = (rows_three, rows_far, grad_own_bf, grad_far)
    ffn_part, *sums = ffn_call(*row_sets, (ffn_own, ffn_first), ())
    ffn_sum = scatter_sum(ffn_part.reshape(-1, 2 * half), "chip")
    ffn_late_part, out_own, out_far, third_own_grad, third_far = ffn_call(
        *row_sets, (ffn_late,), tuple(sums)
    )
    ffn_late_sum = scatter_sum(ffn_late_part.reshape(-1, 2 * half), "chip")
    saved = (
        third_own_grad,
        swap_core(third_far),
        grad_own_bf,
        after_self,
        after_cross,
        cross_q,
        cross_flat,
        cross_k,
        cross_v,
        cross_logs,
    )
    (
        cross_grad,
        cq_flat,
        ck_grad,
        cv_grad,
        self_side,
        self_grad,
        norm_part,
        text_part,
        *mix_grads,
    ) = middle_back_call(*shape, text_flat, norm_gains, saved, split_weights)

    mix_parts = [mix_grads[0]] + [shift(mix_grads[k], -k) for k in range(1, groups)]
    out_far = swap_core(out_far)
    arrays = (
        self_grad,
        rows_two,
        cq_flat,
        cross_flat,
        cross_grad,
        ck_grad,
        cv_grad,
        text_flat,
    )
    small_far = swap_core(weight_grads_call(head_count, 1 - core_index, arrays, mixes))
    small_part = weight_grads_call(head_count, core_index, arrays, mixes, (small_far,))
    small_part, out_far, ffn_sum, *mix_parts = phase(small_part, out_far, ffn_sum, *mix_parts)

    def text_term(k):
        return pick(text_part, (group + groups - k) % groups, 0)

    text_running = shift(text_term(1), 1)
    ffn_late_sum = ffn_late_sum.reshape(groups - 2, -1, 2 * half)
    ffn_parts = [shift(ffn_late_sum[k - 2], -k) for k in range(2, groups)]

    small_parts = chip_scatter_start(small_part.reshape(groups, chips, -1, width))
    moved = chip_scatter_flips(small_parts, 0)
    self_rest = (self_low, self_high, *self_queries, wide, block)
    if head_width % 128 == 0:
        packed_grad = packed_back_call(
            packed, self_mix, mix_parts, self_logs, head_count, group.reshape(1), *self_rest
        )
    else:
        mix_grad = jnp.concatenate([*mix_parts, *mix_parts], 0)
        mix_grad = lax.dynamic_slice_in_dim(
            mix_grad, (groups - group) % groups * own_rows, frame_count, 0
        )
        packed_grad = jnp.concatenate(
            attend_back_call(
                *self_parts, self_mix, mix_grad, self_logs, 1, head_count, *self_rest
            ),
            1,
        )
    ffn_running = shift(ffn_sum[1], 1)
    packed_grad, small_part, text_running, *found = phase(
        packed_grad, small_part, text_running, *moved, *ffn_parts
    )
    moved, ffn_parts = found[: len(moved)], found[len(moved) :]
    small_parts = chip_scatter_start(small_part.reshape(groups, chips, -1, width))

    packed_blocks = packed_grad.reshape(groups, own_rows, -1)

    def first_term(k):
        rows = pick(packed_blocks, (group + groups - k) % groups, 0)
        return times_transposed(rows, w_qkv)

    running, packed_grad, ffn_sum, after_cross, text_running, *found = phase(
        first_term(1).astype(bf16),
        packed_grad,
        ffn_sum,
        after_cross,
        text_running,
        *moved,
        *ffn_parts,
    )
    ffn_own_sum, ffn_near = ffn_sum.reshape(2, -1, 2 * half)
    moved, ffn_parts = found[: len(moved)], found[len(moved) :]
    mixed = (after_cross + out_own + out_far.astype(jnp.float32)).astype(bf16)
    packed_blocks = packed_grad.reshape(groups, own_rows, -1)

    def first_term(k):
        rows = pick(packed_blocks, (group + groups - k) % groups, 0)
        return times_transposed(rows, w_qkv)

    running, packed_grad, ffn_running, *moved = phase(
        first_term(1).astype(bf16), packed_grad, ffn_running, *moved
    )
    packed_blocks = packed_grad.reshape(groups, own_rows, -1)
    small_parts = chip_scatter_adds(small_parts, moved, 0)
    ffn_parts = [ffn_own_sum, *ffn_parts]
    ffn_joined = None
    ffn_step = 0
    ffn_mine = ffn_far = None
    small_part = small_ring = qkv_part = None
    ring_next = 2
    for hop in range(1, groups):
        arrived = shift(running, 1)
        moves = []
        if hop < steps:
            moves.append(("scatter", chip_scatter_flips(small_parts, hop)))
        elif small_ring is not None and ring_next <= groups:
            moves.append(("ring", [shift(small_ring, 1)]))
        if hop < groups - 1:
            moves.append(("text", [shift(text_running + text_term(hop + 1), 1)]))
        if hop == 1:
            moves.append(("ffn_near", [shift(ffn_near, -1), mixed]))
        elif ffn_step < steps:
            moves.append(("ffn", chip_gather_flips(ffn_joined, ffn_step)))
        if hop == groups - 2:
            moves.append(("qkv_grad", [qkv_grad_call(rows_one, packed_grad)]))
        elif hop == groups - 1:
            qkv_part = qkv_part.reshape(2, width // 2, -1)
            far = swap_core(pick(qkv_part, 1 - core, 0))
            moves.append(("qkv_core", [pick(qkv_part, core, 0), far]))
        term = first_term((hop + 1) % groups)
        if hop < groups - 1:
            running = (arrived.astype(jnp.float32) + term).astype(bf16)
        else:
            running = arrived
        running, term, *found = phase(
            running, term, *[array for _, arrays in moves for array in arrays]
        )
        for name, arrays in moves:
            got, found = found[: len(arrays)], found[len(arrays) :]
            if name == "scatter":
                small_parts = chip_scatter_adds(small_parts, got, hop)
                if hop == steps - 1:
                    small_part = jnp.concatenate(small_parts, 1)
                    small_ring = small_part[1]
            elif name == "ring":
                small_ring = got[0] + small_part[ring_next % groups]
                ring_next += 1
            elif name == "text":
                text_running = got[0]
            elif name == "ffn":
                ffn_joined = chip_gather_joins(ffn_joined, got, ffn_step)
                ffn_step += 1
            elif name == "ffn_near":
                mixed = got[1]
                ffn_parts.append(got[0])
                ffn_total = sum(part.astype(jnp.float32) for part in ffn_parts).astype(bf16)
                ffn_joined = chip_gather_start(ffn_total[None])
            elif name == "qkv_grad":
                qkv_part = got[0]
            elif name == "qkv_core":
                qkv_part = got[0] + got[1]
    text_grad = text_running.astype(jnp.float32) + text_term(0).astype(jnp.float32)
    text_grad = text_grad.reshape(clip_count, text_slots, -1)
    frames_grad, norm_first = last_call(own_frames, norm_gains, self_side, running, term)
    norm_part = norm_part.at[0].set(norm_first[0]).at[3].set(norm_first[1]).reshape(2, 3, width)

    small_step, norm_step, qkv_step = 0, 0, 0
    qkv_halves = halves(qkv_part, 0)
    small_joined = small_far = norm_parts = ffn_grads = None
    qkv_far = qkv_grad = small_grads = None
    while small_grads is None or ffn_grads is None or norm_parts is None:
        moves = []
        if ring_next <= groups:
            moves.append(("ring", [shift(small_ring, 1)]))
        elif small_step < steps:
            if small_joined is None:
                small_joined = chip_gather_start(small_ring[None])
            moves.append(("small", chip_gather_flips(small_joined, small_step)))
        elif small_far is None:
            small_mine = chip_gather_end(small_joined)[0].reshape(-1, width)
            moves.append(("small_far", [swap_core(small_mine)]))
        elif small_grads is None:
            small_grads = small_end_call(
                head_count, text_width, core_index, small_mine, small_far
            )
        if norm_step == 0:
            moves.append(("norm", [swap_core(norm_part)]))
        elif norm_step <= steps:
            moves.append(("norm", [flip(norm_part, norm_step - 1)]))
        elif norm_parts is None:
            blocks_of = norm_part.reshape(2, 3, groups, -1)
            norm_parts = [pick(blocks_of, group, 2)]
            moved = [shift(pick(blocks_of, (group + k) % groups, 2), k) for k in range(1, groups)]
            moves.append(("norm_parts", moved))
        if ffn_step < steps:
            moves.append(("ffn", chip_gather_flips(ffn_joined, ffn_step)))
        elif ffn_far is None:
            ffn_mine = chip_gather_end(ffn_joined)[0]
            moves.append(("ffn_far", [swap_core(ffn_mine)]))
        elif ffn_grads is None:
            moves.append(("ffn_grads", ffn_end_call(core_index, ffn_mine, ffn_far)))
        if qkv_step < steps:
            flips = [flip(one, o[qkv_step]) for one, o in zip(qkv_halves, chip_orders())]
            moves.append(("qkv", flips))
        elif qkv_far is None:
            qkv_part = jnp.concatenate(qkv_halves, 0)
            moves.append(("qkv_far", [swap_core(qkv_part)]))
        elif qkv_grad is None:
            moves.append(
                ("qkv_grad", [qkv_end_call(head_count, core_index, qkv_part, qkv_far)])
            )
        found = list(phase(*[array for _, arrays in moves for array in arrays]))
        for name, arrays in moves:
            got, found = found[: len(arrays)], found[len(arrays) :]
            if name == "ring":
                small_ring = got[0] + small_part[ring_next % groups]
                ring_next += 1
            elif name == "small":
                small_joined = chip_gather_joins(small_joined, got, small_step)
                small_step += 1
            elif name == "small_far":
                small_far = got[0]
            elif name == "norm":
                norm_part = norm_part + got[0]
                norm_step += 1
            elif name == "norm_parts":
                norm_parts = norm_parts + got
            elif name == "ffn":
                ffn_joined = chip_gather_joins(ffn_joined, got, ffn_step)
                ffn_step += 1
            elif name == "ffn_far":
                ffn_far = got[0]
            elif name == "ffn_grads":
                ffn_grads = got
            elif name == "qkv":
                qkv_halves = [one + other for one, other in zip(qkv_halves, got)]
                qkv_step += 1
            elif name == "qkv_far":
                qkv_far = got[0]
            elif name == "qkv_grad":
                qkv_grad = got[0]
    norm_grads = sum(norm_parts)
    if qkv_grad is None:
        qkv_grad = qkv_end_call(head_count, core_index, qkv_part, qkv_far)
    ffn_in_grad, ffn_out_grad = ffn_grads
    so_grad, cq_grad, co_grad, kv_grad = small_grads
    return (
        mixed,
        frames_grad,
        text_grad,
        norm_grads,
        qkv_grad,
        so_grad,
        cq_grad,
        kv_grad,
        co_grad,
        ffn_in_grad,
        ffn_out_grad,
    )


def solution(mesh):
    rows, groups = mesh.devices.shape
    inner = Mesh(mesh.devices.reshape(rows // 2, 2, groups), ("chip", "core", "tensor"))
    data = ("chip", "core")
    in_specs = (
        P(data, None),
        P(data, None, None),
        P(data, None),
        P(data, None),
        P(),
        P(),
        P(None, "tensor"),
        P("tensor", None),
        P(None, "tensor"),
        P(None, "tensor"),
        P("tensor", None),
        P(None, "tensor"),
        P("tensor", None),
        P(data, None),
    )
    out_specs = (
        P((*data, "tensor"), None),
        P((*data, "tensor"), None),
        P(data, None, "tensor"),
        P(None, None, "tensor"),
        P(None, "tensor"),
        P("tensor", None),
        P(None, "tensor"),
        P(None, "tensor"),
        P("tensor", None),
        P(None, "tensor"),
        P("tensor", None),
    )
    return jax.shard_map(
        per_device, mesh=inner, in_specs=in_specs, out_specs=out_specs, check_vma=False
    )
```

```python
from functools import partial

import jax
import jax.numpy as jnp
from jax import lax
from jax.experimental import pallas as pl
from jax.experimental.pallas import tpu as pltpu
from jax.sharding import Mesh
from jax.sharding import PartitionSpec as P

HEAD = 64


EPSILON = 1e-05
NEGATIVE = -1e30
VMEM_BYTES = 56 * 1024 * 1024
SCALE = 0.02


def about(microseconds):
    return pl.CostEstimate(
        flops=int(microseconds * SCALE * 1.1e9), bytes_accessed=int(microseconds * SCALE * 3e6), transcendentals=0
    )


def contract_rows(left_side, right_side):
    return lax.dot_general(
        left_side, right_side, (((0,), (0,)), ((), ())), preferred_element_type=jnp.float32
    )


def times_transposed(left_side, right_side):
    return lax.dot_general(
        left_side, right_side, (((1,), (1,)), ((), ())), preferred_element_type=jnp.float32
    )


def phase(*arrays):
    return lax.optimization_barrier(arrays)


def settle(state):
    return lax.optimization_barrier(state)


def axis_bits(name):
    return lax.axis_size(name).bit_length() - 1


def shift(array, steps):
    size = lax.axis_size("tensor")
    return lax.ppermute(array, "tensor", [(i, (i + steps) % size) for i in range(size)])


def flip(array, bit):
    pairs = [(i, i ^ (1 << bit)) for i in range(lax.axis_size("chip"))]
    return lax.ppermute(array, "chip", pairs)


def swap_core(array):
    return lax.ppermute(array, "core", [(0, 1), (1, 0)])


def in_order(mine, other, first, axis):
    return jnp.concatenate(
        [jnp.where(first, mine, other), jnp.where(first, other, mine)], axis
    )


def chip_orders():
    bits = axis_bits("chip")
    return [(0, 1), (1, 0)] if bits == 2 else [tuple(range(bits))]


def halves(array, axis):
    return jnp.split(array, len(chip_orders()), axis)


def chip_gather_start(array):
    bits = axis_bits("chip")
    return [
        part.reshape(part.shape[0], *(1,) * bits, *part.shape[1:]) for part in halves(array, 1)
    ]


def chip_gather_flips(parts, step):
    return [flip(part, order[step]) for part, order in zip(parts, chip_orders())]


def chip_gather_joins(parts, others, step):
    bits = axis_bits("chip")
    chip = lax.axis_index("chip")
    return [
        in_order(part, other, (chip >> order[step]) % 2 == 0, bits - order[step])
        for part, other, order in zip(parts, others, chip_orders())
    ]


def chip_gather_end(parts):
    whole = jnp.concatenate(parts, -2)
    return whole.reshape(whole.shape[0], -1, *whole.shape[-2:])


def pick(array, index, axis):
    return lax.dynamic_index_in_dim(array, index, axis, keepdims=False)


def chip_scatter_start(array):
    bits = axis_bits("chip")
    return [array.reshape(array.shape[0], *(2,) * bits, *array.shape[2:])] * len(chip_orders())


def chip_scatter_pick(part, number, order, step, other_side):
    side = (lax.axis_index("chip") >> order[step]) % 2
    left = sorted(set(order) - set(order[:step]), reverse=True)
    picked = pick(part, 1 - side if other_side else side, 1 + left.index(order[step]))
    return halves(picked, picked.ndim - 2)[number] if step == 0 else picked


def gather(array, axes):
    return lax.all_gather(array, axes, axis=0, tiled=True)


def scatter_sum(array, axes):
    return lax.psum_scatter(array, axes, scatter_dimension=0, tiled=True)


def dot(left, right):
    return jnp.dot(left, right, preferred_element_type=jnp.float32)


def head_mask(width, head):
    lane = lax.broadcasted_iota(jnp.int32, (1, width), 1)
    return ((lane >= head * HEAD) & (lane < (head + 1) * HEAD)).astype(jnp.float32).astype(jnp.bfloat16)


def allowed_keys(low, high, key_first, shape):
    key = key_first + lax.broadcasted_iota(jnp.int32, shape, 0)
    return (key >= low) & (key <= high)


def attend_kernel(heads, key_size, first_ref, last_ref, low_ref, high_ref, q_ref, k_ref, v_ref, out_ref, log_ref, turned, acc):
    block = pl.program_id(1)
    rows, width = q_ref.shape
    key_blocks = k_ref.shape[0] // key_size

    @pl.when(block == 0)
    def _():
        for j in range(key_blocks):
            turned[j] = v_ref[j * key_size : (j + 1) * key_size, :].T

    q_rows = q_ref[...] * jnp.bfloat16(0.125)
    q_heads = [q_rows * head_mask(width, h) for h in range(heads)]
    low, high = low_ref[0], high_ref[0]
    acc[...] = jnp.zeros_like(acc)
    last = last_ref[block]

    def step(t, state):
        j = last - t
        key_first = pl.multiple_of(j * key_size, key_size)
        k_rows = k_ref[pl.ds(key_first, key_size), :]
        allowed = allowed_keys(low, high, key_first, (key_size, rows))
        fresh = []
        for h in range(heads):
            top, total = state[h]
            scores = jnp.where(allowed, times_transposed(k_rows, q_heads[h]), NEGATIVE)
            new_top = jnp.maximum(top, jnp.max(scores, axis=0, keepdims=True))
            probs = jnp.exp(scores - new_top)
            shrink = jnp.exp(top - new_top)
            part = slice(h * HEAD, (h + 1) * HEAD)
            acc[part, :] = acc[part, :] * shrink + dot(turned[j, part, :], probs.astype(jnp.bfloat16))
            fresh.append((new_top, total * shrink + jnp.sum(probs, axis=0, keepdims=True)))
        return tuple(fresh)

    begin = (jnp.full((1, rows), NEGATIVE, jnp.float32), jnp.zeros((1, rows), jnp.float32))
    state = lax.fori_loop(0, last - first_ref[block] + 1, step, (begin,) * heads)
    for h in range(heads):
        top, total = state[h]
        part = slice(h * HEAD, (h + 1) * HEAD)
        acc[part, :] = acc[part, :] / total
        log_ref[0, 0, h : h + 1, :] = top + jnp.log(total)
    out_ref[...] = acc[...].T.astype(jnp.bfloat16)


def attend_back_kernel(heads, query_size, key_size, first_ref, last_ref, low_ref, high_ref, q_ref, k_ref, v_ref, out_ref, grad_ref, log_ref, dq_ref, dk_ref, dv_ref, q_heads, grad_heads, turned, delta, dq_acc, dk_acc, dv_acc):
    block = pl.program_id(1)
    width = q_ref.shape[1]
    query_blocks = q_ref.shape[0] // query_size

    @pl.when(block == 0)
    def _():
        for i in range(query_blocks):
            rows = slice(i * query_size, (i + 1) * query_size)
            product = grad_ref[rows, :].astype(jnp.float32) * out_ref[rows, :].astype(jnp.float32)
            product = product.T
            for h in range(heads):
                mask = head_mask(width, h)
                q_heads[i, h] = q_ref[rows, :] * (mask * jnp.bfloat16(0.125))
                grad_heads[i, h] = grad_ref[rows, :] * mask
                delta[i, h : h + 1, :] = jnp.sum(
                    product[h * HEAD : (h + 1) * HEAD, :], axis=0, keepdims=True
                )
        dq_acc[...] = jnp.zeros_like(dq_acc)

    key_first = pl.multiple_of(block * key_size, key_size)
    k_rows = k_ref[pl.ds(key_first, key_size), :]
    v_rows = v_ref[pl.ds(key_first, key_size), :]
    turned[...] = k_rows.T
    dk_acc[...] = jnp.zeros_like(dk_acc)
    dv_acc[...] = jnp.zeros_like(dv_acc)

    def step(i, carry):
        allowed = allowed_keys(low_ref[i], high_ref[i], key_first, (key_size, query_size))
        for h in range(heads):
            q_rows = q_heads[i, h]
            grad_rows = grad_heads[i, h]
            scores = times_transposed(k_rows, q_rows)
            probs = jnp.where(allowed, jnp.exp(scores - log_ref[0, i, h : h + 1, :]), 0.0)
            prob_grad = times_transposed(v_rows, grad_rows)
            score_grad = (probs * (prob_grad - delta[i, h : h + 1, :])).astype(jnp.bfloat16)
            dv_acc[...] += dot(probs.astype(jnp.bfloat16), grad_rows)
            dk_acc[...] += dot(score_grad, q_rows)
            part = slice(h * HEAD, (h + 1) * HEAD)
            dq_acc[i, part, :] += dot(turned[part, :], score_grad)
        return carry

    lax.fori_loop(first_ref[block], last_ref[block] + 1, step, 0)
    dk_ref[pl.ds(key_first, key_size), :] = dk_acc[...].astype(jnp.bfloat16)
    dv_ref[pl.ds(key_first, key_size), :] = dv_acc[...].astype(jnp.bfloat16)

    @pl.when(block == pl.num_programs(1) - 1)
    def _():
        for i in range(query_blocks):
            dq_ref[i * query_size : (i + 1) * query_size, :] = (
                (dq_acc[i] * 0.125).T.astype(jnp.bfloat16)
            )


def packed_back_kernel(heads, query_size, key_size, groups, *refs):
    first_ref, last_ref, group_ref, low_ref, high_ref, qkv_ref, out_ref = refs[:7]
    parts = refs[7 : 7 + groups]
    log_ref, dqkv_ref = refs[7 + groups : 9 + groups]
    grad_ref = refs[-1]
    width = out_ref.shape[1]
    size = parts[0].shape[0]

    @pl.when(pl.program_id(1) == 0)
    def _():
        for k in range(groups):
            owner = lax.rem(group_ref[0] + k, groups)
            grad_ref[pl.ds(pl.multiple_of(owner * size, size), size), :] = parts[k][...]

    views = [[r.at[:, c * width : (c + 1) * width] for c in range(3)] for r in (qkv_ref, dqkv_ref)]
    attend_back_kernel(
        heads,
        query_size,
        key_size,
        first_ref,
        last_ref,
        low_ref,
        high_ref,
        *views[0],
        out_ref,
        grad_ref,
        log_ref,
        *views[1],
        *refs[9 + groups : -1],
    )


def ffn_kernel(tile, carried, *refs):
    n_own_ref, n_far_ref, g_own_ref, g_far_ref = refs[:4]
    step = pl.program_id(0)
    if carried:
        weights_ref, out_in_ref, back_in_ref = refs[4:7]
    else:
        weights_ref = refs[-1]
        for i, source in enumerate(refs[4:6]):

            @pl.when(step == i)
            def _(source=source):
                weights_ref[:, 0] = source[...]

    results = refs[7:12] if carried else refs[6:9]
    z_rows, du_rows, out_acc, back_acc, n_ref, n_turned, g_ref, g_turned = (
        refs[12:20] if carried else refs[9:17]
    )
    grads_ref = results[0]
    rows, width = n_ref.shape
    chips, piece = weights_ref.shape[0], weights_ref.shape[3]
    units = chips * piece
    share = width // chips
    w_in = weights_ref[:, 0, 0].reshape(units, width)
    w_out = weights_ref[:, 0, 1].reshape(units, width)

    @pl.when(step == 0)
    def _():
        half = rows // 2
        for joined, turned, parts in (
            (n_ref, n_turned, (n_own_ref, n_far_ref)),
            (g_ref, g_turned, (g_own_ref, g_far_ref)),
        ):
            for i, source in enumerate(parts):
                joined[i * half : (i + 1) * half, :] = source[...]
                turned[:, i * half : (i + 1) * half] = source[...].T
        if carried:
            out_acc[...] = out_in_ref[...].astype(jnp.float32)
            back_acc[...] = back_in_ref[...].astype(jnp.float32)
        else:
            out_acc[...] = jnp.zeros_like(out_acc)
            back_acc[...] = jnp.zeros_like(back_acc)

    def row_tile(i, carry):
        part = pl.ds(pl.multiple_of(i * tile, tile), tile)
        pre = times_transposed(n_ref[part, :], w_in)
        scaled = lax.erf(pre * 0.7071067811865476)
        density = jnp.exp(pre * pre * -0.5) * 0.3989422804014327
        below = 0.5 + 0.5 * scaled
        hidden = (pre * below).astype(jnp.bfloat16)
        z_rows[part, :] = hidden
        out_acc[part, :] += dot(hidden, w_out)
        hidden_grad = times_transposed(g_ref[part, :], w_out)
        pre_grad = (hidden_grad * (below + pre * density)).astype(jnp.bfloat16)
        du_rows[part, :] = pre_grad
        back_acc[part, :] += dot(pre_grad, w_in)
        return carry

    lax.fori_loop(0, rows // tile, row_tile, 0, unroll=True)
    for c in range(chips):
        part = slice(c * share, (c + 1) * share)
        grads_ref[c, 0, :, :units] = dot(n_turned[part, :], du_rows[...]).astype(jnp.bfloat16)
        grads_ref[c, 0, :, units:] = dot(g_turned[part, :], z_rows[...]).astype(jnp.bfloat16)

    @pl.when(step == pl.num_programs(0) - 1)
    def _():
        own = rows // 2
        if carried:
            out_ref, out_far_ref, back_ref, back_far_ref = results[1:]
            out_ref[...] = out_acc[:own, :]
            out_far_ref[...] = out_acc[own:, :].astype(jnp.bfloat16)
            back_ref[...] = back_acc[:own, :]
            back_far_ref[...] = back_acc[own:, :].astype(jnp.bfloat16)
        else:
            results[1][...] = out_acc[...].astype(jnp.bfloat16)
            results[2][...] = back_acc[...].astype(jnp.bfloat16)


def ffn_call(n_own, n_far, g_own, g_far, weights, sums):
    rows, width = 2 * n_own.shape[0], n_own.shape[1]
    groups = len(weights) if not sums else weights[0].shape[1]
    chips, piece = weights[0].shape[0], weights[0].shape[-2]
    units = chips * piece
    whole = lambda shape: pl.BlockSpec(shape, lambda t: (0,) * len(shape))
    own = (rows // 2, width)
    grads = (chips, 1, width // chips, 2 * units)
    block = (chips, 1, 2, piece, width)
    f32, bf16 = jnp.float32, jnp.bfloat16
    scratch = [
        pltpu.VMEM((rows, units), bf16),
        pltpu.VMEM((rows, units), bf16),
        pltpu.VMEM((rows, width), f32),
        pltpu.VMEM((rows, width), f32),
        pltpu.VMEM((rows, width), bf16),
        pltpu.VMEM((width, rows), bf16),
        pltpu.VMEM((rows, width), bf16),
        pltpu.VMEM((width, rows), bf16),
    ]
    if sums:
        results = [(own, f32), (own, bf16), (own, f32), (own, bf16)]
        weight_specs = [pl.BlockSpec(block, lambda t: (0, t, 0, 0, 0))]
    else:
        results = [((rows, width), bf16)] * 2
        weight_specs = [whole(one.shape) for one in weights]
        scratch.append(pltpu.VMEM(block, bf16))
    return pl.pallas_call(
        partial(ffn_kernel, min(256, rows), bool(sums)),
        grid=(groups,),
        in_specs=[whole(own)] * 4 + weight_specs + [whole((rows, width))] * len(sums),
        out_specs=[pl.BlockSpec(grads, lambda t: (0, t, 0, 0))]
        + [whole(shape) for shape, _ in results],
        out_shape=[jax.ShapeDtypeStruct((chips, groups, *grads[2:]), bf16)]
        + [jax.ShapeDtypeStruct(*one) for one in results],
        scratch_shapes=scratch,
        compiler_params=pltpu.CompilerParams(vmem_limit_bytes=VMEM_BYTES),
        cost_estimate=about(23),
    )(n_own, n_far, g_own, g_far, *weights, *sums)


def ffn_pack_kernel(core_ref, in_ref, out_ref, packed_ref):
    chips, _, piece, _ = packed_ref.shape
    half = chips * piece
    first = pl.multiple_of(core_ref[0] * half, half)
    turned = in_ref[:, pl.ds(first, half)].T
    for c in range(chips):
        packed_ref[c, 0] = turned[c * piece : (c + 1) * piece, :]
        packed_ref[c, 1] = out_ref[pl.ds(first + c * piece, piece), :]


def ffn_pack_call(core, ffn_in, ffn_out, chips):
    units, width = ffn_out.shape
    return pl.pallas_call(
        ffn_pack_kernel,
        in_specs=[pl.BlockSpec(memory_space=pltpu.SMEM)] + [local_spec()] * 2,
        out_specs=local_spec(),
        out_shape=jax.ShapeDtypeStruct((chips, 2, units // 2 // chips, width), jnp.bfloat16),
        compiler_params=pltpu.CompilerParams(vmem_limit_bytes=VMEM_BYTES),
        cost_estimate=about(5),
    )(core, ffn_in, ffn_out)


def unit_norm(values):
    center = values - jnp.mean(values, axis=1, keepdims=True)
    inverse = lax.rsqrt(jnp.mean(center * center, axis=1, keepdims=True) + EPSILON)
    return center * inverse, inverse


def unit_back(gradient, values, gain):
    unit, inverse = unit_norm(values)
    scaled = gradient * gain
    inner = (
        scaled
        - jnp.mean(scaled, axis=1, keepdims=True)
        - unit * jnp.mean(scaled * unit, axis=1, keepdims=True)
    )
    return (
        inner * inverse,
        jnp.sum(gradient * unit, axis=0, keepdims=True),
        jnp.sum(gradient, axis=0, keepdims=True),
    )


def first_kernel(
    heads, frames_ref, gain_ref, bias_ref, weight_ref, normed_ref, packed_ref, ordered_ref
):
    @pl.when(pl.program_id(0) == 0)
    def _():
        columns = [
            weight_ref[:, (3 * h + c) * HEAD : (3 * h + c + 1) * HEAD]
            for c in range(3)
            for h in range(heads)
        ]
        ordered_ref[...] = jnp.concatenate(columns, 1)

    unit, _ = unit_norm(frames_ref[...].astype(jnp.float32))
    normed = (unit * gain_ref[0:1, :] + bias_ref[0:1, :]).astype(jnp.bfloat16)
    normed_ref[...] = normed
    packed_ref[...] = dot(normed, ordered_ref[...]).astype(jnp.bfloat16)


def first_call(heads, frames, gain, bias, weight, tile):
    rows, width = frames.shape
    columns = weight.shape[1]
    moving = lambda size: pl.BlockSpec((tile, size), lambda i: (i, 0))
    fixed = lambda shape: pl.BlockSpec(shape, lambda i: (0, 0))
    return pl.pallas_call(
        partial(first_kernel, heads),
        grid=(rows // tile,),
        in_specs=[moving(width), fixed(gain.shape), fixed(bias.shape), fixed(weight.shape)],
        out_specs=[moving(width), moving(columns), fixed(weight.shape)],
        out_shape=[
            jax.ShapeDtypeStruct((rows, width), jnp.bfloat16),
            jax.ShapeDtypeStruct((rows, columns), jnp.bfloat16),
            jax.ShapeDtypeStruct(weight.shape, jnp.bfloat16),
        ],
        compiler_params=pltpu.CompilerParams(vmem_limit_bytes=VMEM_BYTES),
        cost_estimate=about(9),
    )(frames, gain, bias, weight)


def pack_kernel(heads, self_ref, query_ref, cross_ref, pair_ref, out_ref):
    width = heads * HEAD
    text_width = pair_ref.shape[0]
    out_ref[0:width, :] = self_ref[...]
    out_ref[width : 2 * width, :] = query_ref[...].T
    out_ref[2 * width : 3 * width, :] = cross_ref[...]
    turned = pair_ref[...].T
    for h in range(heads):
        for c in range(2):
            rows = slice((3 + c) * width + h * HEAD, (3 + c) * width + (h + 1) * HEAD)
            out_ref[rows, :text_width] = turned[(2 * h + c) * HEAD : (2 * h + c + 1) * HEAD, :]
    out_ref[3 * width :, text_width:] = jnp.zeros(
        (2 * width, out_ref.shape[1] - text_width), jnp.bfloat16
    )


def pack_call(heads, self_out, cross_query, cross_out, cross_kv):
    return pl.pallas_call(
        partial(pack_kernel, heads),
        in_specs=[local_spec()] * 4,
        out_specs=local_spec(),
        out_shape=jax.ShapeDtypeStruct((5 * heads * HEAD, self_out.shape[1]), jnp.bfloat16),
        compiler_params=pltpu.CompilerParams(vmem_limit_bytes=VMEM_BYTES),
        cost_estimate=about(3),
    )(self_out, cross_query, cross_out, cross_kv)


def weight_copies(core_ref, local_ref, mine_ref, far_ref, weights, sems):
    half = mine_ref.shape[1]
    core = core_ref[0]
    copies = [pltpu.make_async_copy(local_ref, weights.at[0], sems.at[0])]
    for k in range(1, weights.shape[0]):
        for n, (source, side) in enumerate(((mine_ref, core), (far_ref, 1 - core))):
            rows = pl.ds(pl.multiple_of(side * half, half), half)
            copies.append(
                pltpu.make_async_copy(
                    source.at[k - 1], weights.at[k, rows], sems.at[2 * k - 1 + n]
                )
            )
    return copies


def middle_kernel(
    heads,
    tile,
    core_ref,
    low_ref,
    high_ref,
    inputs_ref,
    text_ref,
    gain_ref,
    bias_ref,
    local_ref,
    mine_ref,
    far_ref,
    *rest,
):
    groups = len(rest) - 9 - 4
    mixes = rest[:groups]
    h1_ref, h2_ref, n2_ref, n3_ref, cq_ref, mix_ref, ck_ref, cv_ref, log_ref = rest[
        groups : groups + 9
    ]
    weights, turned, mix_turned, sems = rest[groups + 9 :]
    width = heads * HEAD
    text_width = text_ref.shape[1]
    keys = text_ref.shape[0]
    copies = weight_copies(core_ref, local_ref, mine_ref, far_ref, weights, sems)
    for copy in copies:
        copy.start()
    for copy in copies:
        copy.wait()
    text = text_ref[...]
    for k in range(groups):
        part = slice(k * width, (k + 1) * width)
        key_weight = weights[k, 3 * width : 4 * width, :text_width]
        value_weight = weights[k, 4 * width : 5 * width, :text_width]
        ck_ref[:, part] = times_transposed(text, key_weight).astype(jnp.bfloat16)
        cv_ref[:, part] = times_transposed(text, value_weight).astype(jnp.bfloat16)
        turned[k] = times_transposed(value_weight, text).astype(jnp.bfloat16)

    def row_tile(i, carry):
        rows = pl.ds(pl.multiple_of(i * tile, tile), tile)
        total = inputs_ref[rows, :].astype(jnp.float32)
        for k in range(groups):
            total += dot(mixes[k][rows, :], weights[k, 0:width, :])
        h1_ref[rows, :] = total
        unit, _ = unit_norm(total)
        normed = (unit * gain_ref[1:2, :] + bias_ref[1:2, :]).astype(jnp.bfloat16)
        n2_ref[rows, :] = normed
        allowed = allowed_keys(low_ref[i], high_ref[i], 0, (keys, tile))
        for k in range(groups):
            part = slice(k * width, (k + 1) * width)
            queries = times_transposed(normed, weights[k, width : 2 * width, :])
            queries = queries.astype(jnp.bfloat16)
            cq_ref[rows, part] = queries
            queries = queries * jnp.bfloat16(0.125)
            for h in range(heads):
                scores = times_transposed(ck_ref[:, part], queries * head_mask(width, h))
                scores = jnp.where(allowed, scores, NEGATIVE)
                top = jnp.max(scores, axis=0, keepdims=True)
                probs = jnp.exp(scores - top)
                sums = jnp.sum(probs, axis=0, keepdims=True)
                lane = slice(h * HEAD, (h + 1) * HEAD)
                mix_turned[lane, :] = dot(turned[k, lane, :], probs.astype(jnp.bfloat16)) / sums
                log_ref[i, k * heads + h : k * heads + h + 1, :] = top + jnp.log(sums)
            mix_ref[rows, part] = mix_turned[...].T.astype(jnp.bfloat16)
        total = h1_ref[rows, :]
        for k in range(groups):
            part = slice(k * width, (k + 1) * width)
            total += dot(mix_ref[rows, part], weights[k, 2 * width : 3 * width, :])
        h2_ref[rows, :] = total
        unit, _ = unit_norm(total)
        n3_ref[rows, :] = (unit * gain_ref[2:3, :] + bias_ref[2:3, :]).astype(jnp.bfloat16)
        return carry

    lax.fori_loop(0, inputs_ref.shape[0] // tile, row_tile, 0)


def middle_back_kernel(
    heads,
    tile,
    core_ref,
    low_ref,
    high_ref,
    text_ref,
    gain_ref,
    third_ref,
    third_far_ref,
    grad_ref,
    h1_ref,
    h2_ref,
    cq_ref,
    mix_ref,
    ck_ref,
    cv_ref,
    log_ref,
    local_ref,
    mine_ref,
    far_ref,
    cross_side_ref,
    dcq_ref,
    dck_ref,
    dcv_ref,
    self_exact_ref,
    self_side_ref,
    norm_ref,
    text_part_ref,
    *rest,
):
    mix_grads = rest[:-6]
    weights, turned, query_turned, dk_acc, dv_acc, sems = rest[-6:]
    groups = weights.shape[0]
    width = heads * HEAD
    text_width = text_ref.shape[1]
    keys = text_ref.shape[0]
    copies = weight_copies(core_ref, local_ref, mine_ref, far_ref, weights, sems)
    for copy in copies:
        copy.start()
    for copy in copies:
        copy.wait()
    text = text_ref[...]
    for k in range(groups):
        key_weight = weights[k, 3 * width : 4 * width, :text_width]
        turned[k] = times_transposed(key_weight, text).astype(jnp.bfloat16)
    dk_acc[...] = jnp.zeros_like(dk_acc)
    dv_acc[...] = jnp.zeros_like(dv_acc)
    norm_ref[...] = jnp.zeros_like(norm_ref)

    def row_tile(i, carry):
        rows = pl.ds(pl.multiple_of(i * tile, tile), tile)
        third = third_ref[rows, :] + third_far_ref[rows, :].astype(jnp.float32)
        back, gain_sum, bias_sum = unit_back(third, h2_ref[rows, :], gain_ref[2:3, :])
        norm_ref[2:3, :] += gain_sum
        norm_ref[5:6, :] += bias_sum
        cross_exact = grad_ref[rows, :].astype(jnp.float32) + back
        cross_side = cross_exact.astype(jnp.bfloat16)
        self_exact_ref[rows, :] = cross_exact
        cross_side_ref[rows, :] = cross_side
        allowed = allowed_keys(low_ref[i], high_ref[i], 0, (keys, tile))
        for k in range(groups):
            part = slice(k * width, (k + 1) * width)
            mix_grad = times_transposed(cross_side, weights[k, 2 * width : 3 * width, :])
            mix_grad = mix_grad.astype(jnp.bfloat16)
            product = mix_grad.astype(jnp.float32) * mix_ref[rows, part].astype(jnp.float32)
            product = product.T
            queries = cq_ref[rows, part] * jnp.bfloat16(0.125)
            for h in range(heads):
                mask = head_mask(width, h)
                lane = slice(h * HEAD, (h + 1) * HEAD)
                one = k * heads + h
                q_rows = queries * mask
                grad_rows = mix_grad * mask
                scores = times_transposed(ck_ref[:, part], q_rows)
                probs = jnp.exp(scores - log_ref[i, one : one + 1, :])
                probs = jnp.where(allowed, probs, 0.0)
                prob_grad = times_transposed(cv_ref[:, part], grad_rows)
                delta = jnp.sum(product[lane, :], axis=0, keepdims=True)
                score_grad = (probs * (prob_grad - delta)).astype(jnp.bfloat16)
                dv_acc[:, part] += dot(probs.astype(jnp.bfloat16), grad_rows)
                dk_acc[:, part] += dot(score_grad, q_rows)
                query_turned[lane, :] = dot(turned[k, lane, :], score_grad)
            dcq_ref[rows, part] = (query_turned[...] * 0.125).T.astype(jnp.bfloat16)
        second = jnp.zeros(cross_exact.shape, jnp.float32)
        for k in range(groups):
            part = slice(k * width, (k + 1) * width)
            second += dot(dcq_ref[rows, part], weights[k, width : 2 * width, :])
        back, gain_sum, bias_sum = unit_back(second, h1_ref[rows, :], gain_ref[1:2, :])
        norm_ref[1:2, :] += gain_sum
        norm_ref[4:5, :] += bias_sum
        self_exact = self_exact_ref[rows, :] + back
        self_exact_ref[rows, :] = self_exact
        self_side = self_exact.astype(jnp.bfloat16)
        self_side_ref[rows, :] = self_side
        for k in range(groups):
            mix_grads[k][rows, :] = times_transposed(self_side, weights[k, 0:width, :]).astype(
                jnp.bfloat16
            )
        return carry

    lax.fori_loop(0, third_ref.shape[0] // tile, row_tile, 0)
    dck_ref[...] = dk_acc[...].astype(jnp.bfloat16)
    dcv_ref[...] = dv_acc[...].astype(jnp.bfloat16)
    text_part = jnp.zeros(text_ref.shape, jnp.float32)
    for k in range(groups):
        part = slice(k * width, (k + 1) * width)
        text_part += dot(dck_ref[:, part], weights[k, 3 * width : 4 * width, :text_width])
        text_part += dot(dcv_ref[:, part], weights[k, 4 * width : 5 * width, :text_width])
    size = text_width // groups
    for k in range(groups):
        text_part_ref[k] = text_part[:, k * size : (k + 1) * size].astype(jnp.bfloat16)


def weight_grads_kernel(heads, added, side_ref, *refs):
    target = refs[-1]
    if added:
        far_ref, refs = refs[0], refs[1:]
    self_ref, n2_ref, cq_ref, mix_ref, cross_ref, dck_ref, dcv_ref, text_ref = refs[:8]
    mixes = refs[8:-1]
    width = heads * HEAD
    half = target.shape[1]
    text_width = text_ref.shape[1]
    for side in range(2):

        @pl.when(side_ref[0] == side)
        def _(side=side):
            for k in range(target.shape[0]):
                first = k * width
                pairs = [
                    (mixes[k], 0, self_ref),
                    (cq_ref, first, n2_ref),
                    (mix_ref, first, cross_ref),
                    (dck_ref, first, text_ref),
                    (dcv_ref, first, text_ref),
                ]
                for n, (left, lane, right) in enumerate(pairs):
                    low = max(n * width, side * half)
                    high = min((n + 1) * width, (side + 1) * half)
                    if low >= high:
                        continue
                    columns = left[:, lane + low - n * width : lane + high - n * width]
                    product = contract_rows(columns, right[...])
                    rows = slice(low - side * half, high - side * half)
                    if added:
                        product += far_ref[k, rows, : product.shape[1]].astype(jnp.float32)
                    product = product.astype(jnp.bfloat16)
                    target[k, rows, : product.shape[1]] = product
                    if product.shape[1] < target.shape[2]:
                        target[k, rows, text_width:] = jnp.zeros(
                            (high - low, target.shape[2] - text_width), jnp.bfloat16
                        )


def weight_grads_call(heads, side, arrays, mixes, far=()):
    groups, width = len(mixes), arrays[0].shape[1]
    half = 5 * heads * HEAD // 2
    return pl.pallas_call(
        partial(weight_grads_kernel, heads, bool(far)),
        in_specs=[pl.BlockSpec(memory_space=pltpu.SMEM)]
        + [local_spec()] * (len(far) + len(arrays) + groups),
        out_specs=local_spec(),
        out_shape=jax.ShapeDtypeStruct((groups, half, width), jnp.bfloat16),
        compiler_params=pltpu.CompilerParams(vmem_limit_bytes=VMEM_BYTES),
        cost_estimate=about(10),
    )(side, *far, *arrays, *mixes)


def last_kernel(frames_ref, gain_ref, exact_ref, sum_ref, term_ref, out_ref, norm_ref):
    gradient = sum_ref[...].astype(jnp.float32) + term_ref[...]
    back, gain_sum, bias_sum = unit_back(
        gradient, frames_ref[...].astype(jnp.float32), gain_ref[0:1, :]
    )
    out_ref[...] = (exact_ref[...] + back).astype(jnp.bfloat16)
    norm_ref[0:1, :] = gain_sum
    norm_ref[1:2, :] = bias_sum


def last_call(frames, gains, exact, sums, term):
    rows, width = frames.shape
    return pl.pallas_call(
        last_kernel,
        in_specs=[local_spec()] * 5,
        out_specs=[local_spec()] * 2,
        out_shape=[
            jax.ShapeDtypeStruct((rows, width), jnp.bfloat16),
            jax.ShapeDtypeStruct((2, width), jnp.float32),
        ],
        compiler_params=pltpu.CompilerParams(vmem_limit_bytes=VMEM_BYTES),
        cost_estimate=about(4),
    )(frames, gains, exact, sums, term)


def ffn_end_kernel(core_ref, mine_ref, far_ref, in_ref, out_ref):
    units = in_ref.shape[1] // 2
    for source, side in ((mine_ref, core_ref[0]), (far_ref, 1 - core_ref[0])):
        part = pl.ds(pl.multiple_of(side * units, units), units)
        in_ref[:, part] = source[0, :, :units].astype(jnp.float32)
        out_ref[part, :] = source[0, :, units:].astype(jnp.float32).T


def ffn_end_call(core, mine, far):
    chips, features, columns = mine.shape
    source = pl.BlockSpec((1, features, columns), lambda c: (c, 0, 0))
    return pl.pallas_call(
        ffn_end_kernel,
        grid=(chips,),
        in_specs=[pl.BlockSpec(memory_space=pltpu.SMEM), source, source],
        out_specs=[
            pl.BlockSpec((features, columns), lambda c: (c, 0)),
            pl.BlockSpec((columns, features), lambda c: (0, c)),
        ],
        out_shape=[
            jax.ShapeDtypeStruct((chips * features, columns), jnp.float32),
            jax.ShapeDtypeStruct((columns, chips * features), jnp.float32),
        ],
        compiler_params=pltpu.CompilerParams(vmem_limit_bytes=VMEM_BYTES),
        cost_estimate=about(5),
    )(core, mine, far)


def qkv_grad_kernel(left_ref, right_ref, out_ref):
    out_ref[...] = contract_rows(left_ref[...], right_ref[...]).astype(jnp.bfloat16)


def qkv_grad_call(normed, packed_grad):
    rows, width = normed.shape
    columns = packed_grad.shape[1]
    tile = min(256, width)
    return pl.pallas_call(
        qkv_grad_kernel,
        grid=(width // tile,),
        in_specs=[
            pl.BlockSpec((rows, tile), lambda i: (0, i)),
            pl.BlockSpec((rows, columns), lambda i: (0, 0)),
        ],
        out_specs=pl.BlockSpec((tile, columns), lambda i: (i, 0)),
        out_shape=jax.ShapeDtypeStruct((width, columns), jnp.bfloat16),
        compiler_params=pltpu.CompilerParams(vmem_limit_bytes=VMEM_BYTES),
        cost_estimate=about(5),
    )(normed, packed_grad)


def qkv_end_kernel(heads, core_ref, mine_ref, far_ref, out_ref):
    width = heads * HEAD
    size = mine_ref.shape[0]
    for source, side in ((mine_ref, core_ref[0]), (far_ref, 1 - core_ref[0])):
        columns = [
            source[:, c * width + h * HEAD : c * width + (h + 1) * HEAD]
            for h in range(heads)
            for c in range(3)
        ]
        rows = pl.ds(pl.multiple_of(side * size, size), size)
        out_ref[rows, :] = jnp.concatenate(columns, 1).astype(jnp.float32)


def qkv_end_call(heads, core, mine, far):
    rows, columns = mine.shape
    return pl.pallas_call(
        partial(qkv_end_kernel, heads),
        in_specs=[pl.BlockSpec(memory_space=pltpu.SMEM)] + [local_spec()] * 2,
        out_specs=local_spec(),
        out_shape=jax.ShapeDtypeStruct((2 * rows, columns), jnp.float32),
        compiler_params=pltpu.CompilerParams(vmem_limit_bytes=VMEM_BYTES),
        cost_estimate=about(3),
    )(core, mine, far)


def small_end_kernel(heads, core_ref, mine_ref, far_ref, *refs):
    self_ref, query_ref, cross_ref, pair_ref, joined = refs
    width = heads * HEAD
    text_width = pair_ref.shape[0]
    half = joined.shape[0] // 2
    for source, side in ((mine_ref, core_ref[0]), (far_ref, 1 - core_ref[0])):
        joined[pl.ds(pl.multiple_of(side * half, half), half), :] = source[...]
    self_ref[...] = joined[0:width, :].astype(jnp.float32)
    query_ref[...] = joined[width : 2 * width, :].astype(jnp.float32).T
    cross_ref[...] = joined[2 * width : 3 * width, :].astype(jnp.float32)
    for h in range(heads):
        rows = [slice((3 + c) * width + h * HEAD, (3 + c) * width + (h + 1) * HEAD) for c in (0, 1)]
        both = jnp.concatenate([joined[part, :text_width] for part in rows], 0)
        pair_ref[:, 2 * h * HEAD : 2 * (h + 1) * HEAD] = both.astype(jnp.float32).T


def small_end_call(heads, text_width, core, mine, far):
    width = mine.shape[1]
    head_width = heads * HEAD
    shapes = [
        (head_width, width),
        (width, head_width),
        (head_width, width),
        (text_width, 2 * head_width),
    ]
    return pl.pallas_call(
        partial(small_end_kernel, heads),
        in_specs=[pl.BlockSpec(memory_space=pltpu.SMEM)] + [local_spec()] * 2,
        out_specs=[local_spec()] * 4,
        out_shape=[jax.ShapeDtypeStruct(shape, jnp.float32) for shape in shapes],
        scratch_shapes=[pltpu.VMEM((5 * head_width, width), jnp.bfloat16)],
        compiler_params=pltpu.CompilerParams(vmem_limit_bytes=VMEM_BYTES),
        cost_estimate=about(4),
    )(core, mine, far)


def local_spec():
    return pl.BlockSpec(memory_space=pltpu.VMEM)


def middle_specs(plain):
    return (
        [pl.BlockSpec(memory_space=pltpu.SMEM)]
        + [local_spec()] * plain
        + [pl.BlockSpec(memory_space=pl.ANY)] * 3
    )


def middle_call(heads, tile, core, low, high, inputs, text, gains, biases, split_weights, mixes):
    rows, width = inputs.shape
    keys = text.shape[0]
    groups = len(mixes)
    f32, bf16 = jnp.float32, jnp.bfloat16
    shapes = [
        ((rows, width), f32),
        ((rows, width), f32),
        ((rows, width), bf16),
        ((rows, width), bf16),
        ((rows, width), bf16),
        ((rows, width), bf16),
        ((keys, width), bf16),
        ((keys, width), bf16),
        ((rows // tile, groups * heads, tile), f32),
    ]
    return pl.pallas_call(
        partial(middle_kernel, heads, tile),
        in_specs=middle_specs(6) + [local_spec()] * groups,
        out_specs=[local_spec()] * len(shapes),
        out_shape=[jax.ShapeDtypeStruct(*one) for one in shapes],
        scratch_shapes=[
            pltpu.VMEM((groups, *split_weights[0].shape), bf16),
            pltpu.VMEM((groups, heads * HEAD, keys), bf16),
            pltpu.VMEM((heads * HEAD, tile), f32),
            pltpu.SemaphoreType.DMA((2 * groups - 1,)),
        ],
        compiler_params=pltpu.CompilerParams(vmem_limit_bytes=VMEM_BYTES),
        cost_estimate=about(30),
    )(core, lanes(low, tile), lanes(high, tile), inputs, text, gains, biases, *split_weights, *mixes)


def middle_back_call(heads, tile, core, low, high, text, gains, saved, split_weights):
    rows, width = saved[0].shape
    keys = text.shape[0]
    groups = width // (heads * HEAD)
    f32, bf16 = jnp.float32, jnp.bfloat16
    shapes = [
        ((rows, width), bf16),
        ((rows, width), bf16),
        ((keys, width), bf16),
        ((keys, width), bf16),
        ((rows, width), f32),
        ((rows, width), bf16),
        ((6, width), f32),
        ((groups, keys, text.shape[1] // groups), bf16),
    ] + [((rows, heads * HEAD), bf16)] * groups
    return pl.pallas_call(
        partial(middle_back_kernel, heads, tile),
        in_specs=middle_specs(4 + len(saved)),
        out_specs=[local_spec()] * len(shapes),
        out_shape=[jax.ShapeDtypeStruct(*one) for one in shapes],
        scratch_shapes=[
            pltpu.VMEM((groups, *split_weights[0].shape), bf16),
            pltpu.VMEM((groups, heads * HEAD, keys), bf16),
            pltpu.VMEM((heads * HEAD, tile), f32),
            pltpu.VMEM((keys, width), f32),
            pltpu.VMEM((keys, width), f32),
            pltpu.SemaphoreType.DMA((2 * groups - 1,)),
        ],
        compiler_params=pltpu.CompilerParams(vmem_limit_bytes=VMEM_BYTES),
        cost_estimate=about(40),
    )(core, lanes(low, tile), lanes(high, tile), text, gains, *saved, *split_weights)


def lanes(values, size):
    return values.astype(jnp.int32).reshape(-1, 1, size)


def attend_call(q, k, v, columns, groups, heads, low, high, first, last, query_size, key_size):
    width = heads * HEAD
    rows, keys = q.shape[0], k.shape[0]
    blocks = rows // query_size
    spec = lambda size, column: pl.BlockSpec((size, width), lambda g, i, *_: (0, column + g))
    vector = pl.BlockSpec((1, 1, query_size), lambda g, i, *_: (i, 0, 0))
    q_column = columns[0]
    return pl.pallas_call(
        partial(attend_kernel, heads, key_size),
        grid_spec=pltpu.PrefetchScalarGridSpec(
            num_scalar_prefetch=2,
            grid=(groups, blocks),
            in_specs=[
                vector,
                vector,
                pl.BlockSpec((query_size, width), lambda g, i, *_: (i, q_column + g)),
                spec(keys, columns[1]),
                spec(keys, columns[2]),
            ],
            out_specs=[
                pl.BlockSpec((query_size, width), lambda g, i, *_: (i, g)),
                pl.BlockSpec((1, 1, heads, query_size), lambda g, i, *_: (g, i, 0, 0)),
            ],
            scratch_shapes=[
                pltpu.VMEM((keys // key_size, width, key_size), jnp.bfloat16),
                pltpu.VMEM((width, query_size), jnp.float32),
            ],
        ),
        out_shape=[
            jax.ShapeDtypeStruct((rows, groups * width), jnp.bfloat16),
            jax.ShapeDtypeStruct((groups, blocks, heads, query_size), jnp.float32),
        ],
        compiler_params=pltpu.CompilerParams(vmem_limit_bytes=VMEM_BYTES),
        cost_estimate=about(30 if groups == 1 else 17),
    )(first, last, lanes(low, query_size), lanes(high, query_size), q, k, v)


def back_scratch(heads, blocks, query_size, key_size):
    width = heads * HEAD
    return [
        pltpu.VMEM((blocks, heads, query_size, width), jnp.bfloat16),
        pltpu.VMEM((blocks, heads, query_size, width), jnp.bfloat16),
        pltpu.VMEM((width, key_size), jnp.bfloat16),
        pltpu.VMEM((blocks, heads, query_size), jnp.float32),
        pltpu.VMEM((blocks, width, query_size), jnp.float32),
        pltpu.VMEM((key_size, width), jnp.float32),
        pltpu.VMEM((key_size, width), jnp.float32),
    ]


def packed_back_call(
    qkv, out, parts, logs, heads, group, low, high, first, last, query_size, key_size
):
    rows, width = out.shape
    blocks = rows // query_size
    whole = lambda shape: pl.BlockSpec(shape, lambda g, j, *_: (0,) * len(shape))
    vector = whole((blocks, 1, query_size))
    return pl.pallas_call(
        partial(packed_back_kernel, heads, query_size, key_size, len(parts)),
        grid_spec=pltpu.PrefetchScalarGridSpec(
            num_scalar_prefetch=3,
            grid=(1, rows // key_size),
            in_specs=[vector, vector, whole(qkv.shape), whole(out.shape)]
            + [whole(part.shape) for part in parts]
            + [whole(logs.shape)],
            out_specs=whole(qkv.shape),
            scratch_shapes=back_scratch(heads, blocks, query_size, key_size)
            + [pltpu.VMEM(out.shape, jnp.bfloat16)],
        ),
        out_shape=jax.ShapeDtypeStruct(qkv.shape, jnp.bfloat16),
        compiler_params=pltpu.CompilerParams(vmem_limit_bytes=VMEM_BYTES),
        cost_estimate=about(30),
    )(
        first,
        last,
        group,
        lanes(low, query_size),
        lanes(high, query_size),
        qkv,
        out,
        *parts,
        logs,
    )


def attend_back_call(q, k, v, out, grad, logs, groups, heads, low, high, first, last, query_size, key_size):
    width = heads * HEAD
    rows, keys = q.shape[0], k.shape[0]
    blocks = rows // query_size
    column = lambda size: pl.BlockSpec((size, width), lambda g, j, *_: (0, g))
    vector = pl.BlockSpec((blocks, 1, query_size), lambda g, j, *_: (0, 0, 0))
    return pl.pallas_call(
        partial(attend_back_kernel, heads, query_size, key_size),
        grid_spec=pltpu.PrefetchScalarGridSpec(
            num_scalar_prefetch=2,
            grid=(groups, keys // key_size),
            in_specs=[
                vector,
                vector,
                column(rows),
                column(keys),
                column(keys),
                column(rows),
                column(rows),
                pl.BlockSpec((1, blocks, heads, query_size), lambda g, j, *_: (g, 0, 0, 0)),
            ],
            out_specs=[column(rows), column(keys), column(keys)],
            scratch_shapes=back_scratch(heads, blocks, query_size, key_size),
        ),
        out_shape=[
            jax.ShapeDtypeStruct((rows, groups * width), jnp.bfloat16),
            jax.ShapeDtypeStruct((keys, groups * width), jnp.bfloat16),
            jax.ShapeDtypeStruct((keys, groups * width), jnp.bfloat16),
        ],
        compiler_params=pltpu.CompilerParams(vmem_limit_bytes=VMEM_BYTES),
        cost_estimate=about(6 * groups),
    )(first, last, lanes(low, query_size), lanes(high, query_size), q, k, v, out, grad, logs)


def per_device(
    frames,
    text_states,
    clip_lengths,
    text_lengths,
    norm_gains,
    norm_biases,
    self_qkv,
    self_out,
    cross_query,
    cross_kv,
    cross_out,
    ffn_in,
    ffn_out,
    out_grad,
):
    groups = lax.axis_size("tensor")
    chips = lax.axis_size("chip")
    group = lax.axis_index("tensor")
    chip = lax.axis_index("chip")
    core = lax.axis_index("core")
    bf16 = jnp.bfloat16
    frame_count, width = frames.shape
    own_rows = frame_count // groups
    offset = group * own_rows
    clip_count, text_slots, text_width = text_states.shape
    head_count = self_out.shape[0] // HEAD
    all_heads = head_count * groups
    ends = jnp.cumsum(clip_lengths[0])
    starts = ends - clip_lengths[0]
    positions = jnp.arange(frame_count, dtype=jnp.int32)[:, None]
    clip_first = jnp.max(jnp.where(positions >= starts, starts, 0), axis=1)
    clip_stop = jnp.min(jnp.where(positions < ends, ends, frame_count), axis=1)
    block = min(256, own_rows)
    blocks = jnp.arange(frame_count // block, dtype=jnp.int32)
    self_low, self_high = clip_first, positions[:, 0]
    wide = min(2 * block, frame_count)
    wides = jnp.arange(frame_count // wide, dtype=jnp.int32)
    self_keys = (clip_first[::wide] // block, (wides * wide + wide - 1) // block)
    self_queries = (blocks * block // wide, (clip_stop[block - 1 :: block] - 1) // wide)
    own_positions = offset + jnp.arange(own_rows, dtype=jnp.int32)[:, None]
    own_clip = jnp.sum((own_positions >= ends).astype(jnp.int32), axis=1)
    own_length = jnp.sum(
        jnp.where(own_clip[:, None] == jnp.arange(clip_count), text_lengths[0], 0), axis=1
    )
    cross_low = own_clip * text_slots
    cross_high = cross_low + own_length - 1
    cross_keys = (own_clip[::block], own_clip[block - 1 :: block])
    inside_first = jnp.clip(starts - offset, 0, own_rows)
    inside_stop = jnp.clip(ends - offset, 0, own_rows)
    cross_first = jnp.minimum(inside_first // block, own_rows // block - 1)
    cross_queries = (
        cross_first,
        jnp.where(inside_stop > inside_first, (inside_stop - 1) // block, cross_first - 1),
    )

    head_width = head_count * HEAD
    local = pack_call(head_count, self_out, cross_query, cross_out, cross_kv)
    pieces = local.reshape(2, chips, -1, width)
    half = ffn_out.shape[0] // 2
    piece = half // chips
    core_index = core.reshape(1).astype(jnp.int32)
    sent_piece = pick(pick(pieces, core, 0), chip, 0)
    sent_piece, frames, self_qkv, ffn_in, ffn_out, out_grad = phase(
        sent_piece, frames, self_qkv, ffn_in, ffn_out, out_grad
    )
    passed = [shift(sent_piece, k) for k in range(1, groups)]
    ffn_own = ffn_pack_call(core_index, ffn_in, ffn_out, chips)
    ffn_piece = pick(ffn_own, chip, 0).reshape(2 * piece, width)
    own_frames = lax.dynamic_slice_in_dim(frames, offset, own_rows, 0)
    grad_own_bf = lax.dynamic_slice_in_dim(out_grad, offset, own_rows, 0)
    rows_one, packed, w_qkv = first_call(
        head_count, frames, norm_gains, norm_biases, self_qkv, block
    )
    packed, ffn_piece, own_frames, grad_own_bf, *passed = phase(
        packed, ffn_piece, own_frames, grad_own_bf, *passed
    )
    if head_width % 128 == 0:
        self_parts, self_columns = (packed,) * 3, (0, 1, 2)
    else:
        self_parts, self_columns = jnp.split(packed, 3, 1), (0, 0, 0)
    steps = axis_bits("chip")
    joined = chip_gather_start(jnp.stack(passed))
    flipped = chip_gather_flips(joined, 0)
    ffn_all = gather(ffn_piece[None], "tensor")
    self_mix, self_logs = attend_call(
        *self_parts, self_columns, 1, head_count, self_low, self_high, *self_keys, wide, block
    )
    joined = chip_gather_joins(joined, flipped, 0)
    self_mix, *joined = phase(self_mix, *joined)

    mix_blocks = self_mix.reshape(groups, own_rows, head_width)
    mixes = [pick(mix_blocks, group, 0)] + [
        shift(pick(mix_blocks, (group + k) % groups, 0), k) for k in range(1, groups)
    ]
    flipped = chip_gather_flips(joined, 1)
    joined = chip_gather_joins(joined, flipped, 1)
    for step in range(2, steps):
        joined = chip_gather_joins(joined, phase(*chip_gather_flips(joined, step)), step)
    mine = chip_gather_end(joined).reshape(groups - 1, -1, width)
    ffn_passed = [pick(ffn_all, (group + groups - k) % groups, 0) for k in range(1, groups)]
    ffn_stack = jnp.stack(ffn_passed[1:])[None]
    mine, ffn_stack, ffn_next, *mixes = phase(mine, ffn_stack, ffn_passed[0], *mixes)
    ffn_joined = chip_gather_start(ffn_next[None])
    ffn_late = gather(ffn_stack, "chip")
    ffn_late = ffn_late.reshape(chips, groups - 2, 2, piece, width)
    flipped = chip_gather_flips(ffn_joined, 0)
    ffn_joined = chip_gather_joins(ffn_joined, flipped, 0)
    far, *ffn_joined = phase(swap_core(mine), *ffn_joined)
    split_weights = (local, mine, far)
    ffn_flipped = chip_gather_flips(ffn_joined, 1)

    text_flat = text_states.reshape(clip_count * text_slots, text_width)
    shape = (head_count, block, core_index, cross_low, cross_high)
    after_self, after_cross, rows_two, rows_three, cross_q, cross_flat, cross_k, cross_v, cross_logs = (
        middle_call(
            *shape, own_frames, text_flat, norm_gains, norm_biases, split_weights, mixes
        )
    )

    grad_far = swap_core(grad_own_bf)
    rows_three, grad_far, *ffn_flipped = phase(rows_three, grad_far, *ffn_flipped)
    rows_far = swap_core(rows_three)
    ffn_joined = chip_gather_joins(ffn_joined, ffn_flipped, 1)
    for step in range(2, steps):
        ffn_joined = chip_gather_joins(ffn_joined, chip_gather_flips(ffn_joined, step), step)
    ffn_first = chip_gather_end(ffn_joined).reshape(chips, 2, piece, width)
    row_sets = (rows_three, rows_far, grad_own_bf, grad_far)
    ffn_part, *sums = ffn_call(*row_sets, (ffn_own, ffn_first), ())
    ffn_sum = scatter_sum(ffn_part.reshape(-1, 2 * half), "chip")
    ffn_late_part, out_own, out_far, third_own_grad, third_far = ffn_call(
        *row_sets, (ffn_late,), tuple(sums)
    )
    ffn_late_sum = scatter_sum(ffn_late_part.reshape(-1, 2 * half), "chip")
    saved = (
        third_own_grad,
        swap_core(third_far),
        grad_own_bf,
        after_self,
        after_cross,
        cross_q,
        cross_flat,
        cross_k,
        cross_v,
        cross_logs,
    )
    (
        cross_grad,
        cq_flat,
        ck_grad,
        cv_grad,
        self_side,
        self_grad,
        norm_part,
        text_part,
        *mix_grads,
    ) = middle_back_call(*shape, text_flat, norm_gains, saved, split_weights)

    mix_parts = [mix_grads[0]] + [shift(mix_grads[k], -k) for k in range(1, groups)]
    out_far = swap_core(out_far)
    arrays = (
        self_grad,
        rows_two,
        cq_flat,
        cross_flat,
        cross_grad,
        ck_grad,
        cv_grad,
        text_flat,
    )
    small_far = swap_core(weight_grads_call(head_count, 1 - core_index, arrays, mixes))
    small_part = weight_grads_call(head_count, core_index, arrays, mixes, (small_far,))

    def text_term(k):
        return pick(text_part, (group + groups - k) % groups, 0)

    orders = chip_orders()
    whole = chip_scatter_start(small_part.reshape(groups, chips, -1, width))
    state = settle(
        dict(
            whole=small_part,
            send=[chip_scatter_pick(whole[n], n, o, 0, True) for n, o in enumerate(orders)],
            text=text_term(1),
            out_far=out_far,
            ffn=list(ffn_sum.reshape(2, -1, 2 * half)),
            mix=mix_parts,
        )
    )
    mix_parts = state.pop("mix")
    text_run = shift(state["text"], 1)
    moved = [flip(one, o[0]) for one, o in zip(state["send"], orders)]
    ffn_run = shift(state["ffn"][1], 1)

    self_rest = (self_low, self_high, *self_queries, wide, block)
    if head_width % 128 == 0:
        packed_grad = packed_back_call(
            packed, self_mix, mix_parts, self_logs, head_count, group.reshape(1), *self_rest
        )
    else:
        mix_grad = jnp.concatenate([*mix_parts, *mix_parts], 0)
        mix_grad = lax.dynamic_slice_in_dim(
            mix_grad, (groups - group) % groups * own_rows, frame_count, 0
        )
        packed_grad = jnp.concatenate(
            attend_back_call(
                *self_parts, self_mix, mix_grad, self_logs, 1, head_count, *self_rest
            ),
            1,
        )
    state = settle(
        dict(
            state,
            grad=packed_grad,
            text=text_run,
            moved=moved,
            run=ffn_run,
            late=ffn_late_sum,
            h2=after_cross,
        )
    )

    def first_term(k):
        blocks = state["grad"].reshape(groups, own_rows, -1)
        rows = pick(blocks, (group + groups - k) % groups, 0)
        return times_transposed(rows, w_qkv)

    state = settle(dict(state, running=first_term(1).astype(bf16)))
    whole = chip_scatter_start(state["whole"].reshape(groups, chips, -1, width))
    small = [
        chip_scatter_pick(whole[n], n, o, 0, False) + one
        for n, (o, one) in enumerate(zip(orders, state["moved"]))
    ]
    late = list(state["late"].reshape(groups - 2, -1, 2 * half))
    state["run"] = state["run"] + late[0]
    ring_next = 1
    ffn_step = 0
    text_next = 2
    state["text"] = state["text"] + text_term(2)
    for hop in range(1, groups):
        arrived = shift(state["running"], 1)
        after_hop = dict(grad=state["grad"])
        if hop < steps:
            small = [
                chip_scatter_pick(one, n, o, hop, False)
                + flip(chip_scatter_pick(one, n, o, hop, True), o[hop])
                for n, (o, one) in enumerate(zip(orders, small))
            ]
            if hop == steps - 1:
                small = jnp.concatenate(small, 1)
        elif ring_next < groups:
            running_small = shift(small[1] if ring_next == 1 else state["ring"], 1)
            ring_next += 1
            after_hop["ring"] = running_small + small[ring_next % groups]
        after_hop["small"] = small
        after_hop["text"] = state["text"]
        if 1 < hop < groups - 1:
            text_next += 1
            after_hop["text"] = shift(state["text"], 1) + text_term(text_next % groups)
        if hop < groups - 1:
            after_hop["own"] = state["own"] if hop > 1 else state["ffn"][0]
            run = shift(state["run"], 1)
            after_hop["run"] = run + (late[hop] if hop < groups - 2 else after_hop["own"])
            late = after_hop["late"] = state["late"] if hop > 1 else late
        else:
            ffn = chip_gather_start(state["run"][None])
            after_hop["ffn"] = chip_gather_joins(ffn, chip_gather_flips(ffn, 0), 0)
            ffn_step = 1
        if hop == 1:
            mixed = state["h2"] + out_own + state["out_far"].astype(jnp.float32)
            after_hop["mixed"] = mixed.astype(bf16)
        else:
            after_hop["mixed"] = state["mixed"]
        if hop == 1:
            grad, run = phase(state["grad"], run)
            qkv_part = qkv_grad_call(rows_one, grad).reshape(2, width // 2, -1)
            far = swap_core(pick(qkv_part, 1 - core, 0))
            after_hop["qkv"] = pick(qkv_part, core, 0) + far
        elif hop - 2 < steps:
            after_hop["qkv"] = state["qkv"] + flip(state["qkv"], hop - 2)
        else:
            after_hop["qkv"] = state["qkv"]
        term = first_term((hop + 1) % groups)
        if hop < groups - 1:
            after_hop["running"] = (arrived.astype(jnp.float32) + term).astype(bf16)
        else:
            after_hop["running"], after_hop["term"] = arrived, term
        state = settle(after_hop)
        small = state["small"]
        late = state.get("late")

    mixed, text = state["mixed"], state["text"]
    frames_grad, norm_first = last_call(
        own_frames, norm_gains, self_side, state["running"], state["term"]
    )
    norm_rows = [norm_first[0:1], norm_part[1:3], norm_first[1:2], norm_part[4:6]]
    norm = jnp.concatenate(norm_rows, 0).reshape(2, 3, width)
    ring, ffn, qkv = state["ring"], state["ffn"], state["qkv"]
    small_step = norm_step = 0
    qkv_mine = qkv
    small_mine = small_far = small_grads = norm_parts = None
    ffn_mine = ffn_far = ffn_grads = qkv_far = qkv_grad = None
    small_sum = None
    while small_grads is None or ffn_grads is None or norm_parts is None or qkv_grad is None:
        if ring_next < groups:
            ring_next += 1
            ring = shift(ring, 1) + small[ring_next % groups]
        elif small_step < steps:
            small_sum = chip_gather_start(ring[None]) if small_sum is None else small_sum
            small_sum = chip_gather_joins(
                small_sum, chip_gather_flips(small_sum, small_step), small_step
            )
            small_step += 1
            if small_step == steps:
                small_mine = chip_gather_end(small_sum)[0].reshape(-1, width)
        elif small_far is None:
            small_far = swap_core(small_mine)
        elif small_grads is None:
            small_grads = small_end_call(
                head_count, text_width, core_index, small_mine, small_far
            )
        if norm_step == 0:
            norm = norm + swap_core(norm)
            norm_step += 1
        elif norm_step <= steps:
            norm = norm + flip(norm, norm_step - 1)
            norm_step += 1
        elif norm_parts is None:
            blocks_of = norm.reshape(2, 3, groups, -1)
            norm_parts = [pick(blocks_of, group, 2)] + [
                shift(pick(blocks_of, (group + k) % groups, 2), k) for k in range(1, groups)
            ]
        if ffn_step < steps:
            ffn = chip_gather_joins(ffn, chip_gather_flips(ffn, ffn_step), ffn_step)
            ffn_step += 1
        elif ffn_far is None:
            ffn_mine = chip_gather_end(ffn)[0]
            ffn_far = swap_core(ffn_mine)
        elif ffn_grads is None:
            ffn_grads = ffn_end_call(core_index, ffn_mine, ffn_far)
        if text_next < groups:
            text_next += 1
            text = shift(text, 1) + text_term(text_next % groups)
        elif qkv_far is None:
            qkv_far = swap_core(qkv_mine)
        elif qkv_grad is None:
            qkv_grad = qkv_end_call(head_count, core_index, qkv_mine, qkv_far)
        names = ["ring", "small", "small_sum", "small_mine", "small_far", "small_grads"]
        names += ["norm", "norm_parts", "ffn", "ffn_mine", "ffn_far", "ffn_grads"]
        names += ["text", "qkv_mine", "qkv_far", "qkv_grad"]
        values = (ring, small, small_sum, small_mine, small_far, small_grads, norm, norm_parts)
        values += (ffn, ffn_mine, ffn_far, ffn_grads, text, qkv_mine, qkv_far, qkv_grad)
        known = {name: one for name, one in zip(names, values) if one is not None}
        known = settle(known)
        ring, small, small_sum, small_mine, small_far, small_grads, norm, norm_parts = [
            known.get(name) for name in names[:8]
        ]
        ffn, ffn_mine, ffn_far, ffn_grads, text, qkv_mine, qkv_far, qkv_grad = [
            known.get(name) for name in names[8:]
        ]
    text_grad = text.astype(jnp.float32).reshape(clip_count, text_slots, -1)
    norm_grads = sum(norm_parts)
    ffn_in_grad, ffn_out_grad = ffn_grads
    so_grad, cq_grad, co_grad, kv_grad = small_grads
    return (
        mixed,
        frames_grad,
        text_grad,
        norm_grads,
        qkv_grad,
        so_grad,
        cq_grad,
        kv_grad,
        co_grad,
        ffn_in_grad,
        ffn_out_grad,
    )


def solution(mesh):
    rows, groups = mesh.devices.shape
    inner = Mesh(mesh.devices.reshape(rows // 2, 2, groups), ("chip", "core", "tensor"))
    data = ("chip", "core")
    in_specs = (
        P(data, None),
        P(data, None, None),
        P(data, None),
        P(data, None),
        P(),
        P(),
        P(None, "tensor"),
        P("tensor", None),
        P(None, "tensor"),
        P(None, "tensor"),
        P("tensor", None),
        P(None, "tensor"),
        P("tensor", None),
        P(data, None),
    )
    out_specs = (
        P((*data, "tensor"), None),
        P((*data, "tensor"), None),
        P(data, None, "tensor"),
        P(None, None, "tensor"),
        P(None, "tensor"),
        P("tensor", None),
        P(None, "tensor"),
        P(None, "tensor"),
        P("tensor", None),
        P(None, "tensor"),
        P("tensor", None),
    )
    return jax.shard_map(
        per_device, mesh=inner, in_specs=in_specs, out_specs=out_specs, check_vma=False
    )
```

```python
from functools import partial

import jax
import jax.numpy as jnp
from jax import lax
from jax.experimental import pallas as pl
from jax.experimental.pallas import tpu as pltpu
from jax.sharding import Mesh
from jax.sharding import PartitionSpec as P

HEAD = 64


EPSILON = 1e-05
NEGATIVE = -1e30
VMEM_BYTES = 56 * 1024 * 1024
SCALE = 0.02


def about(microseconds):
    return pl.CostEstimate(
        flops=int(microseconds * SCALE * 1.1e9), bytes_accessed=int(microseconds * SCALE * 3e6), transcendentals=0
    )


def contract_rows(left_side, right_side):
    return lax.dot_general(
        left_side, right_side, (((0,), (0,)), ((), ())), preferred_element_type=jnp.float32
    )


def times_transposed(left_side, right_side):
    return lax.dot_general(
        left_side, right_side, (((1,), (1,)), ((), ())), preferred_element_type=jnp.float32
    )


def phase(*arrays):
    return lax.optimization_barrier(arrays)


def settle(state):
    return lax.optimization_barrier(state)


def axis_bits(name):
    return lax.axis_size(name).bit_length() - 1


def shift(array, steps):
    size = lax.axis_size("tensor")
    return lax.ppermute(array, "tensor", [(i, (i + steps) % size) for i in range(size)])


def flip(array, bit):
    pairs = [(i, i ^ (1 << bit)) for i in range(lax.axis_size("chip"))]
    return lax.ppermute(array, "chip", pairs)


def swap_core(array):
    return lax.ppermute(array, "core", [(0, 1), (1, 0)])


def in_order(mine, other, first, axis):
    return jnp.concatenate(
        [jnp.where(first, mine, other), jnp.where(first, other, mine)], axis
    )


def chip_orders():
    bits = axis_bits("chip")
    return [(0, 1), (1, 0)] if bits == 2 else [tuple(range(bits))]


def halves(array, axis):
    return jnp.split(array, len(chip_orders()), axis)


def chip_gather_start(array):
    bits = axis_bits("chip")
    return [
        part.reshape(part.shape[0], *(1,) * bits, *part.shape[1:]) for part in halves(array, 1)
    ]


def chip_gather_flips(parts, step):
    return [flip(part, order[step]) for part, order in zip(parts, chip_orders())]


def chip_gather_joins(parts, others, step):
    bits = axis_bits("chip")
    chip = lax.axis_index("chip")
    return [
        in_order(part, other, (chip >> order[step]) % 2 == 0, bits - order[step])
        for part, other, order in zip(parts, others, chip_orders())
    ]


def chip_gather_end(parts):
    whole = jnp.concatenate(parts, -2)
    return whole.reshape(whole.shape[0], -1, *whole.shape[-2:])


def pick(array, index, axis):
    return lax.dynamic_index_in_dim(array, index, axis, keepdims=False)


def chip_scatter_start(array):
    bits = axis_bits("chip")
    return [array.reshape(array.shape[0], *(2,) * bits, *array.shape[2:])] * len(chip_orders())


def chip_scatter_pick(part, number, order, step, other_side):
    side = (lax.axis_index("chip") >> order[step]) % 2
    left = sorted(set(order) - set(order[:step]), reverse=True)
    picked = pick(part, 1 - side if other_side else side, 1 + left.index(order[step]))
    return halves(picked, picked.ndim - 2)[number] if step == 0 else picked


def gather(array, axes):
    return lax.all_gather(array, axes, axis=0, tiled=True)


def scatter_sum(array, axes):
    return lax.psum_scatter(array, axes, scatter_dimension=0, tiled=True)


def dot(left, right):
    return jnp.dot(left, right, preferred_element_type=jnp.float32)


def head_mask(width, head):
    lane = lax.broadcasted_iota(jnp.int32, (1, width), 1)
    return ((lane >= head * HEAD) & (lane < (head + 1) * HEAD)).astype(jnp.float32).astype(jnp.bfloat16)


def allowed_keys(low, high, key_first, shape):
    key = key_first + lax.broadcasted_iota(jnp.int32, shape, 0)
    return (key >= low) & (key <= high)


def attend_kernel(heads, key_size, first_ref, last_ref, low_ref, high_ref, q_ref, k_ref, v_ref, out_ref, log_ref, turned, acc):
    block = pl.program_id(1)
    rows, width = q_ref.shape
    key_blocks = k_ref.shape[0] // key_size

    @pl.when(block == 0)
    def _():
        for j in range(key_blocks):
            turned[j] = v_ref[j * key_size : (j + 1) * key_size, :].T

    q_rows = q_ref[...] * jnp.bfloat16(0.125)
    q_heads = [q_rows * head_mask(width, h) for h in range(heads)]
    low, high = low_ref[0], high_ref[0]
    acc[...] = jnp.zeros_like(acc)
    last = last_ref[block]

    def step(t, state):
        j = last - t
        key_first = pl.multiple_of(j * key_size, key_size)
        k_rows = k_ref[pl.ds(key_first, key_size), :]
        allowed = allowed_keys(low, high, key_first, (key_size, rows))
        fresh = []
        for h in range(heads):
            top, total = state[h]
            scores = jnp.where(allowed, times_transposed(k_rows, q_heads[h]), NEGATIVE)
            new_top = jnp.maximum(top, jnp.max(scores, axis=0, keepdims=True))
            probs = jnp.exp(scores - new_top)
            shrink = jnp.exp(top - new_top)
            part = slice(h * HEAD, (h + 1) * HEAD)
            acc[part, :] = acc[part, :] * shrink + dot(turned[j, part, :], probs.astype(jnp.bfloat16))
            fresh.append((new_top, total * shrink + jnp.sum(probs, axis=0, keepdims=True)))
        return tuple(fresh)

    begin = (jnp.full((1, rows), NEGATIVE, jnp.float32), jnp.zeros((1, rows), jnp.float32))
    state = lax.fori_loop(0, last - first_ref[block] + 1, step, (begin,) * heads)
    for h in range(heads):
        top, total = state[h]
        part = slice(h * HEAD, (h + 1) * HEAD)
        acc[part, :] = acc[part, :] / total
        log_ref[0, 0, h : h + 1, :] = top + jnp.log(total)
    out_ref[...] = acc[...].T.astype(jnp.bfloat16)


def attend_back_kernel(heads, query_size, key_size, first_ref, last_ref, low_ref, high_ref, q_ref, k_ref, v_ref, out_ref, grad_ref, log_ref, dq_ref, dk_ref, dv_ref, q_heads, grad_heads, turned, delta, dq_acc, dk_acc, dv_acc):
    block = pl.program_id(1)
    width = q_ref.shape[1]
    query_blocks = q_ref.shape[0] // query_size

    @pl.when(block == 0)
    def _():
        for i in range(query_blocks):
            rows = slice(i * query_size, (i + 1) * query_size)
            product = grad_ref[rows, :].astype(jnp.float32) * out_ref[rows, :].astype(jnp.float32)
            product = product.T
            for h in range(heads):
                mask = head_mask(width, h)
                q_heads[i, h] = q_ref[rows, :] * (mask * jnp.bfloat16(0.125))
                grad_heads[i, h] = grad_ref[rows, :] * mask
                delta[i, h : h + 1, :] = jnp.sum(
                    product[h * HEAD : (h + 1) * HEAD, :], axis=0, keepdims=True
                )
        dq_acc[...] = jnp.zeros_like(dq_acc)

    key_first = pl.multiple_of(block * key_size, key_size)
    k_rows = k_ref[pl.ds(key_first, key_size), :]
    v_rows = v_ref[pl.ds(key_first, key_size), :]
    turned[...] = k_rows.T
    dk_acc[...] = jnp.zeros_like(dk_acc)
    dv_acc[...] = jnp.zeros_like(dv_acc)

    def step(i, carry):
        allowed = allowed_keys(low_ref[i], high_ref[i], key_first, (key_size, query_size))
        for h in range(heads):
            q_rows = q_heads[i, h]
            grad_rows = grad_heads[i, h]
            scores = times_transposed(k_rows, q_rows)
            probs = jnp.where(allowed, jnp.exp(scores - log_ref[0, i, h : h + 1, :]), 0.0)
            prob_grad = times_transposed(v_rows, grad_rows)
            score_grad = (probs * (prob_grad - delta[i, h : h + 1, :])).astype(jnp.bfloat16)
            dv_acc[...] += dot(probs.astype(jnp.bfloat16), grad_rows)
            dk_acc[...] += dot(score_grad, q_rows)
            part = slice(h * HEAD, (h + 1) * HEAD)
            dq_acc[i, part, :] += dot(turned[part, :], score_grad)
        return carry

    lax.fori_loop(first_ref[block], last_ref[block] + 1, step, 0)
    dk_ref[pl.ds(key_first, key_size), :] = dk_acc[...].astype(jnp.bfloat16)
    dv_ref[pl.ds(key_first, key_size), :] = dv_acc[...].astype(jnp.bfloat16)

    @pl.when(block == pl.num_programs(1) - 1)
    def _():
        for i in range(query_blocks):
            dq_ref[i * query_size : (i + 1) * query_size, :] = (
                (dq_acc[i] * 0.125).T.astype(jnp.bfloat16)
            )


def packed_back_kernel(heads, query_size, key_size, groups, *refs):
    first_ref, last_ref, group_ref, low_ref, high_ref, qkv_ref, out_ref = refs[:7]
    parts = refs[7 : 7 + groups]
    log_ref, dqkv_ref = refs[7 + groups : 9 + groups]
    grad_ref = refs[-1]
    width = out_ref.shape[1]
    size = parts[0].shape[0]

    @pl.when(pl.program_id(1) == 0)
    def _():
        for k in range(groups):
            owner = lax.rem(group_ref[0] + k, groups)
            grad_ref[pl.ds(pl.multiple_of(owner * size, size), size), :] = parts[k][...]

    views = [[r.at[:, c * width : (c + 1) * width] for c in range(3)] for r in (qkv_ref, dqkv_ref)]
    attend_back_kernel(
        heads,
        query_size,
        key_size,
        first_ref,
        last_ref,
        low_ref,
        high_ref,
        *views[0],
        out_ref,
        grad_ref,
        log_ref,
        *views[1],
        *refs[9 + groups : -1],
    )


def ffn_kernel(tile, carried, *refs):
    n_own_ref, n_far_ref, g_own_ref, g_far_ref = refs[:4]
    step = pl.program_id(0)
    if carried:
        weights_ref, out_in_ref, back_in_ref = refs[4:7]
    else:
        weights_ref = refs[-1]
        for i, source in enumerate(refs[4:6]):

            @pl.when(step == i)
            def _(source=source):
                weights_ref[:, 0] = source[...]

    results = refs[7:12] if carried else refs[6:9]
    z_rows, du_rows, out_acc, back_acc, n_ref, n_turned, g_ref, g_turned = (
        refs[12:20] if carried else refs[9:17]
    )
    grads_ref = results[0]
    rows, width = n_ref.shape
    chips, piece = weights_ref.shape[0], weights_ref.shape[3]
    units = chips * piece
    share = width // chips
    w_in = weights_ref[:, 0, 0].reshape(units, width)
    w_out = weights_ref[:, 0, 1].reshape(units, width)

    @pl.when(step == 0)
    def _():
        half = rows // 2
        for joined, turned, parts in (
            (n_ref, n_turned, (n_own_ref, n_far_ref)),
            (g_ref, g_turned, (g_own_ref, g_far_ref)),
        ):
            for i, source in enumerate(parts):
                joined[i * half : (i + 1) * half, :] = source[...]
                turned[:, i * half : (i + 1) * half] = source[...].T
        if carried:
            out_acc[...] = out_in_ref[...].astype(jnp.float32)
            back_acc[...] = back_in_ref[...].astype(jnp.float32)
        else:
            out_acc[...] = jnp.zeros_like(out_acc)
            back_acc[...] = jnp.zeros_like(back_acc)

    def row_tile(i, carry):
        part = pl.ds(pl.multiple_of(i * tile, tile), tile)
        pre = times_transposed(n_ref[part, :], w_in)
        scaled = lax.erf(pre * 0.7071067811865476)
        density = jnp.exp(pre * pre * -0.5) * 0.3989422804014327
        below = 0.5 + 0.5 * scaled
        hidden = (pre * below).astype(jnp.bfloat16)
        z_rows[part, :] = hidden
        out_acc[part, :] += dot(hidden, w_out)
        hidden_grad = times_transposed(g_ref[part, :], w_out)
        pre_grad = (hidden_grad * (below + pre * density)).astype(jnp.bfloat16)
        du_rows[part, :] = pre_grad
        back_acc[part, :] += dot(pre_grad, w_in)
        return carry

    lax.fori_loop(0, rows // tile, row_tile, 0, unroll=True)
    for c in range(chips):
        part = slice(c * share, (c + 1) * share)
        grads_ref[c, 0, :, :units] = dot(n_turned[part, :], du_rows[...]).astype(jnp.bfloat16)
        grads_ref[c, 0, :, units:] = dot(g_turned[part, :], z_rows[...]).astype(jnp.bfloat16)

    @pl.when(step == pl.num_programs(0) - 1)
    def _():
        own = rows // 2
        if carried:
            out_ref, out_far_ref, back_ref, back_far_ref = results[1:]
            out_ref[...] = out_acc[:own, :]
            out_far_ref[...] = out_acc[own:, :].astype(jnp.bfloat16)
            back_ref[...] = back_acc[:own, :]
            back_far_ref[...] = back_acc[own:, :].astype(jnp.bfloat16)
        else:
            results[1][...] = out_acc[...].astype(jnp.bfloat16)
            results[2][...] = back_acc[...].astype(jnp.bfloat16)


def ffn_call(n_own, n_far, g_own, g_far, weights, sums):
    rows, width = 2 * n_own.shape[0], n_own.shape[1]
    groups = len(weights) if not sums else weights[0].shape[1]
    chips, piece = weights[0].shape[0], weights[0].shape[-2]
    units = chips * piece
    whole = lambda shape: pl.BlockSpec(shape, lambda t: (0,) * len(shape))
    own = (rows // 2, width)
    grads = (chips, 1, width // chips, 2 * units)
    block = (chips, 1, 2, piece, width)
    f32, bf16 = jnp.float32, jnp.bfloat16
    scratch = [
        pltpu.VMEM((rows, units), bf16),
        pltpu.VMEM((rows, units), bf16),
        pltpu.VMEM((rows, width), f32),
        pltpu.VMEM((rows, width), f32),
        pltpu.VMEM((rows, width), bf16),
        pltpu.VMEM((width, rows), bf16),
        pltpu.VMEM((rows, width), bf16),
        pltpu.VMEM((width, rows), bf16),
    ]
    if sums:
        results = [(own, f32), (own, bf16), (own, f32), (own, bf16)]
        weight_specs = [pl.BlockSpec(block, lambda t: (0, t, 0, 0, 0))]
    else:
        results = [((rows, width), bf16)] * 2
        weight_specs = [whole(one.shape) for one in weights]
        scratch.append(pltpu.VMEM(block, bf16))
    return pl.pallas_call(
        partial(ffn_kernel, min(512, rows), bool(sums)),
        grid=(groups,),
        in_specs=[whole(own)] * 4 + weight_specs + [whole((rows, width))] * len(sums),
        out_specs=[pl.BlockSpec(grads, lambda t: (0, t, 0, 0))]
        + [whole(shape) for shape, _ in results],
        out_shape=[jax.ShapeDtypeStruct((chips, groups, *grads[2:]), bf16)]
        + [jax.ShapeDtypeStruct(*one) for one in results],
        scratch_shapes=scratch,
        compiler_params=pltpu.CompilerParams(vmem_limit_bytes=VMEM_BYTES),
        cost_estimate=about(23),
    )(n_own, n_far, g_own, g_far, *weights, *sums)


def ffn_pack_kernel(core_ref, in_ref, out_ref, packed_ref):
    chips, _, piece, _ = packed_ref.shape
    half = chips * piece
    first = pl.multiple_of(core_ref[0] * half, half)
    turned = in_ref[:, pl.ds(first, half)].T
    for c in range(chips):
        packed_ref[c, 0] = turned[c * piece : (c + 1) * piece, :]
        packed_ref[c, 1] = out_ref[pl.ds(first + c * piece, piece), :]


def ffn_pack_call(core, ffn_in, ffn_out, chips):
    units, width = ffn_out.shape
    return pl.pallas_call(
        ffn_pack_kernel,
        in_specs=[pl.BlockSpec(memory_space=pltpu.SMEM)] + [local_spec()] * 2,
        out_specs=local_spec(),
        out_shape=jax.ShapeDtypeStruct((chips, 2, units // 2 // chips, width), jnp.bfloat16),
        compiler_params=pltpu.CompilerParams(vmem_limit_bytes=VMEM_BYTES),
        cost_estimate=about(5),
    )(core, ffn_in, ffn_out)


def unit_norm(values):
    center = values - jnp.mean(values, axis=1, keepdims=True)
    inverse = lax.rsqrt(jnp.mean(center * center, axis=1, keepdims=True) + EPSILON)
    return center * inverse, inverse


def unit_back(gradient, values, gain):
    unit, inverse = unit_norm(values)
    scaled = gradient * gain
    inner = (
        scaled
        - jnp.mean(scaled, axis=1, keepdims=True)
        - unit * jnp.mean(scaled * unit, axis=1, keepdims=True)
    )
    return (
        inner * inverse,
        jnp.sum(gradient * unit, axis=0, keepdims=True),
        jnp.sum(gradient, axis=0, keepdims=True),
    )


def first_kernel(
    heads, frames_ref, gain_ref, bias_ref, weight_ref, normed_ref, packed_ref, ordered_ref
):
    @pl.when(pl.program_id(0) == 0)
    def _():
        columns = [
            weight_ref[:, (3 * h + c) * HEAD : (3 * h + c + 1) * HEAD]
            for c in range(3)
            for h in range(heads)
        ]
        ordered_ref[...] = jnp.concatenate(columns, 1)

    unit, _ = unit_norm(frames_ref[...].astype(jnp.float32))
    normed = (unit * gain_ref[0:1, :] + bias_ref[0:1, :]).astype(jnp.bfloat16)
    normed_ref[...] = normed
    packed_ref[...] = dot(normed, ordered_ref[...]).astype(jnp.bfloat16)


def first_call(heads, frames, gain, bias, weight, tile):
    rows, width = frames.shape
    columns = weight.shape[1]
    moving = lambda size: pl.BlockSpec((tile, size), lambda i: (i, 0))
    fixed = lambda shape: pl.BlockSpec(shape, lambda i: (0, 0))
    return pl.pallas_call(
        partial(first_kernel, heads),
        grid=(rows // tile,),
        in_specs=[moving(width), fixed(gain.shape), fixed(bias.shape), fixed(weight.shape)],
        out_specs=[moving(width), moving(columns), fixed(weight.shape)],
        out_shape=[
            jax.ShapeDtypeStruct((rows, width), jnp.bfloat16),
            jax.ShapeDtypeStruct((rows, columns), jnp.bfloat16),
            jax.ShapeDtypeStruct(weight.shape, jnp.bfloat16),
        ],
        compiler_params=pltpu.CompilerParams(vmem_limit_bytes=VMEM_BYTES),
        cost_estimate=about(9),
    )(frames, gain, bias, weight)


def pack_kernel(heads, self_ref, query_ref, cross_ref, pair_ref, out_ref):
    width = heads * HEAD
    text_width = pair_ref.shape[0]
    out_ref[0:width, :] = self_ref[...]
    out_ref[width : 2 * width, :] = query_ref[...].T
    out_ref[2 * width : 3 * width, :] = cross_ref[...]
    turned = pair_ref[...].T
    for h in range(heads):
        for c in range(2):
            rows = slice((3 + c) * width + h * HEAD, (3 + c) * width + (h + 1) * HEAD)
            out_ref[rows, :text_width] = turned[(2 * h + c) * HEAD : (2 * h + c + 1) * HEAD, :]
    out_ref[3 * width :, text_width:] = jnp.zeros(
        (2 * width, out_ref.shape[1] - text_width), jnp.bfloat16
    )


def pack_call(heads, self_out, cross_query, cross_out, cross_kv):
    return pl.pallas_call(
        partial(pack_kernel, heads),
        in_specs=[local_spec()] * 4,
        out_specs=local_spec(),
        out_shape=jax.ShapeDtypeStruct((5 * heads * HEAD, self_out.shape[1]), jnp.bfloat16),
        compiler_params=pltpu.CompilerParams(vmem_limit_bytes=VMEM_BYTES),
        cost_estimate=about(3),
    )(self_out, cross_query, cross_out, cross_kv)


def weight_copies(core_ref, local_ref, mine_ref, far_ref, weights, sems):
    half = mine_ref.shape[1]
    core = core_ref[0]
    copies = [pltpu.make_async_copy(local_ref, weights.at[0], sems.at[0])]
    for k in range(1, weights.shape[0]):
        for n, (source, side) in enumerate(((mine_ref, core), (far_ref, 1 - core))):
            rows = pl.ds(pl.multiple_of(side * half, half), half)
            copies.append(
                pltpu.make_async_copy(
                    source.at[k - 1], weights.at[k, rows], sems.at[2 * k - 1 + n]
                )
            )
    return copies


def middle_kernel(
    heads,
    tile,
    core_ref,
    low_ref,
    high_ref,
    inputs_ref,
    text_ref,
    gain_ref,
    bias_ref,
    local_ref,
    mine_ref,
    far_ref,
    *rest,
):
    groups = len(rest) - 9 - 4
    mixes = rest[:groups]
    h1_ref, h2_ref, n2_ref, n3_ref, cq_ref, mix_ref, ck_ref, cv_ref, log_ref = rest[
        groups : groups + 9
    ]
    weights, turned, mix_turned, sems = rest[groups + 9 :]
    width = heads * HEAD
    text_width = text_ref.shape[1]
    keys = text_ref.shape[0]
    copies = weight_copies(core_ref, local_ref, mine_ref, far_ref, weights, sems)
    for copy in copies:
        copy.start()
    text = text_ref[...]
    for k in range(groups):
        for copy in copies[max(0, 2 * k - 1) : 2 * k + 1]:
            copy.wait()
        part = slice(k * width, (k + 1) * width)
        key_weight = weights[k, 3 * width : 4 * width, :text_width]
        value_weight = weights[k, 4 * width : 5 * width, :text_width]
        ck_ref[:, part] = times_transposed(text, key_weight).astype(jnp.bfloat16)
        cv_ref[:, part] = times_transposed(text, value_weight).astype(jnp.bfloat16)
        turned[k] = times_transposed(value_weight, text).astype(jnp.bfloat16)

    def row_tile(i, carry):
        rows = pl.ds(pl.multiple_of(i * tile, tile), tile)
        total = inputs_ref[rows, :].astype(jnp.float32)
        for k in range(groups):
            total += dot(mixes[k][rows, :], weights[k, 0:width, :])
        h1_ref[rows, :] = total
        unit, _ = unit_norm(total)
        normed = (unit * gain_ref[1:2, :] + bias_ref[1:2, :]).astype(jnp.bfloat16)
        n2_ref[rows, :] = normed
        allowed = allowed_keys(low_ref[i], high_ref[i], 0, (keys, tile))
        for k in range(groups):
            part = slice(k * width, (k + 1) * width)
            queries = times_transposed(normed, weights[k, width : 2 * width, :])
            queries = queries.astype(jnp.bfloat16)
            cq_ref[rows, part] = queries
            queries = queries * jnp.bfloat16(0.125)
            for h in range(heads):
                scores = times_transposed(ck_ref[:, part], queries * head_mask(width, h))
                scores = jnp.where(allowed, scores, NEGATIVE)
                top = jnp.max(scores, axis=0, keepdims=True)
                probs = jnp.exp(scores - top)
                sums = jnp.sum(probs, axis=0, keepdims=True)
                lane = slice(h * HEAD, (h + 1) * HEAD)
                mix_turned[lane, :] = dot(turned[k, lane, :], probs.astype(jnp.bfloat16)) / sums
                log_ref[i, k * heads + h : k * heads + h + 1, :] = top + jnp.log(sums)
            mix_ref[rows, part] = mix_turned[...].T.astype(jnp.bfloat16)
        total = h1_ref[rows, :]
        for k in range(groups):
            part = slice(k * width, (k + 1) * width)
            total += dot(mix_ref[rows, part], weights[k, 2 * width : 3 * width, :])
        h2_ref[rows, :] = total
        unit, _ = unit_norm(total)
        n3_ref[rows, :] = (unit * gain_ref[2:3, :] + bias_ref[2:3, :]).astype(jnp.bfloat16)
        return carry

    lax.fori_loop(0, inputs_ref.shape[0] // tile, row_tile, 0)


def middle_back_kernel(
    heads,
    tile,
    core_ref,
    low_ref,
    high_ref,
    text_ref,
    gain_ref,
    third_ref,
    third_far_ref,
    grad_ref,
    h1_ref,
    h2_ref,
    cq_ref,
    mix_ref,
    ck_ref,
    cv_ref,
    log_ref,
    local_ref,
    mine_ref,
    far_ref,
    cross_side_ref,
    dcq_ref,
    dck_ref,
    dcv_ref,
    self_exact_ref,
    self_side_ref,
    norm_ref,
    text_part_ref,
    *rest,
):
    mix_grads = rest[:-6]
    weights, turned, query_turned, dk_acc, dv_acc, sems = rest[-6:]
    groups = weights.shape[0]
    width = heads * HEAD
    text_width = text_ref.shape[1]
    keys = text_ref.shape[0]
    copies = weight_copies(core_ref, local_ref, mine_ref, far_ref, weights, sems)
    for copy in copies:
        copy.start()
    text = text_ref[...]
    for k in range(groups):
        for copy in copies[max(0, 2 * k - 1) : 2 * k + 1]:
            copy.wait()
        key_weight = weights[k, 3 * width : 4 * width, :text_width]
        turned[k] = times_transposed(key_weight, text).astype(jnp.bfloat16)
    dk_acc[...] = jnp.zeros_like(dk_acc)
    dv_acc[...] = jnp.zeros_like(dv_acc)
    norm_ref[...] = jnp.zeros_like(norm_ref)

    def row_tile(i, carry):
        rows = pl.ds(pl.multiple_of(i * tile, tile), tile)
        third = third_ref[rows, :] + third_far_ref[rows, :].astype(jnp.float32)
        back, gain_sum, bias_sum = unit_back(third, h2_ref[rows, :], gain_ref[2:3, :])
        norm_ref[2:3, :] += gain_sum
        norm_ref[5:6, :] += bias_sum
        cross_exact = grad_ref[rows, :].astype(jnp.float32) + back
        cross_side = cross_exact.astype(jnp.bfloat16)
        self_exact_ref[rows, :] = cross_exact
        cross_side_ref[rows, :] = cross_side
        allowed = allowed_keys(low_ref[i], high_ref[i], 0, (keys, tile))
        for k in range(groups):
            part = slice(k * width, (k + 1) * width)
            mix_grad = times_transposed(cross_side, weights[k, 2 * width : 3 * width, :])
            mix_grad = mix_grad.astype(jnp.bfloat16)
            product = mix_grad.astype(jnp.float32) * mix_ref[rows, part].astype(jnp.float32)
            product = product.T
            queries = cq_ref[rows, part] * jnp.bfloat16(0.125)
            for h in range(heads):
                mask = head_mask(width, h)
                lane = slice(h * HEAD, (h + 1) * HEAD)
                one = k * heads + h
                q_rows = queries * mask
                grad_rows = mix_grad * mask
                scores = times_transposed(ck_ref[:, part], q_rows)
                probs = jnp.exp(scores - log_ref[i, one : one + 1, :])
                probs = jnp.where(allowed, probs, 0.0)
                prob_grad = times_transposed(cv_ref[:, part], grad_rows)
                delta = jnp.sum(product[lane, :], axis=0, keepdims=True)
                score_grad = (probs * (prob_grad - delta)).astype(jnp.bfloat16)
                dv_acc[:, part] += dot(probs.astype(jnp.bfloat16), grad_rows)
                dk_acc[:, part] += dot(score_grad, q_rows)
                query_turned[lane, :] = dot(turned[k, lane, :], score_grad)
            dcq_ref[rows, part] = (query_turned[...] * 0.125).T.astype(jnp.bfloat16)
        second = jnp.zeros(cross_exact.shape, jnp.float32)
        for k in range(groups):
            part = slice(k * width, (k + 1) * width)
            second += dot(dcq_ref[rows, part], weights[k, width : 2 * width, :])
        back, gain_sum, bias_sum = unit_back(second, h1_ref[rows, :], gain_ref[1:2, :])
        norm_ref[1:2, :] += gain_sum
        norm_ref[4:5, :] += bias_sum
        self_exact = self_exact_ref[rows, :] + back
        self_exact_ref[rows, :] = self_exact
        self_side = self_exact.astype(jnp.bfloat16)
        self_side_ref[rows, :] = self_side
        for k in range(groups):
            mix_grads[k][rows, :] = times_transposed(self_side, weights[k, 0:width, :]).astype(
                jnp.bfloat16
            )
        return carry

    lax.fori_loop(0, third_ref.shape[0] // tile, row_tile, 0)
    dck_ref[...] = dk_acc[...].astype(jnp.bfloat16)
    dcv_ref[...] = dv_acc[...].astype(jnp.bfloat16)
    text_part = jnp.zeros(text_ref.shape, jnp.float32)
    for k in range(groups):
        part = slice(k * width, (k + 1) * width)
        text_part += dot(dck_ref[:, part], weights[k, 3 * width : 4 * width, :text_width])
        text_part += dot(dcv_ref[:, part], weights[k, 4 * width : 5 * width, :text_width])
    size = text_width // groups
    for k in range(groups):
        text_part_ref[k] = text_part[:, k * size : (k + 1) * size].astype(jnp.bfloat16)


def weight_grads_kernel(heads, added, side_ref, *refs):
    target = refs[-1]
    if added:
        far_ref, refs = refs[0], refs[1:]
    self_ref, n2_ref, cq_ref, mix_ref, cross_ref, dck_ref, dcv_ref, text_ref = refs[:8]
    mixes = refs[8:-1]
    width = heads * HEAD
    half = target.shape[1]
    text_width = text_ref.shape[1]
    for side in range(2):

        @pl.when(side_ref[0] == side)
        def _(side=side):
            for k in range(target.shape[0]):
                first = k * width
                pairs = [
                    (mixes[k], 0, self_ref),
                    (cq_ref, first, n2_ref),
                    (mix_ref, first, cross_ref),
                    (dck_ref, first, text_ref),
                    (dcv_ref, first, text_ref),
                ]
                for n, (left, lane, right) in enumerate(pairs):
                    low = max(n * width, side * half)
                    high = min((n + 1) * width, (side + 1) * half)
                    if low >= high:
                        continue
                    columns = left[:, lane + low - n * width : lane + high - n * width]
                    product = contract_rows(columns, right[...])
                    rows = slice(low - side * half, high - side * half)
                    if added:
                        product += far_ref[k, rows, : product.shape[1]].astype(jnp.float32)
                    product = product.astype(jnp.bfloat16)
                    target[k, rows, : product.shape[1]] = product
                    if product.shape[1] < target.shape[2]:
                        target[k, rows, text_width:] = jnp.zeros(
                            (high - low, target.shape[2] - text_width), jnp.bfloat16
                        )


def weight_grads_call(heads, side, arrays, mixes, far=()):
    groups, width = len(mixes), arrays[0].shape[1]
    half = 5 * heads * HEAD // 2
    return pl.pallas_call(
        partial(weight_grads_kernel, heads, bool(far)),
        in_specs=[pl.BlockSpec(memory_space=pltpu.SMEM)]
        + [local_spec()] * (len(far) + len(arrays) + groups),
        out_specs=local_spec(),
        out_shape=jax.ShapeDtypeStruct((groups, half, width), jnp.bfloat16),
        compiler_params=pltpu.CompilerParams(vmem_limit_bytes=VMEM_BYTES),
        cost_estimate=about(10),
    )(side, *far, *arrays, *mixes)


def last_kernel(frames_ref, gain_ref, exact_ref, sum_ref, term_ref, out_ref, norm_ref):
    gradient = sum_ref[...].astype(jnp.float32) + term_ref[...]
    back, gain_sum, bias_sum = unit_back(
        gradient, frames_ref[...].astype(jnp.float32), gain_ref[0:1, :]
    )
    out_ref[...] = (exact_ref[...] + back).astype(jnp.bfloat16)
    norm_ref[0:1, :] = gain_sum
    norm_ref[1:2, :] = bias_sum


def last_call(frames, gains, exact, sums, term):
    rows, width = frames.shape
    return pl.pallas_call(
        last_kernel,
        in_specs=[local_spec()] * 5,
        out_specs=[local_spec()] * 2,
        out_shape=[
            jax.ShapeDtypeStruct((rows, width), jnp.bfloat16),
            jax.ShapeDtypeStruct((2, width), jnp.float32),
        ],
        compiler_params=pltpu.CompilerParams(vmem_limit_bytes=VMEM_BYTES),
        cost_estimate=about(4),
    )(frames, gains, exact, sums, term)


def ffn_end_kernel(core_ref, mine_ref, far_ref, in_ref, out_ref):
    units = in_ref.shape[1] // 2
    for source, side in ((mine_ref, core_ref[0]), (far_ref, 1 - core_ref[0])):
        part = pl.ds(pl.multiple_of(side * units, units), units)
        in_ref[:, part] = source[0, :, :units].astype(jnp.float32)
        out_ref[part, :] = source[0, :, units:].astype(jnp.float32).T


def ffn_end_call(core, mine, far):
    chips, features, columns = mine.shape
    source = pl.BlockSpec((1, features, columns), lambda c: (c, 0, 0))
    return pl.pallas_call(
        ffn_end_kernel,
        grid=(chips,),
        in_specs=[pl.BlockSpec(memory_space=pltpu.SMEM), source, source],
        out_specs=[
            pl.BlockSpec((features, columns), lambda c: (c, 0)),
            pl.BlockSpec((columns, features), lambda c: (0, c)),
        ],
        out_shape=[
            jax.ShapeDtypeStruct((chips * features, columns), jnp.float32),
            jax.ShapeDtypeStruct((columns, chips * features), jnp.float32),
        ],
        compiler_params=pltpu.CompilerParams(vmem_limit_bytes=VMEM_BYTES),
        cost_estimate=about(5),
    )(core, mine, far)


def qkv_grad_kernel(left_ref, right_ref, out_ref):
    out_ref[...] = contract_rows(left_ref[...], right_ref[...]).astype(jnp.bfloat16)


def qkv_grad_call(normed, packed_grad):
    rows, width = normed.shape
    columns = packed_grad.shape[1]
    tile = min(256, width)
    return pl.pallas_call(
        qkv_grad_kernel,
        grid=(width // tile,),
        in_specs=[
            pl.BlockSpec((rows, tile), lambda i: (0, i)),
            pl.BlockSpec((rows, columns), lambda i: (0, 0)),
        ],
        out_specs=pl.BlockSpec((tile, columns), lambda i: (i, 0)),
        out_shape=jax.ShapeDtypeStruct((width, columns), jnp.bfloat16),
        compiler_params=pltpu.CompilerParams(vmem_limit_bytes=VMEM_BYTES),
        cost_estimate=about(5),
    )(normed, packed_grad)


def qkv_end_kernel(heads, core_ref, mine_ref, far_ref, out_ref):
    width = heads * HEAD
    size = mine_ref.shape[0]
    for source, side in ((mine_ref, core_ref[0]), (far_ref, 1 - core_ref[0])):
        columns = [
            source[:, c * width + h * HEAD : c * width + (h + 1) * HEAD]
            for h in range(heads)
            for c in range(3)
        ]
        rows = pl.ds(pl.multiple_of(side * size, size), size)
        out_ref[rows, :] = jnp.concatenate(columns, 1).astype(jnp.float32)


def qkv_end_call(heads, core, mine, far):
    rows, columns = mine.shape
    return pl.pallas_call(
        partial(qkv_end_kernel, heads),
        in_specs=[pl.BlockSpec(memory_space=pltpu.SMEM)] + [local_spec()] * 2,
        out_specs=local_spec(),
        out_shape=jax.ShapeDtypeStruct((2 * rows, columns), jnp.float32),
        compiler_params=pltpu.CompilerParams(vmem_limit_bytes=VMEM_BYTES),
        cost_estimate=about(3),
    )(core, mine, far)


def small_end_kernel(heads, core_ref, mine_ref, far_ref, *refs):
    self_ref, query_ref, cross_ref, pair_ref, joined = refs
    width = heads * HEAD
    text_width = pair_ref.shape[0]
    half = joined.shape[0] // 2
    for source, side in ((mine_ref, core_ref[0]), (far_ref, 1 - core_ref[0])):
        joined[pl.ds(pl.multiple_of(side * half, half), half), :] = source[...]
    self_ref[...] = joined[0:width, :].astype(jnp.float32)
    query_ref[...] = joined[width : 2 * width, :].astype(jnp.float32).T
    cross_ref[...] = joined[2 * width : 3 * width, :].astype(jnp.float32)
    for h in range(heads):
        rows = [slice((3 + c) * width + h * HEAD, (3 + c) * width + (h + 1) * HEAD) for c in (0, 1)]
        both = jnp.concatenate([joined[part, :text_width] for part in rows], 0)
        pair_ref[:, 2 * h * HEAD : 2 * (h + 1) * HEAD] = both.astype(jnp.float32).T


def small_end_call(heads, text_width, core, mine, far):
    width = mine.shape[1]
    head_width = heads * HEAD
    shapes = [
        (head_width, width),
        (width, head_width),
        (head_width, width),
        (text_width, 2 * head_width),
    ]
    return pl.pallas_call(
        partial(small_end_kernel, heads),
        in_specs=[pl.BlockSpec(memory_space=pltpu.SMEM)] + [local_spec()] * 2,
        out_specs=[local_spec()] * 4,
        out_shape=[jax.ShapeDtypeStruct(shape, jnp.float32) for shape in shapes],
        scratch_shapes=[pltpu.VMEM((5 * head_width, width), jnp.bfloat16)],
        compiler_params=pltpu.CompilerParams(vmem_limit_bytes=VMEM_BYTES),
        cost_estimate=about(4),
    )(core, mine, far)


def local_spec():
    return pl.BlockSpec(memory_space=pltpu.VMEM)


def middle_specs(plain):
    return (
        [pl.BlockSpec(memory_space=pltpu.SMEM)]
        + [local_spec()] * plain
        + [pl.BlockSpec(memory_space=pl.ANY)] * 3
    )


def middle_call(heads, tile, core, low, high, inputs, text, gains, biases, split_weights, mixes):
    rows, width = inputs.shape
    keys = text.shape[0]
    groups = len(mixes)
    f32, bf16 = jnp.float32, jnp.bfloat16
    shapes = [
        ((rows, width), f32),
        ((rows, width), f32),
        ((rows, width), bf16),
        ((rows, width), bf16),
        ((rows, width), bf16),
        ((rows, width), bf16),
        ((keys, width), bf16),
        ((keys, width), bf16),
        ((rows // tile, groups * heads, tile), f32),
    ]
    return pl.pallas_call(
        partial(middle_kernel, heads, tile),
        in_specs=middle_specs(6) + [local_spec()] * groups,
        out_specs=[local_spec()] * len(shapes),
        out_shape=[jax.ShapeDtypeStruct(*one) for one in shapes],
        scratch_shapes=[
            pltpu.VMEM((groups, *split_weights[0].shape), bf16),
            pltpu.VMEM((groups, heads * HEAD, keys), bf16),
            pltpu.VMEM((heads * HEAD, tile), f32),
            pltpu.SemaphoreType.DMA((2 * groups - 1,)),
        ],
        compiler_params=pltpu.CompilerParams(vmem_limit_bytes=VMEM_BYTES),
        cost_estimate=about(30),
    )(core, lanes(low, tile), lanes(high, tile), inputs, text, gains, biases, *split_weights, *mixes)


def middle_back_call(heads, tile, core, low, high, text, gains, saved, split_weights):
    rows, width = saved[0].shape
    keys = text.shape[0]
    groups = width // (heads * HEAD)
    f32, bf16 = jnp.float32, jnp.bfloat16
    shapes = [
        ((rows, width), bf16),
        ((rows, width), bf16),
        ((keys, width), bf16),
        ((keys, width), bf16),
        ((rows, width), f32),
        ((rows, width), bf16),
        ((6, width), f32),
        ((groups, keys, text.shape[1] // groups), bf16),
    ] + [((rows, heads * HEAD), bf16)] * groups
    return pl.pallas_call(
        partial(middle_back_kernel, heads, tile),
        in_specs=middle_specs(4 + len(saved)),
        out_specs=[local_spec()] * len(shapes),
        out_shape=[jax.ShapeDtypeStruct(*one) for one in shapes],
        scratch_shapes=[
            pltpu.VMEM((groups, *split_weights[0].shape), bf16),
            pltpu.VMEM((groups, heads * HEAD, keys), bf16),
            pltpu.VMEM((heads * HEAD, tile), f32),
            pltpu.VMEM((keys, width), f32),
            pltpu.VMEM((keys, width), f32),
            pltpu.SemaphoreType.DMA((2 * groups - 1,)),
        ],
        compiler_params=pltpu.CompilerParams(vmem_limit_bytes=VMEM_BYTES),
        cost_estimate=about(40),
    )(core, lanes(low, tile), lanes(high, tile), text, gains, *saved, *split_weights)


def lanes(values, size):
    return values.astype(jnp.int32).reshape(-1, 1, size)


def attend_call(q, k, v, columns, groups, heads, low, high, first, last, query_size, key_size):
    width = heads * HEAD
    rows, keys = q.shape[0], k.shape[0]
    blocks = rows // query_size
    spec = lambda size, column: pl.BlockSpec((size, width), lambda g, i, *_: (0, column + g))
    vector = pl.BlockSpec((1, 1, query_size), lambda g, i, *_: (i, 0, 0))
    q_column = columns[0]
    return pl.pallas_call(
        partial(attend_kernel, heads, key_size),
        grid_spec=pltpu.PrefetchScalarGridSpec(
            num_scalar_prefetch=2,
            grid=(groups, blocks),
            in_specs=[
                vector,
                vector,
                pl.BlockSpec((query_size, width), lambda g, i, *_: (i, q_column + g)),
                spec(keys, columns[1]),
                spec(keys, columns[2]),
            ],
            out_specs=[
                pl.BlockSpec((query_size, width), lambda g, i, *_: (i, g)),
                pl.BlockSpec((1, 1, heads, query_size), lambda g, i, *_: (g, i, 0, 0)),
            ],
            scratch_shapes=[
                pltpu.VMEM((keys // key_size, width, key_size), jnp.bfloat16),
                pltpu.VMEM((width, query_size), jnp.float32),
            ],
        ),
        out_shape=[
            jax.ShapeDtypeStruct((rows, groups * width), jnp.bfloat16),
            jax.ShapeDtypeStruct((groups, blocks, heads, query_size), jnp.float32),
        ],
        compiler_params=pltpu.CompilerParams(vmem_limit_bytes=VMEM_BYTES),
        cost_estimate=about(30 if groups == 1 else 17),
    )(first, last, lanes(low, query_size), lanes(high, query_size), q, k, v)


def back_scratch(heads, blocks, query_size, key_size):
    width = heads * HEAD
    return [
        pltpu.VMEM((blocks, heads, query_size, width), jnp.bfloat16),
        pltpu.VMEM((blocks, heads, query_size, width), jnp.bfloat16),
        pltpu.VMEM((width, key_size), jnp.bfloat16),
        pltpu.VMEM((blocks, heads, query_size), jnp.float32),
        pltpu.VMEM((blocks, width, query_size), jnp.float32),
        pltpu.VMEM((key_size, width), jnp.float32),
        pltpu.VMEM((key_size, width), jnp.float32),
    ]


def packed_back_call(
    qkv, out, parts, logs, heads, group, low, high, first, last, query_size, key_size
):
    rows, width = out.shape
    blocks = rows // query_size
    whole = lambda shape: pl.BlockSpec(shape, lambda g, j, *_: (0,) * len(shape))
    vector = whole((blocks, 1, query_size))
    return pl.pallas_call(
        partial(packed_back_kernel, heads, query_size, key_size, len(parts)),
        grid_spec=pltpu.PrefetchScalarGridSpec(
            num_scalar_prefetch=3,
            grid=(1, rows // key_size),
            in_specs=[vector, vector, whole(qkv.shape), whole(out.shape)]
            + [whole(part.shape) for part in parts]
            + [whole(logs.shape)],
            out_specs=whole(qkv.shape),
            scratch_shapes=back_scratch(heads, blocks, query_size, key_size)
            + [pltpu.VMEM(out.shape, jnp.bfloat16)],
        ),
        out_shape=jax.ShapeDtypeStruct(qkv.shape, jnp.bfloat16),
        compiler_params=pltpu.CompilerParams(vmem_limit_bytes=VMEM_BYTES),
        cost_estimate=about(30),
    )(
        first,
        last,
        group,
        lanes(low, query_size),
        lanes(high, query_size),
        qkv,
        out,
        *parts,
        logs,
    )


def attend_back_call(q, k, v, out, grad, logs, groups, heads, low, high, first, last, query_size, key_size):
    width = heads * HEAD
    rows, keys = q.shape[0], k.shape[0]
    blocks = rows // query_size
    column = lambda size: pl.BlockSpec((size, width), lambda g, j, *_: (0, g))
    vector = pl.BlockSpec((blocks, 1, query_size), lambda g, j, *_: (0, 0, 0))
    return pl.pallas_call(
        partial(attend_back_kernel, heads, query_size, key_size),
        grid_spec=pltpu.PrefetchScalarGridSpec(
            num_scalar_prefetch=2,
            grid=(groups, keys // key_size),
            in_specs=[
                vector,
                vector,
                column(rows),
                column(keys),
                column(keys),
                column(rows),
                column(rows),
                pl.BlockSpec((1, blocks, heads, query_size), lambda g, j, *_: (g, 0, 0, 0)),
            ],
            out_specs=[column(rows), column(keys), column(keys)],
            scratch_shapes=back_scratch(heads, blocks, query_size, key_size),
        ),
        out_shape=[
            jax.ShapeDtypeStruct((rows, groups * width), jnp.bfloat16),
            jax.ShapeDtypeStruct((keys, groups * width), jnp.bfloat16),
            jax.ShapeDtypeStruct((keys, groups * width), jnp.bfloat16),
        ],
        compiler_params=pltpu.CompilerParams(vmem_limit_bytes=VMEM_BYTES),
        cost_estimate=about(6 * groups),
    )(first, last, lanes(low, query_size), lanes(high, query_size), q, k, v, out, grad, logs)


def per_device(
    frames,
    text_states,
    clip_lengths,
    text_lengths,
    norm_gains,
    norm_biases,
    self_qkv,
    self_out,
    cross_query,
    cross_kv,
    cross_out,
    ffn_in,
    ffn_out,
    out_grad,
):
    groups = lax.axis_size("tensor")
    chips = lax.axis_size("chip")
    group = lax.axis_index("tensor")
    chip = lax.axis_index("chip")
    core = lax.axis_index("core")
    bf16 = jnp.bfloat16
    frame_count, width = frames.shape
    own_rows = frame_count // groups
    offset = group * own_rows
    clip_count, text_slots, text_width = text_states.shape
    head_count = self_out.shape[0] // HEAD
    all_heads = head_count * groups
    ends = jnp.cumsum(clip_lengths[0])
    starts = ends - clip_lengths[0]
    positions = jnp.arange(frame_count, dtype=jnp.int32)[:, None]
    clip_first = jnp.max(jnp.where(positions >= starts, starts, 0), axis=1)
    clip_stop = jnp.min(jnp.where(positions < ends, ends, frame_count), axis=1)
    block = min(256, own_rows)
    blocks = jnp.arange(frame_count // block, dtype=jnp.int32)
    self_low, self_high = clip_first, positions[:, 0]
    wide = min(2 * block, frame_count)
    wides = jnp.arange(frame_count // wide, dtype=jnp.int32)
    self_keys = (clip_first[::wide] // block, (wides * wide + wide - 1) // block)
    self_queries = (blocks * block // wide, (clip_stop[block - 1 :: block] - 1) // wide)
    own_positions = offset + jnp.arange(own_rows, dtype=jnp.int32)[:, None]
    own_clip = jnp.sum((own_positions >= ends).astype(jnp.int32), axis=1)
    own_length = jnp.sum(
        jnp.where(own_clip[:, None] == jnp.arange(clip_count), text_lengths[0], 0), axis=1
    )
    cross_low = own_clip * text_slots
    cross_high = cross_low + own_length - 1
    cross_keys = (own_clip[::block], own_clip[block - 1 :: block])
    inside_first = jnp.clip(starts - offset, 0, own_rows)
    inside_stop = jnp.clip(ends - offset, 0, own_rows)
    cross_first = jnp.minimum(inside_first // block, own_rows // block - 1)
    cross_queries = (
        cross_first,
        jnp.where(inside_stop > inside_first, (inside_stop - 1) // block, cross_first - 1),
    )

    head_width = head_count * HEAD
    local = pack_call(head_count, self_out, cross_query, cross_out, cross_kv)
    pieces = local.reshape(2, chips, -1, width)
    half = ffn_out.shape[0] // 2
    piece = half // chips
    core_index = core.reshape(1).astype(jnp.int32)
    sent_piece = pick(pick(pieces, core, 0), chip, 0)
    sent_piece, frames, self_qkv, ffn_in, ffn_out, out_grad = phase(
        sent_piece, frames, self_qkv, ffn_in, ffn_out, out_grad
    )
    passed = [shift(sent_piece, k) for k in range(1, groups)]
    ffn_own = ffn_pack_call(core_index, ffn_in, ffn_out, chips)
    ffn_piece = pick(ffn_own, chip, 0).reshape(2 * piece, width)
    own_frames = lax.dynamic_slice_in_dim(frames, offset, own_rows, 0)
    grad_own_bf = lax.dynamic_slice_in_dim(out_grad, offset, own_rows, 0)
    rows_one, packed, w_qkv = first_call(
        head_count, frames, norm_gains, norm_biases, self_qkv, block
    )
    packed, ffn_piece, own_frames, grad_own_bf, *passed = phase(
        packed, ffn_piece, own_frames, grad_own_bf, *passed
    )
    if head_width % 128 == 0:
        self_parts, self_columns = (packed,) * 3, (0, 1, 2)
    else:
        self_parts, self_columns = jnp.split(packed, 3, 1), (0, 0, 0)
    steps = axis_bits("chip")
    joined = chip_gather_start(jnp.stack(passed))
    flipped = chip_gather_flips(joined, 0)
    ffn_all = gather(ffn_piece[None], "tensor")
    self_mix, self_logs = attend_call(
        *self_parts, self_columns, 1, head_count, self_low, self_high, *self_keys, wide, block
    )
    joined = chip_gather_joins(joined, flipped, 0)
    self_mix, *joined = phase(self_mix, *joined)

    mix_blocks = self_mix.reshape(groups, own_rows, head_width)
    mixes = [pick(mix_blocks, group, 0)] + [
        shift(pick(mix_blocks, (group + k) % groups, 0), k) for k in range(1, groups)
    ]
    flipped = chip_gather_flips(joined, 1)
    joined = chip_gather_joins(joined, flipped, 1)
    for step in range(2, steps):
        joined = chip_gather_joins(joined, phase(*chip_gather_flips(joined, step)), step)
    mine = chip_gather_end(joined).reshape(groups - 1, -1, width)
    ffn_passed = [pick(ffn_all, (group + groups - k) % groups, 0) for k in range(1, groups)]
    ffn_stack = jnp.stack(ffn_passed[1:])[None]
    mine, ffn_stack, ffn_next, *mixes = phase(mine, ffn_stack, ffn_passed[0], *mixes)
    ffn_joined = chip_gather_start(ffn_next[None])
    ffn_late = gather(ffn_stack, "chip")
    ffn_late = ffn_late.reshape(chips, groups - 2, 2, piece, width)
    flipped = chip_gather_flips(ffn_joined, 0)
    ffn_joined = chip_gather_joins(ffn_joined, flipped, 0)
    far, *ffn_joined = phase(swap_core(mine), *ffn_joined)
    split_weights = (local, mine, far)
    ffn_flipped = chip_gather_flips(ffn_joined, 1)

    text_flat = text_states.reshape(clip_count * text_slots, text_width)
    shape = (head_count, block, core_index, cross_low, cross_high)
    after_self, after_cross, rows_two, rows_three, cross_q, cross_flat, cross_k, cross_v, cross_logs = (
        middle_call(
            *shape, own_frames, text_flat, norm_gains, norm_biases, split_weights, mixes
        )
    )

    grad_far = swap_core(grad_own_bf)
    rows_three, grad_far, *ffn_flipped = phase(rows_three, grad_far, *ffn_flipped)
    rows_far = swap_core(rows_three)
    ffn_joined = chip_gather_joins(ffn_joined, ffn_flipped, 1)
    for step in range(2, steps):
        ffn_joined = chip_gather_joins(ffn_joined, chip_gather_flips(ffn_joined, step), step)
    ffn_first = chip_gather_end(ffn_joined).reshape(chips, 2, piece, width)
    row_sets = (rows_three, rows_far, grad_own_bf, grad_far)
    ffn_part, *sums = ffn_call(*row_sets, (ffn_own, ffn_first), ())
    ffn_sum = scatter_sum(ffn_part.reshape(-1, 2 * half), "chip")
    ffn_late_part, out_own, out_far, third_own_grad, third_far = ffn_call(
        *row_sets, (ffn_late,), tuple(sums)
    )
    ffn_late_sum = scatter_sum(ffn_late_part.reshape(-1, 2 * half), "chip")
    saved = (
        third_own_grad,
        swap_core(third_far),
        grad_own_bf,
        after_self,
        after_cross,
        cross_q,
        cross_flat,
        cross_k,
        cross_v,
        cross_logs,
    )
    (
        cross_grad,
        cq_flat,
        ck_grad,
        cv_grad,
        self_side,
        self_grad,
        norm_part,
        text_part,
        *mix_grads,
    ) = middle_back_call(*shape, text_flat, norm_gains, saved, split_weights)

    mix_parts = [mix_grads[0]] + [shift(mix_grads[k], -k) for k in range(1, groups)]
    out_far = swap_core(out_far)
    arrays = (
        self_grad,
        rows_two,
        cq_flat,
        cross_flat,
        cross_grad,
        ck_grad,
        cv_grad,
        text_flat,
    )
    small_far = swap_core(weight_grads_call(head_count, 1 - core_index, arrays, mixes))
    small_part = weight_grads_call(head_count, core_index, arrays, mixes, (small_far,))

    def text_term(k):
        return pick(text_part, (group + groups - k) % groups, 0)

    orders = chip_orders()
    whole = chip_scatter_start(small_part.reshape(groups, chips, -1, width))
    state = settle(
        dict(
            whole=small_part,
            send=[chip_scatter_pick(whole[n], n, o, 0, True) for n, o in enumerate(orders)],
            text=text_term(1),
            out_far=out_far,
            ffn=list(ffn_sum.reshape(2, -1, 2 * half)),
            mix=mix_parts,
        )
    )
    mix_parts = state.pop("mix")
    text_run = shift(state["text"], 1)
    moved = [flip(one, o[0]) for one, o in zip(state["send"], orders)]
    ffn_run = shift(state["ffn"][1], 1)

    self_rest = (self_low, self_high, *self_queries, wide, block)
    if head_width % 128 == 0:
        packed_grad = packed_back_call(
            packed, self_mix, mix_parts, self_logs, head_count, group.reshape(1), *self_rest
        )
    else:
        mix_grad = jnp.concatenate([*mix_parts, *mix_parts], 0)
        mix_grad = lax.dynamic_slice_in_dim(
            mix_grad, (groups - group) % groups * own_rows, frame_count, 0
        )
        packed_grad = jnp.concatenate(
            attend_back_call(
                *self_parts, self_mix, mix_grad, self_logs, 1, head_count, *self_rest
            ),
            1,
        )
    state = settle(
        dict(
            state,
            grad=packed_grad,
            text=text_run,
            moved=moved,
            run=ffn_run,
            late=ffn_late_sum,
            h2=after_cross,
        )
    )

    def first_term(k):
        blocks = state["grad"].reshape(groups, own_rows, -1)
        rows = pick(blocks, (group + groups - k) % groups, 0)
        return times_transposed(rows, w_qkv)

    state = settle(dict(state, running=first_term(1).astype(bf16)))
    whole = chip_scatter_start(state["whole"].reshape(groups, chips, -1, width))
    small = [
        chip_scatter_pick(whole[n], n, o, 0, False) + one
        for n, (o, one) in enumerate(zip(orders, state["moved"]))
    ]
    late = list(state["late"].reshape(groups - 2, -1, 2 * half))
    state["run"] = state["run"] + late[0]
    ring_next = 1
    ffn_step = 0
    text_next = 2
    state["text"] = state["text"] + text_term(2)
    for hop in range(1, groups):
        arrived = shift(state["running"], 1)
        after_hop = dict(grad=state["grad"])
        if hop < steps:
            small = [
                chip_scatter_pick(one, n, o, hop, False)
                + flip(chip_scatter_pick(one, n, o, hop, True), o[hop])
                for n, (o, one) in enumerate(zip(orders, small))
            ]
            if hop == steps - 1:
                small = jnp.concatenate(small, 1)
        elif ring_next < groups:
            running_small = shift(small[1] if ring_next == 1 else state["ring"], 1)
            ring_next += 1
            after_hop["ring"] = running_small + small[ring_next % groups]
        after_hop["small"] = small
        after_hop["text"] = state["text"]
        if 1 < hop < groups - 1:
            text_next += 1
            after_hop["text"] = shift(state["text"], 1) + text_term(text_next % groups)
        if hop < groups - 1:
            after_hop["own"] = state["own"] if hop > 1 else state["ffn"][0]
            run = shift(state["run"], 1)
            after_hop["run"] = run + (late[hop] if hop < groups - 2 else after_hop["own"])
            late = after_hop["late"] = state["late"] if hop > 1 else late
        else:
            ffn = chip_gather_start(state["run"][None])
            after_hop["ffn"] = chip_gather_joins(ffn, chip_gather_flips(ffn, 0), 0)
            ffn_step = 1
        if hop == 1:
            mixed = state["h2"] + out_own + state["out_far"].astype(jnp.float32)
            after_hop["mixed"] = mixed.astype(bf16)
        else:
            after_hop["mixed"] = state["mixed"]
        if hop == 1:
            grad, run = phase(state["grad"], run)
            qkv_part = qkv_grad_call(rows_one, grad).reshape(2, width // 2, -1)
            far = swap_core(pick(qkv_part, 1 - core, 0))
            after_hop["qkv"] = pick(qkv_part, core, 0) + far
        elif hop - 2 < steps:
            after_hop["qkv"] = state["qkv"] + flip(state["qkv"], hop - 2)
        else:
            after_hop["qkv"] = state["qkv"]
        term = first_term((hop + 1) % groups)
        if hop < groups - 1:
            after_hop["running"] = (arrived.astype(jnp.float32) + term).astype(bf16)
        else:
            frames_grad, norm_first = last_call(own_frames, norm_gains, self_side, arrived, term)
            after_hop["frames_grad"] = frames_grad
            norm_rows = [norm_first[0:1], norm_part[1:3], norm_first[1:2], norm_part[4:6]]
            after_hop["norm"] = jnp.concatenate(norm_rows, 0).reshape(2, 3, width)
        state = settle(after_hop)
        small = state["small"]
        late = state.get("late")

    mixed, text = state["mixed"], state["text"]
    frames_grad, norm = state["frames_grad"], state["norm"]
    ring, ffn, qkv = state["ring"], state["ffn"], state["qkv"]
    small_step = norm_step = 0
    qkv_mine = qkv
    small_mine = small_far = small_grads = norm_parts = None
    ffn_mine = ffn_far = ffn_grads = qkv_far = qkv_grad = None
    small_sum = None
    while small_grads is None or ffn_grads is None or norm_parts is None or qkv_grad is None:
        if ring_next < groups:
            ring_next += 1
            ring = shift(ring, 1) + small[ring_next % groups]
        elif small_step < steps:
            small_sum = chip_gather_start(ring[None]) if small_sum is None else small_sum
            small_sum = chip_gather_joins(
                small_sum, chip_gather_flips(small_sum, small_step), small_step
            )
            small_step += 1
            if small_step == steps:
                small_mine = chip_gather_end(small_sum)[0].reshape(-1, width)
        elif small_far is None:
            small_far = swap_core(small_mine)
        elif small_grads is None:
            small_grads = small_end_call(
                head_count, text_width, core_index, small_mine, small_far
            )
        if norm_step == 0:
            norm = norm + swap_core(norm)
            norm_step += 1
        elif norm_step <= steps:
            norm = norm + flip(norm, norm_step - 1)
            norm_step += 1
        elif norm_parts is None:
            blocks_of = norm.reshape(2, 3, groups, -1)
            norm_parts = [pick(blocks_of, group, 2)] + [
                shift(pick(blocks_of, (group + k) % groups, 2), k) for k in range(1, groups)
            ]
        if ffn_step < steps:
            ffn = chip_gather_joins(ffn, chip_gather_flips(ffn, ffn_step), ffn_step)
            ffn_step += 1
        elif ffn_far is None:
            ffn_mine = chip_gather_end(ffn)[0]
            ffn_far = swap_core(ffn_mine)
        elif ffn_grads is None:
            ffn_grads = ffn_end_call(core_index, ffn_mine, ffn_far)
        if text_next < groups:
            text_next += 1
            text = shift(text, 1) + text_term(text_next % groups)
        elif qkv_far is None:
            qkv_far = swap_core(qkv_mine)
        elif qkv_grad is None:
            qkv_grad = qkv_end_call(head_count, core_index, qkv_mine, qkv_far)
        names = ["ring", "small", "small_sum", "small_mine", "small_far", "small_grads"]
        names += ["norm", "norm_parts", "ffn", "ffn_mine", "ffn_far", "ffn_grads"]
        names += ["text", "qkv_mine", "qkv_far", "qkv_grad"]
        values = (ring, small, small_sum, small_mine, small_far, small_grads, norm, norm_parts)
        values += (ffn, ffn_mine, ffn_far, ffn_grads, text, qkv_mine, qkv_far, qkv_grad)
        known = {name: one for name, one in zip(names, values) if one is not None}
        known = settle(known)
        ring, small, small_sum, small_mine, small_far, small_grads, norm, norm_parts = [
            known.get(name) for name in names[:8]
        ]
        ffn, ffn_mine, ffn_far, ffn_grads, text, qkv_mine, qkv_far, qkv_grad = [
            known.get(name) for name in names[8:]
        ]
    text_grad = text.astype(jnp.float32).reshape(clip_count, text_slots, -1)
    norm_grads = sum(norm_parts)
    ffn_in_grad, ffn_out_grad = ffn_grads
    so_grad, cq_grad, co_grad, kv_grad = small_grads
    return (
        mixed,
        frames_grad,
        text_grad,
        norm_grads,
        qkv_grad,
        so_grad,
        cq_grad,
        kv_grad,
        co_grad,
        ffn_in_grad,
        ffn_out_grad,
    )


def solution(mesh):
    rows, groups = mesh.devices.shape
    inner = Mesh(mesh.devices.reshape(rows // 2, 2, groups), ("chip", "core", "tensor"))
    data = ("chip", "core")
    in_specs = (
        P(data, None),
        P(data, None, None),
        P(data, None),
        P(data, None),
        P(),
        P(),
        P(None, "tensor"),
        P("tensor", None),
        P(None, "tensor"),
        P(None, "tensor"),
        P("tensor", None),
        P(None, "tensor"),
        P("tensor", None),
        P(data, None),
    )
    out_specs = (
        P((*data, "tensor"), None),
        P((*data, "tensor"), None),
        P(data, None, "tensor"),
        P(None, None, "tensor"),
        P(None, "tensor"),
        P("tensor", None),
        P(None, "tensor"),
        P(None, "tensor"),
        P("tensor", None),
        P(None, "tensor"),
        P("tensor", None),
    )
    return jax.shard_map(
        per_device, mesh=inner, in_specs=in_specs, out_specs=out_specs, check_vma=False
    )
```

```python
from functools import partial

import jax
import jax.numpy as jnp
from jax import lax
from jax.experimental import pallas as pl
from jax.experimental.pallas import tpu as pltpu
from jax.sharding import Mesh
from jax.sharding import PartitionSpec as P

HEAD = 64


EPSILON = 1e-05
NEGATIVE = -1e30
VMEM_BYTES = 56 * 1024 * 1024
SCALE = 0.02


def about(microseconds):
    return pl.CostEstimate(
        flops=int(microseconds * SCALE * 1.1e9), bytes_accessed=int(microseconds * SCALE * 3e6), transcendentals=0
    )


def contract_rows(left_side, right_side):
    return lax.dot_general(
        left_side, right_side, (((0,), (0,)), ((), ())), preferred_element_type=jnp.float32
    )


def times_transposed(left_side, right_side):
    return lax.dot_general(
        left_side, right_side, (((1,), (1,)), ((), ())), preferred_element_type=jnp.float32
    )


def phase(*arrays):
    return lax.optimization_barrier(arrays)


def settle(state):
    return lax.optimization_barrier(state)


def axis_bits(name):
    return lax.axis_size(name).bit_length() - 1


def shift(array, steps):
    size = lax.axis_size("tensor")
    return lax.ppermute(array, "tensor", [(i, (i + steps) % size) for i in range(size)])


def flip(array, bit):
    pairs = [(i, i ^ (1 << bit)) for i in range(lax.axis_size("chip"))]
    return lax.ppermute(array, "chip", pairs)


def swap_core(array):
    return lax.ppermute(array, "core", [(0, 1), (1, 0)])


def in_order(mine, other, first, axis):
    return jnp.concatenate(
        [jnp.where(first, mine, other), jnp.where(first, other, mine)], axis
    )


def chip_orders():
    bits = axis_bits("chip")
    return [(0, 1), (1, 0)] if bits == 2 else [tuple(range(bits))]


def halves(array, axis):
    return jnp.split(array, len(chip_orders()), axis)


def chip_gather_start(array):
    bits = axis_bits("chip")
    return [
        part.reshape(part.shape[0], *(1,) * bits, *part.shape[1:]) for part in halves(array, 1)
    ]


def chip_gather_flips(parts, step):
    return [flip(part, order[step]) for part, order in zip(parts, chip_orders())]


def chip_gather_joins(parts, others, step):
    bits = axis_bits("chip")
    chip = lax.axis_index("chip")
    return [
        in_order(part, other, (chip >> order[step]) % 2 == 0, bits - order[step])
        for part, other, order in zip(parts, others, chip_orders())
    ]


def chip_gather_end(parts):
    whole = jnp.concatenate(parts, -2)
    return whole.reshape(whole.shape[0], -1, *whole.shape[-2:])


def pick(array, index, axis):
    return lax.dynamic_index_in_dim(array, index, axis, keepdims=False)


def chip_scatter_start(array):
    bits = axis_bits("chip")
    return [array.reshape(array.shape[0], *(2,) * bits, *array.shape[2:])] * len(chip_orders())


def chip_scatter_pick(part, number, order, step, other_side):
    side = (lax.axis_index("chip") >> order[step]) % 2
    left = sorted(set(order) - set(order[:step]), reverse=True)
    picked = pick(part, 1 - side if other_side else side, 1 + left.index(order[step]))
    return halves(picked, picked.ndim - 2)[number] if step == 0 else picked


def gather(array, axes):
    return lax.all_gather(array, axes, axis=0, tiled=True)


def scatter_sum(array, axes):
    return lax.psum_scatter(array, axes, scatter_dimension=0, tiled=True)


def dot(left, right):
    return jnp.dot(left, right, preferred_element_type=jnp.float32)


def head_mask(width, head):
    lane = lax.broadcasted_iota(jnp.int32, (1, width), 1)
    return ((lane >= head * HEAD) & (lane < (head + 1) * HEAD)).astype(jnp.float32).astype(jnp.bfloat16)


def allowed_keys(low, high, key_first, shape):
    key = key_first + lax.broadcasted_iota(jnp.int32, shape, 0)
    return (key >= low) & (key <= high)


def attend_kernel(heads, key_size, first_ref, last_ref, low_ref, high_ref, q_ref, k_ref, v_ref, out_ref, log_ref, turned, acc):
    block = pl.program_id(1)
    rows, width = q_ref.shape
    key_blocks = k_ref.shape[0] // key_size

    @pl.when(block == 0)
    def _():
        for j in range(key_blocks):
            turned[j] = v_ref[j * key_size : (j + 1) * key_size, :].T

    q_rows = q_ref[...] * jnp.bfloat16(0.125)
    q_heads = [q_rows * head_mask(width, h) for h in range(heads)]
    low, high = low_ref[0], high_ref[0]
    acc[...] = jnp.zeros_like(acc)
    last = last_ref[block]

    def step(t, state):
        j = last - t
        key_first = pl.multiple_of(j * key_size, key_size)
        k_rows = k_ref[pl.ds(key_first, key_size), :]
        allowed = allowed_keys(low, high, key_first, (key_size, rows))
        fresh, parts = [], []
        scores = [jnp.where(allowed, times_transposed(k_rows, q), NEGATIVE) for q in q_heads]
        tops = [
            jnp.maximum(state[h][0], jnp.max(scores[h], axis=0, keepdims=True))
            for h in range(heads)
        ]
        probs = [jnp.exp(scores[h] - tops[h]) for h in range(heads)]
        for h in range(heads):
            top, total = state[h]
            shrink = jnp.exp(top - tops[h])
            part = slice(h * HEAD, (h + 1) * HEAD)
            parts.append(
                acc[part, :] * shrink + dot(turned[j, part, :], probs[h].astype(jnp.bfloat16))
            )
            fresh.append(
                (tops[h], total * shrink + jnp.sum(probs[h], axis=0, keepdims=True))
            )
        acc[...] = jnp.concatenate(parts, 0)
        return tuple(fresh)

    begin = (jnp.full((1, rows), NEGATIVE, jnp.float32), jnp.zeros((1, rows), jnp.float32))
    state = lax.fori_loop(0, last - first_ref[block] + 1, step, (begin,) * heads)
    for h in range(heads):
        top, total = state[h]
        part = slice(h * HEAD, (h + 1) * HEAD)
        acc[part, :] = acc[part, :] / total
        log_ref[0, 0, h : h + 1, :] = top + jnp.log(total)
    out_ref[...] = acc[...].T.astype(jnp.bfloat16)


def attend_back_kernel(heads, query_size, key_size, first_ref, last_ref, low_ref, high_ref, q_ref, k_ref, v_ref, out_ref, grad_ref, log_ref, dq_ref, dk_ref, dv_ref, q_heads, grad_heads, turned, delta, dq_acc, dk_acc, dv_acc):
    block = pl.program_id(1)
    width = q_ref.shape[1]
    query_blocks = q_ref.shape[0] // query_size

    @pl.when(block == 0)
    def _():
        for i in range(query_blocks):
            rows = slice(i * query_size, (i + 1) * query_size)
            product = grad_ref[rows, :].astype(jnp.float32) * out_ref[rows, :].astype(jnp.float32)
            product = product.T
            for h in range(heads):
                mask = head_mask(width, h)
                q_heads[i, h] = q_ref[rows, :] * (mask * jnp.bfloat16(0.125))
                grad_heads[i, h] = grad_ref[rows, :] * mask
                delta[i, h : h + 1, :] = jnp.sum(
                    product[h * HEAD : (h + 1) * HEAD, :], axis=0, keepdims=True
                )
        dq_acc[...] = jnp.zeros_like(dq_acc)

    key_first = pl.multiple_of(block * key_size, key_size)
    k_rows = k_ref[pl.ds(key_first, key_size), :]
    v_rows = v_ref[pl.ds(key_first, key_size), :]
    turned[...] = k_rows.T
    dk_acc[...] = jnp.zeros_like(dk_acc)
    dv_acc[...] = jnp.zeros_like(dv_acc)

    def step(i, carry):
        allowed = allowed_keys(low_ref[i], high_ref[i], key_first, (key_size, query_size))
        scores = [times_transposed(k_rows, q_heads[i, h]) for h in range(heads)]
        prob_grads = [times_transposed(v_rows, grad_heads[i, h]) for h in range(heads)]
        probs = [
            jnp.where(allowed, jnp.exp(scores[h] - log_ref[0, i, h : h + 1, :]), 0.0)
            for h in range(heads)
        ]
        score_grads = [
            (probs[h] * (prob_grads[h] - delta[i, h : h + 1, :])).astype(jnp.bfloat16)
            for h in range(heads)
        ]
        dv_acc[...] += sum(
            dot(probs[h].astype(jnp.bfloat16), grad_heads[i, h]) for h in range(heads)
        )
        dk_acc[...] += sum(dot(score_grads[h], q_heads[i, h]) for h in range(heads))
        dq_acc[i] += jnp.concatenate(
            [
                dot(turned[h * HEAD : (h + 1) * HEAD, :], score_grads[h])
                for h in range(heads)
            ],
            0,
        )
        return carry

    lax.fori_loop(first_ref[block], last_ref[block] + 1, step, 0)
    dk_ref[pl.ds(key_first, key_size), :] = dk_acc[...].astype(jnp.bfloat16)
    dv_ref[pl.ds(key_first, key_size), :] = dv_acc[...].astype(jnp.bfloat16)

    @pl.when(block == pl.num_programs(1) - 1)
    def _():
        for i in range(query_blocks):
            dq_ref[i * query_size : (i + 1) * query_size, :] = (
                (dq_acc[i] * 0.125).T.astype(jnp.bfloat16)
            )


def packed_back_kernel(heads, query_size, key_size, groups, *refs):
    first_ref, last_ref, group_ref, low_ref, high_ref, qkv_ref, out_ref = refs[:7]
    parts = refs[7 : 7 + groups]
    log_ref, dqkv_ref = refs[7 + groups : 9 + groups]
    grad_ref = refs[-1]
    width = out_ref.shape[1]
    size = parts[0].shape[0]

    @pl.when(pl.program_id(1) == 0)
    def _():
        for k in range(groups):
            owner = lax.rem(group_ref[0] + k, groups)
            grad_ref[pl.ds(pl.multiple_of(owner * size, size), size), :] = parts[k][...]

    views = [[r.at[:, c * width : (c + 1) * width] for c in range(3)] for r in (qkv_ref, dqkv_ref)]
    attend_back_kernel(
        heads,
        query_size,
        key_size,
        first_ref,
        last_ref,
        low_ref,
        high_ref,
        *views[0],
        out_ref,
        grad_ref,
        log_ref,
        *views[1],
        *refs[9 + groups : -1],
    )


def ffn_kernel(tile, carried, *refs):
    n_own_ref, n_far_ref, g_own_ref, g_far_ref = refs[:4]
    step = pl.program_id(0)
    if carried:
        weights_ref, out_in_ref, back_in_ref = refs[4:7]
    else:
        weights_ref = refs[-1]
        for i, source in enumerate(refs[4:6]):

            @pl.when(step == i)
            def _(source=source):
                weights_ref[:, 0] = source[...]

    results = refs[7:12] if carried else refs[6:9]
    z_rows, du_rows, out_acc, back_acc, n_ref, n_turned, g_ref, g_turned = (
        refs[12:20] if carried else refs[9:17]
    )
    grads_ref = results[0]
    rows, width = n_ref.shape
    chips, piece = weights_ref.shape[0], weights_ref.shape[3]
    units = chips * piece
    share = width // chips
    w_in = weights_ref[:, 0, 0].reshape(units, width)
    w_out = weights_ref[:, 0, 1].reshape(units, width)

    @pl.when(step == 0)
    def _():
        half = rows // 2
        for joined, turned, parts in (
            (n_ref, n_turned, (n_own_ref, n_far_ref)),
            (g_ref, g_turned, (g_own_ref, g_far_ref)),
        ):
            for i, source in enumerate(parts):
                joined[i * half : (i + 1) * half, :] = source[...]
                turned[:, i * half : (i + 1) * half] = source[...].T
        if carried:
            out_acc[...] = out_in_ref[...].astype(jnp.float32)
            back_acc[...] = back_in_ref[...].astype(jnp.float32)
        else:
            out_acc[...] = jnp.zeros_like(out_acc)
            back_acc[...] = jnp.zeros_like(back_acc)

    def row_tile(i, carry):
        part = pl.ds(pl.multiple_of(i * tile, tile), tile)
        pre = times_transposed(n_ref[part, :], w_in)
        scaled = lax.erf(pre * 0.7071067811865476)
        density = jnp.exp(pre * pre * -0.5) * 0.3989422804014327
        below = 0.5 + 0.5 * scaled
        hidden = (pre * below).astype(jnp.bfloat16)
        z_rows[part, :] = hidden
        out_acc[part, :] += dot(hidden, w_out)
        hidden_grad = times_transposed(g_ref[part, :], w_out)
        pre_grad = (hidden_grad * (below + pre * density)).astype(jnp.bfloat16)
        du_rows[part, :] = pre_grad
        back_acc[part, :] += dot(pre_grad, w_in)
        return carry

    lax.fori_loop(0, rows // tile, row_tile, 0, unroll=True)
    for c in range(chips):
        part = slice(c * share, (c + 1) * share)
        grads_ref[c, 0, :, :units] = dot(n_turned[part, :], du_rows[...]).astype(jnp.bfloat16)
        grads_ref[c, 0, :, units:] = dot(g_turned[part, :], z_rows[...]).astype(jnp.bfloat16)

    @pl.when(step == pl.num_programs(0) - 1)
    def _():
        own = rows // 2
        if carried:
            out_ref, out_far_ref, back_ref, back_far_ref = results[1:]
            out_ref[...] = out_acc[:own, :]
            out_far_ref[...] = out_acc[own:, :].astype(jnp.bfloat16)
            back_ref[...] = back_acc[:own, :]
            back_far_ref[...] = back_acc[own:, :].astype(jnp.bfloat16)
        else:
            results[1][...] = out_acc[...].astype(jnp.bfloat16)
            results[2][...] = back_acc[...].astype(jnp.bfloat16)


def ffn_call(n_own, n_far, g_own, g_far, weights, sums):
    rows, width = 2 * n_own.shape[0], n_own.shape[1]
    groups = len(weights) if not sums else weights[0].shape[1]
    chips, piece = weights[0].shape[0], weights[0].shape[-2]
    units = chips * piece
    whole = lambda shape: pl.BlockSpec(shape, lambda t: (0,) * len(shape))
    own = (rows // 2, width)
    grads = (chips, 1, width // chips, 2 * units)
    block = (chips, 1, 2, piece, width)
    f32, bf16 = jnp.float32, jnp.bfloat16
    scratch = [
        pltpu.VMEM((rows, units), bf16),
        pltpu.VMEM((rows, units), bf16),
        pltpu.VMEM((rows, width), f32),
        pltpu.VMEM((rows, width), f32),
        pltpu.VMEM((rows, width), bf16),
        pltpu.VMEM((width, rows), bf16),
        pltpu.VMEM((rows, width), bf16),
        pltpu.VMEM((width, rows), bf16),
    ]
    if sums:
        results = [(own, f32), (own, bf16), (own, f32), (own, bf16)]
        weight_specs = [pl.BlockSpec(block, lambda t: (0, t, 0, 0, 0))]
    else:
        results = [((rows, width), bf16)] * 2
        weight_specs = [whole(one.shape) for one in weights]
        scratch.append(pltpu.VMEM(block, bf16))
    return pl.pallas_call(
        partial(ffn_kernel, min(512, rows), bool(sums)),
        grid=(groups,),
        in_specs=[whole(own)] * 4 + weight_specs + [whole((rows, width))] * len(sums),
        out_specs=[pl.BlockSpec(grads, lambda t: (0, t, 0, 0))]
        + [whole(shape) for shape, _ in results],
        out_shape=[jax.ShapeDtypeStruct((chips, groups, *grads[2:]), bf16)]
        + [jax.ShapeDtypeStruct(*one) for one in results],
        scratch_shapes=scratch,
        compiler_params=pltpu.CompilerParams(vmem_limit_bytes=VMEM_BYTES),
        cost_estimate=about(23),
    )(n_own, n_far, g_own, g_far, *weights, *sums)


def ffn_pack_kernel(core_ref, in_ref, out_ref, packed_ref):
    chips, _, piece, _ = packed_ref.shape
    half = chips * piece
    first = pl.multiple_of(core_ref[0] * half, half)
    turned = in_ref[:, pl.ds(first, half)].T
    for c in range(chips):
        packed_ref[c, 0] = turned[c * piece : (c + 1) * piece, :]
        packed_ref[c, 1] = out_ref[pl.ds(first + c * piece, piece), :]


def ffn_pack_call(core, ffn_in, ffn_out, chips):
    units, width = ffn_out.shape
    return pl.pallas_call(
        ffn_pack_kernel,
        in_specs=[pl.BlockSpec(memory_space=pltpu.SMEM)] + [local_spec()] * 2,
        out_specs=local_spec(),
        out_shape=jax.ShapeDtypeStruct((chips, 2, units // 2 // chips, width), jnp.bfloat16),
        compiler_params=pltpu.CompilerParams(vmem_limit_bytes=VMEM_BYTES),
        cost_estimate=about(5),
    )(core, ffn_in, ffn_out)


def unit_norm(values):
    center = values - jnp.mean(values, axis=1, keepdims=True)
    inverse = lax.rsqrt(jnp.mean(center * center, axis=1, keepdims=True) + EPSILON)
    return center * inverse, inverse


def unit_back(gradient, values, gain):
    unit, inverse = unit_norm(values)
    scaled = gradient * gain
    inner = (
        scaled
        - jnp.mean(scaled, axis=1, keepdims=True)
        - unit * jnp.mean(scaled * unit, axis=1, keepdims=True)
    )
    return (
        inner * inverse,
        jnp.sum(gradient * unit, axis=0, keepdims=True),
        jnp.sum(gradient, axis=0, keepdims=True),
    )


def first_kernel(
    heads, frames_ref, gain_ref, bias_ref, weight_ref, normed_ref, packed_ref, ordered_ref
):
    @pl.when(pl.program_id(0) == 0)
    def _():
        columns = [
            weight_ref[:, (3 * h + c) * HEAD : (3 * h + c + 1) * HEAD]
            for c in range(3)
            for h in range(heads)
        ]
        ordered_ref[...] = jnp.concatenate(columns, 1)

    unit, _ = unit_norm(frames_ref[...].astype(jnp.float32))
    normed = (unit * gain_ref[0:1, :] + bias_ref[0:1, :]).astype(jnp.bfloat16)
    normed_ref[...] = normed
    packed_ref[...] = dot(normed, ordered_ref[...]).astype(jnp.bfloat16)


def first_call(heads, frames, gain, bias, weight, tile):
    rows, width = frames.shape
    columns = weight.shape[1]
    moving = lambda size: pl.BlockSpec((tile, size), lambda i: (i, 0))
    fixed = lambda shape: pl.BlockSpec(shape, lambda i: (0, 0))
    return pl.pallas_call(
        partial(first_kernel, heads),
        grid=(rows // tile,),
        in_specs=[moving(width), fixed(gain.shape), fixed(bias.shape), fixed(weight.shape)],
        out_specs=[moving(width), moving(columns), fixed(weight.shape)],
        out_shape=[
            jax.ShapeDtypeStruct((rows, width), jnp.bfloat16),
            jax.ShapeDtypeStruct((rows, columns), jnp.bfloat16),
            jax.ShapeDtypeStruct(weight.shape, jnp.bfloat16),
        ],
        compiler_params=pltpu.CompilerParams(vmem_limit_bytes=VMEM_BYTES),
        cost_estimate=about(9),
    )(frames, gain, bias, weight)


def pack_kernel(heads, self_ref, query_ref, cross_ref, pair_ref, out_ref):
    width = heads * HEAD
    text_width = pair_ref.shape[0]
    out_ref[0:width, :] = self_ref[...]
    out_ref[width : 2 * width, :] = query_ref[...].T
    out_ref[2 * width : 3 * width, :] = cross_ref[...]
    turned = pair_ref[...].T
    for h in range(heads):
        for c in range(2):
            rows = slice((3 + c) * width + h * HEAD, (3 + c) * width + (h + 1) * HEAD)
            out_ref[rows, :text_width] = turned[(2 * h + c) * HEAD : (2 * h + c + 1) * HEAD, :]
    out_ref[3 * width :, text_width:] = jnp.zeros(
        (2 * width, out_ref.shape[1] - text_width), jnp.bfloat16
    )


def pack_call(heads, self_out, cross_query, cross_out, cross_kv):
    return pl.pallas_call(
        partial(pack_kernel, heads),
        in_specs=[local_spec()] * 4,
        out_specs=local_spec(),
        out_shape=jax.ShapeDtypeStruct((5 * heads * HEAD, self_out.shape[1]), jnp.bfloat16),
        compiler_params=pltpu.CompilerParams(vmem_limit_bytes=VMEM_BYTES),
        cost_estimate=about(3),
    )(self_out, cross_query, cross_out, cross_kv)


def weight_copies(core_ref, local_ref, mine_ref, far_ref, weights, sems):
    half = mine_ref.shape[1]
    core = core_ref[0]
    copies = [pltpu.make_async_copy(local_ref, weights.at[0], sems.at[0])]
    for k in range(1, weights.shape[0]):
        for n, (source, side) in enumerate(((mine_ref, core), (far_ref, 1 - core))):
            rows = pl.ds(pl.multiple_of(side * half, half), half)
            copies.append(
                pltpu.make_async_copy(
                    source.at[k - 1], weights.at[k, rows], sems.at[2 * k - 1 + n]
                )
            )
    return copies


def middle_kernel(
    heads,
    tile,
    core_ref,
    low_ref,
    high_ref,
    inputs_ref,
    text_ref,
    gain_ref,
    bias_ref,
    local_ref,
    mine_ref,
    far_ref,
    *rest,
):
    groups = len(rest) - 9 - 4
    mixes = rest[:groups]
    h1_ref, h2_ref, n2_ref, n3_ref, cq_ref, mix_ref, ck_ref, cv_ref, log_ref = rest[
        groups : groups + 9
    ]
    weights, turned, mix_turned, sems = rest[groups + 9 :]
    width = heads * HEAD
    text_width = text_ref.shape[1]
    keys = text_ref.shape[0]
    copies = weight_copies(core_ref, local_ref, mine_ref, far_ref, weights, sems)
    for copy in copies:
        copy.start()
    text = text_ref[...]
    for k in range(groups):
        for copy in copies[max(0, 2 * k - 1) : 2 * k + 1]:
            copy.wait()
        part = slice(k * width, (k + 1) * width)
        key_weight = weights[k, 3 * width : 4 * width, :text_width]
        value_weight = weights[k, 4 * width : 5 * width, :text_width]
        ck_ref[:, part] = times_transposed(text, key_weight).astype(jnp.bfloat16)
        cv_ref[:, part] = times_transposed(text, value_weight).astype(jnp.bfloat16)
        turned[k] = times_transposed(value_weight, text).astype(jnp.bfloat16)

    def row_tile(i, carry):
        rows = pl.ds(pl.multiple_of(i * tile, tile), tile)
        total = inputs_ref[rows, :].astype(jnp.float32)
        for k in range(groups):
            total += dot(mixes[k][rows, :], weights[k, 0:width, :])
        h1_ref[rows, :] = total
        unit, _ = unit_norm(total)
        normed = (unit * gain_ref[1:2, :] + bias_ref[1:2, :]).astype(jnp.bfloat16)
        n2_ref[rows, :] = normed
        allowed = allowed_keys(low_ref[i], high_ref[i], 0, (keys, tile))
        for k in range(groups):
            part = slice(k * width, (k + 1) * width)
            queries = times_transposed(normed, weights[k, width : 2 * width, :])
            queries = queries.astype(jnp.bfloat16)
            cq_ref[rows, part] = queries
            queries = queries * jnp.bfloat16(0.125)
            scores = [
                jnp.where(
                    allowed,
                    times_transposed(ck_ref[:, part], queries * head_mask(width, h)),
                    NEGATIVE,
                )
                for h in range(heads)
            ]
            tops = [jnp.max(one, axis=0, keepdims=True) for one in scores]
            probs = [jnp.exp(one - top) for one, top in zip(scores, tops)]
            sums = [jnp.sum(one, axis=0, keepdims=True) for one in probs]
            for h in range(heads):
                lane = slice(h * HEAD, (h + 1) * HEAD)
                mixed = dot(turned[k, lane, :], probs[h].astype(jnp.bfloat16))
                mix_turned[lane, :] = mixed / sums[h]
                log_ref[i, k * heads + h : k * heads + h + 1, :] = tops[h] + jnp.log(sums[h])
            mix_ref[rows, part] = mix_turned[...].T.astype(jnp.bfloat16)
        total = h1_ref[rows, :]
        for k in range(groups):
            part = slice(k * width, (k + 1) * width)
            total += dot(mix_ref[rows, part], weights[k, 2 * width : 3 * width, :])
        h2_ref[rows, :] = total
        unit, _ = unit_norm(total)
        n3_ref[rows, :] = (unit * gain_ref[2:3, :] + bias_ref[2:3, :]).astype(jnp.bfloat16)
        return carry

    lax.fori_loop(0, inputs_ref.shape[0] // tile, row_tile, 0)


def middle_back_kernel(
    heads,
    tile,
    core_ref,
    low_ref,
    high_ref,
    text_ref,
    gain_ref,
    third_ref,
    third_far_ref,
    grad_ref,
    h1_ref,
    h2_ref,
    cq_ref,
    mix_ref,
    ck_ref,
    cv_ref,
    log_ref,
    local_ref,
    mine_ref,
    far_ref,
    cross_side_ref,
    dcq_ref,
    dck_ref,
    dcv_ref,
    self_exact_ref,
    self_side_ref,
    norm_ref,
    text_part_ref,
    *rest,
):
    mix_grads = rest[:-6]
    weights, turned, query_turned, dk_acc, dv_acc, sems = rest[-6:]
    groups = weights.shape[0]
    width = heads * HEAD
    text_width = text_ref.shape[1]
    keys = text_ref.shape[0]
    copies = weight_copies(core_ref, local_ref, mine_ref, far_ref, weights, sems)
    for copy in copies:
        copy.start()
    text = text_ref[...]
    for k in range(groups):
        for copy in copies[max(0, 2 * k - 1) : 2 * k + 1]:
            copy.wait()
        key_weight = weights[k, 3 * width : 4 * width, :text_width]
        turned[k] = times_transposed(key_weight, text).astype(jnp.bfloat16)
    dk_acc[...] = jnp.zeros_like(dk_acc)
    dv_acc[...] = jnp.zeros_like(dv_acc)
    norm_ref[...] = jnp.zeros_like(norm_ref)

    def row_tile(i, carry):
        rows = pl.ds(pl.multiple_of(i * tile, tile), tile)
        third = third_ref[rows, :] + third_far_ref[rows, :].astype(jnp.float32)
        back, gain_sum, bias_sum = unit_back(third, h2_ref[rows, :], gain_ref[2:3, :])
        norm_ref[2:3, :] += gain_sum
        norm_ref[5:6, :] += bias_sum
        cross_exact = grad_ref[rows, :].astype(jnp.float32) + back
        cross_side = cross_exact.astype(jnp.bfloat16)
        self_exact_ref[rows, :] = cross_exact
        cross_side_ref[rows, :] = cross_side
        allowed = allowed_keys(low_ref[i], high_ref[i], 0, (keys, tile))
        for k in range(groups):
            part = slice(k * width, (k + 1) * width)
            mix_grad = times_transposed(cross_side, weights[k, 2 * width : 3 * width, :])
            mix_grad = mix_grad.astype(jnp.bfloat16)
            product = mix_grad.astype(jnp.float32) * mix_ref[rows, part].astype(jnp.float32)
            product = product.T
            queries = cq_ref[rows, part] * jnp.bfloat16(0.125)
            q_parts = [queries * head_mask(width, h) for h in range(heads)]
            grad_parts = [mix_grad * head_mask(width, h) for h in range(heads)]
            scores = [times_transposed(ck_ref[:, part], one) for one in q_parts]
            prob_grads = [times_transposed(cv_ref[:, part], one) for one in grad_parts]
            score_grads = []
            probs = []
            for h in range(heads):
                one = k * heads + h
                prob = jnp.exp(scores[h] - log_ref[i, one : one + 1, :])
                prob = jnp.where(allowed, prob, 0.0)
                lane = slice(h * HEAD, (h + 1) * HEAD)
                delta = jnp.sum(product[lane, :], axis=0, keepdims=True)
                score_grads.append((prob * (prob_grads[h] - delta)).astype(jnp.bfloat16))
                probs.append(prob.astype(jnp.bfloat16))
            dv_acc[:, part] += sum(dot(probs[h], grad_parts[h]) for h in range(heads))
            dk_acc[:, part] += sum(dot(score_grads[h], q_parts[h]) for h in range(heads))
            for h in range(heads):
                lane = slice(h * HEAD, (h + 1) * HEAD)
                query_turned[lane, :] = dot(turned[k, lane, :], score_grads[h])
            dcq_ref[rows, part] = (query_turned[...] * 0.125).T.astype(jnp.bfloat16)
        second = jnp.zeros(cross_exact.shape, jnp.float32)
        for k in range(groups):
            part = slice(k * width, (k + 1) * width)
            second += dot(dcq_ref[rows, part], weights[k, width : 2 * width, :])
        back, gain_sum, bias_sum = unit_back(second, h1_ref[rows, :], gain_ref[1:2, :])
        norm_ref[1:2, :] += gain_sum
        norm_ref[4:5, :] += bias_sum
        self_exact = self_exact_ref[rows, :] + back
        self_exact_ref[rows, :] = self_exact
        self_side = self_exact.astype(jnp.bfloat16)
        self_side_ref[rows, :] = self_side
        for k in range(groups):
            mix_grads[k][rows, :] = times_transposed(self_side, weights[k, 0:width, :]).astype(
                jnp.bfloat16
            )
        return carry

    lax.fori_loop(0, third_ref.shape[0] // tile, row_tile, 0)
    dck_ref[...] = dk_acc[...].astype(jnp.bfloat16)
    dcv_ref[...] = dv_acc[...].astype(jnp.bfloat16)
    text_part = jnp.zeros(text_ref.shape, jnp.float32)
    for k in range(groups):
        part = slice(k * width, (k + 1) * width)
        text_part += dot(dck_ref[:, part], weights[k, 3 * width : 4 * width, :text_width])
        text_part += dot(dcv_ref[:, part], weights[k, 4 * width : 5 * width, :text_width])
    size = text_width // groups
    for k in range(groups):
        text_part_ref[k] = text_part[:, k * size : (k + 1) * size].astype(jnp.bfloat16)


def weight_grads_kernel(heads, added, side_ref, *refs):
    target = refs[-1]
    if added:
        far_ref, refs = refs[0], refs[1:]
    self_ref, n2_ref, cq_ref, mix_ref, cross_ref, dck_ref, dcv_ref, text_ref = refs[:8]
    mixes = refs[8:-1]
    width = heads * HEAD
    half = target.shape[1]
    text_width = text_ref.shape[1]
    for side in range(2):

        @pl.when(side_ref[0] == side)
        def _(side=side):
            for k in range(target.shape[0]):
                first = k * width
                pairs = [
                    (mixes[k], 0, self_ref),
                    (cq_ref, first, n2_ref),
                    (mix_ref, first, cross_ref),
                    (dck_ref, first, text_ref),
                    (dcv_ref, first, text_ref),
                ]
                for n, (left, lane, right) in enumerate(pairs):
                    low = max(n * width, side * half)
                    high = min((n + 1) * width, (side + 1) * half)
                    if low >= high:
                        continue
                    columns = left[:, lane + low - n * width : lane + high - n * width]
                    product = contract_rows(columns, right[...])
                    rows = slice(low - side * half, high - side * half)
                    if added:
                        product += far_ref[k, rows, : product.shape[1]].astype(jnp.float32)
                    product = product.astype(jnp.bfloat16)
                    target[k, rows, : product.shape[1]] = product
                    if product.shape[1] < target.shape[2]:
                        target[k, rows, text_width:] = jnp.zeros(
                            (high - low, target.shape[2] - text_width), jnp.bfloat16
                        )


def weight_grads_call(heads, side, arrays, mixes, far=()):
    groups, width = len(mixes), arrays[0].shape[1]
    half = 5 * heads * HEAD // 2
    return pl.pallas_call(
        partial(weight_grads_kernel, heads, bool(far)),
        in_specs=[pl.BlockSpec(memory_space=pltpu.SMEM)]
        + [local_spec()] * (len(far) + len(arrays) + groups),
        out_specs=local_spec(),
        out_shape=jax.ShapeDtypeStruct((groups, half, width), jnp.bfloat16),
        compiler_params=pltpu.CompilerParams(vmem_limit_bytes=VMEM_BYTES),
        cost_estimate=about(10),
    )(side, *far, *arrays, *mixes)


def last_kernel(frames_ref, gain_ref, exact_ref, sum_ref, term_ref, out_ref, norm_ref):
    gradient = sum_ref[...].astype(jnp.float32) + term_ref[...]
    back, gain_sum, bias_sum = unit_back(
        gradient, frames_ref[...].astype(jnp.float32), gain_ref[0:1, :]
    )
    out_ref[...] = (exact_ref[...] + back).astype(jnp.bfloat16)
    norm_ref[0:1, :] = gain_sum
    norm_ref[1:2, :] = bias_sum


def last_call(frames, gains, exact, sums, term):
    rows, width = frames.shape
    return pl.pallas_call(
        last_kernel,
        in_specs=[local_spec()] * 5,
        out_specs=[local_spec()] * 2,
        out_shape=[
            jax.ShapeDtypeStruct((rows, width), jnp.bfloat16),
            jax.ShapeDtypeStruct((2, width), jnp.float32),
        ],
        compiler_params=pltpu.CompilerParams(vmem_limit_bytes=VMEM_BYTES),
        cost_estimate=about(4),
    )(frames, gains, exact, sums, term)


def ffn_end_kernel(core_ref, mine_ref, far_ref, in_ref, out_ref):
    units = in_ref.shape[1] // 2
    for source, side in ((mine_ref, core_ref[0]), (far_ref, 1 - core_ref[0])):
        part = pl.ds(pl.multiple_of(side * units, units), units)
        in_ref[:, part] = source[0, :, :units].astype(jnp.float32)
        out_ref[part, :] = source[0, :, units:].astype(jnp.float32).T


def ffn_end_call(core, mine, far):
    chips, features, columns = mine.shape
    source = pl.BlockSpec((1, features, columns), lambda c: (c, 0, 0))
    return pl.pallas_call(
        ffn_end_kernel,
        grid=(chips,),
        in_specs=[pl.BlockSpec(memory_space=pltpu.SMEM), source, source],
        out_specs=[
            pl.BlockSpec((features, columns), lambda c: (c, 0)),
            pl.BlockSpec((columns, features), lambda c: (0, c)),
        ],
        out_shape=[
            jax.ShapeDtypeStruct((chips * features, columns), jnp.float32),
            jax.ShapeDtypeStruct((columns, chips * features), jnp.float32),
        ],
        compiler_params=pltpu.CompilerParams(vmem_limit_bytes=VMEM_BYTES),
        cost_estimate=about(5),
    )(core, mine, far)


def qkv_grad_kernel(left_ref, right_ref, out_ref):
    out_ref[...] = contract_rows(left_ref[...], right_ref[...]).astype(jnp.bfloat16)


def qkv_grad_call(normed, packed_grad):
    rows, width = normed.shape
    columns = packed_grad.shape[1]
    tile = min(256, width)
    return pl.pallas_call(
        qkv_grad_kernel,
        grid=(width // tile,),
        in_specs=[
            pl.BlockSpec((rows, tile), lambda i: (0, i)),
            pl.BlockSpec((rows, columns), lambda i: (0, 0)),
        ],
        out_specs=pl.BlockSpec((tile, columns), lambda i: (i, 0)),
        out_shape=jax.ShapeDtypeStruct((width, columns), jnp.bfloat16),
        compiler_params=pltpu.CompilerParams(vmem_limit_bytes=VMEM_BYTES),
        cost_estimate=about(5),
    )(normed, packed_grad)


def qkv_end_kernel(heads, core_ref, mine_ref, far_ref, out_ref):
    width = heads * HEAD
    size = mine_ref.shape[0]
    for source, side in ((mine_ref, core_ref[0]), (far_ref, 1 - core_ref[0])):
        columns = [
            source[:, c * width + h * HEAD : c * width + (h + 1) * HEAD]
            for h in range(heads)
            for c in range(3)
        ]
        rows = pl.ds(pl.multiple_of(side * size, size), size)
        out_ref[rows, :] = jnp.concatenate(columns, 1).astype(jnp.float32)


def qkv_end_call(heads, core, mine, far):
    rows, columns = mine.shape
    return pl.pallas_call(
        partial(qkv_end_kernel, heads),
        in_specs=[pl.BlockSpec(memory_space=pltpu.SMEM)] + [local_spec()] * 2,
        out_specs=local_spec(),
        out_shape=jax.ShapeDtypeStruct((2 * rows, columns), jnp.float32),
        compiler_params=pltpu.CompilerParams(vmem_limit_bytes=VMEM_BYTES),
        cost_estimate=about(3),
    )(core, mine, far)


def small_end_kernel(heads, core_ref, mine_ref, far_ref, *refs):
    self_ref, query_ref, cross_ref, pair_ref, joined = refs
    width = heads * HEAD
    text_width = pair_ref.shape[0]
    half = joined.shape[0] // 2
    for source, side in ((mine_ref, core_ref[0]), (far_ref, 1 - core_ref[0])):
        joined[pl.ds(pl.multiple_of(side * half, half), half), :] = source[...]
    self_ref[...] = joined[0:width, :].astype(jnp.float32)
    query_ref[...] = joined[width : 2 * width, :].astype(jnp.float32).T
    cross_ref[...] = joined[2 * width : 3 * width, :].astype(jnp.float32)
    for h in range(heads):
        rows = [slice((3 + c) * width + h * HEAD, (3 + c) * width + (h + 1) * HEAD) for c in (0, 1)]
        both = jnp.concatenate([joined[part, :text_width] for part in rows], 0)
        pair_ref[:, 2 * h * HEAD : 2 * (h + 1) * HEAD] = both.astype(jnp.float32).T


def small_end_call(heads, text_width, core, mine, far):
    width = mine.shape[1]
    head_width = heads * HEAD
    shapes = [
        (head_width, width),
        (width, head_width),
        (head_width, width),
        (text_width, 2 * head_width),
    ]
    return pl.pallas_call(
        partial(small_end_kernel, heads),
        in_specs=[pl.BlockSpec(memory_space=pltpu.SMEM)] + [local_spec()] * 2,
        out_specs=[local_spec()] * 4,
        out_shape=[jax.ShapeDtypeStruct(shape, jnp.float32) for shape in shapes],
        scratch_shapes=[pltpu.VMEM((5 * head_width, width), jnp.bfloat16)],
        compiler_params=pltpu.CompilerParams(vmem_limit_bytes=VMEM_BYTES),
        cost_estimate=about(4),
    )(core, mine, far)


def local_spec():
    return pl.BlockSpec(memory_space=pltpu.VMEM)


def middle_specs(plain):
    return (
        [pl.BlockSpec(memory_space=pltpu.SMEM)]
        + [local_spec()] * plain
        + [pl.BlockSpec(memory_space=pl.ANY)] * 3
    )


def middle_call(heads, tile, core, low, high, inputs, text, gains, biases, split_weights, mixes):
    rows, width = inputs.shape
    keys = text.shape[0]
    groups = len(mixes)
    f32, bf16 = jnp.float32, jnp.bfloat16
    shapes = [
        ((rows, width), f32),
        ((rows, width), f32),
        ((rows, width), bf16),
        ((rows, width), bf16),
        ((rows, width), bf16),
        ((rows, width), bf16),
        ((keys, width), bf16),
        ((keys, width), bf16),
        ((rows // tile, groups * heads, tile), f32),
    ]
    return pl.pallas_call(
        partial(middle_kernel, heads, tile),
        in_specs=middle_specs(6) + [local_spec()] * groups,
        out_specs=[local_spec()] * len(shapes),
        out_shape=[jax.ShapeDtypeStruct(*one) for one in shapes],
        scratch_shapes=[
            pltpu.VMEM((groups, *split_weights[0].shape), bf16),
            pltpu.VMEM((groups, heads * HEAD, keys), bf16),
            pltpu.VMEM((heads * HEAD, tile), f32),
            pltpu.SemaphoreType.DMA((2 * groups - 1,)),
        ],
        compiler_params=pltpu.CompilerParams(vmem_limit_bytes=VMEM_BYTES),
        cost_estimate=about(30),
    )(core, lanes(low, tile), lanes(high, tile), inputs, text, gains, biases, *split_weights, *mixes)


def middle_back_call(heads, tile, core, low, high, text, gains, saved, split_weights):
    rows, width = saved[0].shape
    keys = text.shape[0]
    groups = width // (heads * HEAD)
    f32, bf16 = jnp.float32, jnp.bfloat16
    shapes = [
        ((rows, width), bf16),
        ((rows, width), bf16),
        ((keys, width), bf16),
        ((keys, width), bf16),
        ((rows, width), f32),
        ((rows, width), bf16),
        ((6, width), f32),
        ((groups, keys, text.shape[1] // groups), bf16),
    ] + [((rows, heads * HEAD), bf16)] * groups
    return pl.pallas_call(
        partial(middle_back_kernel, heads, tile),
        in_specs=middle_specs(4 + len(saved)),
        out_specs=[local_spec()] * len(shapes),
        out_shape=[jax.ShapeDtypeStruct(*one) for one in shapes],
        scratch_shapes=[
            pltpu.VMEM((groups, *split_weights[0].shape), bf16),
            pltpu.VMEM((groups, heads * HEAD, keys), bf16),
            pltpu.VMEM((heads * HEAD, tile), f32),
            pltpu.VMEM((keys, width), f32),
            pltpu.VMEM((keys, width), f32),
            pltpu.SemaphoreType.DMA((2 * groups - 1,)),
        ],
        compiler_params=pltpu.CompilerParams(vmem_limit_bytes=VMEM_BYTES),
        cost_estimate=about(40),
    )(core, lanes(low, tile), lanes(high, tile), text, gains, *saved, *split_weights)


def lanes(values, size):
    return values.astype(jnp.int32).reshape(-1, 1, size)


def attend_call(q, k, v, columns, groups, heads, low, high, first, last, query_size, key_size):
    width = heads * HEAD
    rows, keys = q.shape[0], k.shape[0]
    blocks = rows // query_size
    spec = lambda size, column: pl.BlockSpec((size, width), lambda g, i, *_: (0, column + g))
    vector = pl.BlockSpec((1, 1, query_size), lambda g, i, *_: (i, 0, 0))
    q_column = columns[0]
    return pl.pallas_call(
        partial(attend_kernel, heads, key_size),
        grid_spec=pltpu.PrefetchScalarGridSpec(
            num_scalar_prefetch=2,
            grid=(groups, blocks),
            in_specs=[
                vector,
                vector,
                pl.BlockSpec((query_size, width), lambda g, i, *_: (i, q_column + g)),
                spec(keys, columns[1]),
                spec(keys, columns[2]),
            ],
            out_specs=[
                pl.BlockSpec((query_size, width), lambda g, i, *_: (i, g)),
                pl.BlockSpec((1, 1, heads, query_size), lambda g, i, *_: (g, i, 0, 0)),
            ],
            scratch_shapes=[
                pltpu.VMEM((keys // key_size, width, key_size), jnp.bfloat16),
                pltpu.VMEM((width, query_size), jnp.float32),
            ],
        ),
        out_shape=[
            jax.ShapeDtypeStruct((rows, groups * width), jnp.bfloat16),
            jax.ShapeDtypeStruct((groups, blocks, heads, query_size), jnp.float32),
        ],
        compiler_params=pltpu.CompilerParams(vmem_limit_bytes=VMEM_BYTES),
        cost_estimate=about(30 if groups == 1 else 17),
    )(first, last, lanes(low, query_size), lanes(high, query_size), q, k, v)


def back_scratch(heads, blocks, query_size, key_size):
    width = heads * HEAD
    return [
        pltpu.VMEM((blocks, heads, query_size, width), jnp.bfloat16),
        pltpu.VMEM((blocks, heads, query_size, width), jnp.bfloat16),
        pltpu.VMEM((width, key_size), jnp.bfloat16),
        pltpu.VMEM((blocks, heads, query_size), jnp.float32),
        pltpu.VMEM((blocks, width, query_size), jnp.float32),
        pltpu.VMEM((key_size, width), jnp.float32),
        pltpu.VMEM((key_size, width), jnp.float32),
    ]


def packed_back_call(
    qkv, out, parts, logs, heads, group, low, high, first, last, query_size, key_size
):
    rows, width = out.shape
    blocks = rows // query_size
    whole = lambda shape: pl.BlockSpec(shape, lambda g, j, *_: (0,) * len(shape))
    vector = whole((blocks, 1, query_size))
    return pl.pallas_call(
        partial(packed_back_kernel, heads, query_size, key_size, len(parts)),
        grid_spec=pltpu.PrefetchScalarGridSpec(
            num_scalar_prefetch=3,
            grid=(1, rows // key_size),
            in_specs=[vector, vector, whole(qkv.shape), whole(out.shape)]
            + [whole(part.shape) for part in parts]
            + [whole(logs.shape)],
            out_specs=whole(qkv.shape),
            scratch_shapes=back_scratch(heads, blocks, query_size, key_size)
            + [pltpu.VMEM(out.shape, jnp.bfloat16)],
        ),
        out_shape=jax.ShapeDtypeStruct(qkv.shape, jnp.bfloat16),
        compiler_params=pltpu.CompilerParams(vmem_limit_bytes=VMEM_BYTES),
        cost_estimate=about(30),
    )(
        first,
        last,
        group,
        lanes(low, query_size),
        lanes(high, query_size),
        qkv,
        out,
        *parts,
        logs,
    )


def attend_back_call(q, k, v, out, grad, logs, groups, heads, low, high, first, last, query_size, key_size):
    width = heads * HEAD
    rows, keys = q.shape[0], k.shape[0]
    blocks = rows // query_size
    column = lambda size: pl.BlockSpec((size, width), lambda g, j, *_: (0, g))
    vector = pl.BlockSpec((blocks, 1, query_size), lambda g, j, *_: (0, 0, 0))
    return pl.pallas_call(
        partial(attend_back_kernel, heads, query_size, key_size),
        grid_spec=pltpu.PrefetchScalarGridSpec(
            num_scalar_prefetch=2,
            grid=(groups, keys // key_size),
            in_specs=[
                vector,
                vector,
                column(rows),
                column(keys),
                column(keys),
                column(rows),
                column(rows),
                pl.BlockSpec((1, blocks, heads, query_size), lambda g, j, *_: (g, 0, 0, 0)),
            ],
            out_specs=[column(rows), column(keys), column(keys)],
            scratch_shapes=back_scratch(heads, blocks, query_size, key_size),
        ),
        out_shape=[
            jax.ShapeDtypeStruct((rows, groups * width), jnp.bfloat16),
            jax.ShapeDtypeStruct((keys, groups * width), jnp.bfloat16),
            jax.ShapeDtypeStruct((keys, groups * width), jnp.bfloat16),
        ],
        compiler_params=pltpu.CompilerParams(vmem_limit_bytes=VMEM_BYTES),
        cost_estimate=about(6 * groups),
    )(first, last, lanes(low, query_size), lanes(high, query_size), q, k, v, out, grad, logs)


def per_device(
    frames,
    text_states,
    clip_lengths,
    text_lengths,
    norm_gains,
    norm_biases,
    self_qkv,
    self_out,
    cross_query,
    cross_kv,
    cross_out,
    ffn_in,
    ffn_out,
    out_grad,
):
    groups = lax.axis_size("tensor")
    chips = lax.axis_size("chip")
    group = lax.axis_index("tensor")
    chip = lax.axis_index("chip")
    core = lax.axis_index("core")
    bf16 = jnp.bfloat16
    frame_count, width = frames.shape
    own_rows = frame_count // groups
    offset = group * own_rows
    clip_count, text_slots, text_width = text_states.shape
    head_count = self_out.shape[0] // HEAD
    all_heads = head_count * groups
    ends = jnp.cumsum(clip_lengths[0])
    starts = ends - clip_lengths[0]
    positions = jnp.arange(frame_count, dtype=jnp.int32)[:, None]
    clip_first = jnp.max(jnp.where(positions >= starts, starts, 0), axis=1)
    clip_stop = jnp.min(jnp.where(positions < ends, ends, frame_count), axis=1)
    block = min(256, own_rows)
    blocks = jnp.arange(frame_count // block, dtype=jnp.int32)
    self_low, self_high = clip_first, positions[:, 0]
    wide = min(2 * block, frame_count)
    wides = jnp.arange(frame_count // wide, dtype=jnp.int32)
    self_keys = (clip_first[::wide] // block, (wides * wide + wide - 1) // block)
    self_queries = (blocks * block // wide, (clip_stop[block - 1 :: block] - 1) // wide)
    own_positions = offset + jnp.arange(own_rows, dtype=jnp.int32)[:, None]
    own_clip = jnp.sum((own_positions >= ends).astype(jnp.int32), axis=1)
    own_length = jnp.sum(
        jnp.where(own_clip[:, None] == jnp.arange(clip_count), text_lengths[0], 0), axis=1
    )
    cross_low = own_clip * text_slots
    cross_high = cross_low + own_length - 1
    cross_keys = (own_clip[::block], own_clip[block - 1 :: block])
    inside_first = jnp.clip(starts - offset, 0, own_rows)
    inside_stop = jnp.clip(ends - offset, 0, own_rows)
    cross_first = jnp.minimum(inside_first // block, own_rows // block - 1)
    cross_queries = (
        cross_first,
        jnp.where(inside_stop > inside_first, (inside_stop - 1) // block, cross_first - 1),
    )

    head_width = head_count * HEAD
    local = pack_call(head_count, self_out, cross_query, cross_out, cross_kv)
    pieces = local.reshape(2, chips, -1, width)
    half = ffn_out.shape[0] // 2
    piece = half // chips
    core_index = core.reshape(1).astype(jnp.int32)
    sent_piece = pick(pick(pieces, core, 0), chip, 0)
    sent_piece, frames, self_qkv, ffn_in, ffn_out, out_grad = phase(
        sent_piece, frames, self_qkv, ffn_in, ffn_out, out_grad
    )
    passed = [shift(sent_piece, k) for k in range(1, groups)]
    ffn_own = ffn_pack_call(core_index, ffn_in, ffn_out, chips)
    ffn_piece = pick(ffn_own, chip, 0).reshape(2 * piece, width)
    own_frames = lax.dynamic_slice_in_dim(frames, offset, own_rows, 0)
    grad_own_bf = lax.dynamic_slice_in_dim(out_grad, offset, own_rows, 0)
    rows_one, packed, w_qkv = first_call(
        head_count, frames, norm_gains, norm_biases, self_qkv, block
    )
    packed, ffn_piece, own_frames, grad_own_bf, *passed = phase(
        packed, ffn_piece, own_frames, grad_own_bf, *passed
    )
    if head_width % 128 == 0:
        self_parts, self_columns = (packed,) * 3, (0, 1, 2)
    else:
        self_parts, self_columns = jnp.split(packed, 3, 1), (0, 0, 0)
    steps = axis_bits("chip")
    joined = chip_gather_start(jnp.stack(passed))
    flipped = chip_gather_flips(joined, 0)
    ffn_all = gather(ffn_piece[None], "tensor")
    self_mix, self_logs = attend_call(
        *self_parts, self_columns, 1, head_count, self_low, self_high, *self_keys, wide, block
    )
    joined = chip_gather_joins(joined, flipped, 0)
    self_mix, *joined = phase(self_mix, *joined)

    mix_blocks = self_mix.reshape(groups, own_rows, head_width)
    mixes = [pick(mix_blocks, group, 0)] + [
        shift(pick(mix_blocks, (group + k) % groups, 0), k) for k in range(1, groups)
    ]
    flipped = chip_gather_flips(joined, 1)
    joined = chip_gather_joins(joined, flipped, 1)
    for step in range(2, steps):
        joined = chip_gather_joins(joined, phase(*chip_gather_flips(joined, step)), step)
    mine = chip_gather_end(joined).reshape(groups - 1, -1, width)
    ffn_passed = [pick(ffn_all, (group + groups - k) % groups, 0) for k in range(1, groups)]
    ffn_stack = jnp.stack(ffn_passed[1:])[None]
    mine, ffn_stack, ffn_next, *mixes = phase(mine, ffn_stack, ffn_passed[0], *mixes)
    ffn_joined = chip_gather_start(ffn_next[None])
    ffn_late = gather(ffn_stack, "chip")
    ffn_late = ffn_late.reshape(chips, groups - 2, 2, piece, width)
    flipped = chip_gather_flips(ffn_joined, 0)
    ffn_joined = chip_gather_joins(ffn_joined, flipped, 0)
    far, *ffn_joined = phase(swap_core(mine), *ffn_joined)
    split_weights = (local, mine, far)
    ffn_flipped = chip_gather_flips(ffn_joined, 1)

    text_flat = text_states.reshape(clip_count * text_slots, text_width)
    shape = (head_count, block, core_index, cross_low, cross_high)
    after_self, after_cross, rows_two, rows_three, cross_q, cross_flat, cross_k, cross_v, cross_logs = (
        middle_call(
            *shape, own_frames, text_flat, norm_gains, norm_biases, split_weights, mixes
        )
    )

    grad_far = swap_core(grad_own_bf)
    rows_three, grad_far, *ffn_flipped = phase(rows_three, grad_far, *ffn_flipped)
    rows_far = swap_core(rows_three)
    ffn_joined = chip_gather_joins(ffn_joined, ffn_flipped, 1)
    for step in range(2, steps):
        ffn_joined = chip_gather_joins(ffn_joined, chip_gather_flips(ffn_joined, step), step)
    ffn_first = chip_gather_end(ffn_joined).reshape(chips, 2, piece, width)
    row_sets = (rows_three, rows_far, grad_own_bf, grad_far)
    ffn_part, *sums = ffn_call(*row_sets, (ffn_own, ffn_first), ())
    ffn_sum = scatter_sum(ffn_part.reshape(-1, 2 * half), "chip")
    ffn_late_part, out_own, out_far, third_own_grad, third_far = ffn_call(
        *row_sets, (ffn_late,), tuple(sums)
    )
    ffn_late_sum = scatter_sum(ffn_late_part.reshape(-1, 2 * half), "chip")
    saved = (
        third_own_grad,
        swap_core(third_far),
        grad_own_bf,
        after_self,
        after_cross,
        cross_q,
        cross_flat,
        cross_k,
        cross_v,
        cross_logs,
    )
    (
        cross_grad,
        cq_flat,
        ck_grad,
        cv_grad,
        self_side,
        self_grad,
        norm_part,
        text_part,
        *mix_grads,
    ) = middle_back_call(*shape, text_flat, norm_gains, saved, split_weights)

    mix_parts = [mix_grads[0]] + [shift(mix_grads[k], -k) for k in range(1, groups)]
    out_far = swap_core(out_far)
    arrays = (
        self_grad,
        rows_two,
        cq_flat,
        cross_flat,
        cross_grad,
        ck_grad,
        cv_grad,
        text_flat,
    )
    small_far = swap_core(weight_grads_call(head_count, 1 - core_index, arrays, mixes))
    small_part = weight_grads_call(head_count, core_index, arrays, mixes, (small_far,))

    def text_term(k):
        return pick(text_part, (group + groups - k) % groups, 0)

    orders = chip_orders()
    whole = chip_scatter_start(small_part.reshape(groups, chips, -1, width))
    state = settle(
        dict(
            whole=small_part,
            send=[chip_scatter_pick(whole[n], n, o, 0, True) for n, o in enumerate(orders)],
            text=text_term(1),
            out_far=out_far,
            ffn=list(ffn_sum.reshape(2, -1, 2 * half)),
            mix=mix_parts,
        )
    )
    mix_parts = state.pop("mix")
    text_run = shift(state["text"], 1)
    moved = [flip(one, o[0]) for one, o in zip(state["send"], orders)]
    ffn_run = shift(state["ffn"][1], 1)

    self_rest = (self_low, self_high, *self_queries, wide, block)
    if head_width % 128 == 0:
        packed_grad = packed_back_call(
            packed, self_mix, mix_parts, self_logs, head_count, group.reshape(1), *self_rest
        )
    else:
        mix_grad = jnp.concatenate([*mix_parts, *mix_parts], 0)
        mix_grad = lax.dynamic_slice_in_dim(
            mix_grad, (groups - group) % groups * own_rows, frame_count, 0
        )
        packed_grad = jnp.concatenate(
            attend_back_call(
                *self_parts, self_mix, mix_grad, self_logs, 1, head_count, *self_rest
            ),
            1,
        )
    state = settle(
        dict(
            state,
            grad=packed_grad,
            text=text_run,
            moved=moved,
            run=ffn_run,
            late=ffn_late_sum,
            h2=after_cross,
        )
    )

    def first_term(k):
        blocks = state["grad"].reshape(groups, own_rows, -1)
        rows = pick(blocks, (group + groups - k) % groups, 0)
        return times_transposed(rows, w_qkv)

    state = settle(dict(state, running=first_term(1).astype(bf16)))
    whole = chip_scatter_start(state["whole"].reshape(groups, chips, -1, width))
    small = [
        chip_scatter_pick(whole[n], n, o, 0, False) + one
        for n, (o, one) in enumerate(zip(orders, state["moved"]))
    ]
    late = list(state["late"].reshape(groups - 2, -1, 2 * half))
    state["run"] = state["run"] + late[0]
    ring_next = 1
    ffn_step = 0
    text_next = 2
    state["text"] = state["text"] + text_term(2)
    for hop in range(1, groups):
        arrived = shift(state["running"], 1)
        after_hop = dict(grad=state["grad"])
        if hop < steps:
            small = [
                chip_scatter_pick(one, n, o, hop, False)
                + flip(chip_scatter_pick(one, n, o, hop, True), o[hop])
                for n, (o, one) in enumerate(zip(orders, small))
            ]
            if hop == steps - 1:
                small = jnp.concatenate(small, 1)
        elif ring_next < groups:
            running_small = shift(small[1] if ring_next == 1 else state["ring"], 1)
            ring_next += 1
            after_hop["ring"] = running_small + small[ring_next % groups]
        after_hop["small"] = small
        after_hop["text"] = state["text"]
        if 1 < hop < groups - 1:
            text_next += 1
            after_hop["text"] = shift(state["text"], 1) + text_term(text_next % groups)
        if hop < groups - 1:
            after_hop["own"] = state["own"] if hop > 1 else state["ffn"][0]
            run = shift(state["run"], 1)
            after_hop["run"] = run + (late[hop] if hop < groups - 2 else after_hop["own"])
            late = after_hop["late"] = state["late"] if hop > 1 else late
        else:
            ffn = chip_gather_start(state["run"][None])
            after_hop["ffn"] = chip_gather_joins(ffn, chip_gather_flips(ffn, 0), 0)
            ffn_step = 1
        if hop == 1:
            mixed = state["h2"] + out_own + state["out_far"].astype(jnp.float32)
            after_hop["mixed"] = mixed.astype(bf16)
        else:
            after_hop["mixed"] = state["mixed"]
        if hop == 1:
            grad, run = phase(state["grad"], run)
            qkv_part = qkv_grad_call(rows_one, grad).reshape(2, width // 2, -1)
            far = swap_core(pick(qkv_part, 1 - core, 0))
            after_hop["qkv"] = pick(qkv_part, core, 0) + far
        elif hop - 2 < steps:
            after_hop["qkv"] = state["qkv"] + flip(state["qkv"], hop - 2)
        else:
            after_hop["qkv"] = state["qkv"]
        term = first_term((hop + 1) % groups)
        if hop < groups - 1:
            after_hop["running"] = (arrived.astype(jnp.float32) + term).astype(bf16)
        else:
            frames_grad, norm_first = last_call(own_frames, norm_gains, self_side, arrived, term)
            after_hop["frames_grad"] = frames_grad
            norm_rows = [norm_first[0:1], norm_part[1:3], norm_first[1:2], norm_part[4:6]]
            after_hop["norm"] = jnp.concatenate(norm_rows, 0).reshape(2, 3, width)
        state = settle(after_hop)
        small = state["small"]
        late = state.get("late")

    mixed, text = state["mixed"], state["text"]
    frames_grad, norm = state["frames_grad"], state["norm"]
    ring, ffn, qkv = state["ring"], state["ffn"], state["qkv"]
    small_step = norm_step = 0
    qkv_mine = qkv
    small_mine = small_far = small_grads = norm_parts = None
    ffn_mine = ffn_far = ffn_grads = qkv_far = qkv_grad = None
    small_sum = None
    while small_grads is None or ffn_grads is None or norm_parts is None or qkv_grad is None:
        if ring_next < groups:
            ring_next += 1
            ring = shift(ring, 1) + small[ring_next % groups]
        elif small_step < steps:
            small_sum = chip_gather_start(ring[None]) if small_sum is None else small_sum
            small_sum = chip_gather_joins(
                small_sum, chip_gather_flips(small_sum, small_step), small_step
            )
            small_step += 1
            if small_step == steps:
                small_mine = chip_gather_end(small_sum)[0].reshape(-1, width)
        elif small_far is None:
            small_far = swap_core(small_mine)
        elif small_grads is None:
            small_grads = small_end_call(
                head_count, text_width, core_index, small_mine, small_far
            )
        if norm_step == 0:
            norm = norm + swap_core(norm)
            norm_step += 1
        elif norm_step <= steps:
            norm = norm + flip(norm, norm_step - 1)
            norm_step += 1
        elif norm_parts is None:
            blocks_of = norm.reshape(2, 3, groups, -1)
            norm_parts = [pick(blocks_of, group, 2)] + [
                shift(pick(blocks_of, (group + k) % groups, 2), k) for k in range(1, groups)
            ]
        if ffn_step < steps:
            ffn = chip_gather_joins(ffn, chip_gather_flips(ffn, ffn_step), ffn_step)
            ffn_step += 1
        elif ffn_far is None:
            ffn_mine = chip_gather_end(ffn)[0]
            ffn_far = swap_core(ffn_mine)
        elif ffn_grads is None:
            ffn_grads = ffn_end_call(core_index, ffn_mine, ffn_far)
        if text_next < groups:
            text_next += 1
            text = shift(text, 1) + text_term(text_next % groups)
        elif qkv_far is None:
            qkv_far = swap_core(qkv_mine)
        elif qkv_grad is None:
            qkv_grad = qkv_end_call(head_count, core_index, qkv_mine, qkv_far)
        names = ["ring", "small", "small_sum", "small_mine", "small_far", "small_grads"]
        names += ["norm", "norm_parts", "ffn", "ffn_mine", "ffn_far", "ffn_grads"]
        names += ["text", "qkv_mine", "qkv_far", "qkv_grad"]
        values = (ring, small, small_sum, small_mine, small_far, small_grads, norm, norm_parts)
        values += (ffn, ffn_mine, ffn_far, ffn_grads, text, qkv_mine, qkv_far, qkv_grad)
        known = {name: one for name, one in zip(names, values) if one is not None}
        known = settle(known)
        ring, small, small_sum, small_mine, small_far, small_grads, norm, norm_parts = [
            known.get(name) for name in names[:8]
        ]
        ffn, ffn_mine, ffn_far, ffn_grads, text, qkv_mine, qkv_far, qkv_grad = [
            known.get(name) for name in names[8:]
        ]
    text_grad = text.astype(jnp.float32).reshape(clip_count, text_slots, -1)
    norm_grads = sum(norm_parts)
    ffn_in_grad, ffn_out_grad = ffn_grads
    so_grad, cq_grad, co_grad, kv_grad = small_grads
    return (
        mixed,
        frames_grad,
        text_grad,
        norm_grads,
        qkv_grad,
        so_grad,
        cq_grad,
        kv_grad,
        co_grad,
        ffn_in_grad,
        ffn_out_grad,
    )


def solution(mesh):
    rows, groups = mesh.devices.shape
    inner = Mesh(mesh.devices.reshape(rows // 2, 2, groups), ("chip", "core", "tensor"))
    data = ("chip", "core")
    in_specs = (
        P(data, None),
        P(data, None, None),
        P(data, None),
        P(data, None),
        P(),
        P(),
        P(None, "tensor"),
        P("tensor", None),
        P(None, "tensor"),
        P(None, "tensor"),
        P("tensor", None),
        P(None, "tensor"),
        P("tensor", None),
        P(data, None),
    )
    out_specs = (
        P((*data, "tensor"), None),
        P((*data, "tensor"), None),
        P(data, None, "tensor"),
        P(None, None, "tensor"),
        P(None, "tensor"),
        P("tensor", None),
        P(None, "tensor"),
        P(None, "tensor"),
        P("tensor", None),
        P(None, "tensor"),
        P("tensor", None),
    )
    return jax.shard_map(
        per_device, mesh=inner, in_specs=in_specs, out_specs=out_specs, check_vma=False
    )
```

```python
from functools import partial

import jax
import jax.numpy as jnp
from jax import lax
from jax.experimental import pallas as pl
from jax.experimental.pallas import tpu as pltpu
from jax.sharding import Mesh
from jax.sharding import PartitionSpec as P

HEAD = 64


EPSILON = 1e-05
NEGATIVE = -1e30
VMEM_BYTES = 56 * 1024 * 1024
SCALE = 0.02


def about(microseconds):
    return pl.CostEstimate(
        flops=int(microseconds * SCALE * 1.1e9), bytes_accessed=int(microseconds * SCALE * 3e6), transcendentals=0
    )


def contract_rows(left_side, right_side):
    return lax.dot_general(
        left_side, right_side, (((0,), (0,)), ((), ())), preferred_element_type=jnp.float32
    )


def times_transposed(left_side, right_side):
    return lax.dot_general(
        left_side, right_side, (((1,), (1,)), ((), ())), preferred_element_type=jnp.float32
    )


def phase(*arrays):
    return lax.optimization_barrier(arrays)


def settle(state):
    return lax.optimization_barrier(state)


def axis_bits(name):
    return lax.axis_size(name).bit_length() - 1


def shift(array, steps):
    size = lax.axis_size("tensor")
    return lax.ppermute(array, "tensor", [(i, (i + steps) % size) for i in range(size)])


def flip(array, bit):
    pairs = [(i, i ^ (1 << bit)) for i in range(lax.axis_size("chip"))]
    return lax.ppermute(array, "chip", pairs)


def swap_core(array):
    return lax.ppermute(array, "core", [(0, 1), (1, 0)])


def in_order(mine, other, first, axis):
    return jnp.concatenate(
        [jnp.where(first, mine, other), jnp.where(first, other, mine)], axis
    )


def chip_orders():
    bits = axis_bits("chip")
    return [(0, 1), (1, 0)] if bits == 2 else [tuple(range(bits))]


def halves(array, axis):
    return jnp.split(array, len(chip_orders()), axis)


def chip_gather_start(array):
    bits = axis_bits("chip")
    return [
        part.reshape(part.shape[0], *(1,) * bits, *part.shape[1:]) for part in halves(array, 1)
    ]


def chip_gather_flips(parts, step):
    return [flip(part, order[step]) for part, order in zip(parts, chip_orders())]


def chip_gather_joins(parts, others, step):
    bits = axis_bits("chip")
    chip = lax.axis_index("chip")
    return [
        in_order(part, other, (chip >> order[step]) % 2 == 0, bits - order[step])
        for part, other, order in zip(parts, others, chip_orders())
    ]


def chip_gather_end(parts):
    whole = jnp.concatenate(parts, -2)
    return whole.reshape(whole.shape[0], -1, *whole.shape[-2:])


def pick(array, index, axis):
    return lax.dynamic_index_in_dim(array, index, axis, keepdims=False)


def chip_scatter_start(array):
    bits = axis_bits("chip")
    return [array.reshape(array.shape[0], *(2,) * bits, *array.shape[2:])] * len(chip_orders())


def chip_scatter_pick(part, number, order, step, other_side):
    side = (lax.axis_index("chip") >> order[step]) % 2
    left = sorted(set(order) - set(order[:step]), reverse=True)
    picked = pick(part, 1 - side if other_side else side, 1 + left.index(order[step]))
    return halves(picked, picked.ndim - 2)[number] if step == 0 else picked


def gather(array, axes):
    return lax.all_gather(array, axes, axis=0, tiled=True)


def scatter_sum(array, axes):
    return lax.psum_scatter(array, axes, scatter_dimension=0, tiled=True)


def dot(left, right):
    return jnp.dot(left, right, preferred_element_type=jnp.float32)


def head_mask(width, head):
    lane = lax.broadcasted_iota(jnp.int32, (1, width), 1)
    return ((lane >= head * HEAD) & (lane < (head + 1) * HEAD)).astype(jnp.float32).astype(jnp.bfloat16)


def allowed_keys(low, high, key_first, shape):
    key = key_first + lax.broadcasted_iota(jnp.int32, shape, 0)
    return (key >= low) & (key <= high)


def attend_kernel(heads, key_size, first_ref, last_ref, low_ref, high_ref, q_ref, k_ref, v_ref, out_ref, log_ref, turned, acc):
    block = pl.program_id(1)
    rows, width = q_ref.shape
    key_blocks = k_ref.shape[0] // key_size

    @pl.when(block == 0)
    def _():
        for j in range(key_blocks):
            turned[j] = v_ref[j * key_size : (j + 1) * key_size, :].T

    q_rows = q_ref[...] * jnp.bfloat16(0.125)
    q_heads = [q_rows * head_mask(width, h) for h in range(heads)]
    low, high = low_ref[0], high_ref[0]
    acc[...] = jnp.zeros_like(acc)
    last = last_ref[block]

    def step(t, state):
        j = last - t
        key_first = pl.multiple_of(j * key_size, key_size)
        k_rows = k_ref[pl.ds(key_first, key_size), :]
        allowed = allowed_keys(low, high, key_first, (key_size, rows))
        fresh, parts = [], []
        scores = [jnp.where(allowed, times_transposed(k_rows, q), NEGATIVE) for q in q_heads]
        tops = [
            jnp.maximum(state[h][0], jnp.max(scores[h], axis=0, keepdims=True))
            for h in range(heads)
        ]
        probs = [jnp.exp(scores[h] - tops[h]) for h in range(heads)]
        for h in range(heads):
            top, total = state[h]
            shrink = jnp.exp(top - tops[h])
            part = slice(h * HEAD, (h + 1) * HEAD)
            parts.append(
                acc[part, :] * shrink + dot(turned[j, part, :], probs[h].astype(jnp.bfloat16))
            )
            fresh.append(
                (tops[h], total * shrink + jnp.sum(probs[h], axis=0, keepdims=True))
            )
        acc[...] = jnp.concatenate(parts, 0)
        return tuple(fresh)

    begin = (jnp.full((1, rows), NEGATIVE, jnp.float32), jnp.zeros((1, rows), jnp.float32))
    state = lax.fori_loop(0, last - first_ref[block] + 1, step, (begin,) * heads)
    for h in range(heads):
        top, total = state[h]
        part = slice(h * HEAD, (h + 1) * HEAD)
        acc[part, :] = acc[part, :] / total
        log_ref[0, 0, h : h + 1, :] = top + jnp.log(total)
    out_ref[...] = acc[...].T.astype(jnp.bfloat16)


def attend_back_kernel(heads, query_size, key_size, first_ref, last_ref, low_ref, high_ref, q_ref, k_ref, v_ref, out_ref, grad_ref, log_ref, dq_ref, dk_ref, dv_ref, q_heads, grad_heads, turned, delta, dq_acc, dk_acc, dv_acc):
    block = pl.program_id(1)
    width = q_ref.shape[1]
    query_blocks = q_ref.shape[0] // query_size

    @pl.when(block == 0)
    def _():
        for i in range(query_blocks):
            rows = slice(i * query_size, (i + 1) * query_size)
            product = grad_ref[rows, :].astype(jnp.float32) * out_ref[rows, :].astype(jnp.float32)
            product = product.T
            for h in range(heads):
                mask = head_mask(width, h)
                q_heads[i, h] = q_ref[rows, :] * (mask * jnp.bfloat16(0.125))
                grad_heads[i, h] = grad_ref[rows, :] * mask
                delta[i, h : h + 1, :] = jnp.sum(
                    product[h * HEAD : (h + 1) * HEAD, :], axis=0, keepdims=True
                )
        dq_acc[...] = jnp.zeros_like(dq_acc)

    key_first = pl.multiple_of(block * key_size, key_size)
    k_rows = k_ref[pl.ds(key_first, key_size), :]
    v_rows = v_ref[pl.ds(key_first, key_size), :]
    turned[...] = k_rows.T
    dk_acc[...] = jnp.zeros_like(dk_acc)
    dv_acc[...] = jnp.zeros_like(dv_acc)

    def step(i, carry):
        allowed = allowed_keys(low_ref[i], high_ref[i], key_first, (key_size, query_size))
        scores = [times_transposed(k_rows, q_heads[i, h]) for h in range(heads)]
        prob_grads = [times_transposed(v_rows, grad_heads[i, h]) for h in range(heads)]
        probs = [
            jnp.where(allowed, jnp.exp(scores[h] - log_ref[0, i, h : h + 1, :]), 0.0)
            for h in range(heads)
        ]
        score_grads = [
            (probs[h] * (prob_grads[h] - delta[i, h : h + 1, :])).astype(jnp.bfloat16)
            for h in range(heads)
        ]
        dv_acc[...] += sum(
            dot(probs[h].astype(jnp.bfloat16), grad_heads[i, h]) for h in range(heads)
        )
        dk_acc[...] += sum(dot(score_grads[h], q_heads[i, h]) for h in range(heads))
        dq_acc[i] += jnp.concatenate(
            [
                dot(turned[h * HEAD : (h + 1) * HEAD, :], score_grads[h])
                for h in range(heads)
            ],
            0,
        )
        return carry

    lax.fori_loop(first_ref[block], last_ref[block] + 1, step, 0)
    dk_ref[pl.ds(key_first, key_size), :] = dk_acc[...].astype(jnp.bfloat16)
    dv_ref[pl.ds(key_first, key_size), :] = dv_acc[...].astype(jnp.bfloat16)

    @pl.when(block == pl.num_programs(1) - 1)
    def _():
        for i in range(query_blocks):
            dq_ref[i * query_size : (i + 1) * query_size, :] = (
                (dq_acc[i] * 0.125).T.astype(jnp.bfloat16)
            )


def packed_back_kernel(heads, query_size, key_size, groups, *refs):
    first_ref, last_ref, group_ref, low_ref, high_ref, qkv_ref, out_ref = refs[:7]
    parts = refs[7 : 7 + groups]
    log_ref, dqkv_ref = refs[7 + groups : 9 + groups]
    grad_ref = refs[-1]
    width = out_ref.shape[1]
    size = parts[0].shape[0]

    @pl.when(pl.program_id(1) == 0)
    def _():
        for k in range(groups):
            owner = lax.rem(group_ref[0] + k, groups)
            grad_ref[pl.ds(pl.multiple_of(owner * size, size), size), :] = parts[k][...]

    views = [[r.at[:, c * width : (c + 1) * width] for c in range(3)] for r in (qkv_ref, dqkv_ref)]
    attend_back_kernel(
        heads,
        query_size,
        key_size,
        first_ref,
        last_ref,
        low_ref,
        high_ref,
        *views[0],
        out_ref,
        grad_ref,
        log_ref,
        *views[1],
        *refs[9 + groups : -1],
    )


def ffn_kernel(tile, carried, *refs):
    n_own_ref, n_far_ref, g_own_ref, g_far_ref = refs[:4]
    step = pl.program_id(0)
    if carried:
        weights_ref, out_in_ref, back_in_ref = refs[4:7]
    else:
        weights_ref = refs[-1]
        for i, source in enumerate(refs[4:6]):

            @pl.when(step == i)
            def _(source=source):
                weights_ref[:, 0] = source[...]

    results = refs[7:12] if carried else refs[6:9]
    z_rows, du_rows, out_acc, back_acc, n_ref, n_turned, g_ref, g_turned = (
        refs[12:20] if carried else refs[9:17]
    )
    grads_ref = results[0]
    rows, width = n_ref.shape
    chips, piece = weights_ref.shape[0], weights_ref.shape[3]
    units = chips * piece
    share = width // chips
    w_in = weights_ref[:, 0, 0].reshape(units, width)
    w_out = weights_ref[:, 0, 1].reshape(units, width)

    @pl.when(step == 0)
    def _():
        half = rows // 2
        for joined, turned, parts in (
            (n_ref, n_turned, (n_own_ref, n_far_ref)),
            (g_ref, g_turned, (g_own_ref, g_far_ref)),
        ):
            for i, source in enumerate(parts):
                joined[i * half : (i + 1) * half, :] = source[...]
                turned[:, i * half : (i + 1) * half] = source[...].T
        if carried:
            out_acc[...] = out_in_ref[...].astype(jnp.float32)
            back_acc[...] = back_in_ref[...].astype(jnp.float32)
        else:
            out_acc[...] = jnp.zeros_like(out_acc)
            back_acc[...] = jnp.zeros_like(back_acc)

    def row_tile(i, carry):
        part = pl.ds(pl.multiple_of(i * tile, tile), tile)
        pre = times_transposed(n_ref[part, :], w_in)
        scaled = lax.erf(pre * 0.7071067811865476)
        density = jnp.exp(pre * pre * -0.5) * 0.3989422804014327
        below = 0.5 + 0.5 * scaled
        hidden = (pre * below).astype(jnp.bfloat16)
        z_rows[part, :] = hidden
        out_acc[part, :] += dot(hidden, w_out)
        hidden_grad = times_transposed(g_ref[part, :], w_out)
        pre_grad = (hidden_grad * (below + pre * density)).astype(jnp.bfloat16)
        du_rows[part, :] = pre_grad
        back_acc[part, :] += dot(pre_grad, w_in)
        return carry

    lax.fori_loop(0, rows // tile, row_tile, 0, unroll=True)
    for c in range(chips):
        part = slice(c * share, (c + 1) * share)
        grads_ref[c, 0, :, :units] = dot(n_turned[part, :], du_rows[...]).astype(jnp.bfloat16)
        grads_ref[c, 0, :, units:] = dot(g_turned[part, :], z_rows[...]).astype(jnp.bfloat16)

    @pl.when(step == pl.num_programs(0) - 1)
    def _():
        own = rows // 2
        if carried:
            out_ref, out_far_ref, back_ref, back_far_ref = results[1:]
            out_ref[...] = out_acc[:own, :]
            out_far_ref[...] = out_acc[own:, :].astype(jnp.bfloat16)
            back_ref[...] = back_acc[:own, :]
            back_far_ref[...] = back_acc[own:, :].astype(jnp.bfloat16)
        else:
            results[1][...] = out_acc[...].astype(jnp.bfloat16)
            results[2][...] = back_acc[...].astype(jnp.bfloat16)


def ffn_call(n_own, n_far, g_own, g_far, weights, sums):
    rows, width = 2 * n_own.shape[0], n_own.shape[1]
    groups = len(weights) if not sums else weights[0].shape[1]
    chips, piece = weights[0].shape[0], weights[0].shape[-2]
    units = chips * piece
    whole = lambda shape: pl.BlockSpec(shape, lambda t: (0,) * len(shape))
    own = (rows // 2, width)
    grads = (chips, 1, width // chips, 2 * units)
    block = (chips, 1, 2, piece, width)
    f32, bf16 = jnp.float32, jnp.bfloat16
    scratch = [
        pltpu.VMEM((rows, units), bf16),
        pltpu.VMEM((rows, units), bf16),
        pltpu.VMEM((rows, width), f32),
        pltpu.VMEM((rows, width), f32),
        pltpu.VMEM((rows, width), bf16),
        pltpu.VMEM((width, rows), bf16),
        pltpu.VMEM((rows, width), bf16),
        pltpu.VMEM((width, rows), bf16),
    ]
    if sums:
        results = [(own, f32), (own, bf16), (own, f32), (own, bf16)]
        weight_specs = [pl.BlockSpec(block, lambda t: (0, t, 0, 0, 0))]
    else:
        results = [((rows, width), bf16)] * 2
        weight_specs = [whole(one.shape) for one in weights]
        scratch.append(pltpu.VMEM(block, bf16))
    return pl.pallas_call(
        partial(ffn_kernel, min(512, rows), bool(sums)),
        grid=(groups,),
        in_specs=[whole(own)] * 4 + weight_specs + [whole((rows, width))] * len(sums),
        out_specs=[pl.BlockSpec(grads, lambda t: (0, t, 0, 0))]
        + [whole(shape) for shape, _ in results],
        out_shape=[jax.ShapeDtypeStruct((chips, groups, *grads[2:]), bf16)]
        + [jax.ShapeDtypeStruct(*one) for one in results],
        scratch_shapes=scratch,
        compiler_params=pltpu.CompilerParams(vmem_limit_bytes=VMEM_BYTES),
        cost_estimate=about(23),
    )(n_own, n_far, g_own, g_far, *weights, *sums)


def ffn_pack_kernel(core_ref, in_ref, out_ref, packed_ref):
    chips, _, piece, _ = packed_ref.shape
    half = chips * piece
    first = pl.multiple_of(core_ref[0] * half, half)
    turned = in_ref[:, pl.ds(first, half)].T
    for c in range(chips):
        packed_ref[c, 0] = turned[c * piece : (c + 1) * piece, :]
        packed_ref[c, 1] = out_ref[pl.ds(first + c * piece, piece), :]


def ffn_pack_call(core, ffn_in, ffn_out, chips):
    units, width = ffn_out.shape
    return pl.pallas_call(
        ffn_pack_kernel,
        in_specs=[pl.BlockSpec(memory_space=pltpu.SMEM)] + [local_spec()] * 2,
        out_specs=local_spec(),
        out_shape=jax.ShapeDtypeStruct((chips, 2, units // 2 // chips, width), jnp.bfloat16),
        compiler_params=pltpu.CompilerParams(vmem_limit_bytes=VMEM_BYTES),
        cost_estimate=about(5),
    )(core, ffn_in, ffn_out)


def unit_norm(values):
    center = values - jnp.mean(values, axis=1, keepdims=True)
    inverse = lax.rsqrt(jnp.mean(center * center, axis=1, keepdims=True) + EPSILON)
    return center * inverse, inverse


def unit_back(gradient, values, gain):
    unit, inverse = unit_norm(values)
    scaled = gradient * gain
    inner = (
        scaled
        - jnp.mean(scaled, axis=1, keepdims=True)
        - unit * jnp.mean(scaled * unit, axis=1, keepdims=True)
    )
    return (
        inner * inverse,
        jnp.sum(gradient * unit, axis=0, keepdims=True),
        jnp.sum(gradient, axis=0, keepdims=True),
    )


def first_kernel(
    heads, frames_ref, gain_ref, bias_ref, weight_ref, normed_ref, packed_ref, ordered_ref
):
    @pl.when(pl.program_id(0) == 0)
    def _():
        columns = [
            weight_ref[:, (3 * h + c) * HEAD : (3 * h + c + 1) * HEAD]
            for c in range(3)
            for h in range(heads)
        ]
        ordered_ref[...] = jnp.concatenate(columns, 1)

    unit, _ = unit_norm(frames_ref[...].astype(jnp.float32))
    normed = (unit * gain_ref[0:1, :] + bias_ref[0:1, :]).astype(jnp.bfloat16)
    normed_ref[...] = normed
    packed_ref[...] = dot(normed, ordered_ref[...]).astype(jnp.bfloat16)


def first_call(heads, frames, gain, bias, weight, tile):
    rows, width = frames.shape
    columns = weight.shape[1]
    moving = lambda size: pl.BlockSpec((tile, size), lambda i: (i, 0))
    fixed = lambda shape: pl.BlockSpec(shape, lambda i: (0, 0))
    return pl.pallas_call(
        partial(first_kernel, heads),
        grid=(rows // tile,),
        in_specs=[moving(width), fixed(gain.shape), fixed(bias.shape), fixed(weight.shape)],
        out_specs=[moving(width), moving(columns), fixed(weight.shape)],
        out_shape=[
            jax.ShapeDtypeStruct((rows, width), jnp.bfloat16),
            jax.ShapeDtypeStruct((rows, columns), jnp.bfloat16),
            jax.ShapeDtypeStruct(weight.shape, jnp.bfloat16),
        ],
        compiler_params=pltpu.CompilerParams(vmem_limit_bytes=VMEM_BYTES),
        cost_estimate=about(9),
    )(frames, gain, bias, weight)


def value_rows(source, heads, text_width):
    width = heads * HEAD
    beside = source[3 * width : 4 * width, text_width:]
    rest = 2 * text_width - source.shape[1]
    below = source[4 * width : 4 * width + width // 2, :]
    return jnp.concatenate(
        [beside, jnp.concatenate([below[:, :rest], below[:, rest:]], 0)], 1
    )


def pack_kernel(heads, self_ref, query_ref, cross_ref, pair_ref, out_ref):
    width = heads * HEAD
    text_width = pair_ref.shape[0]
    out_ref[0:width, :] = self_ref[...]
    out_ref[width : 2 * width, :] = query_ref[...].T
    out_ref[2 * width : 3 * width, :] = cross_ref[...]
    turned = pair_ref[...].T
    keys, values = [
        jnp.concatenate(
            [turned[(2 * h + c) * HEAD : (2 * h + c + 1) * HEAD, :] for h in range(heads)], 0
        )
        for c in range(2)
    ]
    side = out_ref.shape[1] - text_width
    out_ref[3 * width : 4 * width, :text_width] = keys
    out_ref[3 * width : 4 * width, text_width:] = values[:, :side]
    rest = text_width - side
    out_ref[4 * width :, :rest] = values[: width // 2, side:]
    out_ref[4 * width :, rest:] = values[width // 2 :, side:]


def pack_call(heads, self_out, cross_query, cross_out, cross_kv):
    return pl.pallas_call(
        partial(pack_kernel, heads),
        in_specs=[local_spec()] * 4,
        out_specs=local_spec(),
        out_shape=jax.ShapeDtypeStruct((9 * heads * HEAD // 2, self_out.shape[1]), jnp.bfloat16),
        compiler_params=pltpu.CompilerParams(vmem_limit_bytes=VMEM_BYTES),
        cost_estimate=about(3),
    )(self_out, cross_query, cross_out, cross_kv)


def weight_copies(core_ref, local_ref, mine_ref, far_ref, weights, sems):
    half = mine_ref.shape[1]
    core = core_ref[0]
    copies = [pltpu.make_async_copy(local_ref, weights.at[0], sems.at[0])]
    for k in range(1, weights.shape[0]):
        for n, (source, side) in enumerate(((mine_ref, core), (far_ref, 1 - core))):
            rows = pl.ds(pl.multiple_of(side * half, half), half)
            copies.append(
                pltpu.make_async_copy(
                    source.at[k - 1], weights.at[k, rows], sems.at[2 * k - 1 + n]
                )
            )
    return copies


def middle_kernel(
    heads,
    tile,
    core_ref,
    low_ref,
    high_ref,
    inputs_ref,
    text_ref,
    gain_ref,
    bias_ref,
    local_ref,
    mine_ref,
    far_ref,
    *rest,
):
    groups = len(rest) - 9 - 4
    mixes = rest[:groups]
    h1_ref, h2_ref, n2_ref, n3_ref, cq_ref, mix_ref, ck_ref, cv_ref, log_ref = rest[
        groups : groups + 9
    ]
    weights, turned, mix_turned, sems = rest[groups + 9 :]
    width = heads * HEAD
    text_width = text_ref.shape[1]
    keys = text_ref.shape[0]
    copies = weight_copies(core_ref, local_ref, mine_ref, far_ref, weights, sems)
    for copy in copies:
        copy.start()
    text = text_ref[...]
    for k in range(groups):
        for copy in copies[max(0, 2 * k - 1) : 2 * k + 1]:
            copy.wait()
        part = slice(k * width, (k + 1) * width)
        key_weight = weights[k, 3 * width : 4 * width, :text_width]
        value_weight = value_rows(weights.at[k], heads, text_width)
        ck_ref[:, part] = times_transposed(text, key_weight).astype(jnp.bfloat16)
        cv_ref[:, part] = times_transposed(text, value_weight).astype(jnp.bfloat16)
        turned[k] = times_transposed(value_weight, text).astype(jnp.bfloat16)

    def row_tile(i, carry):
        rows = pl.ds(pl.multiple_of(i * tile, tile), tile)
        total = inputs_ref[rows, :].astype(jnp.float32)
        for k in range(groups):
            total += dot(mixes[k][rows, :], weights[k, 0:width, :])
        h1_ref[rows, :] = total
        unit, _ = unit_norm(total)
        normed = (unit * gain_ref[1:2, :] + bias_ref[1:2, :]).astype(jnp.bfloat16)
        n2_ref[rows, :] = normed
        allowed = allowed_keys(low_ref[i], high_ref[i], 0, (keys, tile))
        for k in range(groups):
            part = slice(k * width, (k + 1) * width)
            queries = times_transposed(normed, weights[k, width : 2 * width, :])
            queries = queries.astype(jnp.bfloat16)
            cq_ref[rows, part] = queries
            queries = queries * jnp.bfloat16(0.125)
            scores = [
                jnp.where(
                    allowed,
                    times_transposed(ck_ref[:, part], queries * head_mask(width, h)),
                    NEGATIVE,
                )
                for h in range(heads)
            ]
            tops = [jnp.max(one, axis=0, keepdims=True) for one in scores]
            probs = [jnp.exp(one - top) for one, top in zip(scores, tops)]
            sums = [jnp.sum(one, axis=0, keepdims=True) for one in probs]
            for h in range(heads):
                lane = slice(h * HEAD, (h + 1) * HEAD)
                mixed = dot(turned[k, lane, :], probs[h].astype(jnp.bfloat16))
                mix_turned[lane, :] = mixed / sums[h]
                log_ref[i, k * heads + h : k * heads + h + 1, :] = tops[h] + jnp.log(sums[h])
            mix_ref[rows, part] = mix_turned[...].T.astype(jnp.bfloat16)
        total = h1_ref[rows, :]
        for k in range(groups):
            part = slice(k * width, (k + 1) * width)
            total += dot(mix_ref[rows, part], weights[k, 2 * width : 3 * width, :])
        h2_ref[rows, :] = total
        unit, _ = unit_norm(total)
        n3_ref[rows, :] = (unit * gain_ref[2:3, :] + bias_ref[2:3, :]).astype(jnp.bfloat16)
        return carry

    lax.fori_loop(0, inputs_ref.shape[0] // tile, row_tile, 0)


def middle_back_kernel(
    heads,
    tile,
    core_ref,
    low_ref,
    high_ref,
    text_ref,
    gain_ref,
    third_ref,
    third_far_ref,
    grad_ref,
    h1_ref,
    h2_ref,
    cq_ref,
    mix_ref,
    ck_ref,
    cv_ref,
    log_ref,
    local_ref,
    mine_ref,
    far_ref,
    cross_side_ref,
    dcq_ref,
    dck_ref,
    dcv_ref,
    self_exact_ref,
    self_side_ref,
    norm_ref,
    text_part_ref,
    *rest,
):
    mix_grads = rest[:-6]
    weights, turned, query_turned, dk_acc, dv_acc, sems = rest[-6:]
    groups = weights.shape[0]
    width = heads * HEAD
    text_width = text_ref.shape[1]
    keys = text_ref.shape[0]
    copies = weight_copies(core_ref, local_ref, mine_ref, far_ref, weights, sems)
    for copy in copies:
        copy.start()
    text = text_ref[...]
    for k in range(groups):
        for copy in copies[max(0, 2 * k - 1) : 2 * k + 1]:
            copy.wait()
        key_weight = weights[k, 3 * width : 4 * width, :text_width]
        turned[k] = times_transposed(key_weight, text).astype(jnp.bfloat16)
    dk_acc[...] = jnp.zeros_like(dk_acc)
    dv_acc[...] = jnp.zeros_like(dv_acc)
    norm_ref[...] = jnp.zeros_like(norm_ref)

    def row_tile(i, carry):
        rows = pl.ds(pl.multiple_of(i * tile, tile), tile)
        third = third_ref[rows, :] + third_far_ref[rows, :].astype(jnp.float32)
        back, gain_sum, bias_sum = unit_back(third, h2_ref[rows, :], gain_ref[2:3, :])
        norm_ref[2:3, :] += gain_sum
        norm_ref[5:6, :] += bias_sum
        cross_exact = grad_ref[rows, :].astype(jnp.float32) + back
        cross_side = cross_exact.astype(jnp.bfloat16)
        self_exact_ref[rows, :] = cross_exact
        cross_side_ref[rows, :] = cross_side
        allowed = allowed_keys(low_ref[i], high_ref[i], 0, (keys, tile))
        for k in range(groups):
            part = slice(k * width, (k + 1) * width)
            mix_grad = times_transposed(cross_side, weights[k, 2 * width : 3 * width, :])
            mix_grad = mix_grad.astype(jnp.bfloat16)
            product = mix_grad.astype(jnp.float32) * mix_ref[rows, part].astype(jnp.float32)
            product = product.T
            queries = cq_ref[rows, part] * jnp.bfloat16(0.125)
            q_parts = [queries * head_mask(width, h) for h in range(heads)]
            grad_parts = [mix_grad * head_mask(width, h) for h in range(heads)]
            scores = [times_transposed(ck_ref[:, part], one) for one in q_parts]
            prob_grads = [times_transposed(cv_ref[:, part], one) for one in grad_parts]
            score_grads = []
            probs = []
            for h in range(heads):
                one = k * heads + h
                prob = jnp.exp(scores[h] - log_ref[i, one : one + 1, :])
                prob = jnp.where(allowed, prob, 0.0)
                lane = slice(h * HEAD, (h + 1) * HEAD)
                delta = jnp.sum(product[lane, :], axis=0, keepdims=True)
                score_grads.append((prob * (prob_grads[h] - delta)).astype(jnp.bfloat16))
                probs.append(prob.astype(jnp.bfloat16))
            dv_acc[:, part] += sum(dot(probs[h], grad_parts[h]) for h in range(heads))
            dk_acc[:, part] += sum(dot(score_grads[h], q_parts[h]) for h in range(heads))
            for h in range(heads):
                lane = slice(h * HEAD, (h + 1) * HEAD)
                query_turned[lane, :] = dot(turned[k, lane, :], score_grads[h])
            dcq_ref[rows, part] = (query_turned[...] * 0.125).T.astype(jnp.bfloat16)
        second = jnp.zeros(cross_exact.shape, jnp.float32)
        for k in range(groups):
            part = slice(k * width, (k + 1) * width)
            second += dot(dcq_ref[rows, part], weights[k, width : 2 * width, :])
        back, gain_sum, bias_sum = unit_back(second, h1_ref[rows, :], gain_ref[1:2, :])
        norm_ref[1:2, :] += gain_sum
        norm_ref[4:5, :] += bias_sum
        self_exact = self_exact_ref[rows, :] + back
        self_exact_ref[rows, :] = self_exact
        self_side = self_exact.astype(jnp.bfloat16)
        self_side_ref[rows, :] = self_side
        for k in range(groups):
            mix_grads[k][rows, :] = times_transposed(self_side, weights[k, 0:width, :]).astype(
                jnp.bfloat16
            )
        return carry

    lax.fori_loop(0, third_ref.shape[0] // tile, row_tile, 0)
    dck_ref[...] = dk_acc[...].astype(jnp.bfloat16)
    dcv_ref[...] = dv_acc[...].astype(jnp.bfloat16)
    text_part = jnp.zeros(text_ref.shape, jnp.float32)
    for k in range(groups):
        part = slice(k * width, (k + 1) * width)
        text_part += dot(dck_ref[:, part], weights[k, 3 * width : 4 * width, :text_width])
        text_part += dot(dcv_ref[:, part], value_rows(weights.at[k], heads, text_width))
    size = text_width // groups
    for k in range(groups):
        text_part_ref[k] = text_part[:, k * size : (k + 1) * size].astype(jnp.bfloat16)


def weight_grads_kernel(heads, added, side_ref, *refs):
    target = refs[-1]
    if added:
        far_ref, refs = refs[0], refs[1:]
    self_ref, n2_ref, cq_ref, mix_ref, cross_ref, dck_ref, dcv_ref, text_ref = refs[:8]
    mixes = refs[8:-1]
    width = heads * HEAD
    half = target.shape[1]
    text_width = text_ref.shape[1]
    for side in range(2):

        @pl.when(side_ref[0] == side)
        def _(side=side):
            for k in range(target.shape[0]):
                first = k * width
                def store(rows, lanes_of, product):
                    if added:
                        product += far_ref[k, rows, lanes_of].astype(jnp.float32)
                    target[k, rows, lanes_of] = product.astype(jnp.bfloat16)

                pairs = [
                    (mixes[k], 0, self_ref),
                    (cq_ref, first, n2_ref),
                    (mix_ref, first, cross_ref),
                ]
                for n, (left, lane, right) in enumerate(pairs):
                    low = max(n * width, side * half)
                    high = min((n + 1) * width, (side + 1) * half)
                    if low >= high:
                        continue
                    columns = left[:, lane + low - n * width : lane + high - n * width]
                    rows = slice(low - side * half, high - side * half)
                    store(rows, slice(0, target.shape[2]), contract_rows(columns, right[...]))
                if side == 0:
                    continue
                part = slice(first, first + width)
                keys = contract_rows(dck_ref[:, part], text_ref[...])
                values = contract_rows(dcv_ref[:, part], text_ref[...])
                begin = 3 * width - half
                beside = target.shape[2] - text_width
                rest = text_width - beside
                rows = slice(begin, begin + width)
                store(rows, slice(0, text_width), keys)
                store(rows, slice(text_width, target.shape[2]), values[:, :beside])
                rows = slice(begin + width, half)
                store(rows, slice(0, rest), values[: width // 2, beside:])
                store(rows, slice(rest, target.shape[2]), values[width // 2 :, beside:])


def weight_grads_call(heads, side, arrays, mixes, far=()):
    groups, width = len(mixes), arrays[0].shape[1]
    half = 9 * heads * HEAD // 4
    return pl.pallas_call(
        partial(weight_grads_kernel, heads, bool(far)),
        in_specs=[pl.BlockSpec(memory_space=pltpu.SMEM)]
        + [local_spec()] * (len(far) + len(arrays) + groups),
        out_specs=local_spec(),
        out_shape=jax.ShapeDtypeStruct((groups, half, width), jnp.bfloat16),
        compiler_params=pltpu.CompilerParams(vmem_limit_bytes=VMEM_BYTES),
        cost_estimate=about(10),
    )(side, *far, *arrays, *mixes)


def last_kernel(frames_ref, gain_ref, exact_ref, sum_ref, term_ref, out_ref, norm_ref):
    gradient = sum_ref[...].astype(jnp.float32) + term_ref[...]
    back, gain_sum, bias_sum = unit_back(
        gradient, frames_ref[...].astype(jnp.float32), gain_ref[0:1, :]
    )
    out_ref[...] = (exact_ref[...] + back).astype(jnp.bfloat16)
    norm_ref[0:1, :] = gain_sum
    norm_ref[1:2, :] = bias_sum


def last_call(frames, gains, exact, sums, term):
    rows, width = frames.shape
    return pl.pallas_call(
        last_kernel,
        in_specs=[local_spec()] * 5,
        out_specs=[local_spec()] * 2,
        out_shape=[
            jax.ShapeDtypeStruct((rows, width), jnp.bfloat16),
            jax.ShapeDtypeStruct((2, width), jnp.float32),
        ],
        compiler_params=pltpu.CompilerParams(vmem_limit_bytes=VMEM_BYTES),
        cost_estimate=about(4),
    )(frames, gains, exact, sums, term)


def ffn_end_kernel(core_ref, mine_ref, far_ref, in_ref, out_ref):
    units = in_ref.shape[1] // 2
    for source, side in ((mine_ref, core_ref[0]), (far_ref, 1 - core_ref[0])):
        part = pl.ds(pl.multiple_of(side * units, units), units)
        in_ref[:, part] = source[0, :, :units].astype(jnp.float32)
        out_ref[part, :] = source[0, :, units:].astype(jnp.float32).T


def ffn_end_call(core, mine, far):
    chips, features, columns = mine.shape
    source = pl.BlockSpec((1, features, columns), lambda c: (c, 0, 0))
    return pl.pallas_call(
        ffn_end_kernel,
        grid=(chips,),
        in_specs=[pl.BlockSpec(memory_space=pltpu.SMEM), source, source],
        out_specs=[
            pl.BlockSpec((features, columns), lambda c: (c, 0)),
            pl.BlockSpec((columns, features), lambda c: (0, c)),
        ],
        out_shape=[
            jax.ShapeDtypeStruct((chips * features, columns), jnp.float32),
            jax.ShapeDtypeStruct((columns, chips * features), jnp.float32),
        ],
        compiler_params=pltpu.CompilerParams(vmem_limit_bytes=VMEM_BYTES),
        cost_estimate=about(5),
    )(core, mine, far)


def qkv_grad_kernel(left_ref, right_ref, out_ref):
    out_ref[...] = contract_rows(left_ref[...], right_ref[...]).astype(jnp.bfloat16)


def qkv_grad_call(normed, packed_grad):
    rows, width = normed.shape
    columns = packed_grad.shape[1]
    tile = min(256, width)
    return pl.pallas_call(
        qkv_grad_kernel,
        grid=(width // tile,),
        in_specs=[
            pl.BlockSpec((rows, tile), lambda i: (0, i)),
            pl.BlockSpec((rows, columns), lambda i: (0, 0)),
        ],
        out_specs=pl.BlockSpec((tile, columns), lambda i: (i, 0)),
        out_shape=jax.ShapeDtypeStruct((width, columns), jnp.bfloat16),
        compiler_params=pltpu.CompilerParams(vmem_limit_bytes=VMEM_BYTES),
        cost_estimate=about(5),
    )(normed, packed_grad)


def qkv_end_kernel(heads, core_ref, mine_ref, far_ref, out_ref):
    width = heads * HEAD
    size = mine_ref.shape[0]
    for source, side in ((mine_ref, core_ref[0]), (far_ref, 1 - core_ref[0])):
        columns = [
            source[:, c * width + h * HEAD : c * width + (h + 1) * HEAD]
            for h in range(heads)
            for c in range(3)
        ]
        rows = pl.ds(pl.multiple_of(side * size, size), size)
        out_ref[rows, :] = jnp.concatenate(columns, 1).astype(jnp.float32)


def qkv_end_call(heads, core, mine, far):
    rows, columns = mine.shape
    return pl.pallas_call(
        partial(qkv_end_kernel, heads),
        in_specs=[pl.BlockSpec(memory_space=pltpu.SMEM)] + [local_spec()] * 2,
        out_specs=local_spec(),
        out_shape=jax.ShapeDtypeStruct((2 * rows, columns), jnp.float32),
        compiler_params=pltpu.CompilerParams(vmem_limit_bytes=VMEM_BYTES),
        cost_estimate=about(3),
    )(core, mine, far)


def small_end_kernel(heads, core_ref, mine_ref, far_ref, *refs):
    self_ref, query_ref, cross_ref, pair_ref, joined = refs
    width = heads * HEAD
    text_width = pair_ref.shape[0]
    half = joined.shape[0] // 2
    for source, side in ((mine_ref, core_ref[0]), (far_ref, 1 - core_ref[0])):
        joined[pl.ds(pl.multiple_of(side * half, half), half), :] = source[...]
    self_ref[...] = joined[0:width, :].astype(jnp.float32)
    query_ref[...] = joined[width : 2 * width, :].astype(jnp.float32).T
    cross_ref[...] = joined[2 * width : 3 * width, :].astype(jnp.float32)
    keys = joined[3 * width : 4 * width, :text_width]
    values = value_rows(joined, heads, text_width)
    for h in range(heads):
        part = slice(h * HEAD, (h + 1) * HEAD)
        both = jnp.concatenate([keys[part, :], values[part, :]], 0)
        pair_ref[:, 2 * h * HEAD : 2 * (h + 1) * HEAD] = both.astype(jnp.float32).T


def small_end_call(heads, text_width, core, mine, far):
    width = mine.shape[1]
    head_width = heads * HEAD
    shapes = [
        (head_width, width),
        (width, head_width),
        (head_width, width),
        (text_width, 2 * head_width),
    ]
    return pl.pallas_call(
        partial(small_end_kernel, heads),
        in_specs=[pl.BlockSpec(memory_space=pltpu.SMEM)] + [local_spec()] * 2,
        out_specs=[local_spec()] * 4,
        out_shape=[jax.ShapeDtypeStruct(shape, jnp.float32) for shape in shapes],
        scratch_shapes=[pltpu.VMEM((9 * head_width // 2, width), jnp.bfloat16)],
        compiler_params=pltpu.CompilerParams(vmem_limit_bytes=VMEM_BYTES),
        cost_estimate=about(4),
    )(core, mine, far)


def local_spec():
    return pl.BlockSpec(memory_space=pltpu.VMEM)


def middle_specs(plain):
    return (
        [pl.BlockSpec(memory_space=pltpu.SMEM)]
        + [local_spec()] * plain
        + [pl.BlockSpec(memory_space=pl.ANY)] * 3
    )


def middle_call(heads, tile, core, low, high, inputs, text, gains, biases, split_weights, mixes):
    rows, width = inputs.shape
    keys = text.shape[0]
    groups = len(mixes)
    f32, bf16 = jnp.float32, jnp.bfloat16
    shapes = [
        ((rows, width), f32),
        ((rows, width), f32),
        ((rows, width), bf16),
        ((rows, width), bf16),
        ((rows, width), bf16),
        ((rows, width), bf16),
        ((keys, width), bf16),
        ((keys, width), bf16),
        ((rows // tile, groups * heads, tile), f32),
    ]
    return pl.pallas_call(
        partial(middle_kernel, heads, tile),
        in_specs=middle_specs(6) + [local_spec()] * groups,
        out_specs=[local_spec()] * len(shapes),
        out_shape=[jax.ShapeDtypeStruct(*one) for one in shapes],
        scratch_shapes=[
            pltpu.VMEM((groups, *split_weights[0].shape), bf16),
            pltpu.VMEM((groups, heads * HEAD, keys), bf16),
            pltpu.VMEM((heads * HEAD, tile), f32),
            pltpu.SemaphoreType.DMA((2 * groups - 1,)),
        ],
        compiler_params=pltpu.CompilerParams(vmem_limit_bytes=VMEM_BYTES),
        cost_estimate=about(30),
    )(core, lanes(low, tile), lanes(high, tile), inputs, text, gains, biases, *split_weights, *mixes)


def middle_back_call(heads, tile, core, low, high, text, gains, saved, split_weights):
    rows, width = saved[0].shape
    keys = text.shape[0]
    groups = width // (heads * HEAD)
    f32, bf16 = jnp.float32, jnp.bfloat16
    shapes = [
        ((rows, width), bf16),
        ((rows, width), bf16),
        ((keys, width), bf16),
        ((keys, width), bf16),
        ((rows, width), f32),
        ((rows, width), bf16),
        ((6, width), f32),
        ((groups, keys, text.shape[1] // groups), bf16),
    ] + [((rows, heads * HEAD), bf16)] * groups
    return pl.pallas_call(
        partial(middle_back_kernel, heads, tile),
        in_specs=middle_specs(4 + len(saved)),
        out_specs=[local_spec()] * len(shapes),
        out_shape=[jax.ShapeDtypeStruct(*one) for one in shapes],
        scratch_shapes=[
            pltpu.VMEM((groups, *split_weights[0].shape), bf16),
            pltpu.VMEM((groups, heads * HEAD, keys), bf16),
            pltpu.VMEM((heads * HEAD, tile), f32),
            pltpu.VMEM((keys, width), f32),
            pltpu.VMEM((keys, width), f32),
            pltpu.SemaphoreType.DMA((2 * groups - 1,)),
        ],
        compiler_params=pltpu.CompilerParams(vmem_limit_bytes=VMEM_BYTES),
        cost_estimate=about(40),
    )(core, lanes(low, tile), lanes(high, tile), text, gains, *saved, *split_weights)


def lanes(values, size):
    return values.astype(jnp.int32).reshape(-1, 1, size)


def attend_call(q, k, v, columns, groups, heads, low, high, first, last, query_size, key_size):
    width = heads * HEAD
    rows, keys = q.shape[0], k.shape[0]
    blocks = rows // query_size
    spec = lambda size, column: pl.BlockSpec((size, width), lambda g, i, *_: (0, column + g))
    vector = pl.BlockSpec((1, 1, query_size), lambda g, i, *_: (i, 0, 0))
    q_column = columns[0]
    return pl.pallas_call(
        partial(attend_kernel, heads, key_size),
        grid_spec=pltpu.PrefetchScalarGridSpec(
            num_scalar_prefetch=2,
            grid=(groups, blocks),
            in_specs=[
                vector,
                vector,
                pl.BlockSpec((query_size, width), lambda g, i, *_: (i, q_column + g)),
                spec(keys, columns[1]),
                spec(keys, columns[2]),
            ],
            out_specs=[
                pl.BlockSpec((query_size, width), lambda g, i, *_: (i, g)),
                pl.BlockSpec((1, 1, heads, query_size), lambda g, i, *_: (g, i, 0, 0)),
            ],
            scratch_shapes=[
                pltpu.VMEM((keys // key_size, width, key_size), jnp.bfloat16),
                pltpu.VMEM((width, query_size), jnp.float32),
            ],
        ),
        out_shape=[
            jax.ShapeDtypeStruct((rows, groups * width), jnp.bfloat16),
            jax.ShapeDtypeStruct((groups, blocks, heads, query_size), jnp.float32),
        ],
        compiler_params=pltpu.CompilerParams(vmem_limit_bytes=VMEM_BYTES),
        cost_estimate=about(30 if groups == 1 else 17),
    )(first, last, lanes(low, query_size), lanes(high, query_size), q, k, v)


def back_scratch(heads, blocks, query_size, key_size):
    width = heads * HEAD
    return [
        pltpu.VMEM((blocks, heads, query_size, width), jnp.bfloat16),
        pltpu.VMEM((blocks, heads, query_size, width), jnp.bfloat16),
        pltpu.VMEM((width, key_size), jnp.bfloat16),
        pltpu.VMEM((blocks, heads, query_size), jnp.float32),
        pltpu.VMEM((blocks, width, query_size), jnp.float32),
        pltpu.VMEM((key_size, width), jnp.float32),
        pltpu.VMEM((key_size, width), jnp.float32),
    ]


def packed_back_call(
    qkv, out, parts, logs, heads, group, low, high, first, last, query_size, key_size
):
    rows, width = out.shape
    blocks = rows // query_size
    whole = lambda shape: pl.BlockSpec(shape, lambda g, j, *_: (0,) * len(shape))
    vector = whole((blocks, 1, query_size))
    return pl.pallas_call(
        partial(packed_back_kernel, heads, query_size, key_size, len(parts)),
        grid_spec=pltpu.PrefetchScalarGridSpec(
            num_scalar_prefetch=3,
            grid=(1, rows // key_size),
            in_specs=[vector, vector, whole(qkv.shape), whole(out.shape)]
            + [whole(part.shape) for part in parts]
            + [whole(logs.shape)],
            out_specs=whole(qkv.shape),
            scratch_shapes=back_scratch(heads, blocks, query_size, key_size)
            + [pltpu.VMEM(out.shape, jnp.bfloat16)],
        ),
        out_shape=jax.ShapeDtypeStruct(qkv.shape, jnp.bfloat16),
        compiler_params=pltpu.CompilerParams(vmem_limit_bytes=VMEM_BYTES),
        cost_estimate=about(30),
    )(
        first,
        last,
        group,
        lanes(low, query_size),
        lanes(high, query_size),
        qkv,
        out,
        *parts,
        logs,
    )


def attend_back_call(q, k, v, out, grad, logs, groups, heads, low, high, first, last, query_size, key_size):
    width = heads * HEAD
    rows, keys = q.shape[0], k.shape[0]
    blocks = rows // query_size
    column = lambda size: pl.BlockSpec((size, width), lambda g, j, *_: (0, g))
    vector = pl.BlockSpec((blocks, 1, query_size), lambda g, j, *_: (0, 0, 0))
    return pl.pallas_call(
        partial(attend_back_kernel, heads, query_size, key_size),
        grid_spec=pltpu.PrefetchScalarGridSpec(
            num_scalar_prefetch=2,
            grid=(groups, keys // key_size),
            in_specs=[
                vector,
                vector,
                column(rows),
                column(keys),
                column(keys),
                column(rows),
                column(rows),
                pl.BlockSpec((1, blocks, heads, query_size), lambda g, j, *_: (g, 0, 0, 0)),
            ],
            out_specs=[column(rows), column(keys), column(keys)],
            scratch_shapes=back_scratch(heads, blocks, query_size, key_size),
        ),
        out_shape=[
            jax.ShapeDtypeStruct((rows, groups * width), jnp.bfloat16),
            jax.ShapeDtypeStruct((keys, groups * width), jnp.bfloat16),
            jax.ShapeDtypeStruct((keys, groups * width), jnp.bfloat16),
        ],
        compiler_params=pltpu.CompilerParams(vmem_limit_bytes=VMEM_BYTES),
        cost_estimate=about(6 * groups),
    )(first, last, lanes(low, query_size), lanes(high, query_size), q, k, v, out, grad, logs)


def per_device(
    frames,
    text_states,
    clip_lengths,
    text_lengths,
    norm_gains,
    norm_biases,
    self_qkv,
    self_out,
    cross_query,
    cross_kv,
    cross_out,
    ffn_in,
    ffn_out,
    out_grad,
):
    groups = lax.axis_size("tensor")
    chips = lax.axis_size("chip")
    group = lax.axis_index("tensor")
    chip = lax.axis_index("chip")
    core = lax.axis_index("core")
    bf16 = jnp.bfloat16
    frame_count, width = frames.shape
    own_rows = frame_count // groups
    offset = group * own_rows
    clip_count, text_slots, text_width = text_states.shape
    head_count = self_out.shape[0] // HEAD
    all_heads = head_count * groups
    ends = jnp.cumsum(clip_lengths[0])
    starts = ends - clip_lengths[0]
    positions = jnp.arange(frame_count, dtype=jnp.int32)[:, None]
    clip_first = jnp.max(jnp.where(positions >= starts, starts, 0), axis=1)
    clip_stop = jnp.min(jnp.where(positions < ends, ends, frame_count), axis=1)
    block = min(256, own_rows)
    blocks = jnp.arange(frame_count // block, dtype=jnp.int32)
    self_low, self_high = clip_first, positions[:, 0]
    wide = min(2 * block, frame_count)
    wides = jnp.arange(frame_count // wide, dtype=jnp.int32)
    self_keys = (clip_first[::wide] // block, (wides * wide + wide - 1) // block)
    self_queries = (blocks * block // wide, (clip_stop[block - 1 :: block] - 1) // wide)
    own_positions = offset + jnp.arange(own_rows, dtype=jnp.int32)[:, None]
    own_clip = jnp.sum((own_positions >= ends).astype(jnp.int32), axis=1)
    own_length = jnp.sum(
        jnp.where(own_clip[:, None] == jnp.arange(clip_count), text_lengths[0], 0), axis=1
    )
    cross_low = own_clip * text_slots
    cross_high = cross_low + own_length - 1
    cross_keys = (own_clip[::block], own_clip[block - 1 :: block])
    inside_first = jnp.clip(starts - offset, 0, own_rows)
    inside_stop = jnp.clip(ends - offset, 0, own_rows)
    cross_first = jnp.minimum(inside_first // block, own_rows // block - 1)
    cross_queries = (
        cross_first,
        jnp.where(inside_stop > inside_first, (inside_stop - 1) // block, cross_first - 1),
    )

    head_width = head_count * HEAD
    local = pack_call(head_count, self_out, cross_query, cross_out, cross_kv)
    pieces = local.reshape(2, chips, -1, width)
    half = ffn_out.shape[0] // 2
    piece = half // chips
    core_index = core.reshape(1).astype(jnp.int32)
    sent_piece = pick(pick(pieces, core, 0), chip, 0)
    sent_piece, frames, self_qkv, ffn_in, ffn_out, out_grad = phase(
        sent_piece, frames, self_qkv, ffn_in, ffn_out, out_grad
    )
    passed = [shift(sent_piece, k) for k in range(1, groups)]
    ffn_own = ffn_pack_call(core_index, ffn_in, ffn_out, chips)
    ffn_piece = pick(ffn_own, chip, 0).reshape(2 * piece, width)
    own_frames = lax.dynamic_slice_in_dim(frames, offset, own_rows, 0)
    grad_own_bf = lax.dynamic_slice_in_dim(out_grad, offset, own_rows, 0)
    rows_one, packed, w_qkv = first_call(
        head_count, frames, norm_gains, norm_biases, self_qkv, block
    )
    packed, ffn_piece, own_frames, grad_own_bf, *passed = phase(
        packed, ffn_piece, own_frames, grad_own_bf, *passed
    )
    if head_width % 128 == 0:
        self_parts, self_columns = (packed,) * 3, (0, 1, 2)
    else:
        self_parts, self_columns = jnp.split(packed, 3, 1), (0, 0, 0)
    steps = axis_bits("chip")
    joined = chip_gather_start(jnp.stack(passed))
    flipped = chip_gather_flips(joined, 0)
    ffn_all = gather(ffn_piece[None], "tensor")
    self_mix, self_logs = attend_call(
        *self_parts, self_columns, 1, head_count, self_low, self_high, *self_keys, wide, block
    )
    joined = chip_gather_joins(joined, flipped, 0)
    self_mix, *joined = phase(self_mix, *joined)

    mix_blocks = self_mix.reshape(groups, own_rows, head_width)
    mixes = [pick(mix_blocks, group, 0)] + [
        shift(pick(mix_blocks, (group + k) % groups, 0), k) for k in range(1, groups)
    ]
    flipped = chip_gather_flips(joined, 1)
    joined = chip_gather_joins(joined, flipped, 1)
    for step in range(2, steps):
        joined = chip_gather_joins(joined, phase(*chip_gather_flips(joined, step)), step)
    mine = chip_gather_end(joined).reshape(groups - 1, -1, width)
    ffn_passed = [pick(ffn_all, (group + groups - k) % groups, 0) for k in range(1, groups)]
    ffn_stack = jnp.stack(ffn_passed[1:])[None]
    mine, ffn_stack, ffn_next, *mixes = phase(mine, ffn_stack, ffn_passed[0], *mixes)
    ffn_joined = chip_gather_start(ffn_next[None])
    ffn_late = gather(ffn_stack, "chip")
    ffn_late = ffn_late.reshape(chips, groups - 2, 2, piece, width)
    flipped = chip_gather_flips(ffn_joined, 0)
    ffn_joined = chip_gather_joins(ffn_joined, flipped, 0)
    far, *ffn_joined = phase(swap_core(mine), *ffn_joined)
    split_weights = (local, mine, far)
    ffn_flipped = chip_gather_flips(ffn_joined, 1)

    text_flat = text_states.reshape(clip_count * text_slots, text_width)
    shape = (head_count, block, core_index, cross_low, cross_high)
    after_self, after_cross, rows_two, rows_three, cross_q, cross_flat, cross_k, cross_v, cross_logs = (
        middle_call(
            *shape, own_frames, text_flat, norm_gains, norm_biases, split_weights, mixes
        )
    )

    grad_far = swap_core(grad_own_bf)
    rows_three, grad_far, *ffn_flipped = phase(rows_three, grad_far, *ffn_flipped)
    rows_far = swap_core(rows_three)
    ffn_joined = chip_gather_joins(ffn_joined, ffn_flipped, 1)
    for step in range(2, steps):
        ffn_joined = chip_gather_joins(ffn_joined, chip_gather_flips(ffn_joined, step), step)
    ffn_first = chip_gather_end(ffn_joined).reshape(chips, 2, piece, width)
    row_sets = (rows_three, rows_far, grad_own_bf, grad_far)
    ffn_part, *sums = ffn_call(*row_sets, (ffn_own, ffn_first), ())
    ffn_sum = scatter_sum(ffn_part.reshape(-1, 2 * half), "chip")
    ffn_late_part, out_own, out_far, third_own_grad, third_far = ffn_call(
        *row_sets, (ffn_late,), tuple(sums)
    )
    ffn_late_sum = scatter_sum(ffn_late_part.reshape(-1, 2 * half), "chip")
    saved = (
        third_own_grad,
        swap_core(third_far),
        grad_own_bf,
        after_self,
        after_cross,
        cross_q,
        cross_flat,
        cross_k,
        cross_v,
        cross_logs,
    )
    (
        cross_grad,
        cq_flat,
        ck_grad,
        cv_grad,
        self_side,
        self_grad,
        norm_part,
        text_part,
        *mix_grads,
    ) = middle_back_call(*shape, text_flat, norm_gains, saved, split_weights)

    mix_parts = [mix_grads[0]] + [shift(mix_grads[k], -k) for k in range(1, groups)]
    out_far = swap_core(out_far)
    arrays = (
        self_grad,
        rows_two,
        cq_flat,
        cross_flat,
        cross_grad,
        ck_grad,
        cv_grad,
        text_flat,
    )
    small_far = swap_core(weight_grads_call(head_count, 1 - core_index, arrays, mixes))
    small_part = weight_grads_call(head_count, core_index, arrays, mixes, (small_far,))

    def text_term(k):
        return pick(text_part, (group + groups - k) % groups, 0)

    orders = chip_orders()
    whole = chip_scatter_start(small_part.reshape(groups, chips, -1, width))
    state = settle(
        dict(
            whole=small_part,
            send=[chip_scatter_pick(whole[n], n, o, 0, True) for n, o in enumerate(orders)],
            text=text_term(1),
            out_far=out_far,
            ffn=list(ffn_sum.reshape(2, -1, 2 * half)),
            mix=mix_parts,
        )
    )
    mix_parts = state.pop("mix")
    text_run = shift(state["text"], 1)
    moved = [flip(one, o[0]) for one, o in zip(state["send"], orders)]
    ffn_run = shift(state["ffn"][1], 1)

    self_rest = (self_low, self_high, *self_queries, wide, block)
    if head_width % 128 == 0:
        packed_grad = packed_back_call(
            packed, self_mix, mix_parts, self_logs, head_count, group.reshape(1), *self_rest
        )
    else:
        mix_grad = jnp.concatenate([*mix_parts, *mix_parts], 0)
        mix_grad = lax.dynamic_slice_in_dim(
            mix_grad, (groups - group) % groups * own_rows, frame_count, 0
        )
        packed_grad = jnp.concatenate(
            attend_back_call(
                *self_parts, self_mix, mix_grad, self_logs, 1, head_count, *self_rest
            ),
            1,
        )
    state = settle(
        dict(
            state,
            grad=packed_grad,
            text=text_run,
            moved=moved,
            run=ffn_run,
            late=ffn_late_sum,
            h2=after_cross,
        )
    )

    def first_term(k):
        blocks = state["grad"].reshape(groups, own_rows, -1)
        rows = pick(blocks, (group + groups - k) % groups, 0)
        return times_transposed(rows, w_qkv)

    state = settle(dict(state, running=first_term(1).astype(bf16)))
    whole = chip_scatter_start(state["whole"].reshape(groups, chips, -1, width))
    small = [
        chip_scatter_pick(whole[n], n, o, 0, False) + one
        for n, (o, one) in enumerate(zip(orders, state["moved"]))
    ]
    late = list(state["late"].reshape(groups - 2, -1, 2 * half))
    state["run"] = state["run"] + late[0]
    ring_next = 1
    ffn_step = 0
    text_next = 2
    state["text"] = state["text"] + text_term(2)
    for hop in range(1, groups):
        arrived = shift(state["running"], 1)
        after_hop = dict(grad=state["grad"])
        if hop < steps:
            small = [
                chip_scatter_pick(one, n, o, hop, False)
                + flip(chip_scatter_pick(one, n, o, hop, True), o[hop])
                for n, (o, one) in enumerate(zip(orders, small))
            ]
            if hop == steps - 1:
                small = jnp.concatenate(small, 1)
        elif ring_next < groups:
            running_small = shift(small[1] if ring_next == 1 else state["ring"], 1)
            ring_next += 1
            after_hop["ring"] = running_small + small[ring_next % groups]
        after_hop["small"] = small
        after_hop["text"] = state["text"]
        if 1 < hop < groups - 1:
            text_next += 1
            after_hop["text"] = shift(state["text"], 1) + text_term(text_next % groups)
        if hop < groups - 1:
            after_hop["own"] = state["own"] if hop > 1 else state["ffn"][0]
            run = shift(state["run"], 1)
            after_hop["run"] = run + (late[hop] if hop < groups - 2 else after_hop["own"])
            late = after_hop["late"] = state["late"] if hop > 1 else late
        else:
            ffn = chip_gather_start(state["run"][None])
            after_hop["ffn"] = chip_gather_joins(ffn, chip_gather_flips(ffn, 0), 0)
            ffn_step = 1
        if hop == 1:
            mixed = state["h2"] + out_own + state["out_far"].astype(jnp.float32)
            after_hop["mixed"] = mixed.astype(bf16)
        else:
            after_hop["mixed"] = state["mixed"]
        if hop == 1:
            grad, run = phase(state["grad"], run)
            qkv_part = qkv_grad_call(rows_one, grad).reshape(2, width // 2, -1)
            far = swap_core(pick(qkv_part, 1 - core, 0))
            after_hop["qkv"] = pick(qkv_part, core, 0) + far
        elif hop - 2 < steps:
            after_hop["qkv"] = state["qkv"] + flip(state["qkv"], hop - 2)
        else:
            after_hop["qkv"] = state["qkv"]
        term = first_term((hop + 1) % groups)
        if hop < groups - 1:
            after_hop["running"] = (arrived.astype(jnp.float32) + term).astype(bf16)
        else:
            frames_grad, norm_first = last_call(own_frames, norm_gains, self_side, arrived, term)
            after_hop["frames_grad"] = frames_grad
            norm_rows = [norm_first[0:1], norm_part[1:3], norm_first[1:2], norm_part[4:6]]
            after_hop["norm"] = jnp.concatenate(norm_rows, 0).reshape(2, 3, width)
        state = settle(after_hop)
        small = state["small"]
        late = state.get("late")

    mixed, text = state["mixed"], state["text"]
    frames_grad, norm = state["frames_grad"], state["norm"]
    ring, ffn, qkv = state["ring"], state["ffn"], state["qkv"]
    small_step = norm_step = 0
    qkv_mine = qkv
    small_mine = small_far = small_grads = norm_parts = None
    ffn_mine = ffn_far = ffn_grads = qkv_far = qkv_grad = None
    small_sum = None
    while small_grads is None or ffn_grads is None or norm_parts is None or qkv_grad is None:
        if ring_next < groups:
            ring_next += 1
            ring = shift(ring, 1) + small[ring_next % groups]
        elif small_step < steps:
            small_sum = chip_gather_start(ring[None]) if small_sum is None else small_sum
            small_sum = chip_gather_joins(
                small_sum, chip_gather_flips(small_sum, small_step), small_step
            )
            small_step += 1
            if small_step == steps:
                small_mine = chip_gather_end(small_sum)[0].reshape(-1, width)
        elif small_far is None:
            small_far = swap_core(small_mine)
        elif small_grads is None:
            small_grads = small_end_call(
                head_count, text_width, core_index, small_mine, small_far
            )
        if norm_step == 0:
            norm = norm + swap_core(norm)
            norm_step += 1
        elif norm_step <= steps:
            norm = norm + flip(norm, norm_step - 1)
            norm_step += 1
        elif norm_parts is None:
            blocks_of = norm.reshape(2, 3, groups, -1)
            norm_parts = [pick(blocks_of, group, 2)] + [
                shift(pick(blocks_of, (group + k) % groups, 2), k) for k in range(1, groups)
            ]
        if ffn_step < steps:
            ffn = chip_gather_joins(ffn, chip_gather_flips(ffn, ffn_step), ffn_step)
            ffn_step += 1
        elif ffn_far is None:
            ffn_mine = chip_gather_end(ffn)[0]
            ffn_far = swap_core(ffn_mine)
        elif ffn_grads is None:
            ffn_grads = ffn_end_call(core_index, ffn_mine, ffn_far)
        if text_next < groups:
            text_next += 1
            text = shift(text, 1) + text_term(text_next % groups)
        elif qkv_far is None:
            qkv_far = swap_core(qkv_mine)
        elif qkv_grad is None:
            qkv_grad = qkv_end_call(head_count, core_index, qkv_mine, qkv_far)
        names = ["ring", "small", "small_sum", "small_mine", "small_far", "small_grads"]
        names += ["norm", "norm_parts", "ffn", "ffn_mine", "ffn_far", "ffn_grads"]
        names += ["text", "qkv_mine", "qkv_far", "qkv_grad"]
        values = (ring, small, small_sum, small_mine, small_far, small_grads, norm, norm_parts)
        values += (ffn, ffn_mine, ffn_far, ffn_grads, text, qkv_mine, qkv_far, qkv_grad)
        known = {name: one for name, one in zip(names, values) if one is not None}
        known = settle(known)
        ring, small, small_sum, small_mine, small_far, small_grads, norm, norm_parts = [
            known.get(name) for name in names[:8]
        ]
        ffn, ffn_mine, ffn_far, ffn_grads, text, qkv_mine, qkv_far, qkv_grad = [
            known.get(name) for name in names[8:]
        ]
    text_grad = text.astype(jnp.float32).reshape(clip_count, text_slots, -1)
    norm_grads = sum(norm_parts)
    ffn_in_grad, ffn_out_grad = ffn_grads
    so_grad, cq_grad, co_grad, kv_grad = small_grads
    return (
        mixed,
        frames_grad,
        text_grad,
        norm_grads,
        qkv_grad,
        so_grad,
        cq_grad,
        kv_grad,
        co_grad,
        ffn_in_grad,
        ffn_out_grad,
    )


def solution(mesh):
    rows, groups = mesh.devices.shape
    inner = Mesh(mesh.devices.reshape(rows // 2, 2, groups), ("chip", "core", "tensor"))
    data = ("chip", "core")
    in_specs = (
        P(data, None),
        P(data, None, None),
        P(data, None),
        P(data, None),
        P(),
        P(),
        P(None, "tensor"),
        P("tensor", None),
        P(None, "tensor"),
        P(None, "tensor"),
        P("tensor", None),
        P(None, "tensor"),
        P("tensor", None),
        P(data, None),
    )
    out_specs = (
        P((*data, "tensor"), None),
        P((*data, "tensor"), None),
        P(data, None, "tensor"),
        P(None, None, "tensor"),
        P(None, "tensor"),
        P("tensor", None),
        P(None, "tensor"),
        P(None, "tensor"),
        P("tensor", None),
        P(None, "tensor"),
        P("tensor", None),
    )
    return jax.shard_map(
        per_device, mesh=inner, in_specs=in_specs, out_specs=out_specs, check_vma=False
    )
```

```python
from functools import partial

import jax
import jax.numpy as jnp
from jax import lax
from jax.experimental import pallas as pl
from jax.experimental.pallas import tpu as pltpu
from jax.sharding import Mesh
from jax.sharding import PartitionSpec as P

HEAD = 64


EPSILON = 1e-05
NEGATIVE = -1e30
VMEM_BYTES = 56 * 1024 * 1024
SCALE = 0.02


def about(microseconds):
    return pl.CostEstimate(
        flops=int(microseconds * SCALE * 1.1e9), bytes_accessed=int(microseconds * SCALE * 3e6), transcendentals=0
    )


def contract_rows(left_side, right_side):
    return lax.dot_general(
        left_side, right_side, (((0,), (0,)), ((), ())), preferred_element_type=jnp.float32
    )


def times_transposed(left_side, right_side):
    return lax.dot_general(
        left_side, right_side, (((1,), (1,)), ((), ())), preferred_element_type=jnp.float32
    )


def phase(*arrays):
    return lax.optimization_barrier(arrays)


def settle(state):
    return lax.optimization_barrier(state)


def axis_bits(name):
    return lax.axis_size(name).bit_length() - 1


def shift(array, steps):
    size = lax.axis_size("tensor")
    return lax.ppermute(array, "tensor", [(i, (i + steps) % size) for i in range(size)])


def flip(array, bit):
    pairs = [(i, i ^ (1 << bit)) for i in range(lax.axis_size("chip"))]
    return lax.ppermute(array, "chip", pairs)


def swap_core(array):
    return lax.ppermute(array, "core", [(0, 1), (1, 0)])


def in_order(mine, other, first, axis):
    return jnp.concatenate(
        [jnp.where(first, mine, other), jnp.where(first, other, mine)], axis
    )


def chip_orders():
    bits = axis_bits("chip")
    return [(0, 1), (1, 0)] if bits == 2 else [tuple(range(bits))]


def halves(array, axis):
    return jnp.split(array, len(chip_orders()), axis)


def chip_gather_start(array):
    bits = axis_bits("chip")
    return [
        part.reshape(part.shape[0], *(1,) * bits, *part.shape[1:]) for part in halves(array, 1)
    ]


def chip_gather_flips(parts, step):
    return [flip(part, order[step]) for part, order in zip(parts, chip_orders())]


def chip_gather_joins(parts, others, step):
    bits = axis_bits("chip")
    chip = lax.axis_index("chip")
    return [
        in_order(part, other, (chip >> order[step]) % 2 == 0, bits - order[step])
        for part, other, order in zip(parts, others, chip_orders())
    ]


def chip_gather_end(parts):
    whole = jnp.concatenate(parts, -2)
    return whole.reshape(whole.shape[0], -1, *whole.shape[-2:])


def pick(array, index, axis):
    return lax.dynamic_index_in_dim(array, index, axis, keepdims=False)


def chip_scatter_start(array):
    bits = axis_bits("chip")
    return [array.reshape(array.shape[0], *(2,) * bits, *array.shape[2:])] * len(chip_orders())


def chip_scatter_pick(part, number, order, step, other_side):
    side = (lax.axis_index("chip") >> order[step]) % 2
    left = sorted(set(order) - set(order[:step]), reverse=True)
    picked = pick(part, 1 - side if other_side else side, 1 + left.index(order[step]))
    return halves(picked, picked.ndim - 2)[number] if step == 0 else picked


def gather(array, axes):
    return lax.all_gather(array, axes, axis=0, tiled=True)


def scatter_sum(array, axes):
    return lax.psum_scatter(array, axes, scatter_dimension=0, tiled=True)


def dot(left, right):
    return jnp.dot(left, right, preferred_element_type=jnp.float32)


def head_mask(width, head):
    lane = lax.broadcasted_iota(jnp.int32, (1, width), 1)
    return ((lane >= head * HEAD) & (lane < (head + 1) * HEAD)).astype(jnp.float32).astype(jnp.bfloat16)


def allowed_keys(low, high, key_first, shape):
    key = key_first + lax.broadcasted_iota(jnp.int32, shape, 0)
    return (key >= low) & (key <= high)


def attend_kernel(heads, key_size, first_ref, last_ref, low_ref, high_ref, q_ref, k_ref, v_ref, out_ref, log_ref, turned, acc):
    block = pl.program_id(1)
    rows, width = q_ref.shape
    key_blocks = k_ref.shape[0] // key_size

    @pl.when(block == 0)
    def _():
        for j in range(key_blocks):
            turned[j] = v_ref[j * key_size : (j + 1) * key_size, :].T

    q_rows = q_ref[...] * jnp.bfloat16(0.125)
    q_heads = [q_rows * head_mask(width, h) for h in range(heads)]
    low, high = low_ref[0], high_ref[0]
    acc[...] = jnp.zeros_like(acc)
    last = last_ref[block]

    def step(t, state):
        j = last - t
        key_first = pl.multiple_of(j * key_size, key_size)
        k_rows = k_ref[pl.ds(key_first, key_size), :]
        allowed = allowed_keys(low, high, key_first, (key_size, rows))
        fresh, parts = [], []
        scores = [jnp.where(allowed, times_transposed(k_rows, q), NEGATIVE) for q in q_heads]
        tops = [
            jnp.maximum(state[h][0], jnp.max(scores[h], axis=0, keepdims=True))
            for h in range(heads)
        ]
        probs = [jnp.exp(scores[h] - tops[h]) for h in range(heads)]
        for h in range(heads):
            top, total = state[h]
            shrink = jnp.exp(top - tops[h])
            part = slice(h * HEAD, (h + 1) * HEAD)
            parts.append(
                acc[part, :] * shrink + dot(turned[j, part, :], probs[h].astype(jnp.bfloat16))
            )
            fresh.append(
                (tops[h], total * shrink + jnp.sum(probs[h], axis=0, keepdims=True))
            )
        acc[...] = jnp.concatenate(parts, 0)
        return tuple(fresh)

    begin = (jnp.full((1, rows), NEGATIVE, jnp.float32), jnp.zeros((1, rows), jnp.float32))
    state = lax.fori_loop(0, last - first_ref[block] + 1, step, (begin,) * heads)
    for h in range(heads):
        top, total = state[h]
        part = slice(h * HEAD, (h + 1) * HEAD)
        acc[part, :] = acc[part, :] / total
        log_ref[0, 0, h : h + 1, :] = top + jnp.log(total)
    out_ref[...] = acc[...].T.astype(jnp.bfloat16)


def attend_back_kernel(heads, query_size, key_size, first_ref, last_ref, low_ref, high_ref, q_ref, k_ref, v_ref, out_ref, grad_ref, log_ref, dq_ref, dk_ref, dv_ref, q_heads, grad_heads, turned, delta, dq_acc, dk_acc, dv_acc):
    block = pl.program_id(1)
    width = q_ref.shape[1]
    query_blocks = q_ref.shape[0] // query_size

    @pl.when(block == 0)
    def _():
        for i in range(query_blocks):
            rows = slice(i * query_size, (i + 1) * query_size)
            product = grad_ref[rows, :].astype(jnp.float32) * out_ref[rows, :].astype(jnp.float32)
            product = product.T
            for h in range(heads):
                mask = head_mask(width, h)
                q_heads[i, h] = q_ref[rows, :] * (mask * jnp.bfloat16(0.125))
                grad_heads[i, h] = grad_ref[rows, :] * mask
                delta[i, h : h + 1, :] = jnp.sum(
                    product[h * HEAD : (h + 1) * HEAD, :], axis=0, keepdims=True
                )
        dq_acc[...] = jnp.zeros_like(dq_acc)

    key_first = pl.multiple_of(block * key_size, key_size)
    k_rows = k_ref[pl.ds(key_first, key_size), :]
    v_rows = v_ref[pl.ds(key_first, key_size), :]
    turned[...] = k_rows.T
    dk_acc[...] = jnp.zeros_like(dk_acc)
    dv_acc[...] = jnp.zeros_like(dv_acc)

    def step(i, carry):
        allowed = allowed_keys(low_ref[i], high_ref[i], key_first, (key_size, query_size))
        scores = [times_transposed(k_rows, q_heads[i, h]) for h in range(heads)]
        prob_grads = [times_transposed(v_rows, grad_heads[i, h]) for h in range(heads)]
        probs = [
            jnp.where(allowed, jnp.exp(scores[h] - log_ref[0, i, h : h + 1, :]), 0.0)
            for h in range(heads)
        ]
        score_grads = [
            (probs[h] * (prob_grads[h] - delta[i, h : h + 1, :])).astype(jnp.bfloat16)
            for h in range(heads)
        ]
        dv_acc[...] += sum(
            dot(probs[h].astype(jnp.bfloat16), grad_heads[i, h]) for h in range(heads)
        )
        dk_acc[...] += sum(dot(score_grads[h], q_heads[i, h]) for h in range(heads))
        dq_acc[i] += jnp.concatenate(
            [
                dot(turned[h * HEAD : (h + 1) * HEAD, :], score_grads[h])
                for h in range(heads)
            ],
            0,
        )
        return carry

    lax.fori_loop(first_ref[block], last_ref[block] + 1, step, 0)
    dk_ref[pl.ds(key_first, key_size), :] = dk_acc[...].astype(jnp.bfloat16)
    dv_ref[pl.ds(key_first, key_size), :] = dv_acc[...].astype(jnp.bfloat16)

    @pl.when(block == pl.num_programs(1) - 1)
    def _():
        for i in range(query_blocks):
            dq_ref[i * query_size : (i + 1) * query_size, :] = (
                (dq_acc[i] * 0.125).T.astype(jnp.bfloat16)
            )


def packed_back_kernel(heads, query_size, key_size, groups, *refs):
    first_ref, last_ref, group_ref, low_ref, high_ref, qkv_ref, out_ref = refs[:7]
    parts = refs[7 : 7 + groups]
    log_ref, dqkv_ref = refs[7 + groups : 9 + groups]
    grad_ref = refs[-1]
    width = out_ref.shape[1]
    size = parts[0].shape[0]

    @pl.when(pl.program_id(1) == 0)
    def _():
        for k in range(groups):
            owner = lax.rem(group_ref[0] + k, groups)
            grad_ref[pl.ds(pl.multiple_of(owner * size, size), size), :] = parts[k][...]

    views = [[r.at[:, c * width : (c + 1) * width] for c in range(3)] for r in (qkv_ref, dqkv_ref)]
    attend_back_kernel(
        heads,
        query_size,
        key_size,
        first_ref,
        last_ref,
        low_ref,
        high_ref,
        *views[0],
        out_ref,
        grad_ref,
        log_ref,
        *views[1],
        *refs[9 + groups : -1],
    )


def ffn_kernel(tile, carried, *refs):
    n_own_ref, n_far_ref, g_own_ref, g_far_ref = refs[:4]
    step = pl.program_id(0)
    if carried:
        weights_ref, out_in_ref, back_in_ref = refs[4:7]
    else:
        weights_ref = refs[-1]
        for i, source in enumerate(refs[4:6]):

            @pl.when(step == i)
            def _(source=source):
                weights_ref[:, 0] = source[...]

    results = refs[7:12] if carried else refs[6:9]
    z_rows, du_rows, out_acc, back_acc, n_ref, n_turned, g_ref, g_turned = (
        refs[12:20] if carried else refs[9:17]
    )
    grads_ref = results[0]
    rows, width = n_ref.shape
    chips, piece = weights_ref.shape[0], weights_ref.shape[3]
    units = chips * piece
    share = width // chips
    w_in = weights_ref[:, 0, 0].reshape(units, width)
    w_out = weights_ref[:, 0, 1].reshape(units, width)

    @pl.when(step == 0)
    def _():
        half = rows // 2
        for joined, turned, parts in (
            (n_ref, n_turned, (n_own_ref, n_far_ref)),
            (g_ref, g_turned, (g_own_ref, g_far_ref)),
        ):
            for i, source in enumerate(parts):
                joined[i * half : (i + 1) * half, :] = source[...]
                turned[:, i * half : (i + 1) * half] = source[...].T
        if carried:
            out_acc[...] = out_in_ref[...].astype(jnp.float32)
            back_acc[...] = back_in_ref[...].astype(jnp.float32)
        else:
            out_acc[...] = jnp.zeros_like(out_acc)
            back_acc[...] = jnp.zeros_like(back_acc)

    def row_tile(i, carry):
        part = pl.ds(pl.multiple_of(i * tile, tile), tile)
        pre = times_transposed(n_ref[part, :], w_in)
        scaled = lax.erf(pre * 0.7071067811865476)
        density = jnp.exp(pre * pre * -0.5) * 0.3989422804014327
        below = 0.5 + 0.5 * scaled
        hidden = (pre * below).astype(jnp.bfloat16)
        z_rows[part, :] = hidden
        out_acc[part, :] += dot(hidden, w_out)
        hidden_grad = times_transposed(g_ref[part, :], w_out)
        pre_grad = (hidden_grad * (below + pre * density)).astype(jnp.bfloat16)
        du_rows[part, :] = pre_grad
        back_acc[part, :] += dot(pre_grad, w_in)
        return carry

    lax.fori_loop(0, rows // tile, row_tile, 0, unroll=True)
    for c in range(chips):
        part = slice(c * share, (c + 1) * share)
        grads_ref[c, 0, :, :units] = dot(n_turned[part, :], du_rows[...]).astype(jnp.bfloat16)
        grads_ref[c, 0, :, units:] = dot(g_turned[part, :], z_rows[...]).astype(jnp.bfloat16)

    @pl.when(step == pl.num_programs(0) - 1)
    def _():
        own = rows // 2
        if carried:
            out_ref, out_far_ref, back_ref, back_far_ref = results[1:]
            out_ref[...] = out_acc[:own, :]
            out_far_ref[...] = out_acc[own:, :].astype(jnp.bfloat16)
            back_ref[...] = back_acc[:own, :]
            back_far_ref[...] = back_acc[own:, :].astype(jnp.bfloat16)
        else:
            results[1][...] = out_acc[...].astype(jnp.bfloat16)
            results[2][...] = back_acc[...].astype(jnp.bfloat16)


def ffn_call(n_own, n_far, g_own, g_far, weights, sums):
    rows, width = 2 * n_own.shape[0], n_own.shape[1]
    groups = len(weights) if not sums else weights[0].shape[1]
    chips, piece = weights[0].shape[0], weights[0].shape[-2]
    units = chips * piece
    whole = lambda shape: pl.BlockSpec(shape, lambda t: (0,) * len(shape))
    own = (rows // 2, width)
    grads = (chips, 1, width // chips, 2 * units)
    block = (chips, 1, 2, piece, width)
    f32, bf16 = jnp.float32, jnp.bfloat16
    scratch = [
        pltpu.VMEM((rows, units), bf16),
        pltpu.VMEM((rows, units), bf16),
        pltpu.VMEM((rows, width), f32),
        pltpu.VMEM((rows, width), f32),
        pltpu.VMEM((rows, width), bf16),
        pltpu.VMEM((width, rows), bf16),
        pltpu.VMEM((rows, width), bf16),
        pltpu.VMEM((width, rows), bf16),
    ]
    if sums:
        results = [(own, f32), (own, bf16), (own, f32), (own, bf16)]
        weight_specs = [pl.BlockSpec(block, lambda t: (0, t, 0, 0, 0))]
    else:
        results = [((rows, width), bf16)] * 2
        weight_specs = [whole(one.shape) for one in weights]
        scratch.append(pltpu.VMEM(block, bf16))
    return pl.pallas_call(
        partial(ffn_kernel, min(512, rows), bool(sums)),
        grid=(groups,),
        in_specs=[whole(own)] * 4 + weight_specs + [whole((rows, width))] * len(sums),
        out_specs=[pl.BlockSpec(grads, lambda t: (0, t, 0, 0))]
        + [whole(shape) for shape, _ in results],
        out_shape=[jax.ShapeDtypeStruct((chips, groups, *grads[2:]), bf16)]
        + [jax.ShapeDtypeStruct(*one) for one in results],
        scratch_shapes=scratch,
        compiler_params=pltpu.CompilerParams(vmem_limit_bytes=VMEM_BYTES),
        cost_estimate=about(23),
    )(n_own, n_far, g_own, g_far, *weights, *sums)


def ffn_pack_kernel(core_ref, in_ref, out_ref, packed_ref):
    chips, _, piece, _ = packed_ref.shape
    half = chips * piece
    first = pl.multiple_of(core_ref[0] * half, half)
    turned = in_ref[:, pl.ds(first, half)].T
    for c in range(chips):
        packed_ref[c, 0] = turned[c * piece : (c + 1) * piece, :]
        packed_ref[c, 1] = out_ref[pl.ds(first + c * piece, piece), :]


def ffn_pack_call(core, ffn_in, ffn_out, chips):
    units, width = ffn_out.shape
    return pl.pallas_call(
        ffn_pack_kernel,
        in_specs=[pl.BlockSpec(memory_space=pltpu.SMEM)] + [local_spec()] * 2,
        out_specs=local_spec(),
        out_shape=jax.ShapeDtypeStruct((chips, 2, units // 2 // chips, width), jnp.bfloat16),
        compiler_params=pltpu.CompilerParams(vmem_limit_bytes=VMEM_BYTES),
        cost_estimate=about(5),
    )(core, ffn_in, ffn_out)


def unit_norm(values):
    center = values - jnp.mean(values, axis=1, keepdims=True)
    inverse = lax.rsqrt(jnp.mean(center * center, axis=1, keepdims=True) + EPSILON)
    return center * inverse, inverse


def unit_back(gradient, values, gain):
    unit, inverse = unit_norm(values)
    scaled = gradient * gain
    inner = (
        scaled
        - jnp.mean(scaled, axis=1, keepdims=True)
        - unit * jnp.mean(scaled * unit, axis=1, keepdims=True)
    )
    return (
        inner * inverse,
        jnp.sum(gradient * unit, axis=0, keepdims=True),
        jnp.sum(gradient, axis=0, keepdims=True),
    )


def first_kernel(
    heads, frames_ref, gain_ref, bias_ref, weight_ref, normed_ref, packed_ref, ordered_ref
):
    @pl.when(pl.program_id(0) == 0)
    def _():
        columns = [
            weight_ref[:, (3 * h + c) * HEAD : (3 * h + c + 1) * HEAD]
            for c in range(3)
            for h in range(heads)
        ]
        ordered_ref[...] = jnp.concatenate(columns, 1)

    unit, _ = unit_norm(frames_ref[...].astype(jnp.float32))
    normed = (unit * gain_ref[0:1, :] + bias_ref[0:1, :]).astype(jnp.bfloat16)
    normed_ref[...] = normed
    packed_ref[...] = dot(normed, ordered_ref[...]).astype(jnp.bfloat16)


def first_call(heads, frames, gain, bias, weight, tile):
    rows, width = frames.shape
    columns = weight.shape[1]
    moving = lambda size: pl.BlockSpec((tile, size), lambda i: (i, 0))
    fixed = lambda shape: pl.BlockSpec(shape, lambda i: (0, 0))
    return pl.pallas_call(
        partial(first_kernel, heads),
        grid=(rows // tile,),
        in_specs=[moving(width), fixed(gain.shape), fixed(bias.shape), fixed(weight.shape)],
        out_specs=[moving(width), moving(columns), fixed(weight.shape)],
        out_shape=[
            jax.ShapeDtypeStruct((rows, width), jnp.bfloat16),
            jax.ShapeDtypeStruct((rows, columns), jnp.bfloat16),
            jax.ShapeDtypeStruct(weight.shape, jnp.bfloat16),
        ],
        compiler_params=pltpu.CompilerParams(vmem_limit_bytes=VMEM_BYTES),
        cost_estimate=about(9),
    )(frames, gain, bias, weight)


def value_rows(source, heads, text_width):
    width = heads * HEAD
    beside = source[3 * width : 4 * width, text_width:]
    rest = 2 * text_width - source.shape[1]
    below = source[4 * width : 4 * width + width // 2, :]
    return jnp.concatenate(
        [beside, jnp.concatenate([below[:, :rest], below[:, rest:]], 0)], 1
    )


def pack_kernel(heads, self_ref, query_ref, cross_ref, pair_ref, out_ref):
    width = heads * HEAD
    text_width = pair_ref.shape[0]
    out_ref[0:width, :] = self_ref[...]
    out_ref[width : 2 * width, :] = query_ref[...].T
    out_ref[2 * width : 3 * width, :] = cross_ref[...]
    turned = pair_ref[...].T
    keys, values = [
        jnp.concatenate(
            [turned[(2 * h + c) * HEAD : (2 * h + c + 1) * HEAD, :] for h in range(heads)], 0
        )
        for c in range(2)
    ]
    side = out_ref.shape[1] - text_width
    out_ref[3 * width : 4 * width, :text_width] = keys
    out_ref[3 * width : 4 * width, text_width:] = values[:, :side]
    rest = text_width - side
    out_ref[4 * width :, :rest] = values[: width // 2, side:]
    out_ref[4 * width :, rest:] = values[width // 2 :, side:]


def pack_call(heads, self_out, cross_query, cross_out, cross_kv):
    return pl.pallas_call(
        partial(pack_kernel, heads),
        in_specs=[local_spec()] * 4,
        out_specs=local_spec(),
        out_shape=jax.ShapeDtypeStruct((9 * heads * HEAD // 2, self_out.shape[1]), jnp.bfloat16),
        compiler_params=pltpu.CompilerParams(vmem_limit_bytes=VMEM_BYTES),
        cost_estimate=about(3),
    )(self_out, cross_query, cross_out, cross_kv)


def weight_copies(core_ref, local_ref, mine_ref, far_ref, weights, sems):
    half = mine_ref.shape[1]
    core = core_ref[0]
    copies = [pltpu.make_async_copy(local_ref, weights.at[0], sems.at[0])]
    for k in range(1, weights.shape[0]):
        for n, (source, side) in enumerate(((mine_ref, core), (far_ref, 1 - core))):
            rows = pl.ds(pl.multiple_of(side * half, half), half)
            copies.append(
                pltpu.make_async_copy(
                    source.at[k - 1], weights.at[k, rows], sems.at[2 * k - 1 + n]
                )
            )
    return copies


def middle_kernel(
    heads,
    tile,
    core_ref,
    low_ref,
    high_ref,
    inputs_ref,
    text_ref,
    gain_ref,
    bias_ref,
    local_ref,
    mine_ref,
    far_ref,
    *rest,
):
    groups = len(rest) - 9 - 4
    mixes = rest[:groups]
    h1_ref, h2_ref, n2_ref, n3_ref, cq_ref, mix_ref, ck_ref, cv_ref, log_ref = rest[
        groups : groups + 9
    ]
    weights, turned, mix_turned, sems = rest[groups + 9 :]
    width = heads * HEAD
    text_width = text_ref.shape[1]
    keys = text_ref.shape[0]
    copies = weight_copies(core_ref, local_ref, mine_ref, far_ref, weights, sems)
    for copy in copies:
        copy.start()
    text = text_ref[...]
    for k in range(groups):
        for copy in copies[max(0, 2 * k - 1) : 2 * k + 1]:
            copy.wait()
        part = slice(k * width, (k + 1) * width)
        key_weight = weights[k, 3 * width : 4 * width, :text_width]
        value_weight = value_rows(weights.at[k], heads, text_width)
        ck_ref[:, part] = times_transposed(text, key_weight).astype(jnp.bfloat16)
        cv_ref[:, part] = times_transposed(text, value_weight).astype(jnp.bfloat16)
        turned[k] = times_transposed(value_weight, text).astype(jnp.bfloat16)

    def row_tile(i, carry):
        rows = pl.ds(pl.multiple_of(i * tile, tile), tile)
        total = inputs_ref[rows, :].astype(jnp.float32)
        for k in range(groups):
            total += dot(mixes[k][rows, :], weights[k, 0:width, :])
        h1_ref[rows, :] = total
        unit, _ = unit_norm(total)
        normed = (unit * gain_ref[1:2, :] + bias_ref[1:2, :]).astype(jnp.bfloat16)
        n2_ref[rows, :] = normed
        allowed = allowed_keys(low_ref[i], high_ref[i], 0, (keys, tile))
        for k in range(groups):
            part = slice(k * width, (k + 1) * width)
            queries = times_transposed(normed, weights[k, width : 2 * width, :])
            queries = queries.astype(jnp.bfloat16)
            cq_ref[rows, part] = queries
            queries = queries * jnp.bfloat16(0.125)
            scores = [
                jnp.where(
                    allowed,
                    times_transposed(ck_ref[:, part], queries * head_mask(width, h)),
                    NEGATIVE,
                )
                for h in range(heads)
            ]
            tops = [jnp.max(one, axis=0, keepdims=True) for one in scores]
            probs = [jnp.exp(one - top) for one, top in zip(scores, tops)]
            sums = [jnp.sum(one, axis=0, keepdims=True) for one in probs]
            for h in range(heads):
                lane = slice(h * HEAD, (h + 1) * HEAD)
                mixed = dot(turned[k, lane, :], probs[h].astype(jnp.bfloat16))
                mix_turned[lane, :] = mixed / sums[h]
                log_ref[i, k * heads + h : k * heads + h + 1, :] = tops[h] + jnp.log(sums[h])
            mix_ref[rows, part] = mix_turned[...].T.astype(jnp.bfloat16)
        total = h1_ref[rows, :]
        for k in range(groups):
            part = slice(k * width, (k + 1) * width)
            total += dot(mix_ref[rows, part], weights[k, 2 * width : 3 * width, :])
        h2_ref[rows, :] = total
        unit, _ = unit_norm(total)
        n3_ref[rows, :] = (unit * gain_ref[2:3, :] + bias_ref[2:3, :]).astype(jnp.bfloat16)
        return carry

    lax.fori_loop(0, inputs_ref.shape[0] // tile, row_tile, 0)


def middle_back_kernel(
    heads,
    tile,
    core_ref,
    low_ref,
    high_ref,
    text_ref,
    gain_ref,
    third_ref,
    third_far_ref,
    grad_ref,
    h1_ref,
    h2_ref,
    cq_ref,
    mix_ref,
    ck_ref,
    cv_ref,
    log_ref,
    local_ref,
    mine_ref,
    far_ref,
    cross_side_ref,
    dcq_ref,
    dck_ref,
    dcv_ref,
    self_exact_ref,
    self_side_ref,
    norm_ref,
    text_part_ref,
    *rest,
):
    mix_grads = rest[:-6]
    weights, turned, query_turned, dk_acc, dv_acc, sems = rest[-6:]
    groups = weights.shape[0]
    width = heads * HEAD
    text_width = text_ref.shape[1]
    keys = text_ref.shape[0]
    copies = weight_copies(core_ref, local_ref, mine_ref, far_ref, weights, sems)
    for copy in copies:
        copy.start()
    text = text_ref[...]
    for k in range(groups):
        for copy in copies[max(0, 2 * k - 1) : 2 * k + 1]:
            copy.wait()
        key_weight = weights[k, 3 * width : 4 * width, :text_width]
        turned[k] = times_transposed(key_weight, text).astype(jnp.bfloat16)
    dk_acc[...] = jnp.zeros_like(dk_acc)
    dv_acc[...] = jnp.zeros_like(dv_acc)
    norm_ref[...] = jnp.zeros_like(norm_ref)

    def row_tile(i, carry):
        rows = pl.ds(pl.multiple_of(i * tile, tile), tile)
        third = third_ref[rows, :] + third_far_ref[rows, :].astype(jnp.float32)
        back, gain_sum, bias_sum = unit_back(third, h2_ref[rows, :], gain_ref[2:3, :])
        norm_ref[2:3, :] += gain_sum
        norm_ref[5:6, :] += bias_sum
        cross_exact = grad_ref[rows, :].astype(jnp.float32) + back
        cross_side = cross_exact.astype(jnp.bfloat16)
        self_exact_ref[rows, :] = cross_exact
        cross_side_ref[rows, :] = cross_side
        allowed = allowed_keys(low_ref[i], high_ref[i], 0, (keys, tile))
        for k in range(groups):
            part = slice(k * width, (k + 1) * width)
            mix_grad = times_transposed(cross_side, weights[k, 2 * width : 3 * width, :])
            mix_grad = mix_grad.astype(jnp.bfloat16)
            product = mix_grad.astype(jnp.float32) * mix_ref[rows, part].astype(jnp.float32)
            product = product.T
            queries = cq_ref[rows, part] * jnp.bfloat16(0.125)
            q_parts = [queries * head_mask(width, h) for h in range(heads)]
            grad_parts = [mix_grad * head_mask(width, h) for h in range(heads)]
            scores = [times_transposed(ck_ref[:, part], one) for one in q_parts]
            prob_grads = [times_transposed(cv_ref[:, part], one) for one in grad_parts]
            score_grads = []
            probs = []
            for h in range(heads):
                one = k * heads + h
                prob = jnp.exp(scores[h] - log_ref[i, one : one + 1, :])
                prob = jnp.where(allowed, prob, 0.0)
                lane = slice(h * HEAD, (h + 1) * HEAD)
                delta = jnp.sum(product[lane, :], axis=0, keepdims=True)
                score_grads.append((prob * (prob_grads[h] - delta)).astype(jnp.bfloat16))
                probs.append(prob.astype(jnp.bfloat16))
            dv_acc[:, part] += sum(dot(probs[h], grad_parts[h]) for h in range(heads))
            dk_acc[:, part] += sum(dot(score_grads[h], q_parts[h]) for h in range(heads))
            for h in range(heads):
                lane = slice(h * HEAD, (h + 1) * HEAD)
                query_turned[lane, :] = dot(turned[k, lane, :], score_grads[h])
            dcq_ref[rows, part] = (query_turned[...] * 0.125).T.astype(jnp.bfloat16)
        second = jnp.zeros(cross_exact.shape, jnp.float32)
        for k in range(groups):
            part = slice(k * width, (k + 1) * width)
            second += dot(dcq_ref[rows, part], weights[k, width : 2 * width, :])
        back, gain_sum, bias_sum = unit_back(second, h1_ref[rows, :], gain_ref[1:2, :])
        norm_ref[1:2, :] += gain_sum
        norm_ref[4:5, :] += bias_sum
        self_exact = self_exact_ref[rows, :] + back
        self_exact_ref[rows, :] = self_exact
        self_side = self_exact.astype(jnp.bfloat16)
        self_side_ref[rows, :] = self_side
        for k in range(groups):
            mix_grads[k][rows, :] = times_transposed(self_side, weights[k, 0:width, :]).astype(
                jnp.bfloat16
            )
        return carry

    lax.fori_loop(0, third_ref.shape[0] // tile, row_tile, 0)
    dck_ref[...] = dk_acc[...].astype(jnp.bfloat16)
    dcv_ref[...] = dv_acc[...].astype(jnp.bfloat16)
    text_part = jnp.zeros(text_ref.shape, jnp.float32)
    for k in range(groups):
        part = slice(k * width, (k + 1) * width)
        text_part += dot(dck_ref[:, part], weights[k, 3 * width : 4 * width, :text_width])
        text_part += dot(dcv_ref[:, part], value_rows(weights.at[k], heads, text_width))
    size = text_width // groups
    for k in range(groups):
        text_part_ref[k] = text_part[:, k * size : (k + 1) * size].astype(jnp.bfloat16)


def weight_grads_kernel(heads, added, side_ref, *refs):
    target = refs[-1]
    if added:
        far_ref, refs = refs[0], refs[1:]
    self_ref, n2_ref, cq_ref, mix_ref, cross_ref, dck_ref, dcv_ref, text_ref = refs[:8]
    mixes = refs[8:-1]
    width = heads * HEAD
    half = target.shape[1]
    text_width = text_ref.shape[1]
    for side in range(2):

        @pl.when(side_ref[0] == side)
        def _(side=side):
            for k in range(target.shape[0]):
                first = k * width
                def store(rows, lanes_of, product):
                    if added:
                        product += far_ref[k, rows, lanes_of].astype(jnp.float32)
                    target[k, rows, lanes_of] = product.astype(jnp.bfloat16)

                pairs = [
                    (mixes[k], 0, self_ref),
                    (cq_ref, first, n2_ref),
                    (mix_ref, first, cross_ref),
                ]
                for n, (left, lane, right) in enumerate(pairs):
                    low = max(n * width, side * half)
                    high = min((n + 1) * width, (side + 1) * half)
                    if low >= high:
                        continue
                    columns = left[:, lane + low - n * width : lane + high - n * width]
                    rows = slice(low - side * half, high - side * half)
                    store(rows, slice(0, target.shape[2]), contract_rows(columns, right[...]))
                if side == 0:
                    continue
                part = slice(first, first + width)
                keys = contract_rows(dck_ref[:, part], text_ref[...])
                values = contract_rows(dcv_ref[:, part], text_ref[...])
                begin = 3 * width - half
                beside = target.shape[2] - text_width
                rest = text_width - beside
                rows = slice(begin, begin + width)
                store(rows, slice(0, text_width), keys)
                store(rows, slice(text_width, target.shape[2]), values[:, :beside])
                rows = slice(begin + width, half)
                store(rows, slice(0, rest), values[: width // 2, beside:])
                store(rows, slice(rest, target.shape[2]), values[width // 2 :, beside:])


def weight_grads_call(heads, side, arrays, mixes, far=()):
    groups, width = len(mixes), arrays[0].shape[1]
    half = 9 * heads * HEAD // 4
    return pl.pallas_call(
        partial(weight_grads_kernel, heads, bool(far)),
        in_specs=[pl.BlockSpec(memory_space=pltpu.SMEM)]
        + [local_spec()] * (len(far) + len(arrays) + groups),
        out_specs=local_spec(),
        out_shape=jax.ShapeDtypeStruct((groups, half, width), jnp.bfloat16),
        compiler_params=pltpu.CompilerParams(vmem_limit_bytes=VMEM_BYTES),
        cost_estimate=about(10),
    )(side, *far, *arrays, *mixes)


def last_kernel(frames_ref, gain_ref, exact_ref, sum_ref, term_ref, out_ref, norm_ref):
    gradient = sum_ref[...].astype(jnp.float32) + term_ref[...]
    back, gain_sum, bias_sum = unit_back(
        gradient, frames_ref[...].astype(jnp.float32), gain_ref[0:1, :]
    )
    out_ref[...] = (exact_ref[...] + back).astype(jnp.bfloat16)
    norm_ref[0:1, :] = gain_sum
    norm_ref[1:2, :] = bias_sum


def last_call(frames, gains, exact, sums, term):
    rows, width = frames.shape
    return pl.pallas_call(
        last_kernel,
        in_specs=[local_spec()] * 5,
        out_specs=[local_spec()] * 2,
        out_shape=[
            jax.ShapeDtypeStruct((rows, width), jnp.bfloat16),
            jax.ShapeDtypeStruct((2, width), jnp.float32),
        ],
        compiler_params=pltpu.CompilerParams(vmem_limit_bytes=VMEM_BYTES),
        cost_estimate=about(4),
    )(frames, gains, exact, sums, term)


def ffn_end_kernel(core_ref, mine_ref, far_ref, in_ref, out_ref):
    units = in_ref.shape[1] // 2
    for source, side in ((mine_ref, core_ref[0]), (far_ref, 1 - core_ref[0])):
        part = pl.ds(pl.multiple_of(side * units, units), units)
        in_ref[:, part] = source[0, :, :units].astype(jnp.float32)
        out_ref[part, :] = source[0, :, units:].astype(jnp.float32).T


def ffn_end_call(core, mine, far):
    chips, features, columns = mine.shape
    source = pl.BlockSpec((1, features, columns), lambda c: (c, 0, 0))
    return pl.pallas_call(
        ffn_end_kernel,
        grid=(chips,),
        in_specs=[pl.BlockSpec(memory_space=pltpu.SMEM), source, source],
        out_specs=[
            pl.BlockSpec((features, columns), lambda c: (c, 0)),
            pl.BlockSpec((columns, features), lambda c: (0, c)),
        ],
        out_shape=[
            jax.ShapeDtypeStruct((chips * features, columns), jnp.float32),
            jax.ShapeDtypeStruct((columns, chips * features), jnp.float32),
        ],
        compiler_params=pltpu.CompilerParams(vmem_limit_bytes=VMEM_BYTES),
        cost_estimate=about(5),
    )(core, mine, far)


def qkv_grad_kernel(left_ref, right_ref, out_ref):
    out_ref[...] = contract_rows(left_ref[...], right_ref[...]).astype(jnp.bfloat16)


def qkv_grad_call(normed, packed_grad):
    rows, width = normed.shape
    columns = packed_grad.shape[1]
    tile = min(256, width)
    return pl.pallas_call(
        qkv_grad_kernel,
        grid=(width // tile,),
        in_specs=[
            pl.BlockSpec((rows, tile), lambda i: (0, i)),
            pl.BlockSpec((rows, columns), lambda i: (0, 0)),
        ],
        out_specs=pl.BlockSpec((tile, columns), lambda i: (i, 0)),
        out_shape=jax.ShapeDtypeStruct((width, columns), jnp.bfloat16),
        compiler_params=pltpu.CompilerParams(vmem_limit_bytes=VMEM_BYTES),
        cost_estimate=about(5),
    )(normed, packed_grad)


def qkv_end_kernel(heads, core_ref, mine_ref, far_ref, out_ref):
    width = heads * HEAD
    size = mine_ref.shape[0]
    for source, side in ((mine_ref, core_ref[0]), (far_ref, 1 - core_ref[0])):
        columns = [
            source[:, c * width + h * HEAD : c * width + (h + 1) * HEAD]
            for h in range(heads)
            for c in range(3)
        ]
        rows = pl.ds(pl.multiple_of(side * size, size), size)
        out_ref[rows, :] = jnp.concatenate(columns, 1).astype(jnp.float32)


def qkv_end_call(heads, core, mine, far):
    rows, columns = mine.shape
    return pl.pallas_call(
        partial(qkv_end_kernel, heads),
        in_specs=[pl.BlockSpec(memory_space=pltpu.SMEM)] + [local_spec()] * 2,
        out_specs=local_spec(),
        out_shape=jax.ShapeDtypeStruct((2 * rows, columns), jnp.float32),
        compiler_params=pltpu.CompilerParams(vmem_limit_bytes=VMEM_BYTES),
        cost_estimate=about(3),
    )(core, mine, far)


def small_end_kernel(heads, core_ref, mine_ref, far_ref, *refs):
    self_ref, query_ref, cross_ref, pair_ref, joined = refs
    width = heads * HEAD
    text_width = pair_ref.shape[0]
    half = joined.shape[0] // 2
    for source, side in ((mine_ref, core_ref[0]), (far_ref, 1 - core_ref[0])):
        joined[pl.ds(pl.multiple_of(side * half, half), half), :] = source[...]
    self_ref[...] = joined[0:width, :].astype(jnp.float32)
    query_ref[...] = joined[width : 2 * width, :].astype(jnp.float32).T
    cross_ref[...] = joined[2 * width : 3 * width, :].astype(jnp.float32)
    keys = joined[3 * width : 4 * width, :text_width]
    values = value_rows(joined, heads, text_width)
    for h in range(heads):
        part = slice(h * HEAD, (h + 1) * HEAD)
        both = jnp.concatenate([keys[part, :], values[part, :]], 0)
        pair_ref[:, 2 * h * HEAD : 2 * (h + 1) * HEAD] = both.astype(jnp.float32).T


def small_end_call(heads, text_width, core, mine, far):
    width = mine.shape[1]
    head_width = heads * HEAD
    shapes = [
        (head_width, width),
        (width, head_width),
        (head_width, width),
        (text_width, 2 * head_width),
    ]
    return pl.pallas_call(
        partial(small_end_kernel, heads),
        in_specs=[pl.BlockSpec(memory_space=pltpu.SMEM)] + [local_spec()] * 2,
        out_specs=[local_spec()] * 4,
        out_shape=[jax.ShapeDtypeStruct(shape, jnp.float32) for shape in shapes],
        scratch_shapes=[pltpu.VMEM((9 * head_width // 2, width), jnp.bfloat16)],
        compiler_params=pltpu.CompilerParams(vmem_limit_bytes=VMEM_BYTES),
        cost_estimate=about(4),
    )(core, mine, far)


def local_spec():
    return pl.BlockSpec(memory_space=pltpu.VMEM)


def middle_specs(plain):
    return (
        [pl.BlockSpec(memory_space=pltpu.SMEM)]
        + [local_spec()] * plain
        + [pl.BlockSpec(memory_space=pl.ANY)] * 3
    )


def middle_call(heads, tile, core, low, high, inputs, text, gains, biases, split_weights, mixes):
    rows, width = inputs.shape
    keys = text.shape[0]
    groups = len(mixes)
    f32, bf16 = jnp.float32, jnp.bfloat16
    shapes = [
        ((rows, width), f32),
        ((rows, width), f32),
        ((rows, width), bf16),
        ((rows, width), bf16),
        ((rows, width), bf16),
        ((rows, width), bf16),
        ((keys, width), bf16),
        ((keys, width), bf16),
        ((rows // tile, groups * heads, tile), f32),
    ]
    return pl.pallas_call(
        partial(middle_kernel, heads, tile),
        in_specs=middle_specs(6) + [local_spec()] * groups,
        out_specs=[local_spec()] * len(shapes),
        out_shape=[jax.ShapeDtypeStruct(*one) for one in shapes],
        scratch_shapes=[
            pltpu.VMEM((groups, *split_weights[0].shape), bf16),
            pltpu.VMEM((groups, heads * HEAD, keys), bf16),
            pltpu.VMEM((heads * HEAD, tile), f32),
            pltpu.SemaphoreType.DMA((2 * groups - 1,)),
        ],
        compiler_params=pltpu.CompilerParams(vmem_limit_bytes=VMEM_BYTES),
        cost_estimate=about(30),
    )(core, lanes(low, tile), lanes(high, tile), inputs, text, gains, biases, *split_weights, *mixes)


def middle_back_call(heads, tile, core, low, high, text, gains, saved, split_weights):
    rows, width = saved[0].shape
    keys = text.shape[0]
    groups = width // (heads * HEAD)
    f32, bf16 = jnp.float32, jnp.bfloat16
    shapes = [
        ((rows, width), bf16),
        ((rows, width), bf16),
        ((keys, width), bf16),
        ((keys, width), bf16),
        ((rows, width), f32),
        ((rows, width), bf16),
        ((6, width), f32),
        ((groups, keys, text.shape[1] // groups), bf16),
    ] + [((rows, heads * HEAD), bf16)] * groups
    return pl.pallas_call(
        partial(middle_back_kernel, heads, tile),
        in_specs=middle_specs(4 + len(saved)),
        out_specs=[local_spec()] * len(shapes),
        out_shape=[jax.ShapeDtypeStruct(*one) for one in shapes],
        scratch_shapes=[
            pltpu.VMEM((groups, *split_weights[0].shape), bf16),
            pltpu.VMEM((groups, heads * HEAD, keys), bf16),
            pltpu.VMEM((heads * HEAD, tile), f32),
            pltpu.VMEM((keys, width), f32),
            pltpu.VMEM((keys, width), f32),
            pltpu.SemaphoreType.DMA((2 * groups - 1,)),
        ],
        compiler_params=pltpu.CompilerParams(vmem_limit_bytes=VMEM_BYTES),
        cost_estimate=about(40),
    )(core, lanes(low, tile), lanes(high, tile), text, gains, *saved, *split_weights)


def lanes(values, size):
    return values.astype(jnp.int32).reshape(-1, 1, size)


def attend_call(q, k, v, columns, groups, heads, low, high, first, last, query_size, key_size):
    width = heads * HEAD
    rows, keys = q.shape[0], k.shape[0]
    blocks = rows // query_size
    spec = lambda size, column: pl.BlockSpec((size, width), lambda g, i, *_: (0, column + g))
    vector = pl.BlockSpec((1, 1, query_size), lambda g, i, *_: (i, 0, 0))
    q_column = columns[0]
    return pl.pallas_call(
        partial(attend_kernel, heads, key_size),
        grid_spec=pltpu.PrefetchScalarGridSpec(
            num_scalar_prefetch=2,
            grid=(groups, blocks),
            in_specs=[
                vector,
                vector,
                pl.BlockSpec((query_size, width), lambda g, i, *_: (i, q_column + g)),
                spec(keys, columns[1]),
                spec(keys, columns[2]),
            ],
            out_specs=[
                pl.BlockSpec((query_size, width), lambda g, i, *_: (i, g)),
                pl.BlockSpec((1, 1, heads, query_size), lambda g, i, *_: (g, i, 0, 0)),
            ],
            scratch_shapes=[
                pltpu.VMEM((keys // key_size, width, key_size), jnp.bfloat16),
                pltpu.VMEM((width, query_size), jnp.float32),
            ],
        ),
        out_shape=[
            jax.ShapeDtypeStruct((rows, groups * width), jnp.bfloat16),
            jax.ShapeDtypeStruct((groups, blocks, heads, query_size), jnp.float32),
        ],
        compiler_params=pltpu.CompilerParams(vmem_limit_bytes=VMEM_BYTES),
        cost_estimate=about(30 if groups == 1 else 17),
    )(first, last, lanes(low, query_size), lanes(high, query_size), q, k, v)


def back_scratch(heads, blocks, query_size, key_size):
    width = heads * HEAD
    return [
        pltpu.VMEM((blocks, heads, query_size, width), jnp.bfloat16),
        pltpu.VMEM((blocks, heads, query_size, width), jnp.bfloat16),
        pltpu.VMEM((width, key_size), jnp.bfloat16),
        pltpu.VMEM((blocks, heads, query_size), jnp.float32),
        pltpu.VMEM((blocks, width, query_size), jnp.float32),
        pltpu.VMEM((key_size, width), jnp.float32),
        pltpu.VMEM((key_size, width), jnp.float32),
    ]


def packed_back_call(
    qkv, out, parts, logs, heads, group, low, high, first, last, query_size, key_size
):
    rows, width = out.shape
    blocks = rows // query_size
    whole = lambda shape: pl.BlockSpec(shape, lambda g, j, *_: (0,) * len(shape))
    vector = whole((blocks, 1, query_size))
    return pl.pallas_call(
        partial(packed_back_kernel, heads, query_size, key_size, len(parts)),
        grid_spec=pltpu.PrefetchScalarGridSpec(
            num_scalar_prefetch=3,
            grid=(1, rows // key_size),
            in_specs=[vector, vector, whole(qkv.shape), whole(out.shape)]
            + [whole(part.shape) for part in parts]
            + [whole(logs.shape)],
            out_specs=whole(qkv.shape),
            scratch_shapes=back_scratch(heads, blocks, query_size, key_size)
            + [pltpu.VMEM(out.shape, jnp.bfloat16)],
        ),
        out_shape=jax.ShapeDtypeStruct(qkv.shape, jnp.bfloat16),
        compiler_params=pltpu.CompilerParams(vmem_limit_bytes=VMEM_BYTES),
        cost_estimate=about(30),
    )(
        first,
        last,
        group,
        lanes(low, query_size),
        lanes(high, query_size),
        qkv,
        out,
        *parts,
        logs,
    )


def attend_back_call(q, k, v, out, grad, logs, groups, heads, low, high, first, last, query_size, key_size):
    width = heads * HEAD
    rows, keys = q.shape[0], k.shape[0]
    blocks = rows // query_size
    column = lambda size: pl.BlockSpec((size, width), lambda g, j, *_: (0, g))
    vector = pl.BlockSpec((blocks, 1, query_size), lambda g, j, *_: (0, 0, 0))
    return pl.pallas_call(
        partial(attend_back_kernel, heads, query_size, key_size),
        grid_spec=pltpu.PrefetchScalarGridSpec(
            num_scalar_prefetch=2,
            grid=(groups, keys // key_size),
            in_specs=[
                vector,
                vector,
                column(rows),
                column(keys),
                column(keys),
                column(rows),
                column(rows),
                pl.BlockSpec((1, blocks, heads, query_size), lambda g, j, *_: (g, 0, 0, 0)),
            ],
            out_specs=[column(rows), column(keys), column(keys)],
            scratch_shapes=back_scratch(heads, blocks, query_size, key_size),
        ),
        out_shape=[
            jax.ShapeDtypeStruct((rows, groups * width), jnp.bfloat16),
            jax.ShapeDtypeStruct((keys, groups * width), jnp.bfloat16),
            jax.ShapeDtypeStruct((keys, groups * width), jnp.bfloat16),
        ],
        compiler_params=pltpu.CompilerParams(vmem_limit_bytes=VMEM_BYTES),
        cost_estimate=about(6 * groups),
    )(first, last, lanes(low, query_size), lanes(high, query_size), q, k, v, out, grad, logs)


def per_device(
    frames,
    text_states,
    clip_lengths,
    text_lengths,
    norm_gains,
    norm_biases,
    self_qkv,
    self_out,
    cross_query,
    cross_kv,
    cross_out,
    ffn_in,
    ffn_out,
    out_grad,
):
    groups = lax.axis_size("tensor")
    chips = lax.axis_size("chip")
    group = lax.axis_index("tensor")
    chip = lax.axis_index("chip")
    core = lax.axis_index("core")
    bf16 = jnp.bfloat16
    frame_count, width = frames.shape
    own_rows = frame_count // groups
    offset = group * own_rows
    clip_count, text_slots, text_width = text_states.shape
    head_count = self_out.shape[0] // HEAD
    all_heads = head_count * groups
    ends = jnp.cumsum(clip_lengths[0])
    starts = ends - clip_lengths[0]
    positions = jnp.arange(frame_count, dtype=jnp.int32)[:, None]
    clip_first = jnp.max(jnp.where(positions >= starts, starts, 0), axis=1)
    clip_stop = jnp.min(jnp.where(positions < ends, ends, frame_count), axis=1)
    block = min(256, own_rows)
    blocks = jnp.arange(frame_count // block, dtype=jnp.int32)
    self_low, self_high = clip_first, positions[:, 0]
    wide = min(2 * block, frame_count)
    wides = jnp.arange(frame_count // wide, dtype=jnp.int32)
    self_keys = (clip_first[::wide] // block, (wides * wide + wide - 1) // block)
    self_queries = (blocks * block // wide, (clip_stop[block - 1 :: block] - 1) // wide)
    own_positions = offset + jnp.arange(own_rows, dtype=jnp.int32)[:, None]
    own_clip = jnp.sum((own_positions >= ends).astype(jnp.int32), axis=1)
    own_length = jnp.sum(
        jnp.where(own_clip[:, None] == jnp.arange(clip_count), text_lengths[0], 0), axis=1
    )
    cross_low = own_clip * text_slots
    cross_high = cross_low + own_length - 1
    cross_keys = (own_clip[::block], own_clip[block - 1 :: block])
    inside_first = jnp.clip(starts - offset, 0, own_rows)
    inside_stop = jnp.clip(ends - offset, 0, own_rows)
    cross_first = jnp.minimum(inside_first // block, own_rows // block - 1)
    cross_queries = (
        cross_first,
        jnp.where(inside_stop > inside_first, (inside_stop - 1) // block, cross_first - 1),
    )

    head_width = head_count * HEAD
    local = pack_call(head_count, self_out, cross_query, cross_out, cross_kv)
    pieces = local.reshape(2, chips, -1, width)
    half = ffn_out.shape[0] // 2
    piece = half // chips
    core_index = core.reshape(1).astype(jnp.int32)
    sent_piece = pick(pick(pieces, core, 0), chip, 0)
    sent_piece, frames, self_qkv, ffn_in, ffn_out, out_grad = phase(
        sent_piece, frames, self_qkv, ffn_in, ffn_out, out_grad
    )
    passed = [shift(sent_piece, k) for k in range(1, groups)]
    ffn_own = ffn_pack_call(core_index, ffn_in, ffn_out, chips)
    ffn_piece = pick(ffn_own, chip, 0).reshape(2 * piece, width)
    own_frames = lax.dynamic_slice_in_dim(frames, offset, own_rows, 0)
    grad_own_bf = lax.dynamic_slice_in_dim(out_grad, offset, own_rows, 0)
    rows_one, packed, w_qkv = first_call(
        head_count, frames, norm_gains, norm_biases, self_qkv, block
    )
    packed, ffn_piece, own_frames, grad_own_bf, *passed = phase(
        packed, ffn_piece, own_frames, grad_own_bf, *passed
    )
    if head_width % 128 == 0:
        self_parts, self_columns = (packed,) * 3, (0, 1, 2)
    else:
        self_parts, self_columns = jnp.split(packed, 3, 1), (0, 0, 0)
    steps = axis_bits("chip")
    joined = chip_gather_start(jnp.stack(passed))
    flipped = chip_gather_flips(joined, 0)
    ffn_all = gather(ffn_piece[None], "tensor")
    self_mix, self_logs = attend_call(
        *self_parts, self_columns, 1, head_count, self_low, self_high, *self_keys, wide, block
    )
    joined = chip_gather_joins(joined, flipped, 0)
    self_mix, *joined = phase(self_mix, *joined)

    mix_blocks = self_mix.reshape(groups, own_rows, head_width)
    mixes = [pick(mix_blocks, group, 0)] + [
        shift(pick(mix_blocks, (group + k) % groups, 0), k) for k in range(1, groups)
    ]
    flipped = chip_gather_flips(joined, 1)
    joined = chip_gather_joins(joined, flipped, 1)
    for step in range(2, steps):
        joined = chip_gather_joins(joined, phase(*chip_gather_flips(joined, step)), step)
    mine = chip_gather_end(joined).reshape(groups - 1, -1, width)
    ffn_passed = [pick(ffn_all, (group + groups - k) % groups, 0) for k in range(1, groups)]
    ffn_stack = jnp.stack(ffn_passed[1:])[None]
    mine, ffn_stack, ffn_next, *mixes = phase(mine, ffn_stack, ffn_passed[0], *mixes)
    ffn_joined = chip_gather_start(ffn_next[None])
    ffn_late = gather(ffn_stack, "chip")
    ffn_late = ffn_late.reshape(chips, groups - 2, 2, piece, width)
    flipped = chip_gather_flips(ffn_joined, 0)
    ffn_joined = chip_gather_joins(ffn_joined, flipped, 0)
    far, *ffn_joined = phase(swap_core(mine), *ffn_joined)
    split_weights = (local, mine, far)
    ffn_flipped = chip_gather_flips(ffn_joined, 1)

    text_flat = text_states.reshape(clip_count * text_slots, text_width)
    shape = (head_count, block, core_index, cross_low, cross_high)
    after_self, after_cross, rows_two, rows_three, cross_q, cross_flat, cross_k, cross_v, cross_logs = (
        middle_call(
            *shape, own_frames, text_flat, norm_gains, norm_biases, split_weights, mixes
        )
    )

    grad_far = swap_core(grad_own_bf)
    rows_three, grad_far, *ffn_flipped = phase(rows_three, grad_far, *ffn_flipped)
    rows_far = swap_core(rows_three)
    ffn_joined = chip_gather_joins(ffn_joined, ffn_flipped, 1)
    for step in range(2, steps):
        ffn_joined = chip_gather_joins(ffn_joined, chip_gather_flips(ffn_joined, step), step)
    ffn_first = chip_gather_end(ffn_joined).reshape(chips, 2, piece, width)
    row_sets = (rows_three, rows_far, grad_own_bf, grad_far)
    ffn_part, *sums = ffn_call(*row_sets, (ffn_own, ffn_first), ())
    ffn_sum = scatter_sum(ffn_part.reshape(-1, 2 * half), "chip")
    ffn_late_part, out_own, out_far, third_own_grad, third_far = ffn_call(
        *row_sets, (ffn_late,), tuple(sums)
    )
    ffn_late_sum = scatter_sum(ffn_late_part.reshape(-1, 2 * half), "chip")
    saved = (
        third_own_grad,
        swap_core(third_far),
        grad_own_bf,
        after_self,
        after_cross,
        cross_q,
        cross_flat,
        cross_k,
        cross_v,
        cross_logs,
    )
    (
        cross_grad,
        cq_flat,
        ck_grad,
        cv_grad,
        self_side,
        self_grad,
        norm_part,
        text_part,
        *mix_grads,
    ) = middle_back_call(*shape, text_flat, norm_gains, saved, split_weights)

    mix_parts = [mix_grads[0]] + [shift(mix_grads[k], -k) for k in range(1, groups)]
    out_far = swap_core(out_far)
    arrays = (
        self_grad,
        rows_two,
        cq_flat,
        cross_flat,
        cross_grad,
        ck_grad,
        cv_grad,
        text_flat,
    )
    small_far = swap_core(weight_grads_call(head_count, 1 - core_index, arrays, mixes))
    small_part = weight_grads_call(head_count, core_index, arrays, mixes, (small_far,))

    def text_term(k):
        return pick(text_part, (group + groups - k) % groups, 0)

    orders = chip_orders()
    whole = chip_scatter_start(small_part.reshape(groups, chips, -1, width))
    state = settle(
        dict(
            whole=small_part,
            send=[chip_scatter_pick(whole[n], n, o, 0, True) for n, o in enumerate(orders)],
            text=text_term(1),
            out_far=out_far,
            ffn=list(ffn_sum.reshape(2, -1, 2 * half)),
            mix=mix_parts,
        )
    )
    mix_parts = state.pop("mix")
    text_run = shift(state["text"], 1)
    moved = [flip(one, o[0]) for one, o in zip(state["send"], orders)]
    ffn_run = shift(state["ffn"][1], 1)

    self_rest = (self_low, self_high, *self_queries, wide, block)
    if head_width % 128 == 0:
        packed_grad = packed_back_call(
            packed, self_mix, mix_parts, self_logs, head_count, group.reshape(1), *self_rest
        )
    else:
        mix_grad = jnp.concatenate([*mix_parts, *mix_parts], 0)
        mix_grad = lax.dynamic_slice_in_dim(
            mix_grad, (groups - group) % groups * own_rows, frame_count, 0
        )
        packed_grad = jnp.concatenate(
            attend_back_call(
                *self_parts, self_mix, mix_grad, self_logs, 1, head_count, *self_rest
            ),
            1,
        )
    state = settle(
        dict(
            state,
            grad=packed_grad,
            text=text_run,
            moved=moved,
            run=ffn_run,
            late=ffn_late_sum,
            h2=after_cross,
        )
    )

    def first_term(k):
        blocks = state["grad"].reshape(groups, own_rows, -1)
        rows = pick(blocks, (group + groups - k) % groups, 0)
        return times_transposed(rows, w_qkv)

    state = settle(dict(state, running=first_term(1).astype(bf16)))
    whole = chip_scatter_start(state["whole"].reshape(groups, chips, -1, width))
    small = [
        chip_scatter_pick(whole[n], n, o, 0, False) + one
        for n, (o, one) in enumerate(zip(orders, state["moved"]))
    ]
    late = list(state["late"].reshape(groups - 2, -1, 2 * half))
    state["run"] = state["run"] + late[0]
    ring_next = 1
    ffn_step = 0
    text_next = 2
    state["text"] = state["text"] + text_term(2)
    for hop in range(1, groups):
        arrived = shift(state["running"], 1)
        after_hop = dict(grad=state["grad"])
        if hop < steps:
            small = [
                chip_scatter_pick(one, n, o, hop, False)
                + flip(chip_scatter_pick(one, n, o, hop, True), o[hop])
                for n, (o, one) in enumerate(zip(orders, small))
            ]
            if hop == steps - 1:
                small = jnp.concatenate(small, 1)
        elif ring_next < groups:
            running_small = shift(small[1] if ring_next == 1 else state["ring"], 1)
            ring_next += 1
            after_hop["ring"] = running_small + small[ring_next % groups]
        after_hop["small"] = small
        after_hop["text"] = state["text"]
        if 1 < hop < groups - 1:
            text_next += 1
            after_hop["text"] = shift(state["text"], 1) + text_term(text_next % groups)
        if hop < groups - 1:
            after_hop["own"] = state["own"] if hop > 1 else state["ffn"][0]
            run = shift(state["run"], 1)
            after_hop["run"] = run + (late[hop] if hop < groups - 2 else after_hop["own"])
            late = after_hop["late"] = state["late"] if hop > 1 else late
        else:
            ffn = chip_gather_start(state["run"][None])
            after_hop["ffn"] = chip_gather_joins(ffn, chip_gather_flips(ffn, 0), 0)
            ffn_step = 1
        if hop == 1:
            mixed = state["h2"] + out_own + state["out_far"].astype(jnp.float32)
            after_hop["mixed"] = mixed.astype(bf16)
        else:
            after_hop["mixed"] = state["mixed"]
        if hop == 1:
            grad, run = phase(state["grad"], run)
            qkv_part = qkv_grad_call(rows_one, grad).reshape(2, width // 2, -1)
            far = swap_core(pick(qkv_part, 1 - core, 0))
            after_hop["qkv"] = pick(qkv_part, core, 0) + far
        elif hop - 2 < steps:
            after_hop["qkv"] = state["qkv"] + flip(state["qkv"], hop - 2)
        else:
            after_hop["qkv"] = state["qkv"]
        term = first_term((hop + 1) % groups)
        if hop < groups - 1:
            after_hop["running"] = (arrived.astype(jnp.float32) + term).astype(bf16)
        else:
            frames_grad, norm_first = last_call(own_frames, norm_gains, self_side, arrived, term)
            after_hop["frames_grad"] = frames_grad
            norm_rows = [norm_first[0:1], norm_part[1:3], norm_first[1:2], norm_part[4:6]]
            after_hop["norm"] = jnp.concatenate(norm_rows, 0).reshape(2, 3, width)
        state = settle(after_hop)
        small = state["small"]
        late = state.get("late")

    mixed, text = state["mixed"], state["text"]
    frames_grad, norm = state["frames_grad"], state["norm"]
    ring, ffn, qkv = state["ring"], state["ffn"], state["qkv"]
    small_step = norm_step = 0
    qkv_mine = qkv
    small_mine = small_far = small_grads = norm_parts = None
    ffn_mine = ffn_far = ffn_grads = qkv_far = qkv_grad = None
    small_sum = None
    while small_grads is None or ffn_grads is None or norm_parts is None or qkv_grad is None:
        if ring_next < groups:
            ring_next += 1
            ring = shift(ring, 1) + small[ring_next % groups]
        elif small_step < steps:
            small_sum = chip_gather_start(ring[None]) if small_sum is None else small_sum
            small_sum = chip_gather_joins(
                small_sum, chip_gather_flips(small_sum, small_step), small_step
            )
            small_step += 1
            if small_step == steps:
                small_mine = chip_gather_end(small_sum)[0].reshape(-1, width)
        elif small_far is None:
            small_far = swap_core(small_mine)
        elif small_grads is None:
            small_grads = small_end_call(
                head_count, text_width, core_index, small_mine, small_far
            )
        if norm_step == 0:
            norm = norm + swap_core(norm)
            norm_step += 1
        elif norm_step <= steps:
            norm = norm + flip(norm, norm_step - 1)
            norm_step += 1
        elif norm_parts is None:
            blocks_of = norm.reshape(2, 3, groups, -1)
            norm_parts = [pick(blocks_of, group, 2)] + [
                shift(pick(blocks_of, (group + k) % groups, 2), k) for k in range(1, groups)
            ]
        if ffn_step < steps:
            ffn = chip_gather_joins(ffn, chip_gather_flips(ffn, ffn_step), ffn_step)
            ffn_step += 1
        elif ffn_far is None:
            ffn_mine = chip_gather_end(ffn)[0]
            ffn_far = swap_core(ffn_mine)
        elif ffn_grads is None:
            ffn_grads = ffn_end_call(core_index, ffn_mine, ffn_far)
        if qkv_far is None:
            qkv_far = swap_core(qkv_mine)
        else:
            if qkv_grad is None:
                qkv_grad = qkv_end_call(head_count, core_index, qkv_mine, qkv_far)
            if text_next < groups:
                text_next += 1
                text = shift(text, 1) + text_term(text_next % groups)
        names = ["ring", "small", "small_sum", "small_mine", "small_far", "small_grads"]
        names += ["norm", "norm_parts", "ffn", "ffn_mine", "ffn_far", "ffn_grads"]
        names += ["text", "qkv_mine", "qkv_far", "qkv_grad"]
        values = (ring, small, small_sum, small_mine, small_far, small_grads, norm, norm_parts)
        values += (ffn, ffn_mine, ffn_far, ffn_grads, text, qkv_mine, qkv_far, qkv_grad)
        known = {name: one for name, one in zip(names, values) if one is not None}
        known = settle(known)
        ring, small, small_sum, small_mine, small_far, small_grads, norm, norm_parts = [
            known.get(name) for name in names[:8]
        ]
        ffn, ffn_mine, ffn_far, ffn_grads, text, qkv_mine, qkv_far, qkv_grad = [
            known.get(name) for name in names[8:]
        ]
    text_grad = text.astype(jnp.float32).reshape(clip_count, text_slots, -1)
    norm_grads = sum(norm_parts)
    ffn_in_grad, ffn_out_grad = ffn_grads
    so_grad, cq_grad, co_grad, kv_grad = small_grads
    return (
        mixed,
        frames_grad,
        text_grad,
        norm_grads,
        qkv_grad,
        so_grad,
        cq_grad,
        kv_grad,
        co_grad,
        ffn_in_grad,
        ffn_out_grad,
    )


def solution(mesh):
    rows, groups = mesh.devices.shape
    inner = Mesh(mesh.devices.reshape(rows // 2, 2, groups), ("chip", "core", "tensor"))
    data = ("chip", "core")
    in_specs = (
        P(data, None),
        P(data, None, None),
        P(data, None),
        P(data, None),
        P(),
        P(),
        P(None, "tensor"),
        P("tensor", None),
        P(None, "tensor"),
        P(None, "tensor"),
        P("tensor", None),
        P(None, "tensor"),
        P("tensor", None),
        P(data, None),
    )
    out_specs = (
        P((*data, "tensor"), None),
        P((*data, "tensor"), None),
        P(data, None, "tensor"),
        P(None, None, "tensor"),
        P(None, "tensor"),
        P("tensor", None),
        P(None, "tensor"),
        P(None, "tensor"),
        P("tensor", None),
        P(None, "tensor"),
        P("tensor", None),
    )
    return jax.shard_map(
        per_device, mesh=inner, in_specs=in_specs, out_specs=out_specs, check_vma=False
    )
```
